32 devices in a mesh: phi: 16 (over z, y, core), row: 2 (over x).
Axes of the slice: x: 2, y: 2, z: 4, core: 2. Of those that a mesh axis runs over, the one named last changes fastest.
Arguments:
- density: float32 [2, 512, 512], P(None, 'phi', 'row'), may hold values from 0.6 to 1.8
- momentum: float32 [2, 2, 512, 512], P(None, None, 'phi', 'row'), may hold values from -1 to 1
- magnetic: float32 [2, 2, 512, 512], P(None, None, 'phi', 'row'), may hold values from -1 to 1
- rotation: float32 [512], P('row'), may hold values from 1 to 4
- shifts: int32 [512], P('row'), may hold values from 8 to 56, as said below
Outputs:
- density_out: float32 [2, 512, 512], P(None, 'phi', 'row')
- momentum_out: float32 [2, 2, 512, 512], P(None, None, 'phi', 'row')
- magnetic_out: float32 [2, 2, 512, 512], P(None, None, 'phi', 'row')
The draws below stay inside these ranges and needn't reach their ends.
Inputs may be any that keep to these rules, and one draw needn't show every extreme that they name: shifts[r] = 8 + floor((47) d^2 / 511^2) + j_r with d = 511 - r and j_r either 0 or 1, except that row 0 shifts by exactly 56 and the last row by exactly 8.
All inputs are finite; a program needn't handle non-finite values.
Results may differ from the reference program's by a relative error of at most 0.0003.
Values sent between devices are 32-bit elements; how exact they have to be, the bound alone decides.
No kernel may reach another device: no remote copies, remote signals or barrier semaphores. Data moves between devices by JAX's collectives and lax.ppermute only.
A program may use at most 64 MiB of HBM per device.

```python
import math
import jax
import jax.numpy as jnp
from jax import lax

CPHI = 32
LEVELS = 2
STEPS = 2
SMIN = 8
SMAX = 56
NPHI = 512
NR = 512


def draw_shifts(key, part):
    radius_rows = jnp.arange(NR, dtype=jnp.int32)
    distance = NR - 1 - radius_rows
    spread = SMAX - SMIN - 1
    smooth_part = SMIN + spread * distance * distance // ((NR - 1) * (NR - 1))
    jitter = jax.random.randint(key, (NR,), 0, 2, dtype=jnp.int32)
    values = smooth_part + jitter
    values = values.at[0].set(SMAX).at[NR - 1].set(SMIN)
    return values.astype(jnp.int32)


def band_layout():
    radius_rows = jnp.arange(NR, dtype=jnp.int32)
    phi_cells = jnp.arange(NPHI, dtype=jnp.int32)
    middle = NR // 2
    radial_band = jnp.logical_and(radius_rows >= middle - 12, radius_rows < middle + 12)
    offset = phi_cells % CPHI
    phi_band = jnp.logical_or(offset < 6, offset >= CPHI - 6)
    radial_flip = jnp.where(radial_band, 1.0 - 2.0 * (radius_rows % 2).astype(jnp.float32), 1.0)
    phi_flip = jnp.where(phi_band, 1.0 - 2.0 * (phi_cells % 2).astype(jnp.float32), 1.0)
    pattern = phi_flip[:, None] * radial_flip[None, :]
    radial_mask = jnp.broadcast_to(radial_band[None, :], (NPHI, NR))
    phi_mask = jnp.broadcast_to(phi_band[:, None], (NPHI, NR))
    return (radial_mask, phi_mask, pattern)


def random_sign(key, shape):
    return jax.random.randint(key, shape, 0, 2, dtype=jnp.int32).astype(jnp.float32) * 2.0 - 1.0


def band_signs(key, leading):
    radial_mask, phi_mask, pattern = band_layout()
    keys = jax.random.split(key, 3)
    along_phi = random_sign(keys[0], leading + (NPHI, 1))
    along_rad = random_sign(keys[1], leading + (1, NR))
    shared = random_sign(keys[2], leading + (1, 1))
    both = jnp.logical_and(radial_mask, phi_mask)
    chosen = jnp.where(both, shared, jnp.where(radial_mask, along_phi, along_rad))
    return (chosen * pattern, jnp.logical_or(radial_mask, phi_mask))


def draw_density(key, part):
    base = jax.random.fold_in(key, 11)
    keys = jax.random.split(base, 4)
    shape = (LEVELS, NPHI, NR)
    signs, band_mask = band_signs(keys[0], (LEVELS,))
    high = jax.random.uniform(keys[1], shape, jnp.float32, 1.5, 1.8)
    low = jax.random.uniform(keys[2], shape, jnp.float32, 0.6, 0.8)
    banded = jnp.where(signs > 0.0, high, low)
    drawn = jax.random.uniform(keys[3], shape, jnp.float32, 0.6, 1.8)
    return jnp.where(band_mask[None], banded, drawn).astype(jnp.float32)


def draw_momentum(key, part):
    base = jax.random.fold_in(key, 23)
    keys = jax.random.split(base, 3)
    shape = (2, LEVELS, NPHI, NR)
    signs, band_mask = band_signs(keys[0], (2, LEVELS))
    banded = signs * jax.random.uniform(keys[1], shape, jnp.float32, 0.6, 1.0)
    drawn = jnp.clip(0.3 * jax.random.normal(keys[2], shape, jnp.float32), -1.0, 1.0)
    return jnp.where(band_mask[None, None], banded, drawn).astype(jnp.float32)


def draw_magnetic(key, part):
    base = jax.random.fold_in(key, 37)
    keys = jax.random.split(base, 3)
    shape = (2, LEVELS, NPHI, NR)
    signs, band_mask = band_signs(keys[0], (2, LEVELS))
    banded = signs * jax.random.uniform(keys[1], shape, jnp.float32, 0.6, 1.0)
    drawn = jnp.clip(0.3 * jax.random.normal(keys[2], shape, jnp.float32), -1.0, 1.0)
    return jnp.where(band_mask[None, None], banded, drawn).astype(jnp.float32)


def level_of(rng, extent, shards, least, high):
    factor_of, own = 1.0, jax.random.fold_in(rng, 6)
    for position, parts in shards:
        draws = jnp.exp(jax.random.uniform(jax.random.fold_in(own, position), (parts,), jnp.float32, least / len(shards), high / len(shards)))
        factor_of = factor_of * jnp.repeat(draws, extent[position] // parts).reshape([-1 if axis == position else 1 for axis in range(len(extent))])
    return factor_of


def setup_inputs(seed: int = 0) -> dict:
    splits = jax.random.split(jax.random.key(seed), 6)
    return {
        "density": draw_density(jax.random.fold_in(splits[5], 71), 0),
        "momentum": draw_momentum(jax.random.fold_in(splits[5], 71), 0),
        "magnetic": draw_magnetic(jax.random.fold_in(splits[5], 71), 0),
        "rotation": jnp.clip(jnp.exp(math.log(4.0) - 1.3862944 * jax.random.uniform(splits[3], (NR,), jnp.float32) ** level_of(splits[3], (NR,), ((0, 2),), -0.2, 0.2)), 1.0, 4.0),
        "shifts": draw_shifts(jax.random.fold_in(splits[5], 71), 0),
    }


time_step = 0.08
sound_sq = 1.0
block_rows = 128

def window(values, begin_at, end_at, along_axis):
    return lax.slice_in_dim(values, begin_at, values.shape[along_axis] + end_at, 1, along_axis)

def minmod(lower_jump, upper_jump):
    return 0.5 * (jnp.sign(lower_jump) + jnp.sign(upper_jump)) * jnp.minimum(jnp.abs(lower_jump), jnp.abs(upper_jump))

def physical(fields, normal):
    density, mom_phi, mom_rad, mag_phi, mag_rad = (fields[0], fields[1], fields[2], fields[3], fields[4])
    vel_phi = mom_phi / density
    vel_rad = mom_rad / density
    magnetic_sq = mag_phi * mag_phi + mag_rad * mag_rad
    pressure = sound_sq * density + 0.5 * magnetic_sq
    nothing = jnp.zeros_like(density)
    if normal == 0:
        fluxes = jnp.stack([mom_phi, mom_phi * vel_phi + pressure - mag_phi * mag_phi, mom_rad * vel_phi - mag_phi * mag_rad, nothing, mag_rad * vel_phi - mag_phi * vel_rad])
        normal_vel = vel_phi
    else:
        fluxes = jnp.stack([mom_rad, mom_phi * vel_rad - mag_phi * mag_rad, mom_rad * vel_rad + pressure - mag_rad * mag_rad, mag_phi * vel_rad - mag_rad * vel_phi, nothing])
        normal_vel = vel_rad
    speeds = jnp.abs(normal_vel) + jnp.sqrt(sound_sq + magnetic_sq / density)
    return (fluxes, speeds)

def interfaces(fields, along_axis, normal):
    differences = window(fields, 1, 0, along_axis) - window(fields, 0, -1, along_axis)
    slopes = minmod(window(differences, 0, -1, along_axis), window(differences, 1, 0, along_axis))
    centres = window(fields, 1, -1, along_axis)
    left_state = window(centres + 0.5 * slopes, 0, -1, along_axis)
    right_state = window(centres - 0.5 * slopes, 1, 0, along_axis)
    left_flux, left_speed = physical(left_state, normal)
    right_flux, right_speed = physical(right_state, normal)
    wave_bound = jnp.maximum(left_speed, right_speed)
    return 0.5 * (left_flux + right_flux) - 0.5 * wave_bound * (right_state - left_state)

def tendency(along_phi, along_rad, rotation):
    phi_flux = interfaces(along_phi, 2, 0)
    rad_flux = interfaces(along_rad, 3, 1)
    centre = window(along_phi, 2, -2, 2)
    change = -(window(phi_flux, 1, 0, 2) - window(phi_flux, 0, -1, 2)) - (window(rad_flux, 1, 0, 3) - window(rad_flux, 0, -1, 3))
    spin_rate = rotation[None, None, :]
    nothing = jnp.zeros_like(centre[0])
    source = jnp.stack([nothing, -0.5 * spin_rate * centre[2], 2.0 * spin_rate * centre[1], -1.5 * spin_rate * centre[4], nothing])
    return change + source

def blocked(fields, rotation):
    along_phi_all = jnp.concatenate([fields[:, :, -2:], fields, fields[:, :, :2]], axis=2)
    along_rad_all = jnp.concatenate([fields[..., :1], fields[..., :1], fields, fields[..., -1:], fields[..., -1:]], axis=3)
    block_count = NR // block_rows

    def one_block(number):
        first_row = number * block_rows
        phi_part = lax.dynamic_slice_in_dim(along_phi_all, first_row, block_rows, 3)
        rad_part = lax.dynamic_slice_in_dim(along_rad_all, first_row, block_rows + 4, 3)
        spin_part = lax.dynamic_slice_in_dim(rotation, first_row, block_rows, 0)
        return tendency(phi_part, rad_part, spin_part)
    result = lax.map(one_block, jnp.arange(block_count, dtype=jnp.int32))
    return jnp.moveaxis(result, 0, 3).reshape(fields.shape)

def fargo_shift(fields, shifts):
    cell_ids = jnp.arange(NPHI, dtype=jnp.int32)
    source_cell = (cell_ids[:, None] - shifts[None, :]) % NPHI
    return jnp.take_along_axis(fields, jnp.broadcast_to(source_cell, fields.shape), axis=2)

def reference(density, momentum, magnetic, rotation, shifts):
    fields = jnp.concatenate([density[None], momentum, magnetic], axis=0)
    for step_number in range(STEPS):
        first_section = fields + time_step * blocked(fields, rotation)
        second_section = 0.75 * fields + 0.25 * (first_section + time_step * blocked(first_section, rotation))
        third_section = fields / 3.0 + 2.0 / 3.0 * (second_section + time_step * blocked(second_section, rotation))
        fields = fargo_shift(third_section, shifts)
    return (fields[0], fields[1:3], fields[3:5])
```

```python
import functools

import jax
import jax.numpy as jnp
from jax import lax
from jax.experimental import pallas as pl
from jax.experimental.pallas import tpu as pltpu
from jax.sharding import PartitionSpec as P

STEPS = 2
SMIN = 8
SMAX = 56
STAGES = 3
REACH = 2 * STAGES
LANES = 128
SUB = 8
HALF = LANES // 2
SLOTS = 2 * SUB
CHUNK = 4
VMEM_LIMIT = 32 * 1024 * 1024

time_step = 0.08
sound_sq = 1.0


def shift_bound(first_row, rows):
    d = rows - 1 - first_row
    return min(SMIN + (SMAX - SMIN - 1) * d * d // ((rows - 1) * (rows - 1)) + 1, SMAX)


def minmod(lower, upper):
    return jnp.maximum(jnp.minimum(lower, 0.0), jnp.minimum(upper, jnp.maximum(lower, 0.0)))


def physical(state):
    rho, mn, mt, bn, bt = state
    inverse = 1.0 / rho
    vn = mn * inverse
    vt = mt * inverse
    bn_sq = bn * bn
    bt_sq = bt * bt
    flux_n = mn * vn + (sound_sq * rho + 0.5 * (bt_sq - bn_sq))
    flux_t = mt * vn - bn * bt
    flux_b = bt * vn - bn * vt
    inside = sound_sq + (bn_sq + bt_sq) * inverse
    speed = jnp.abs(vn) + inside * lax.rsqrt(inside)
    return (mn, flux_n, flux_t, None, flux_b), speed


def face_twice(left, right):
    left_flux, left_speed = physical(left)
    right_flux, right_speed = physical(right)
    bound = jnp.maximum(left_speed, right_speed)
    out = []
    for k in range(5):
        jump = bound * (right[k] - left[k])
        if left_flux[k] is None:
            out.append(-jump)
        else:
            out.append((left_flux[k] + right_flux[k]) - jump)
    return out


def swapped(five):
    return [five[0], five[2], five[1], five[4], five[3]]


def run_stage(start, src, dst, spin, lo, hi, keep, weight, edges):
    half_dt = 0.5 * time_step
    low_mask, high_mask, first, last = edges
    for f in range(5):
        row = lambda i: pl.ds(i * SUB, SUB)
        inner = src[f, row(first), :]
        outer = src[f, row(last), :]
        for k in (1, 2):
            src[f, row(first - k), :] = jnp.where(low_mask, inner, src[f, row(first - k), :])
            src[f, row(last + k), :] = jnp.where(high_mask, outer, src[f, row(last + k), :])

    def load(ref, f, i):
        if isinstance(i, int):
            return ref[f, i * SUB : (i + 1) * SUB, :]
        return ref[f, pl.ds(pl.multiple_of(i * SUB, SUB), SUB), :]

    def radial_states(rows):
        halves = [[0.5 * x for x in r] for r in rows]
        jumps = [[b - a for a, b in zip(p, q)] for p, q in zip(halves[:-1], halves[1:])]
        slopes = [[minmod(a, b) for a, b in zip(p, q)] for p, q in zip(jumps[:-1], jumps[1:])]
        upper = [[x + s for x, s in zip(r, sl)] for r, sl in zip(rows[1:-1], slopes)]
        lower = [[x - s for x, s in zip(r, sl)] for r, sl in zip(rows[1:-1], slopes)]
        return lower, upper

    def radial_faces(rows):
        lower, upper = radial_states(rows)
        return [
            swapped(face_twice(swapped(u), swapped(l))) for u, l in zip(upper[:-1], lower[1:])
        ]

    def azimuth_change(fields):
        right_of = lambda x: pltpu.roll(x, LANES - 1, 1)
        left_of = lambda x: pltpu.roll(x, 1, 1)
        lower = []
        upper = []
        for x in fields:
            half = 0.5 * x
            jump = right_of(half) - half
            slope = minmod(left_of(jump), jump)
            upper.append(x + slope)
            lower.append(right_of(x - slope))
        faces = face_twice(upper, lower)
        return [x - left_of(x) for x in faces]

    def work(i0, count, before):
        rows = [[load(src, f, i0 + k) for f in range(5)] for k in range(-1, count + 2)]
        faces = [before] + radial_faces(rows)
        for k in range(count):
            fields = rows[k + 1]
            change = azimuth_change(fields)
            i = i0 + k
            turn = load(spin, 0, i)
            source = [
                None,
                (-0.5 * turn) * fields[2],
                (2.0 * turn) * fields[1],
                (-1.5 * turn) * fields[4],
                None,
            ]
            for f in range(5):
                new = fields[f] - half_dt * (change[f] + (faces[k + 1][f] - faces[k][f]))
                if source[f] is not None:
                    new = new + source[f]
                if weight != 1.0:
                    new = weight * new + keep * load(start, f, i)
                if isinstance(i, int):
                    dst[f, i * SUB : (i + 1) * SUB, :] = new
                else:
                    dst[f, pl.ds(pl.multiple_of(i * SUB, SUB), SUB), :] = new
        return faces[-1]

    before = radial_faces([[load(src, f, lo + k) for f in range(5)] for k in range(-2, 2)])[0]
    if CHUNK >= hi - lo:
        work(lo, hi - lo, before)
    else:

        def step(c, carried):
            return tuple(work(lo + c * CHUNK, CHUNK, list(carried)))

        lax.fori_loop(0, (hi - lo) // CHUNK, step, tuple(before))


def step_kernel(
    plan, place, own, near, far, side, corner, spin_rows, shift_rows, out, far_out, edge_out, cells, a, b, c, spin, extra
):
    n, radius, own_cells, total, row_count, spare = plan
    row = place[0]
    lane = lax.broadcasted_iota(jnp.int32, (SUB, LANES), 1)
    sublane = lax.broadcasted_iota(jnp.int32, (SUB, LANES), 0)

    def bound_of(slot):
        d = (total - 1) - (row * radius + n * slot)
        smooth = lax.div((SMAX - SMIN - 1) * d * d, jnp.int32((total - 1) * (total - 1)))
        return jnp.minimum(SMIN + smooth + 1, SMAX)

    bounds = [bound_of(k) for k in range(SLOTS)]
    tall = n + 2 * SUB
    front = lax.broadcasted_iota(jnp.int32, (tall, LANES), 1) < HALF
    narrow = lax.broadcasted_iota(jnp.int32, (n, LANES), 1) < HALF

    for f in range(5):
        for part in range(radius // LANES):
            columns = slice(part * LANES, (part + 1) * LANES)
            if part == 0:
                top = far[f, 0:own_cells, :]
            else:
                rest = far[f, 0:SUB, :]
                top = jnp.concatenate(
                    [
                        jnp.zeros((own_cells - 2 * SUB, LANES), jnp.float32),
                        pltpu.roll(rest, SUB - spare, 0),
                        far[f, own_cells : own_cells + SUB, :],
                    ],
                    axis=0,
                )
            block = jnp.concatenate(
                [top, near[f, :, columns], own[f, :, columns], jnp.zeros((own_cells, LANES), jnp.float32)], axis=0
            )
            cells[f, SUB + part * LANES : SUB + (part + 1) * LANES, :] = block.T
        beside = jnp.where(
            lane < 2 * own_cells, pltpu.roll(corner[f], own_cells, 1), pltpu.roll(side[f], 2 * own_cells, 1)
        )
        cells[f, 0:SUB, :] = pltpu.roll(beside, SUB - REACH, 0)
        cells[f, SUB + radius : 2 * SUB + radius, :] = beside

    for j in range(SUB):
        low, high = j, SUB + j
        at = [slice(SUB - REACH + n * k, SUB - REACH + n * k + tall) for k in (low, high)]
        turn_low = (LANES - (2 * own_cells - REACH)) + bounds[low]
        turn_high = (HALF - (2 * own_cells - REACH)) + bounds[high]
        for f in range(5):
            a[f, pl.ds(j, tall, stride=SUB), :] = jnp.where(
                front, pltpu.roll(cells[f, at[0], :], turn_low, 1), pltpu.roll(cells[f, at[1], :], turn_high, 1)
            )
        spin[0, pl.ds(j, tall, stride=SUB), :] = jnp.where(front, spin_rows[at[0], :], spin_rows[at[1], :])
        extra[pl.ds(j, n, stride=SUB), :] = jnp.where(
            narrow,
            bounds[low] - shift_rows[n * low : n * low + n, :],
            bounds[high] - shift_rows[n * high : n * high + n, :],
        )

    first, last = REACH, REACH + n - 1
    edges = (
        (sublane == 0) & (lane < HALF) & (row == 0),
        (sublane == SUB - 1) & (lane >= HALF) & (row == row_count - 1),
        first,
        last,
    )
    run_stage(a, a, b, spin, 2, n + 10, 0.0, 1.0, edges)
    run_stage(a, b, c, spin, 4, n + 8, 0.75, 0.25, edges)
    run_stage(a, c, b, spin, 6, n + 6, 1.0 / 3.0, 2.0 / 3.0, edges)

    for i in range(n):
        more = extra[i * SUB : (i + 1) * SUB, :]
        picks = [((more >> bit) & 1) == 1 for bit in range(3)]
        for f in range(5):
            x = pltpu.roll(b[f, (REACH + i) * SUB : (REACH + i + 1) * SUB, :], LANES - REACH, 1)
            for bit in range(3):
                x = jnp.where(picks[bit], pltpu.roll(x, LANES - (1 << bit), 1), x)
            a[f, i * SUB : (i + 1) * SUB, :] = x
    for f in range(5):
        block = jnp.concatenate([a[f, pl.ds(j, n, stride=SUB), :] for j in range(SUB)], axis=0)
        turned = block.T
        low, high = turned[0:own_cells], turned[HALF : HALF + own_cells]
        out[f, :, 0:LANES] = low
        out[f, :, LANES : 2 * LANES] = high
        if far_out is not None:
            far_out[f, 0:own_cells, :] = low
            far_out[f, 0:SUB, :] = jnp.where(
                sublane < spare, pltpu.roll(high[own_cells - 2 * SUB : own_cells - SUB], spare, 0), low[0:SUB]
            )
            far_out[f, own_cells : own_cells + SUB, :] = high[own_cells - SUB : own_cells]
            final_rows = pltpu.roll(pltpu.roll(block[LANES - SUB : LANES], REACH, 0), HALF, 1)
            edge_out[f] = jnp.where(row == 0, final_rows, block[0:SUB])


def step_call(plan, operands, more):
    n, radius, own_cells, total, row_count, spare = plan
    shape = lambda *s: jax.ShapeDtypeStruct(s, jnp.float32)
    out_shape = [shape(5, own_cells, radius)]
    if more:
        out_shape += [shape(5, own_cells + SUB, LANES), shape(5, SUB, LANES)]

    def kernel(*refs):
        ins, rest = refs[:8], refs[8:]
        if more:
            outs, scratch = rest[:3], rest[3:]
        else:
            outs, scratch = (rest[0], None, None), rest[1:]
        step_kernel(plan, *ins, *outs, *scratch)

    stage = pltpu.VMEM((5, (n + 2 * SUB) * SUB, LANES), jnp.float32)
    vmem = pl.BlockSpec(memory_space=pltpu.VMEM)
    return pl.pallas_call(
        kernel,
        out_shape=out_shape,
        in_specs=[pl.BlockSpec(memory_space=pltpu.SMEM)] + [vmem] * 7,
        out_specs=[vmem] * len(out_shape),
        scratch_shapes=[
            pltpu.VMEM((5, radius + 3 * SUB, LANES), jnp.float32),
            stage,
            stage,
            stage,
            pltpu.VMEM((1, (n + 2 * SUB) * SUB, LANES), jnp.float32),
            pltpu.VMEM((n * SUB, LANES), jnp.int32),
        ],
        compiler_params=pltpu.CompilerParams(vmem_limit_bytes=VMEM_LIMIT),
        cost_estimate=pl.CostEstimate(flops=20_000_000, bytes_accessed=600_000, transcendentals=0),
        name="disc_step",
    )(*operands)


def body(density, momentum, magnetic, rotation, shifts):
    phi_count = lax.axis_size("phi")
    row_count = lax.axis_size("row")
    levels, own_cells, radius = density.shape
    total = radius * row_count
    n = radius // SLOTS
    need = [max(shift_bound(part * LANES, total) + REACH - own_cells, 0) for part in range(radius // LANES)]
    spare = own_cells - need[0]
    assert row_count == 2 and radius == 2 * LANES and own_cells == HALF // 2
    assert 0 < need[0] < own_cells and need[1] <= SUB + spare and spare <= SUB
    plan = (n, radius, own_cells, total, row_count, spare)

    row = lax.axis_index("row")
    place = jnp.reshape(row, (1,)).astype(jnp.int32)
    here = lambda p, r: (p % phi_count) * row_count + r
    everyone = [(p, r) for p in range(phi_count) for r in range(row_count)]
    both = ("phi", "row")
    send_near = lambda x: lax.ppermute(x, "phi", [(p, (p + 1) % phi_count) for p in range(phi_count)])
    send_far = lambda x: lax.ppermute(x, both, [(here(p, 0), here(p + 2, 0)) for p in range(phi_count)])
    send_side = lambda x: lax.ppermute(x, "row", [(0, 1), (1, 0)])
    send_corner = lambda x: lax.ppermute(x, both, [(here(p, r), here(p + 1, 1 - r)) for p, r in everyone])

    edge_spin = jnp.where(row == 0, rotation[radius - REACH :], rotation[:REACH])
    beside_spin = lax.ppermute(edge_spin, "row", [(0, 1), (1, 0)])
    gap = jnp.zeros((SUB - REACH,), rotation.dtype)
    spins = jnp.concatenate([gap, beside_spin, rotation, beside_spin, gap, jnp.zeros((SUB,), rotation.dtype)])
    spin_rows = jnp.broadcast_to((time_step * spins)[:, None], (radius + 3 * SUB, LANES))
    shift_rows = jnp.broadcast_to(shifts[:, None], (radius, LANES))

    states = []
    for level in range(levels):
        fields = jnp.concatenate([density[level][None], momentum[:, level], magnetic[:, level]], axis=0)
        far = jnp.concatenate(
            [
                fields[:, own_cells - SUB - spare : own_cells - SUB, LANES:],
                fields[:, spare:, :LANES],
                fields[:, own_cells - SUB :, LANES:],
            ],
            axis=1,
        )
        edge = jnp.where(row == 0, fields[..., radius - REACH :], fields[..., :REACH])
        edge = jnp.swapaxes(edge, 1, 2)
        edge = jnp.pad(edge, ((0, 0), (0, SUB - REACH), (0, LANES - own_cells)))
        states.append((fields, far, edge))

    for step in range(STEPS):
        moved = [(own, send_near(own), send_far(far), send_side(edge), send_corner(edge)) for own, far, edge in states]
        more = step < STEPS - 1
        states = []
        for own, near, far, side, corner in moved:
            states.append(step_call(plan, (place, own, near, far, side, corner, spin_rows, shift_rows), more))
    fields = jnp.stack([s[0] for s in states], axis=1)
    return (fields[0], fields[1:3], fields[3:5])


def solution(mesh):
    placed = (
        P(None, "phi", "row"),
        P(None, None, "phi", "row"),
        P(None, None, "phi", "row"),
        P("row"),
        P("row"),
    )
    return jax.shard_map(
        body,
        mesh=mesh,
        in_specs=placed,
        out_specs=(P(None, "phi", "row"), P(None, None, "phi", "row"), P(None, None, "phi", "row")),
        check_vma=False,
    )
```

```python
import jax
import jax.numpy as jnp
from jax import lax
from jax.experimental import pallas as pl
from jax.experimental.pallas import tpu as pltpu
from jax.sharding import PartitionSpec as P

STEPS = 2
SMIN = 8
SMAX = 56
STAGES = 3
REACH = 2 * STAGES
FIELDS = 5
LANES = 128
SUB = 8
HALF = LANES // 2
SLOTS = 2 * SUB
EXTRA = 2 * SUB
TALL = 32
BITS = 3
UNROLL = 64
VMEM_LIMIT = 32 * 1024 * 1024

time_step = 0.08
sound_sq = 1.0


def shift_bound(first_row, rows):
    d = rows - 1 - first_row
    return min(SMIN + (SMAX - SMIN - 1) * d * d // ((rows - 1) * (rows - 1)) + 1, SMAX)


def minmod(lower, upper):
    return jnp.maximum(jnp.minimum(lower, 0.0), jnp.minimum(upper, jnp.maximum(lower, 0.0)))


def physical(state):
    rho, mn, mt, bn, bt = state
    inverse = pltpu.reciprocal(rho, approx=True)
    vn = mn * inverse
    vt = mt * inverse
    bn_sq = bn * bn
    bt_sq = bt * bt
    flux_n = mn * vn + (sound_sq * rho + 0.5 * (bt_sq - bn_sq))
    flux_t = mt * vn - bn * bt
    flux_b = bt * vn - bn * vt
    inside = sound_sq + (bn_sq + bt_sq) * inverse
    speed = jnp.abs(vn) + inside * lax.rsqrt(inside)
    return (mn, flux_n, flux_t, None, flux_b), speed


def face_twice(left, right):
    left_flux, left_speed = physical(left)
    right_flux, right_speed = physical(right)
    bound = jnp.maximum(left_speed, right_speed)
    out = []
    for k in range(FIELDS):
        jump = bound * (right[k] - left[k])
        if left_flux[k] is None:
            out.append(-jump)
        else:
            out.append((left_flux[k] + right_flux[k]) - jump)
    return out


def swapped(five):
    return [five[0], five[2], five[1], five[4], five[3]]


def run_stage(start, src, dst, spin, lo, hi, keep, weight, edges):
    half_dt = 0.5 * time_step
    low_mask, high_mask, first, last = edges
    for f in range(FIELDS):
        row = lambda i: pl.ds(i * SUB, SUB)
        inner = src[f, row(first), :]
        outer = src[f, row(last), :]
        for k in (1, 2):
            src[f, row(first - k), :] = jnp.where(low_mask, inner, src[f, row(first - k), :])
            src[f, row(last + k), :] = jnp.where(high_mask, outer, src[f, row(last + k), :])

    def at(i):
        if isinstance(i, int):
            return pl.ds(i * SUB, SUB)
        return pl.ds(pl.multiple_of(i * SUB, SUB), SUB)

    def radial_faces(rows):
        halves = [[0.5 * x for x in r] for r in rows]
        jumps = [[b - a for a, b in zip(p, q)] for p, q in zip(halves[:-1], halves[1:])]
        slopes = [[minmod(a, b) for a, b in zip(p, q)] for p, q in zip(jumps[:-1], jumps[1:])]
        upper = [[x + s for x, s in zip(r, sl)] for r, sl in zip(rows[1:-1], slopes)]
        lower = [[x - s for x, s in zip(r, sl)] for r, sl in zip(rows[1:-1], slopes)]
        return [swapped(face_twice(swapped(u), swapped(l))) for u, l in zip(upper[:-1], lower[1:])]

    def azimuth_change(fields):
        right_of = lambda x: pltpu.roll(x, LANES - 1, 1)
        left_of = lambda x: pltpu.roll(x, 1, 1)
        lower = []
        upper = []
        for x in fields:
            half = 0.5 * x
            slope = minmod(half - left_of(half), right_of(half) - half)
            upper.append(x + slope)
            lower.append(right_of(x - slope))
        faces = face_twice(upper, lower)
        return [x - left_of(x) for x in faces]

    def work(i0, count, before):
        rows = [[src[f, at(i0 + k), :] for f in range(FIELDS)] for k in range(-1, count + 2)]
        faces = [before] + radial_faces(rows)
        for k in range(count):
            fields = rows[k + 1]
            change = azimuth_change(fields)
            i = i0 + k
            turn = spin[at(i), :]
            source = [
                None,
                (-0.5 * turn) * fields[2],
                (2.0 * turn) * fields[1],
                (-1.5 * turn) * fields[4],
                None,
            ]
            for f in range(FIELDS):
                new = fields[f] - half_dt * (change[f] + (faces[k + 1][f] - faces[k][f]))
                if source[f] is not None:
                    new = new + source[f]
                if weight != 1.0:
                    new = weight * new + keep * start[f, at(i), :]
                dst[f, at(i), :] = new
        return faces[-1]

    before = radial_faces([[src[f, at(lo + k), :] for f in range(FIELDS)] for k in range(-2, 2)])[0]
    if UNROLL >= hi - lo:
        work(lo, hi - lo, before)
    else:

        def step(c, carried):
            return tuple(work(lo + c * UNROLL, UNROLL, list(carried)))

        lax.fori_loop(0, (hi - lo) // UNROLL, step, tuple(before))


def spread(block, first, width):
    block = pltpu.roll(block, (LANES - first) % LANES, 1)
    lane = lax.broadcasted_iota(jnp.int32, block.shape, 1)
    while width < LANES:
        block = jnp.where(lane < width, block, pltpu.roll(block, width, 1))
        width *= 2
    return block


def pack_kernel(spare, place, density, momentum, magnetic, rotation, shifts, *outs):
    levels, own_cells, radius = density.shape
    nears, fars, edge, spin_rows, shift_rows = outs[:levels], outs[levels : 2 * levels], *outs[2 * levels :]
    on_low = place[0] == 0
    parts = radius // LANES
    for part in range(parts):
        rows = slice(part * LANES, (part + 1) * LANES)
        spin_rows[rows, :] = jnp.broadcast_to(rotation[part : part + 1, :], (LANES, LANES)).T * time_step
        shift_rows[rows, :] = jnp.broadcast_to(shifts[part : part + 1, :].astype(jnp.float32), (LANES, LANES)).T
    wide = lambda ref: jnp.broadcast_to(
        jnp.where(on_low, ref[parts - 1 : parts, :], ref[0:1, :]).astype(jnp.float32), (own_cells, LANES)
    )
    for level in range(levels):
        fields = [density[level], momentum[0, level], momentum[1, level], magnetic[0, level], magnetic[1, level]]
        for f, x in enumerate(fields):
            nears[level][f * own_cells : (f + 1) * own_cells, :] = x
            pack_far(fars[level], f, x[:, 0:LANES], x[:, LANES : 2 * LANES], spare)
        ends = [jnp.where(on_low, x[:, radius - LANES :], x[:, 0:LANES]) for x in fields]
        last = [ends[4], wide(rotation) * time_step, wide(shifts), jnp.zeros((own_cells, LANES), jnp.float32)]
        for side, group in enumerate((ends[:4], last)):
            turned = jnp.concatenate(group, axis=0).T
            edge[level * EXTRA : (level + 1) * EXTRA, side * LANES : (side + 1) * LANES] = jnp.where(
                on_low, turned[LANES - EXTRA :], turned[0:EXTRA]
            )


def pack_far(far, f, low, high, spare):
    own_cells = low.shape[0]
    base = f * (own_cells + SUB)
    sublane = lax.broadcasted_iota(jnp.int32, (SUB, LANES), 0)
    moved = pltpu.roll(high[own_cells - 2 * SUB : own_cells - SUB], spare, 0)
    far[base : base + SUB, :] = jnp.where(sublane < spare, moved, low[0:SUB])
    far[base + SUB : base + own_cells, :] = low[SUB:]
    far[base + own_cells : base + own_cells + SUB, :] = high[own_cells - SUB :]


def step_kernel(plan, refs, write, scratch):
    n, radius, own_cells, total, row_count, spare, moved = plan
    place, own, own_edge, near, near_edge, far, side, spin_rows, shift_rows = refs
    cells, a, b, c, spin, extra, packed = scratch
    row = place[0]
    on_low = row == 0
    lane = lax.broadcasted_iota(jnp.int32, (SUB, LANES), 1)
    sublane = lax.broadcasted_iota(jnp.int32, (SUB, LANES), 0)
    base = jnp.where(on_low, 0, -moved)
    own_at = pl.multiple_of(EXTRA - base, SUB)
    edge_at = pl.multiple_of(jnp.where(on_low, EXTRA + radius, moved), SUB)

    def bound_of(slot):
        d = (total - 1) - (row * radius + base + n * slot)
        smooth = lax.div((SMAX - SMIN - 1) * d * d, jnp.int32((total - 1) * (total - 1)))
        return jnp.minimum(SMIN + smooth + 1, SMAX)

    bounds = [bound_of(k) for k in range(SLOTS)]

    edge_lane = lax.broadcasted_iota(jnp.int32, (EXTRA, LANES), 1)
    for f in range(FIELDS):
        rows = slice(f * own_cells, (f + 1) * own_cells)
        start = f * (own_cells + SUB)
        for part in range(radius // LANES):
            columns = slice(part * LANES, (part + 1) * LANES)
            if part == 0:
                top = far[start : start + own_cells, :]
            else:
                top = jnp.concatenate(
                    [
                        jnp.zeros((own_cells - 2 * SUB, LANES), jnp.float32),
                        pltpu.roll(far[start : start + SUB, :], SUB - spare, 0),
                        far[start + own_cells : start + own_cells + SUB, :],
                    ],
                    axis=0,
                )
            block = jnp.concatenate(
                [top, near[rows, columns], own[rows, columns], jnp.zeros((own_cells, LANES), jnp.float32)], axis=0
            )
            cells[f, pl.ds(own_at + part * LANES, LANES), :] = block.T
        columns = slice(f // 4 * LANES, (f // 4 + 1) * LANES)
        lanes_at = f % 4 * own_cells
        cells[f, pl.ds(edge_at, EXTRA), :] = jnp.where(
            edge_lane < 2 * own_cells,
            pltpu.roll(near_edge[:, columns], (LANES + own_cells - lanes_at) % LANES, 1),
            pltpu.roll(own_edge[:, columns], (LANES + 2 * own_cells - lanes_at) % LANES, 1),
        )
    more = side[0:EXTRA, LANES : 2 * LANES]
    packed[0, pl.ds(own_at, radius), :] = spin_rows[...]
    packed[0, pl.ds(edge_at, EXTRA), :] = spread(more, own_cells, own_cells)
    packed[1, pl.ds(own_at, radius), :] = shift_rows[...]
    packed[1, pl.ds(edge_at, EXTRA), :] = spread(more, 2 * own_cells, own_cells)

    front = lax.broadcasted_iota(jnp.int32, (TALL, LANES), 1) < HALF
    for j in range(SUB):
        low, high = j, SUB + j
        at = [slice(EXTRA - REACH + n * k, EXTRA - REACH + n * k + TALL) for k in (low, high)]
        turn_low = (LANES - (2 * own_cells - REACH)) + bounds[low]
        turn_high = (HALF - (2 * own_cells - REACH)) + bounds[high]
        for f in range(FIELDS):
            a[f, pl.ds(j, TALL, stride=SUB), :] = jnp.where(
                front, pltpu.roll(cells[f, at[0], :], turn_low, 1), pltpu.roll(cells[f, at[1], :], turn_high, 1)
            )
        spin[pl.ds(j, TALL, stride=SUB), :] = jnp.where(front, packed[0, at[0], :], packed[0, at[1], :])
        behind = jnp.where(front, bounds[low], bounds[high]) - jnp.where(
            front, packed[1, at[0], :], packed[1, at[1], :]
        ).astype(jnp.int32)
        extra[pl.ds(j, TALL, stride=SUB), :] = behind

    first, last = REACH, REACH + n - 1
    edges = (
        (sublane == 0) & (lane < HALF) & on_low,
        (sublane == SUB - 1) & (lane >= HALF) & (row == row_count - 1),
        first,
        last,
    )
    run_stage(a, a, b, spin, 2, n + 10, 0.0, 1.0, edges)
    run_stage(a, b, c, spin, 4, n + 8, 0.75, 0.25, edges)
    run_stage(a, c, b, spin, 6, n + 6, 1.0 / 3.0, 2.0 / 3.0, edges)

    even = (lane // own_cells) % 2 == 0
    for i in range(n):
        rows = slice((REACH + i) * SUB, (REACH + i + 1) * SUB)
        behind = extra[rows, :]
        picks = [((behind >> bit) & 1) == 1 for bit in range(BITS)]
        turned = []
        for f in range(FIELDS):
            x = b[f, rows, :]
            for bit in range(BITS):
                x = jnp.where(picks[bit], pltpu.roll(x, LANES - (1 << bit), 1), x)
            turned.append(pltpu.roll(x, (LANES - REACH + f % 2 * own_cells) % LANES, 1))
        here = slice(i * SUB, (i + 1) * SUB)
        a[0, here, :] = jnp.where(even, turned[0], turned[1])
        a[1, here, :] = jnp.where(even, turned[2], turned[3])
        a[2, here, :] = turned[4]
    narrow = lax.broadcasted_iota(jnp.int32, (n, LANES), 1) < HALF
    for j in range(SUB):
        one, two, three = [a[g, pl.ds(j, n, stride=SUB), :] for g in range(3)]
        low = slice(EXTRA + n * j, EXTRA + n * (j + 1))
        high = slice(EXTRA + n * (SUB + j), EXTRA + n * (SUB + j + 1))
        packed[0, low, :] = jnp.where(narrow, one, pltpu.roll(two, HALF, 1))
        packed[0, high, :] = jnp.where(narrow, pltpu.roll(one, HALF, 1), two)
        packed[1, low, :] = three
        packed[1, high, :] = pltpu.roll(three, HALF, 1)
    for part in range(radius // LANES):
        rows = pl.ds(own_at + part * LANES, LANES)
        turned = packed[0, rows, :].T
        fourth = packed[1, rows, :].T
        write.fields(part, [turned[f * own_cells : (f + 1) * own_cells] for f in range(4)] + [fourth[0:own_cells]])
    write.rest(packed[0, pl.ds(edge_at, EXTRA), :], packed[1, pl.ds(edge_at, EXTRA), :])


class ToMessage:
    def __init__(self, near, far, spare):
        self.near, self.far, self.spare = near, far, spare
        self.low = None

    def fields(self, part, five):
        own_cells = five[0].shape[0]
        columns = slice(part * LANES, (part + 1) * LANES)
        for f, x in enumerate(five):
            self.near[f * own_cells : (f + 1) * own_cells, columns] = x
        if part == 0:
            self.low = five
        else:
            for f, (low, high) in enumerate(zip(self.low, five)):
                pack_far(self.far, f, low, high, self.spare)

    def rest(self, first, second):
        tail = self.near.shape[0] - EXTRA
        self.near[tail:, 0:LANES] = first
        self.near[tail:, LANES : 2 * LANES] = second


class ToResult:
    def __init__(self, density, momentum, magnetic):
        self.outs = (density, momentum, magnetic)

    def fields(self, part, five):
        columns = slice(part * LANES, (part + 1) * LANES)
        density, momentum, magnetic = self.outs
        density[0, :, columns] = five[0]
        for k in range(2):
            momentum[k, 0, :, columns] = five[1 + k]
            magnetic[k, 0, :, columns] = five[3 + k]

    def rest(self, first, second):
        pass


def step_scratch(n, radius):
    tall = EXTRA + SLOTS * n + 2 * SUB
    stage = pltpu.VMEM((FIELDS, TALL * SUB, LANES), jnp.float32)
    return [
        pltpu.VMEM((FIELDS, tall, LANES), jnp.float32),
        stage,
        stage,
        stage,
        pltpu.VMEM((TALL * SUB, LANES), jnp.float32),
        pltpu.VMEM((TALL * SUB, LANES), jnp.int32),
        pltpu.VMEM((2, tall, LANES), jnp.float32),
    ]


vmem = pl.BlockSpec(memory_space=pltpu.VMEM)
smem = pl.BlockSpec(memory_space=pltpu.SMEM)
f32 = lambda *s: jax.ShapeDtypeStruct(s, jnp.float32)
params = pltpu.CompilerParams(vmem_limit_bytes=VMEM_LIMIT)
cost = pl.CostEstimate(flops=20_000_000, bytes_accessed=600_000, transcendentals=0)


def first_step(plan, level, operands):
    n, radius, own_cells, total, row_count, spare, moved = plan
    edge_rows = slice(level * EXTRA, (level + 1) * EXTRA)

    def kernel(place, own, near, far, side, corner, spin_rows, shift_rows, near_out, far_out, *scratch):
        refs = (place, own, side.at[edge_rows], near, corner.at[edge_rows], far, side, spin_rows, shift_rows)
        step_kernel(plan, refs, ToMessage(near_out, far_out, spare), scratch)

    return pl.pallas_call(
        kernel,
        out_shape=[f32(FIELDS * own_cells + EXTRA, radius), f32(FIELDS * (own_cells + SUB), LANES)],
        in_specs=[smem] + [vmem] * 7,
        out_specs=[vmem] * 2,
        scratch_shapes=step_scratch(n, radius),
        compiler_params=params,
        cost_estimate=cost,
        name="first_step",
    )(*operands)


def last_step(plan, level, operands, results, levels):
    n, radius, own_cells, total, row_count, spare, moved = plan
    tail = slice(FIELDS * own_cells, FIELDS * own_cells + EXTRA)
    count = len(results)

    def kernel(place, own, near, far, side, spin_rows, shift_rows, *rest):
        outs, scratch = rest[count : count + 3], rest[count + 3 :]
        refs = (place, own, own.at[tail], near, near.at[tail], far, side, spin_rows, shift_rows)
        step_kernel(plan, refs, ToResult(*outs), scratch)

    pair = pl.BlockSpec((2, 1, own_cells, radius), lambda i: (0, level, 0, 0))
    return pl.pallas_call(
        kernel,
        grid=(1,),
        out_shape=[f32(levels, own_cells, radius), f32(2, levels, own_cells, radius), f32(2, levels, own_cells, radius)],
        in_specs=[smem] + [vmem] * 6 + [pl.BlockSpec(memory_space=pl.ANY)] * count,
        out_specs=[pl.BlockSpec((1, own_cells, radius), lambda i: (level, 0, 0)), pair, pair],
        scratch_shapes=step_scratch(n, radius),
        input_output_aliases={len(operands) + k: k for k in range(count)},
        compiler_params=params,
        cost_estimate=cost,
        name="last_step",
    )(*operands, *results)


def body(density, momentum, magnetic, rotation, shifts):
    phi_count = lax.axis_size("phi")
    row_count = lax.axis_size("row")
    levels, own_cells, radius = density.shape
    total = radius * row_count
    parts = radius // LANES
    n = radius // SLOTS
    need = [max(shift_bound(part * LANES, total) + REACH - own_cells, 0) for part in range(parts)]
    spare = own_cells - need[0]
    assert row_count == 2 and radius == 2 * LANES and own_cells == HALF // 2
    assert 0 < need[0] < own_cells and need[1] <= SUB + spare and spare <= SUB

    row = lax.axis_index("row")
    place = jnp.reshape(row, (1,)).astype(jnp.int32)
    here = lambda p, r: (p % phi_count) * row_count + r
    everyone = [(p, r) for p in range(phi_count) for r in range(row_count)]
    both = ("phi", "row")
    send_near = lambda x: lax.ppermute(x, "phi", [(p, (p + 1) % phi_count) for p in range(phi_count)])
    send_far = lambda x: lax.ppermute(x, both, [(here(p, 0), here(p + 2, 0)) for p in range(phi_count)])
    send_side = lambda x: lax.ppermute(x, "row", [(0, 1), (1, 0)])
    send_corner = lambda x: lax.ppermute(x, both, [(here(p, r), here(p + 1, 1 - r)) for p, r in everyone])

    message = f32(FIELDS * own_cells, radius)
    far_message = f32(FIELDS * (own_cells + SUB), LANES)
    packed = pl.pallas_call(
        lambda *refs: pack_kernel(spare, *refs),
        out_shape=[message] * levels
        + [far_message] * levels
        + [f32(levels * EXTRA, 2 * LANES), f32(radius, LANES), f32(radius, LANES)],
        in_specs=[smem] + [vmem] * 5,
        out_specs=[vmem] * (2 * levels + 3),
        compiler_params=params,
        name="pack",
    )(place, density, momentum, magnetic, rotation.reshape(parts, LANES), shifts.reshape(parts, LANES))
    owns, fars, (edge, spin_rows, shift_rows) = packed[:levels], packed[levels : 2 * levels], packed[2 * levels :]

    side = send_side(edge)
    corner = send_corner(edge)
    plan = (n + 1, radius, own_cells, total, row_count, spare, EXTRA)
    moved = [(send_near(own), send_far(far)) for own, far in zip(owns, fars)]
    states = []
    for level in range(levels):
        near, far = moved[level]
        states.append(first_step(plan, level, (place, owns[level], near, far, side, corner, spin_rows, shift_rows)))
    plan = (n, radius, own_cells, total, row_count, spare, 0)
    moved = [(send_near(own), send_far(far)) for own, far in states]
    results = ()
    for level in range(levels):
        near, far = moved[level]
        operands = (place, states[level][0], near, far, side, spin_rows, shift_rows)
        results = last_step(plan, level, operands, results, levels)
    return tuple(results)


def solution(mesh):
    placed = (
        P(None, "phi", "row"),
        P(None, None, "phi", "row"),
        P(None, None, "phi", "row"),
        P("row"),
        P("row"),
    )
    return jax.shard_map(
        body,
        mesh=mesh,
        in_specs=placed,
        out_specs=(P(None, "phi", "row"), P(None, None, "phi", "row"), P(None, None, "phi", "row")),
        check_vma=False,
    )
```

```python
import jax
import jax.numpy as jnp
from jax import lax
from jax.experimental import pallas as pl
from jax.experimental.pallas import tpu as pltpu
from jax.sharding import PartitionSpec as P

STEPS = 2
SMIN = 8
SMAX = 56
STAGES = 3
REACH = 2 * STAGES
FIELDS = 5
LANES = 128
SUB = 8
HALF = LANES // 2
SLOTS = 2 * SUB
EXTRA = 2 * SUB
TALL = 32
ROWS = 4
VMEM_LIMIT = 32 * 1024 * 1024

time_step = 0.08
sound_sq = 1.0


def shift_bound(first_row, rows):
    d = rows - 1 - first_row
    return min(SMIN + (SMAX - SMIN - 1) * d * d // ((rows - 1) * (rows - 1)) + 1, SMAX)


def minmod(lower, upper):
    return jnp.maximum(jnp.minimum(lower, 0.0), jnp.minimum(upper, jnp.maximum(lower, 0.0)))


def physical(state):
    rho, mn, mt, bn, bt = state
    inverse = pltpu.reciprocal(rho, approx=True)
    vn = mn * inverse
    vt = mt * inverse
    bn_sq = bn * bn
    bt_sq = bt * bt
    flux_n = mn * vn + (sound_sq * rho + 0.5 * (bt_sq - bn_sq))
    flux_t = mt * vn - bn * bt
    flux_b = bt * vn - bn * vt
    inside = sound_sq + (bn_sq + bt_sq) * inverse
    speed = jnp.abs(vn) + inside * lax.rsqrt(inside)
    return (mn, flux_n, flux_t, None, flux_b), speed


def face_twice(left, right):
    left_flux, left_speed = physical(left)
    right_flux, right_speed = physical(right)
    bound = jnp.maximum(left_speed, right_speed)
    out = []
    for k in range(FIELDS):
        jump = bound * (right[k] - left[k])
        if left_flux[k] is None:
            out.append(-jump)
        else:
            out.append((left_flux[k] + right_flux[k]) - jump)
    return out


def swapped(five):
    return [five[0], five[2], five[1], five[4], five[3]]


def radial_faces(rows):
    halves = [[0.5 * x for x in r] for r in rows]
    jumps = [[b - a for a, b in zip(p, q)] for p, q in zip(halves[:-1], halves[1:])]
    slopes = [[minmod(a, b) for a, b in zip(p, q)] for p, q in zip(jumps[:-1], jumps[1:])]
    upper = [[x + s for x, s in zip(r, sl)] for r, sl in zip(rows[1:-1], slopes)]
    lower = [[x - s for x, s in zip(r, sl)] for r, sl in zip(rows[1:-1], slopes)]
    return [swapped(face_twice(swapped(u), swapped(l))) for u, l in zip(upper[:-1], lower[1:])]


def azimuth_change(fields):
    right_of = lambda x: pltpu.roll(x, LANES - 1, 1)
    left_of = lambda x: pltpu.roll(x, 1, 1)
    lower = []
    upper = []
    for x in fields:
        half = 0.5 * x
        slope = minmod(half - left_of(half), right_of(half) - half)
        upper.append(x + slope)
        lower.append(right_of(x - slope))
    return [x - left_of(x) for x in face_twice(upper, lower)]


def tile(i):
    return pl.ds(pl.multiple_of(i * SUB, SUB), SUB)


def run_stages(n, levels, stages, edges):
    half_dt = 0.5 * time_step
    low_mask, high_mask = edges
    first, last = REACH, REACH + n - 1
    spin_at = levels * FIELDS

    def work(stage, i0, count, before):
        src, dst = stage, (stage & 1) + 1
        later = stage > 0
        weight = jnp.where(later, jnp.where(stage == 1, 0.25, 2.0 / 3.0), 1.0)
        keep = jnp.where(later, jnp.where(stage == 1, 0.75, 1.0 / 3.0), 0.0)
        load = lambda level, k: [stages[src, level * FIELDS + f, tile(i0 + k), :] for f in range(FIELDS)]
        rows = [[load(level, k) for k in range(-1, count + 2)] for level in range(levels)]
        turns = [stages[0, spin_at, tile(i0 + k), :] for k in range(count)]
        after = []
        for level in range(levels):
            faces = [before[level * FIELDS : (level + 1) * FIELDS]] + radial_faces(rows[level])
            for k in range(count):
                fields = rows[level][k + 1]
                change = azimuth_change(fields)
                turn = turns[k]
                source = [
                    None,
                    (-0.5 * turn) * fields[2],
                    (2.0 * turn) * fields[1],
                    (-1.5 * turn) * fields[4],
                    None,
                ]
                for f in range(FIELDS):
                    new = fields[f] - half_dt * (change[f] + (faces[k + 1][f] - faces[k][f]))
                    if source[f] is not None:
                        new = new + source[f]
                    at = level * FIELDS + f
                    stages[dst, at, tile(i0 + k), :] = weight * new + keep * stages[0, at, tile(i0 + k), :]
            after += faces[-1]
        return after

    def run(stage, _):
        for at in range(levels * FIELDS):
            inner = stages[stage, at, tile(first), :]
            outer = stages[stage, at, tile(last), :]
            for k in (1, 2):
                stages[stage, at, tile(first - k), :] = jnp.where(low_mask, inner, stages[stage, at, tile(first - k), :])
                stages[stage, at, tile(last + k), :] = jnp.where(high_mask, outer, stages[stage, at, tile(last + k), :])
        lo = 2 * stage + 2
        count = n + 2 * REACH - 4 - 4 * stage
        before = []
        for level in range(levels):
            rows = [[stages[stage, level * FIELDS + f, tile(lo + k), :] for f in range(FIELDS)] for k in range(-2, 2)]
            before += radial_faces(rows)[0]
        turns = lax.div(count + ROWS - 1, ROWS)
        lax.fori_loop(0, turns, lambda c, carried: tuple(work(stage, lo + c * ROWS, ROWS, list(carried))), tuple(before))
        return 0

    lax.fori_loop(0, STAGES, run, 0)


def spread(block, first, width):
    block = pltpu.roll(block, (LANES - first) % LANES, 1)
    lane = lax.broadcasted_iota(jnp.int32, block.shape, 1)
    while width < LANES:
        block = jnp.where(lane < width, block, pltpu.roll(block, width, 1))
        width *= 2
    return block


def pack_far(far, near, levels, own_cells, spare):
    sublane = lax.broadcasted_iota(jnp.int32, (SUB, LANES), 0)

    def one(k, _):
        level, f = lax.div(k, FIELDS), lax.rem(k, FIELDS)
        start = pl.multiple_of(f * own_cells, SUB)
        base = pl.multiple_of(f * (own_cells + SUB), SUB)
        low = near[level, pl.ds(start, own_cells), 0:LANES]
        high = near[level, pl.ds(start + own_cells - 2 * SUB, 2 * SUB), LANES : 2 * LANES]
        moved = pltpu.roll(high[0:SUB], spare, 0)
        far[level, pl.ds(base, SUB), :] = jnp.where(sublane < spare, moved, low[0:SUB])
        far[level, pl.ds(base + SUB, own_cells - SUB), :] = low[SUB:]
        far[level, pl.ds(base + own_cells, SUB), :] = high[SUB:]
        return 0

    lax.fori_loop(0, levels * FIELDS, one, 0)


def pack_kernel(spare, place, density, momentum, magnetic, rotation, shifts, near, far, edge, spin_rows, shift_rows, arrived):
    levels, own_cells, radius = density.shape
    on_low = place[0] == 0
    parts = radius // LANES
    copies = []
    for level in range(levels):
        sources = [density.at[level]] + [x.at[k, level] for x in (momentum, magnetic) for k in range(2)]
        for f, x in enumerate(sources):
            at = near.at[level, pl.ds(f * own_cells, own_cells), :]
            copies.append(pltpu.make_async_copy(x, at, arrived.at[level * FIELDS + f]))
    for copy in copies:
        copy.start()
    for part in range(parts):
        rows = slice(part * LANES, (part + 1) * LANES)
        spin_rows[rows, :] = jnp.broadcast_to(rotation[part : part + 1, :], (LANES, LANES)).T * time_step
        shift_rows[rows, :] = jnp.broadcast_to(shifts[part : part + 1, :].astype(jnp.float32), (LANES, LANES)).T
    wide = lambda ref: jnp.broadcast_to(
        jnp.where(on_low, ref[parts - 1 : parts, :], ref[0:1, :]).astype(jnp.float32), (own_cells, LANES)
    )
    for copy in copies:
        copy.wait()
    pack_far(far, near, levels, own_cells, spare)
    turn = wide(rotation) * time_step
    shift = wide(shifts)
    zero = jnp.zeros((own_cells, LANES), jnp.float32)

    def ends(level, _):
        rows = near[level, 0 : FIELDS * own_cells, :]
        block = jnp.where(on_low, rows[:, radius - LANES :], rows[:, 0:LANES])
        split = 4 * own_cells
        for side, group in enumerate((block[0:split], jnp.concatenate([block[split:], turn, shift, zero], axis=0))):
            turned = group.T
            edge[level, :, side * LANES : (side + 1) * LANES] = jnp.where(on_low, turned[LANES - EXTRA :], turned[0:EXTRA])
        return 0

    lax.fori_loop(0, levels, ends, 0)


def step_kernel(plan, refs, write, scratch):
    n, levels, radius, own_cells, total, row_count, spare, moved = plan
    place, own, own_edge, near, near_edge, far, side, spin_rows, shift_rows = refs
    cells, stages, packed = scratch
    row = place[0]
    on_low = row == 0
    lane = lax.broadcasted_iota(jnp.int32, (SUB, LANES), 1)
    sublane = lax.broadcasted_iota(jnp.int32, (SUB, LANES), 0)
    base = jnp.where(on_low, 0, -moved)
    own_at = pl.multiple_of(EXTRA - base, SUB)
    edge_at = pl.multiple_of(jnp.where(on_low, EXTRA + radius, moved), SUB)
    bounds = []
    for k in range(SLOTS):
        known = [shift_bound(r * radius - (moved if r else 0) + n * k, total) for r in range(row_count)]
        bounds.append(jnp.where(on_low, known[0], known[1]))

    edge_lane = lax.broadcasted_iota(jnp.int32, (EXTRA, LANES), 1)
    parts = radius // LANES

    def gather(k, _):
        level, f = lax.div(k, FIELDS), lax.rem(k, FIELDS)
        rows = pl.ds(pl.multiple_of(f * own_cells, SUB), own_cells)
        start = pl.multiple_of(f * (own_cells + SUB), SUB)
        for part in range(parts):
            columns = slice(part * LANES, (part + 1) * LANES)
            if part == 0:
                top = far[level, pl.ds(start, own_cells), :]
            else:
                top = jnp.concatenate(
                    [
                        jnp.zeros((own_cells - 2 * SUB, LANES), jnp.float32),
                        pltpu.roll(far[level, pl.ds(start, SUB), :], SUB - spare, 0),
                        far[level, pl.ds(start + own_cells, SUB), :],
                    ],
                    axis=0,
                )
            fill = jnp.zeros((own_cells, LANES), jnp.float32)
            block = jnp.concatenate([top, near[level, rows, columns], own[level, rows, columns], fill], axis=0)
            cells[k, pl.ds(own_at + part * LANES, LANES), :] = block.T
        columns = pl.ds(pl.multiple_of(lax.div(f, 4) * LANES, LANES), LANES)
        lanes_at = lax.rem(f, 4) * own_cells
        cells[k, pl.ds(edge_at, EXTRA), :] = jnp.where(
            edge_lane < 2 * own_cells,
            pltpu.roll(near_edge[level, :, columns], lax.rem(LANES + own_cells - lanes_at, LANES), 1),
            pltpu.roll(own_edge[level, :, columns], lax.rem(LANES + 2 * own_cells - lanes_at, LANES), 1),
        )
        return 0

    lax.fori_loop(0, levels * FIELDS, gather, 0)
    spin_at = levels * FIELDS
    more = side[0, :, LANES : 2 * LANES]
    cells[spin_at, pl.ds(own_at, radius), :] = spin_rows[...]
    cells[spin_at, pl.ds(edge_at, EXTRA), :] = spread(more, own_cells, own_cells)
    cells[spin_at + 1, pl.ds(own_at, radius), :] = shift_rows[...]
    cells[spin_at + 1, pl.ds(edge_at, EXTRA), :] = spread(more, 2 * own_cells, own_cells)

    front = lax.broadcasted_iota(jnp.int32, (TALL, LANES), 1) < HALF

    def deal(k, _):
        for j in range(SUB):
            low, high = j, SUB + j
            at = [slice(EXTRA - REACH + n * b, EXTRA - REACH + n * b + TALL) for b in (low, high)]
            turn_low = (LANES - (2 * own_cells - REACH)) + bounds[low]
            turn_high = (HALF - (2 * own_cells - REACH)) + bounds[high]
            stages[0, k, pl.ds(j, TALL, stride=SUB), :] = jnp.where(
                front, pltpu.roll(cells[k, at[0], :], turn_low, 1), pltpu.roll(cells[k, at[1], :], turn_high, 1)
            )
        return 0

    lax.fori_loop(0, levels * FIELDS + 2, deal, 0)

    edges = (
        (sublane == 0) & (lane < HALF) & on_low,
        (sublane == SUB - 1) & (lane >= HALF) & (row == row_count - 1),
    )
    run_stages(n, levels, stages, edges)

    bound = jnp.zeros((SUB, LANES), jnp.int32)
    for j in range(SUB):
        bound = jnp.where(sublane == j, jnp.where(lane < HALF, bounds[j], bounds[SUB + j]), bound)
    even = (lane & own_cells) == 0

    def shift(i, _):
        rows = tile(REACH + i)
        source = (lane + (REACH + bound)) - stages[0, spin_at + 1, rows, :].astype(jnp.int32)
        picks = [source & (LANES - 1), (source - own_cells) & (LANES - 1)]
        for level in range(levels):
            turned = [
                jnp.take_along_axis(
                    stages[1, level * FIELDS + f, rows, :], picks[f % 2], axis=1, mode="promise_in_bounds"
                )
                for f in range(FIELDS)
            ]
            stages[2, level * FIELDS, tile(i), :] = jnp.where(even, turned[0], turned[1])
            stages[2, level * FIELDS + 1, tile(i), :] = jnp.where(even, turned[2], turned[3])
            stages[2, level * FIELDS + 2, tile(i), :] = turned[4]
        return 0

    lax.fori_loop(0, n, shift, 0)
    narrow = lax.broadcasted_iota(jnp.int32, (n, LANES), 1) < HALF

    def finish(level, _):
        for j in range(SUB):
            one, two, three = [stages[2, level * FIELDS + g, pl.ds(j, n, stride=SUB), :] for g in range(3)]
            low = slice(EXTRA + n * j, EXTRA + n * (j + 1))
            high = slice(EXTRA + n * (SUB + j), EXTRA + n * (SUB + j + 1))
            packed[0, low, :] = jnp.where(narrow, one, pltpu.roll(two, HALF, 1))
            packed[0, high, :] = jnp.where(narrow, pltpu.roll(one, HALF, 1), two)
            packed[1, low, :] = three
            packed[1, high, :] = pltpu.roll(three, HALF, 1)
        for part in range(parts):
            rows = pl.ds(own_at + part * LANES, LANES)
            write.fields(level, slice(part * LANES, (part + 1) * LANES), packed[0, rows, :].T, packed[1, rows, :].T)
        write.edge(level, packed[0, pl.ds(edge_at, EXTRA), :], packed[1, pl.ds(edge_at, EXTRA), :])
        return 0

    lax.fori_loop(0, levels, finish, 0)
    write.end()


class ToMessage:
    def __init__(self, near, far, own_cells, spare):
        self.near, self.far, self.own_cells, self.spare = near, far, own_cells, spare

    def fields(self, level, columns, four, fifth):
        split = 4 * self.own_cells
        self.near[level, 0:split, columns] = four
        self.near[level, split : split + self.own_cells, columns] = fifth[0 : self.own_cells]

    def edge(self, level, first, second):
        tail = FIELDS * self.own_cells
        self.near[level, tail : tail + EXTRA, 0:LANES] = first
        self.near[level, tail : tail + EXTRA, LANES : 2 * LANES] = second

    def end(self):
        pack_far(self.far, self.near, self.near.shape[0], self.own_cells, self.spare)


class ToResult:
    def __init__(self, density, momentum, magnetic):
        self.outs = (density, momentum, magnetic)

    def fields(self, level, columns, four, fifth):
        density, momentum, magnetic = self.outs
        cells = density.shape[1]
        density[level, :, columns] = four[0:cells]
        momentum[0, level, :, columns] = four[cells : 2 * cells]
        momentum[1, level, :, columns] = four[2 * cells : 3 * cells]
        magnetic[0, level, :, columns] = four[3 * cells : 4 * cells]
        magnetic[1, level, :, columns] = fifth[0:cells]

    def edge(self, level, first, second):
        pass

    def end(self):
        pass


def step_scratch(n, levels):
    tall = EXTRA + SLOTS * n + 2 * SUB
    count = levels * FIELDS + 2
    return [
        pltpu.VMEM((count, tall, LANES), jnp.float32),
        pltpu.VMEM((STAGES, count, TALL * SUB, LANES), jnp.float32),
        pltpu.VMEM((2, tall, LANES), jnp.float32),
    ]


vmem = pl.BlockSpec(memory_space=pltpu.VMEM)
smem = pl.BlockSpec(memory_space=pltpu.SMEM)
f32 = lambda *s: jax.ShapeDtypeStruct(s, jnp.float32)
params = pltpu.CompilerParams(vmem_limit_bytes=VMEM_LIMIT)
cost = pl.CostEstimate(flops=20_000_000, bytes_accessed=600_000, transcendentals=0)


def first_step(plan, operands):
    n, levels, radius, own_cells, total, row_count, spare, moved = plan

    def kernel(place, own, near, far, side, corner, spin_rows, shift_rows, near_out, far_out, *scratch):
        refs = (place, own, side, near, corner, far, side, spin_rows, shift_rows)
        step_kernel(plan, refs, ToMessage(near_out, far_out, own_cells, spare), scratch)

    return pl.pallas_call(
        kernel,
        out_shape=[f32(levels, FIELDS * own_cells + EXTRA, radius), f32(levels, FIELDS * (own_cells + SUB), LANES)],
        in_specs=[smem] + [vmem] * 7,
        out_specs=[vmem] * 2,
        scratch_shapes=step_scratch(n, levels),
        compiler_params=params,
        cost_estimate=cost,
        name="first_step",
    )(*operands)


def last_step(plan, operands):
    n, levels, radius, own_cells, total, row_count, spare, moved = plan
    tail = pl.ds(FIELDS * own_cells, EXTRA)

    def kernel(place, own, near, far, side, spin_rows, shift_rows, density, momentum, magnetic, *scratch):
        edge_of = lambda ref: ref.at[:, tail, :]
        refs = (place, own, edge_of(own), near, edge_of(near), far, side, spin_rows, shift_rows)
        step_kernel(plan, refs, ToResult(density, momentum, magnetic), scratch)

    return pl.pallas_call(
        kernel,
        out_shape=[f32(levels, own_cells, radius), f32(2, levels, own_cells, radius), f32(2, levels, own_cells, radius)],
        in_specs=[smem] + [vmem] * 6,
        out_specs=[vmem] * 3,
        scratch_shapes=step_scratch(n, levels),
        compiler_params=params,
        cost_estimate=cost,
        name="last_step",
    )(*operands)


def body(density, momentum, magnetic, rotation, shifts):
    phi_count = lax.axis_size("phi")
    row_count = lax.axis_size("row")
    levels, own_cells, radius = density.shape
    total = radius * row_count
    parts = radius // LANES
    n = radius // SLOTS
    need = [max(shift_bound(part * LANES, total) + REACH - own_cells, 0) for part in range(parts)]
    spare = own_cells - need[0]
    assert row_count == 2 and radius == 2 * LANES and own_cells == HALF // 2
    assert 0 < need[0] < own_cells and need[1] <= SUB + spare and spare <= SUB

    row = lax.axis_index("row")
    place = jnp.reshape(row, (1,)).astype(jnp.int32)
    here = lambda p, r: (p % phi_count) * row_count + r
    everyone = [(p, r) for p in range(phi_count) for r in range(row_count)]
    both = ("phi", "row")
    send_near = lambda x: lax.ppermute(x, "phi", [(p, (p + 1) % phi_count) for p in range(phi_count)])
    send_far = lambda x: lax.ppermute(x, both, [(here(p, 0), here(p + 2, 0)) for p in range(phi_count)])
    send_side = lambda x: lax.ppermute(x, "row", [(0, 1), (1, 0)])
    send_corner = lambda x: lax.ppermute(x, both, [(here(p, r), here(p + 1, 1 - r)) for p, r in everyone])

    own, far, edge, spin_rows, shift_rows = pl.pallas_call(
        lambda *refs: pack_kernel(spare, *refs),
        out_shape=[
            f32(levels, FIELDS * own_cells, radius),
            f32(levels, FIELDS * (own_cells + SUB), LANES),
            f32(levels, EXTRA, 2 * LANES),
            f32(radius, LANES),
            f32(radius, LANES),
        ],
        in_specs=[smem] + [pl.BlockSpec(memory_space=pl.ANY)] * 3 + [vmem] * 2,
        out_specs=[vmem] * 5,
        scratch_shapes=[pltpu.SemaphoreType.DMA((levels * FIELDS,))],
        compiler_params=params,
        name="pack",
    )(place, density, momentum, magnetic, rotation.reshape(parts, LANES), shifts.reshape(parts, LANES))

    side = send_side(edge)
    corner = send_corner(edge)
    plan = (n + 1, levels, radius, own_cells, total, row_count, spare, EXTRA)
    own, far = first_step(plan, (place, own, send_near(own), send_far(far), side, corner, spin_rows, shift_rows))
    plan = (n, levels, radius, own_cells, total, row_count, spare, 0)
    return tuple(last_step(plan, (place, own, send_near(own), send_far(far), side, spin_rows, shift_rows)))


def solution(mesh):
    placed = (
        P(None, "phi", "row"),
        P(None, None, "phi", "row"),
        P(None, None, "phi", "row"),
        P("row"),
        P("row"),
    )
    return jax.shard_map(
        body,
        mesh=mesh,
        in_specs=placed,
        out_specs=(P(None, "phi", "row"), P(None, None, "phi", "row"), P(None, None, "phi", "row")),
        check_vma=False,
    )
```

```python
import jax
import jax.numpy as jnp
from jax import lax
from jax.experimental import pallas as pl
from jax.experimental.pallas import tpu as pltpu
from jax.sharding import PartitionSpec as P

STEPS = 2
SMIN = 8
SMAX = 56
STAGES = 3
REACH = 2 * STAGES
FIELDS = 5
LANES = 128
SUB = 8
HALF = LANES // 2
SLOTS = 2 * SUB
EXTRA = 2 * SUB
TALL = 32
ROWS = 4
VMEM_LIMIT = 32 * 1024 * 1024

time_step = 0.08


def shift_bound(first_row, rows):
    d = rows - 1 - first_row
    return min(SMIN + (SMAX - SMIN - 1) * d * d // ((rows - 1) * (rows - 1)) + 1, SMAX)


def minmod(lower, upper):
    return jnp.maximum(jnp.minimum(lower, 0.0), jnp.minimum(upper, jnp.maximum(lower, 0.0)))


def physical(state):
    rho, mn, mt, bn, bt = state
    inverse = pltpu.reciprocal(rho, approx=True)
    vn = mn * inverse
    vt = mt * inverse
    bn_sq = bn * bn
    bt_sq = bt * bt
    ram = mn * vn + rho
    tension = bt_sq - bn_sq
    flux_t = mt * vn - bn * bt
    flux_b = bt * vn - bn * vt
    inside = (bn_sq + bt_sq) * inverse + 1.0
    speed = jnp.abs(vn) + inside * lax.rsqrt(inside)
    return ram, tension, flux_t, flux_b, speed


def face_twice(left, right):
    left_ram, left_tension, left_t, left_b, left_speed = physical(left)
    right_ram, right_tension, right_t, right_b, right_speed = physical(right)
    bound = jnp.maximum(left_speed, right_speed)
    jumps = [bound * (l - r) for l, r in zip(left, right)]
    return [
        (left[1] + right[1]) + jumps[0],
        ((left_ram + right_ram) + 0.5 * (left_tension + right_tension)) + jumps[1],
        (left_t + right_t) + jumps[2],
        jumps[3],
        (left_b + right_b) + jumps[4],
    ]


def swapped(five):
    return [five[0], five[2], five[1], five[4], five[3]]


def radial_faces(rows):
    halves = [[0.5 * x for x in r] for r in rows]
    jumps = [[b - a for a, b in zip(p, q)] for p, q in zip(halves[:-1], halves[1:])]
    slopes = [[minmod(a, b) for a, b in zip(p, q)] for p, q in zip(jumps[:-1], jumps[1:])]
    upper = [[x + s for x, s in zip(r, sl)] for r, sl in zip(rows[1:-1], slopes)]
    lower = [[x - s for x, s in zip(r, sl)] for r, sl in zip(rows[1:-1], slopes)]
    return [swapped(face_twice(swapped(u), swapped(l))) for u, l in zip(upper[:-1], lower[1:])]


def azimuth_change(fields):
    right_of = lambda x: pltpu.roll(x, LANES - 1, 1)
    left_of = lambda x: pltpu.roll(x, 1, 1)
    lower = []
    upper = []
    for x in fields:
        half = 0.5 * x
        jump = right_of(half) - half
        slope = minmod(left_of(jump), jump)
        upper.append(x + slope)
        lower.append(right_of(x - slope))
    return [x - left_of(x) for x in face_twice(upper, lower)]


def tile(i):
    return pl.ds(pl.multiple_of(i * SUB, SUB), SUB)


def run_stages(n, stages, spin, edges):
    half_dt = 0.5 * time_step
    low_mask, high_mask = edges
    first, last = REACH, REACH + n - 1

    def work(stage, i0, count, before):
        src, dst = stage, (stage & 1) + 1
        weight = jnp.where(stage == 0, 1.0, jnp.where(stage == 1, 0.25, 2.0 / 3.0))
        keep = jnp.where(stage == 0, 0.0, jnp.where(stage == 1, 0.75, 1.0 / 3.0))
        rows = [[stages[src, f, tile(i0 + k), :] for f in range(FIELDS)] for k in range(-1, count + 2)]
        starts = [[stages[0, f, tile(i0 + k), :] for f in range(FIELDS)] for k in range(count)]
        turns = [spin[tile(i0 + k), :] for k in range(count)]
        faces = [before] + radial_faces(rows)
        for k in range(count):
            fields = rows[k + 1]
            change = azimuth_change(fields)
            turn = turns[k]
            source = [
                None,
                (-0.5 * turn) * fields[2],
                (2.0 * turn) * fields[1],
                (-1.5 * turn) * fields[4],
                None,
            ]
            for f in range(FIELDS):
                new = fields[f] - half_dt * (change[f] + (faces[k + 1][f] - faces[k][f]))
                if source[f] is not None:
                    new = new + source[f]
                stages[dst, f, tile(i0 + k), :] = weight * new + keep * starts[k][f]
        return faces[-1]

    def run(stage, _):
        for f in range(FIELDS):
            inner = stages[stage, f, tile(first), :]
            outer = stages[stage, f, tile(last), :]
            for k in (1, 2):
                stages[stage, f, tile(first - k), :] = jnp.where(low_mask, inner, stages[stage, f, tile(first - k), :])
                stages[stage, f, tile(last + k), :] = jnp.where(high_mask, outer, stages[stage, f, tile(last + k), :])
        lo = 2 * stage + 2
        count = n + 2 * REACH - 4 - 4 * stage
        before = radial_faces([[stages[stage, f, tile(lo + k), :] for f in range(FIELDS)] for k in range(-2, 2)])[0]
        turns = lax.div(count + ROWS - 1, ROWS)
        lax.fori_loop(0, turns, lambda c, carried: tuple(work(stage, lo + c * ROWS, ROWS, list(carried))), tuple(before))
        return 0

    lax.fori_loop(0, STAGES, run, 0)


def spread(block, first, width):
    block = pltpu.roll(block, (LANES - first) % LANES, 1)
    lane = lax.broadcasted_iota(jnp.int32, block.shape, 1)
    while width < LANES:
        block = jnp.where(lane < width, block, pltpu.roll(block, width, 1))
        width *= 2
    return block


def pack_far(far, near, own_cells, spare):
    sublane = lax.broadcasted_iota(jnp.int32, (SUB, LANES), 0)

    def one(f, _):
        start = pl.multiple_of(f * own_cells, SUB)
        base = pl.multiple_of(f * (own_cells + SUB), SUB)
        low = near[pl.ds(start, own_cells), 0:LANES]
        high = near[pl.ds(start + own_cells - 2 * SUB, 2 * SUB), LANES : 2 * LANES]
        moved = pltpu.roll(high[0:SUB], spare, 0)
        far[pl.ds(base, SUB), :] = jnp.where(sublane < spare, moved, low[0:SUB])
        far[pl.ds(base + SUB, own_cells - SUB), :] = low[SUB:]
        far[pl.ds(base + own_cells, SUB), :] = high[SUB:]
        return 0

    lax.fori_loop(0, FIELDS, one, 0)


def pack_kernel(spare, levels, place, density, momentum, magnetic, rotation, shifts, *rest):
    nears, fars, rest = rest[:levels], rest[levels : 2 * levels], rest[2 * levels :]
    edge, spin_rows, shift_rows, spin_in, shift_in, arrived = rest
    own_cells, radius = density.shape[1:]
    on_low = place[0] == 0
    parts = radius // LANES
    copies = [
        pltpu.make_async_copy(rotation, spin_in, arrived.at[levels * FIELDS]),
        pltpu.make_async_copy(shifts, shift_in, arrived.at[levels * FIELDS + 1]),
    ]
    for level in range(levels):
        sources = [density.at[level]] + [x.at[k, level] for x in (momentum, magnetic) for k in range(2)]
        for f, x in enumerate(sources):
            at = nears[level].at[pl.ds(f * own_cells, own_cells), :]
            copies.append(pltpu.make_async_copy(x, at, arrived.at[level * FIELDS + f]))
    for copy in copies:
        copy.start()
    for copy in copies[:2]:
        copy.wait()
    for part in range(parts):
        rows = slice(part * LANES, (part + 1) * LANES)
        spin_rows[rows, :] = jnp.broadcast_to(spin_in[part : part + 1, :], (LANES, LANES)).T * time_step
        shift_rows[rows, :] = jnp.broadcast_to(shift_in[part : part + 1, :].astype(jnp.float32), (LANES, LANES)).T
    wide = lambda ref: jnp.broadcast_to(
        jnp.where(on_low, ref[parts - 1 : parts, :], ref[0:1, :]).astype(jnp.float32), (own_cells, LANES)
    )
    turn = wide(spin_in) * time_step
    shift = wide(shift_in)
    zero = jnp.zeros((own_cells, LANES), jnp.float32)
    for copy in copies[2:]:
        copy.wait()
    for level in range(levels):
        near = nears[level]
        pack_far(fars[level], near, own_cells, spare)
        block = jnp.where(on_low, near[:, radius - LANES :], near[:, 0:LANES])
        split = 4 * own_cells
        for side, group in enumerate((block[0:split], jnp.concatenate([block[split:], turn, shift, zero], axis=0))):
            turned = group.T
            edge[level, :, side * LANES : (side + 1) * LANES] = jnp.where(on_low, turned[LANES - EXTRA :], turned[0:EXTRA])


class Blocks:
    def __init__(self, row, n, radius, total, moved):
        self.on_low = row == 0
        self.n = n
        self.own_at = pl.multiple_of(jnp.where(self.on_low, EXTRA, EXTRA + moved), SUB)
        self.edge_at = pl.multiple_of(jnp.where(self.on_low, EXTRA + radius, moved), SUB)
        bounds = [[shift_bound(r * radius - (moved if r else 0) + n * k, total) for k in range(SLOTS)] for r in range(2)]
        self.bounds = [jnp.where(self.on_low, a, b) for a, b in zip(*bounds)]

    def rows_of(self, k):
        start = EXTRA - REACH + self.n * k
        return slice(start, start + TALL)


def table_kernel(plans, place, side, spin_rows, shift_rows, *rest):
    outs, held = rest[:-1], rest[-1]
    lane = lax.broadcasted_iota(jnp.int32, (SUB, LANES), 1)
    sublane = lax.broadcasted_iota(jnp.int32, (SUB, LANES), 0)
    front = lax.broadcasted_iota(jnp.int32, (TALL, LANES), 1) < HALF
    more = side[0, :, LANES : 2 * LANES]
    for which, (n, radius, own_cells, total, spare, moved) in enumerate(plans):
        spin, pick = outs[2 * which : 2 * which + 2]
        blocks = Blocks(place[0], n, radius, total, moved)
        held[0, pl.ds(blocks.own_at, radius), :] = spin_rows[...]
        held[0, pl.ds(blocks.edge_at, EXTRA), :] = spread(more, own_cells, own_cells)
        held[1, pl.ds(blocks.own_at, radius), :] = shift_rows[...]
        held[1, pl.ds(blocks.edge_at, EXTRA), :] = spread(more, 2 * own_cells, own_cells)
        bound = jnp.zeros((SUB, LANES), jnp.int32)
        for j in range(SUB):
            low, high = blocks.rows_of(j), blocks.rows_of(SUB + j)
            spin[pl.ds(j, TALL, stride=SUB), :] = jnp.where(front, held[0, low, :], held[0, high, :])
            pick[pl.ds(j, TALL, stride=SUB), :] = jnp.where(front, held[1, low, :], held[1, high, :]).astype(jnp.int32)
            bound = jnp.where(sublane == j, jnp.where(lane < HALF, blocks.bounds[j], blocks.bounds[SUB + j]), bound)

        def one(i, _):
            pick[tile(i), :] = (lane + (REACH + bound)) - pick[tile(i), :]
            return 0

        lax.fori_loop(0, TALL, one, 0)


def step_kernel(plan, refs, write, scratch):
    n, radius, own_cells, total, spare, moved = plan
    place, own, own_edge, near, near_edge, far, spin, pick = refs
    cells, stages, packed = scratch
    row = place[0]
    lane = lax.broadcasted_iota(jnp.int32, (SUB, LANES), 1)
    sublane = lax.broadcasted_iota(jnp.int32, (SUB, LANES), 0)
    blocks = Blocks(row, n, radius, total, moved)

    edge_lane = lax.broadcasted_iota(jnp.int32, (EXTRA, LANES), 1)
    parts = radius // LANES

    def gather(f, _):
        rows = pl.ds(pl.multiple_of(f * own_cells, SUB), own_cells)
        start = pl.multiple_of(f * (own_cells + SUB), SUB)
        for part in range(parts):
            columns = slice(part * LANES, (part + 1) * LANES)
            if part == 0:
                top = far[pl.ds(start, own_cells), :]
            else:
                top = jnp.concatenate(
                    [
                        jnp.zeros((own_cells - 2 * SUB, LANES), jnp.float32),
                        pltpu.roll(far[pl.ds(start, SUB), :], SUB - spare, 0),
                        far[pl.ds(start + own_cells, SUB), :],
                    ],
                    axis=0,
                )
            fill = jnp.zeros((own_cells, LANES), jnp.float32)
            block = jnp.concatenate([top, near[rows, columns], own[rows, columns], fill], axis=0)
            cells[f, pl.ds(blocks.own_at + part * LANES, LANES), :] = block.T
        columns = pl.ds(pl.multiple_of(lax.div(f, 4) * LANES, LANES), LANES)
        lanes_at = lax.rem(f, 4) * own_cells
        cells[f, pl.ds(blocks.edge_at, EXTRA), :] = jnp.where(
            edge_lane < 2 * own_cells,
            pltpu.roll(near_edge[:, columns], lax.rem(LANES + own_cells - lanes_at, LANES), 1),
            pltpu.roll(own_edge[:, columns], lax.rem(LANES + 2 * own_cells - lanes_at, LANES), 1),
        )
        return 0

    lax.fori_loop(0, FIELDS, gather, 0)

    front = lax.broadcasted_iota(jnp.int32, (TALL, LANES), 1) < HALF

    def deal(f, _):
        for j in range(SUB):
            low, high = j, SUB + j
            turn_low = (LANES - (2 * own_cells - REACH)) + blocks.bounds[low]
            turn_high = (HALF - (2 * own_cells - REACH)) + blocks.bounds[high]
            stages[0, f, pl.ds(j, TALL, stride=SUB), :] = jnp.where(
                front,
                pltpu.roll(cells[f, blocks.rows_of(low), :], turn_low, 1),
                pltpu.roll(cells[f, blocks.rows_of(high), :], turn_high, 1),
            )
        return 0

    lax.fori_loop(0, FIELDS, deal, 0)

    edges = (
        (sublane == 0) & (lane < HALF) & (row == 0),
        (sublane == SUB - 1) & (lane >= HALF) & (row == total // radius - 1),
    )
    run_stages(n, stages, spin, edges)

    even = (lane & own_cells) == 0

    def shift(i, _):
        rows = tile(REACH + i)
        source = pick[rows, :]
        picks = [source & (LANES - 1), (source - own_cells) & (LANES - 1)]
        turned = [
            jnp.take_along_axis(stages[1, f, rows, :], picks[f % 2], axis=1, mode="promise_in_bounds")
            for f in range(FIELDS)
        ]
        stages[2, 0, tile(i), :] = jnp.where(even, turned[0], turned[1])
        stages[2, 1, tile(i), :] = jnp.where(even, turned[2], turned[3])
        stages[2, 2, tile(i), :] = turned[4]
        return 0

    lax.fori_loop(0, n, shift, 0)
    narrow = lax.broadcasted_iota(jnp.int32, (n, LANES), 1) < HALF
    for j in range(SUB):
        one, two, three = [stages[2, g, pl.ds(j, n, stride=SUB), :] for g in range(3)]
        low = slice(EXTRA + n * j, EXTRA + n * (j + 1))
        high = slice(EXTRA + n * (SUB + j), EXTRA + n * (SUB + j + 1))
        packed[0, low, :] = jnp.where(narrow, one, pltpu.roll(two, HALF, 1))
        packed[0, high, :] = jnp.where(narrow, pltpu.roll(one, HALF, 1), two)
        packed[1, low, :] = three
        packed[1, high, :] = pltpu.roll(three, HALF, 1)
    for part in range(parts):
        rows = pl.ds(blocks.own_at + part * LANES, LANES)
        write.fields(slice(part * LANES, (part + 1) * LANES), packed[0, rows, :].T, packed[1, rows, :].T)
    write.edge(packed[0, pl.ds(blocks.edge_at, EXTRA), :], packed[1, pl.ds(blocks.edge_at, EXTRA), :])
    write.end()


class ToMessage:
    def __init__(self, near, far, own_cells, spare):
        self.near, self.far, self.own_cells, self.spare = near, far, own_cells, spare

    def fields(self, columns, four, fifth):
        split = 4 * self.own_cells
        self.near[0:split, columns] = four
        self.near[split : split + self.own_cells, columns] = fifth[0 : self.own_cells]

    def edge(self, first, second):
        tail = FIELDS * self.own_cells
        self.near[tail : tail + EXTRA, 0:LANES] = first
        self.near[tail : tail + EXTRA, LANES : 2 * LANES] = second

    def end(self):
        pack_far(self.far, self.near, self.own_cells, self.spare)


class ToResult:
    def __init__(self, density, momentum, magnetic):
        self.outs = (density, momentum, magnetic)

    def fields(self, columns, four, fifth):
        density, momentum, magnetic = self.outs
        cells = density.shape[1]
        density[0, :, columns] = four[0:cells]
        momentum[0, 0, :, columns] = four[cells : 2 * cells]
        momentum[1, 0, :, columns] = four[2 * cells : 3 * cells]
        magnetic[0, 0, :, columns] = four[3 * cells : 4 * cells]
        magnetic[1, 0, :, columns] = fifth[0:cells]

    def edge(self, first, second):
        pass

    def end(self):
        pass


def tall_of(n):
    return EXTRA + SLOTS * n + 2 * SUB


def step_scratch(n):
    return [
        pltpu.VMEM((FIELDS, tall_of(n), LANES), jnp.float32),
        pltpu.VMEM((STAGES, FIELDS, TALL * SUB, LANES), jnp.float32),
        pltpu.VMEM((2, tall_of(n), LANES), jnp.float32),
    ]


vmem = pl.BlockSpec(memory_space=pltpu.VMEM)
smem = pl.BlockSpec(memory_space=pltpu.SMEM)
f32 = lambda *s: jax.ShapeDtypeStruct(s, jnp.float32)
params = pltpu.CompilerParams(vmem_limit_bytes=VMEM_LIMIT)
cost = pl.CostEstimate(flops=20_000_000, bytes_accessed=600_000, transcendentals=0)


def first_step(plan, level, operands):
    n, radius, own_cells, total, spare, moved = plan

    def kernel(place, own, near, far, side, corner, spin, pick, near_out, far_out, *scratch):
        refs = (place, own, side.at[level], near, corner.at[level], far, spin, pick)
        step_kernel(plan, refs, ToMessage(near_out, far_out, own_cells, spare), scratch)

    return pl.pallas_call(
        kernel,
        out_shape=[f32(FIELDS * own_cells + EXTRA, radius), f32(FIELDS * (own_cells + SUB), LANES)],
        in_specs=[smem] + [vmem] * 7,
        out_specs=[vmem] * 2,
        scratch_shapes=step_scratch(n),
        compiler_params=params,
        cost_estimate=cost,
        name="first_step",
    )(*operands)


def last_step(plan, level, operands, results, levels):
    n, radius, own_cells, total, spare, moved = plan
    tail = pl.ds(FIELDS * own_cells, EXTRA)
    count = len(results)

    def kernel(place, own, near, far, spin, pick, *rest):
        outs, scratch = rest[count : count + 3], rest[count + 3 :]
        refs = (place, own, own.at[tail, :], near, near.at[tail, :], far, spin, pick)
        step_kernel(plan, refs, ToResult(*outs), scratch)

    pair = pl.BlockSpec((2, 1, own_cells, radius), lambda i: (0, level, 0, 0))
    return pl.pallas_call(
        kernel,
        grid=(1,),
        out_shape=[f32(levels, own_cells, radius), f32(2, levels, own_cells, radius), f32(2, levels, own_cells, radius)],
        in_specs=[smem] + [vmem] * 5 + [pl.BlockSpec(memory_space=pl.ANY)] * count,
        out_specs=[pl.BlockSpec((1, own_cells, radius), lambda i: (level, 0, 0)), pair, pair],
        scratch_shapes=step_scratch(n),
        input_output_aliases={len(operands) + k: k for k in range(count)},
        compiler_params=params,
        cost_estimate=cost,
        name="last_step",
    )(*operands, *results)


def body(density, momentum, magnetic, rotation, shifts):
    phi_count = lax.axis_size("phi")
    row_count = lax.axis_size("row")
    levels, own_cells, radius = density.shape
    total = radius * row_count
    parts = radius // LANES
    n = radius // SLOTS
    need = [max(shift_bound(part * LANES, total) + REACH - own_cells, 0) for part in range(parts)]
    spare = own_cells - need[0]
    assert row_count == 2 and radius == 2 * LANES and own_cells == HALF // 2
    assert 0 < need[0] < own_cells and need[1] <= SUB + spare and spare <= SUB

    row = lax.axis_index("row")
    place = jnp.reshape(row, (1,)).astype(jnp.int32)
    here = lambda p, r: (p % phi_count) * row_count + r
    everyone = [(p, r) for p in range(phi_count) for r in range(row_count)]
    both = ("phi", "row")
    send_near = lambda x: lax.ppermute(x, "phi", [(p, (p + 1) % phi_count) for p in range(phi_count)])
    send_far = lambda x: lax.ppermute(x, both, [(here(p, 0), here(p + 2, 0)) for p in range(phi_count)])
    send_side = lambda x: lax.ppermute(x, "row", [(0, 1), (1, 0)])
    send_corner = lambda x: lax.ppermute(x, both, [(here(p, r), here(p + 1, 1 - r)) for p, r in everyone])

    near_message = f32(FIELDS * own_cells, radius)
    far_message = f32(FIELDS * (own_cells + SUB), LANES)
    packed = pl.pallas_call(
        lambda *refs: pack_kernel(spare, levels, *refs),
        out_shape=[near_message] * levels
        + [far_message] * levels
        + [f32(levels, EXTRA, 2 * LANES), f32(radius, LANES), f32(radius, LANES)],
        in_specs=[smem] + [pl.BlockSpec(memory_space=pltpu.HBM)] * 5,
        out_specs=[vmem] * (2 * levels + 3),
        scratch_shapes=[
            pltpu.VMEM((parts, LANES), jnp.float32),
            pltpu.VMEM((parts, LANES), jnp.int32),
            pltpu.SemaphoreType.DMA((levels * FIELDS + 2,)),
        ],
        compiler_params=params,
        name="pack",
    )(place, density, momentum, magnetic, rotation.reshape(parts, LANES), shifts.reshape(parts, LANES))
    owns, fars, (edge, spin_rows, shift_rows) = packed[:levels], packed[levels : 2 * levels], packed[2 * levels :]

    side = send_side(edge)
    corner = send_corner(edge)
    wide = (n + 1, radius, own_cells, total, spare, EXTRA)
    plain = (n, radius, own_cells, total, spare, 0)
    i32 = jax.ShapeDtypeStruct((TALL * SUB, LANES), jnp.int32)
    tables = pl.pallas_call(
        lambda *refs: table_kernel((wide, plain), *refs),
        out_shape=[f32(TALL * SUB, LANES), i32] * 2,
        in_specs=[smem] + [vmem] * 3,
        out_specs=[vmem] * 4,
        scratch_shapes=[pltpu.VMEM((2, tall_of(n + 1), LANES), jnp.float32)],
        compiler_params=params,
        name="tables",
    )(place, side, spin_rows, shift_rows)
    moved = [(send_near(own), send_far(far)) for own, far in zip(owns, fars)]
    states = []
    for level in range(levels):
        near, far = moved[level]
        states.append(first_step(wide, level, (place, owns[level], near, far, side, corner, *tables[:2])))
    moved = [(send_near(own), send_far(far)) for own, far in states]
    results = ()
    for level in range(levels):
        near, far = moved[level]
        results = last_step(plain, level, (place, states[level][0], near, far, *tables[2:]), results, levels)
    return tuple(results)


def solution(mesh):
    placed = (
        P(None, "phi", "row"),
        P(None, None, "phi", "row"),
        P(None, None, "phi", "row"),
        P("row"),
        P("row"),
    )
    return jax.shard_map(
        body,
        mesh=mesh,
        in_specs=placed,
        out_specs=(P(None, "phi", "row"), P(None, None, "phi", "row"), P(None, None, "phi", "row")),
        check_vma=False,
    )
```

```python
import jax
import jax.numpy as jnp
from jax import lax
from jax.experimental import pallas as pl
from jax.experimental.pallas import tpu as pltpu
from jax.sharding import PartitionSpec as P

STEPS = 2
SMIN = 8
SMAX = 56
STAGES = 3
REACH = 2 * STAGES
FIELDS = 5
LANES = 128
SUB = 8
HALF = LANES // 2
SLOTS = 2 * SUB
EXTRA = 2 * SUB
TALL = 32
ROWS = 4
VMEM_LIMIT = 32 * 1024 * 1024
PACK_LIMIT = 60 * 1024 * 1024

time_step = 0.08


def shift_bound(first_row, rows):
    d = rows - 1 - first_row
    return min(SMIN + (SMAX - SMIN - 1) * d * d // ((rows - 1) * (rows - 1)) + 1, SMAX)


def minmod(lower, upper):
    return jnp.maximum(jnp.minimum(lower, 0.0), jnp.minimum(upper, jnp.maximum(lower, 0.0)))


def physical(state):
    rho, mn, mt, bn, bt = state
    inverse = pltpu.reciprocal(rho, approx=True)
    vn = mn * inverse
    vt = mt * inverse
    bn_sq = bn * bn
    bt_sq = bt * bt
    ram = mn * vn + rho
    tension = bt_sq - bn_sq
    flux_t = mt * vn - bn * bt
    flux_b = bt * vn - bn * vt
    inside = (bn_sq + bt_sq) * inverse + 1.0
    speed = jnp.abs(vn) + inside * lax.rsqrt(inside)
    return ram, tension, flux_t, flux_b, speed


def face_twice(left, right):
    left_ram, left_tension, left_t, left_b, left_speed = physical(left)
    right_ram, right_tension, right_t, right_b, right_speed = physical(right)
    bound = jnp.maximum(left_speed, right_speed)
    jumps = [bound * (l - r) for l, r in zip(left, right)]
    return [
        (left[1] + right[1]) + jumps[0],
        ((left_ram + right_ram) + 0.5 * (left_tension + right_tension)) + jumps[1],
        (left_t + right_t) + jumps[2],
        jumps[3],
        (left_b + right_b) + jumps[4],
    ]


def swapped(five):
    return [five[0], five[2], five[1], five[4], five[3]]


def radial_faces(rows):
    halves = [[0.5 * x for x in r] for r in rows]
    jumps = [[b - a for a, b in zip(p, q)] for p, q in zip(halves[:-1], halves[1:])]
    slopes = [[minmod(a, b) for a, b in zip(p, q)] for p, q in zip(jumps[:-1], jumps[1:])]
    upper = [[x + s for x, s in zip(r, sl)] for r, sl in zip(rows[1:-1], slopes)]
    lower = [[x - s for x, s in zip(r, sl)] for r, sl in zip(rows[1:-1], slopes)]
    return [swapped(face_twice(swapped(u), swapped(l))) for u, l in zip(upper[:-1], lower[1:])]


def azimuth_change(fields):
    right_of = lambda x: pltpu.roll(x, LANES - 1, 1)
    left_of = lambda x: pltpu.roll(x, 1, 1)
    lower = []
    upper = []
    for x in fields:
        half = 0.5 * x
        jump = right_of(half) - half
        slope = minmod(left_of(jump), jump)
        upper.append(x + slope)
        lower.append(right_of(x - slope))
    return [x - left_of(x) for x in face_twice(upper, lower)]


def tile(i):
    return pl.ds(pl.multiple_of(i * SUB, SUB), SUB)


def run_stages(n, stages, spin, edges):
    half_dt = 0.5 * time_step
    low_mask, high_mask = edges
    first, last = REACH, REACH + n - 1

    def work(stage, i0, count, before):
        src, dst = stage, (stage & 1) + 1
        weight = jnp.where(stage == 0, 1.0, jnp.where(stage == 1, 0.25, 2.0 / 3.0))
        keep = jnp.where(stage == 0, 0.0, jnp.where(stage == 1, 0.75, 1.0 / 3.0))
        rows = [[stages[src, f, tile(i0 + k), :] for f in range(FIELDS)] for k in range(-1, count + 2)]
        starts = [[stages[0, f, tile(i0 + k), :] for f in range(FIELDS)] for k in range(count)]
        turns = [spin[tile(i0 + k), :] for k in range(count)]
        faces = [before] + radial_faces(rows)
        for k in range(count):
            fields = rows[k + 1]
            change = azimuth_change(fields)
            turn = turns[k]
            source = [
                None,
                (-0.5 * turn) * fields[2],
                (2.0 * turn) * fields[1],
                (-1.5 * turn) * fields[4],
                None,
            ]
            for f in range(FIELDS):
                new = fields[f] - half_dt * (change[f] + (faces[k + 1][f] - faces[k][f]))
                if source[f] is not None:
                    new = new + source[f]
                stages[dst, f, tile(i0 + k), :] = weight * new + keep * starts[k][f]
        return faces[-1]

    def run(stage, _):
        for f in range(FIELDS):
            inner = stages[stage, f, tile(first), :]
            outer = stages[stage, f, tile(last), :]
            for k in (1, 2):
                stages[stage, f, tile(first - k), :] = jnp.where(low_mask, inner, stages[stage, f, tile(first - k), :])
                stages[stage, f, tile(last + k), :] = jnp.where(high_mask, outer, stages[stage, f, tile(last + k), :])
        lo = 2 * stage + 2
        count = n + 2 * REACH - 4 - 4 * stage
        before = radial_faces([[stages[stage, f, tile(lo + k), :] for f in range(FIELDS)] for k in range(-2, 2)])[0]
        turns = lax.div(count + ROWS - 1, ROWS)
        lax.fori_loop(0, turns, lambda c, carried: tuple(work(stage, lo + c * ROWS, ROWS, list(carried))), tuple(before))
        return 0

    lax.fori_loop(0, STAGES, run, 0)


def spread(block, first, width):
    block = pltpu.roll(block, (LANES - first) % LANES, 1)
    lane = lax.broadcasted_iota(jnp.int32, block.shape, 1)
    while width < LANES:
        block = jnp.where(lane < width, block, pltpu.roll(block, width, 1))
        width *= 2
    return block


def pack_far(far, near, own_cells, spare):
    sublane = lax.broadcasted_iota(jnp.int32, (SUB, LANES), 0)

    def one(f, _):
        start = pl.multiple_of(f * own_cells, SUB)
        base = pl.multiple_of(f * (own_cells + SUB), SUB)
        low = near[pl.ds(start, own_cells), 0:LANES]
        high = near[pl.ds(start + own_cells - 2 * SUB, 2 * SUB), LANES : 2 * LANES]
        moved = pltpu.roll(high[0:SUB], spare, 0)
        far[pl.ds(base, SUB), :] = jnp.where(sublane < spare, moved, low[0:SUB])
        far[pl.ds(base + SUB, own_cells - SUB), :] = low[SUB:]
        far[pl.ds(base + own_cells, SUB), :] = high[SUB:]
        return 0

    lax.fori_loop(0, FIELDS, one, 0)


def pack_kernel(spare, levels, place, density, momentum, magnetic, rotation, shifts, *rest):
    nears, fars, rest = rest[:levels], rest[levels : 2 * levels], rest[2 * levels :]
    edge, spin_rows, shift_rows, spin_in, shift_in, arrived = rest
    own_cells, radius = density.shape[1:]
    on_low = place[0] == 0
    parts = radius // LANES
    copies = [
        pltpu.make_async_copy(rotation, spin_in, arrived.at[levels * FIELDS]),
        pltpu.make_async_copy(shifts, shift_in, arrived.at[levels * FIELDS + 1]),
    ]
    for level in range(levels):
        sources = [density.at[level]] + [x.at[k, level] for x in (momentum, magnetic) for k in range(2)]
        for f, x in enumerate(sources):
            at = nears[level].at[pl.ds(f * own_cells, own_cells), :]
            copies.append(pltpu.make_async_copy(x, at, arrived.at[level * FIELDS + f]))
    for copy in copies:
        copy.start()
    for copy in copies[:2]:
        copy.wait()
    for part in range(parts):
        rows = slice(part * LANES, (part + 1) * LANES)
        spin_rows[rows, :] = jnp.broadcast_to(spin_in[part : part + 1, :], (LANES, LANES)).T * time_step
        shift_rows[rows, :] = jnp.broadcast_to(shift_in[part : part + 1, :].astype(jnp.float32), (LANES, LANES)).T
    wide = lambda ref: jnp.broadcast_to(
        jnp.where(on_low, ref[parts - 1 : parts, :], ref[0:1, :]).astype(jnp.float32), (own_cells, LANES)
    )
    turn = wide(spin_in) * time_step
    shift = wide(shift_in)
    zero = jnp.zeros((own_cells, LANES), jnp.float32)
    for copy in copies[2:]:
        copy.wait()
    for level in range(levels):
        near = nears[level]
        pack_far(fars[level], near, own_cells, spare)
        block = jnp.where(on_low, near[:, radius - LANES :], near[:, 0:LANES])
        split = 4 * own_cells
        for side, group in enumerate((block[0:split], jnp.concatenate([block[split:], turn, shift, zero], axis=0))):
            turned = group.T
            edge[level, :, side * LANES : (side + 1) * LANES] = jnp.where(on_low, turned[LANES - EXTRA :], turned[0:EXTRA])


class Blocks:
    def __init__(self, row, n, radius, total, moved):
        self.on_low = row == 0
        self.n = n
        self.own_at = pl.multiple_of(jnp.where(self.on_low, EXTRA, EXTRA + moved), SUB)
        self.edge_at = pl.multiple_of(jnp.where(self.on_low, EXTRA + radius, moved), SUB)
        bounds = [[shift_bound(r * radius - (moved if r else 0) + n * k, total) for k in range(SLOTS)] for r in range(2)]
        self.bounds = [jnp.where(self.on_low, a, b) for a, b in zip(*bounds)]

    def rows_of(self, k):
        start = EXTRA - REACH + self.n * k
        return slice(start, start + TALL)


def table_kernel(plans, place, side, spin_rows, shift_rows, *rest):
    outs, held = rest[:-1], rest[-1]
    lane = lax.broadcasted_iota(jnp.int32, (SUB, LANES), 1)
    sublane = lax.broadcasted_iota(jnp.int32, (SUB, LANES), 0)
    front = lax.broadcasted_iota(jnp.int32, (TALL, LANES), 1) < HALF
    more = side[0, :, LANES : 2 * LANES]
    for which, (n, radius, own_cells, total, spare, moved) in enumerate(plans):
        spin, pick = outs[2 * which : 2 * which + 2]
        blocks = Blocks(place[0], n, radius, total, moved)
        held[0, pl.ds(blocks.own_at, radius), :] = spin_rows[...]
        held[0, pl.ds(blocks.edge_at, EXTRA), :] = spread(more, own_cells, own_cells)
        held[1, pl.ds(blocks.own_at, radius), :] = shift_rows[...]
        held[1, pl.ds(blocks.edge_at, EXTRA), :] = spread(more, 2 * own_cells, own_cells)
        bound = jnp.zeros((SUB, LANES), jnp.int32)
        for j in range(SUB):
            low, high = blocks.rows_of(j), blocks.rows_of(SUB + j)
            spin[pl.ds(j, TALL, stride=SUB), :] = jnp.where(front, held[0, low, :], held[0, high, :])
            pick[pl.ds(j, TALL, stride=SUB), :] = jnp.where(front, held[1, low, :], held[1, high, :]).astype(jnp.int32)
            bound = jnp.where(sublane == j, jnp.where(lane < HALF, blocks.bounds[j], blocks.bounds[SUB + j]), bound)

        def one(i, _):
            pick[tile(i), :] = (lane + (REACH + bound)) - pick[tile(i), :]
            return 0

        lax.fori_loop(0, TALL, one, 0)


def step_kernel(plan, refs, write, scratch):
    n, radius, own_cells, total, spare, moved = plan
    place, own, own_edge, near, near_edge, far, spin, pick = refs
    cells, stages, packed = scratch
    row = place[0]
    lane = lax.broadcasted_iota(jnp.int32, (SUB, LANES), 1)
    sublane = lax.broadcasted_iota(jnp.int32, (SUB, LANES), 0)
    blocks = Blocks(row, n, radius, total, moved)

    edge_lane = lax.broadcasted_iota(jnp.int32, (EXTRA, LANES), 1)
    parts = radius // LANES

    def gather(f, _):
        rows = pl.ds(pl.multiple_of(f * own_cells, SUB), own_cells)
        start = pl.multiple_of(f * (own_cells + SUB), SUB)
        for part in range(parts):
            columns = slice(part * LANES, (part + 1) * LANES)
            if part == 0:
                top = far[pl.ds(start, own_cells), :]
            else:
                top = jnp.concatenate(
                    [
                        jnp.zeros((own_cells - 2 * SUB, LANES), jnp.float32),
                        pltpu.roll(far[pl.ds(start, SUB), :], SUB - spare, 0),
                        far[pl.ds(start + own_cells, SUB), :],
                    ],
                    axis=0,
                )
            fill = jnp.zeros((own_cells, LANES), jnp.float32)
            block = jnp.concatenate([top, near[rows, columns], own[rows, columns], fill], axis=0)
            cells[f, pl.ds(blocks.own_at + part * LANES, LANES), :] = block.T
        columns = pl.ds(pl.multiple_of(lax.div(f, 4) * LANES, LANES), LANES)
        lanes_at = lax.rem(f, 4) * own_cells
        cells[f, pl.ds(blocks.edge_at, EXTRA), :] = jnp.where(
            edge_lane < 2 * own_cells,
            pltpu.roll(near_edge[:, columns], lax.rem(LANES + own_cells - lanes_at, LANES), 1),
            pltpu.roll(own_edge[:, columns], lax.rem(LANES + 2 * own_cells - lanes_at, LANES), 1),
        )
        return 0

    lax.fori_loop(0, FIELDS, gather, 0)

    front = lax.broadcasted_iota(jnp.int32, (TALL, LANES), 1) < HALF

    def deal(f, _):
        for j in range(SUB):
            low, high = j, SUB + j
            turn_low = (LANES - (2 * own_cells - REACH)) + blocks.bounds[low]
            turn_high = (HALF - (2 * own_cells - REACH)) + blocks.bounds[high]
            stages[0, f, pl.ds(j, TALL, stride=SUB), :] = jnp.where(
                front,
                pltpu.roll(cells[f, blocks.rows_of(low), :], turn_low, 1),
                pltpu.roll(cells[f, blocks.rows_of(high), :], turn_high, 1),
            )
        return 0

    lax.fori_loop(0, FIELDS, deal, 0)

    edges = (
        (sublane == 0) & (lane < HALF) & (row == 0),
        (sublane == SUB - 1) & (lane >= HALF) & (row == total // radius - 1),
    )
    run_stages(n, stages, spin, edges)

    even = (lane & own_cells) == 0

    def shift(turn, _):
        for k in range(ROWS):
            i = turn * ROWS + k
            rows = tile(REACH + i)
            source = pick[rows, :]
            picks = [source & (LANES - 1), (source - own_cells) & (LANES - 1)]
            turned = [
                jnp.take_along_axis(stages[1, f, rows, :], picks[f % 2], axis=1, mode="promise_in_bounds")
                for f in range(FIELDS)
            ]
            stages[2, 0, tile(i), :] = jnp.where(even, turned[0], turned[1])
            stages[2, 1, tile(i), :] = jnp.where(even, turned[2], turned[3])
            stages[2, 2, tile(i), :] = turned[4]
        return 0

    lax.fori_loop(0, (n + ROWS - 1) // ROWS, shift, 0)
    narrow = lax.broadcasted_iota(jnp.int32, (n, LANES), 1) < HALF
    for j in range(SUB):
        one, two, three = [stages[2, g, pl.ds(j, n, stride=SUB), :] for g in range(3)]
        low = slice(EXTRA + n * j, EXTRA + n * (j + 1))
        high = slice(EXTRA + n * (SUB + j), EXTRA + n * (SUB + j + 1))
        packed[0, low, :] = jnp.where(narrow, one, pltpu.roll(two, HALF, 1))
        packed[0, high, :] = jnp.where(narrow, pltpu.roll(one, HALF, 1), two)
        packed[1, low, :] = three
        packed[1, high, :] = pltpu.roll(three, HALF, 1)
    for part in range(parts):
        rows = pl.ds(blocks.own_at + part * LANES, LANES)
        write.fields(slice(part * LANES, (part + 1) * LANES), packed[0, rows, :].T, packed[1, rows, :].T)
    write.edge(packed[0, pl.ds(blocks.edge_at, EXTRA), :], packed[1, pl.ds(blocks.edge_at, EXTRA), :])
    write.end()


class ToMessage:
    def __init__(self, near, far, own_cells, spare):
        self.near, self.far, self.own_cells, self.spare = near, far, own_cells, spare

    def fields(self, columns, four, fifth):
        split = 4 * self.own_cells
        self.near[0:split, columns] = four
        self.near[split : split + self.own_cells, columns] = fifth[0 : self.own_cells]

    def edge(self, first, second):
        tail = FIELDS * self.own_cells
        self.near[tail : tail + EXTRA, 0:LANES] = first
        self.near[tail : tail + EXTRA, LANES : 2 * LANES] = second

    def end(self):
        pack_far(self.far, self.near, self.own_cells, self.spare)


class ToResult:
    def __init__(self, density, momentum, magnetic):
        self.outs = (density, momentum, magnetic)

    def fields(self, columns, four, fifth):
        density, momentum, magnetic = self.outs
        cells = density.shape[1]
        density[0, :, columns] = four[0:cells]
        momentum[0, 0, :, columns] = four[cells : 2 * cells]
        momentum[1, 0, :, columns] = four[2 * cells : 3 * cells]
        magnetic[0, 0, :, columns] = four[3 * cells : 4 * cells]
        magnetic[1, 0, :, columns] = fifth[0:cells]

    def edge(self, first, second):
        pass

    def end(self):
        pass


def tall_of(n):
    return EXTRA + SLOTS * n + 2 * SUB


def step_scratch(n):
    return [
        pltpu.VMEM((FIELDS, tall_of(n), LANES), jnp.float32),
        pltpu.VMEM((STAGES, FIELDS, TALL * SUB, LANES), jnp.float32),
        pltpu.VMEM((2, tall_of(n), LANES), jnp.float32),
    ]


vmem = pl.BlockSpec(memory_space=pltpu.VMEM)
smem = pl.BlockSpec(memory_space=pltpu.SMEM)
f32 = lambda *s: jax.ShapeDtypeStruct(s, jnp.float32)
params = pltpu.CompilerParams(vmem_limit_bytes=VMEM_LIMIT)
cost = pl.CostEstimate(flops=9_000_000_000, bytes_accessed=29_000_000, transcendentals=0)


def first_step(plan, level, operands):
    n, radius, own_cells, total, spare, moved = plan

    def kernel(place, own, near, far, side, corner, spin, pick, near_out, far_out, *scratch):
        refs = (place, own, side.at[level], near, corner.at[level], far, spin, pick)
        step_kernel(plan, refs, ToMessage(near_out, far_out, own_cells, spare), scratch)

    return pl.pallas_call(
        kernel,
        out_shape=[f32(FIELDS * own_cells + EXTRA, radius), f32(FIELDS * (own_cells + SUB), LANES)],
        in_specs=[smem] + [vmem] * 7,
        out_specs=[vmem] * 2,
        scratch_shapes=step_scratch(n),
        compiler_params=params,
        cost_estimate=cost,
        name="first_step",
    )(*operands)


def last_step(plan, level, operands, results, levels):
    n, radius, own_cells, total, spare, moved = plan
    tail = pl.ds(FIELDS * own_cells, EXTRA)
    count = len(results)

    def kernel(place, own, near, far, spin, pick, *rest):
        outs, scratch = rest[count : count + 3], rest[count + 3 :]
        refs = (place, own, own.at[tail, :], near, near.at[tail, :], far, spin, pick)
        step_kernel(plan, refs, ToResult(*outs), scratch)

    pair = pl.BlockSpec((2, 1, own_cells, radius), lambda i: (0, level, 0, 0))
    return pl.pallas_call(
        kernel,
        grid=(1,),
        out_shape=[f32(levels, own_cells, radius), f32(2, levels, own_cells, radius), f32(2, levels, own_cells, radius)],
        in_specs=[smem] + [vmem] * 5 + [pl.BlockSpec(memory_space=pl.ANY)] * count,
        out_specs=[pl.BlockSpec((1, own_cells, radius), lambda i: (level, 0, 0)), pair, pair],
        scratch_shapes=step_scratch(n),
        input_output_aliases={len(operands) + k: k for k in range(count)},
        compiler_params=params,
        cost_estimate=cost,
        name="last_step",
    )(*operands, *results)


def body(density, momentum, magnetic, rotation, shifts):
    phi_count = lax.axis_size("phi")
    row_count = lax.axis_size("row")
    levels, own_cells, radius = density.shape
    total = radius * row_count
    parts = radius // LANES
    n = radius // SLOTS
    need = [max(shift_bound(part * LANES, total) + REACH - own_cells, 0) for part in range(parts)]
    spare = own_cells - need[0]
    assert row_count == 2 and radius == 2 * LANES and own_cells == HALF // 2
    assert 0 < need[0] < own_cells and need[1] <= SUB + spare and spare <= SUB

    row = lax.axis_index("row")
    place = jnp.reshape(row, (1,)).astype(jnp.int32)
    here = lambda p, r: (p % phi_count) * row_count + r
    everyone = [(p, r) for p in range(phi_count) for r in range(row_count)]
    both = ("phi", "row")
    send_near = lambda x: lax.ppermute(x, "phi", [(p, (p + 1) % phi_count) for p in range(phi_count)])
    send_far = lambda x: lax.ppermute(x, both, [(here(p, 0), here(p + 2, 0)) for p in range(phi_count)])
    send_side = lambda x: lax.ppermute(x, "row", [(0, 1), (1, 0)])
    send_corner = lambda x: lax.ppermute(x, both, [(here(p, r), here(p + 1, 1 - r)) for p, r in everyone])

    near_message = f32(FIELDS * own_cells, radius)
    far_message = f32(FIELDS * (own_cells + SUB), LANES)
    packed = pl.pallas_call(
        lambda *refs: pack_kernel(spare, levels, *refs),
        out_shape=[near_message] * levels
        + [far_message] * levels
        + [f32(levels, EXTRA, 2 * LANES), f32(radius, LANES), f32(radius, LANES)],
        in_specs=[smem] + [pl.BlockSpec(memory_space=pltpu.HBM)] * 5,
        out_specs=[vmem] * (2 * levels + 3),
        scratch_shapes=[
            pltpu.VMEM((parts, LANES), jnp.float32),
            pltpu.VMEM((parts, LANES), jnp.int32),
            pltpu.SemaphoreType.DMA((levels * FIELDS + 2,)),
        ],
        compiler_params=pltpu.CompilerParams(vmem_limit_bytes=PACK_LIMIT),
        name="pack",
    )(place, density, momentum, magnetic, rotation.reshape(parts, LANES), shifts.reshape(parts, LANES))
    owns, fars, (edge, spin_rows, shift_rows) = packed[:levels], packed[levels : 2 * levels], packed[2 * levels :]

    side = send_side(edge)
    corner = send_corner(edge)
    wide = (n + 1, radius, own_cells, total, spare, EXTRA)
    plain = (n, radius, own_cells, total, spare, 0)
    i32 = jax.ShapeDtypeStruct((TALL * SUB, LANES), jnp.int32)
    tables = pl.pallas_call(
        lambda *refs: table_kernel((wide, plain), *refs),
        out_shape=[f32(TALL * SUB, LANES), i32] * 2,
        in_specs=[smem] + [vmem] * 3,
        out_specs=[vmem] * 4,
        scratch_shapes=[pltpu.VMEM((2, tall_of(n + 1), LANES), jnp.float32)],
        compiler_params=params,
        name="tables",
    )(place, side, spin_rows, shift_rows)
    moved = [(send_near(own), send_far(far)) for own, far in zip(owns, fars)]
    states = []
    for level in range(levels):
        near, far = moved[level]
        states.append(first_step(wide, level, (place, owns[level], near, far, side, corner, *tables[:2])))
    moved = [(send_near(own), send_far(far)) for own, far in states]
    results = ()
    for level in range(levels):
        near, far = moved[level]
        results = last_step(plain, level, (place, states[level][0], near, far, *tables[2:]), results, levels)
    return tuple(results)


def solution(mesh):
    placed = (
        P(None, "phi", "row"),
        P(None, None, "phi", "row"),
        P(None, None, "phi", "row"),
        P("row"),
        P("row"),
    )
    return jax.shard_map(
        body,
        mesh=mesh,
        in_specs=placed,
        out_specs=(P(None, "phi", "row"), P(None, None, "phi", "row"), P(None, None, "phi", "row")),
        check_vma=False,
    )
```

```python
import jax
import jax.numpy as jnp
from jax import lax
from jax.experimental import pallas as pl
from jax.experimental.pallas import tpu as pltpu
from jax.sharding import PartitionSpec as P

STEPS = 2
SMIN = 8
SMAX = 56
STAGES = 3
REACH = 2 * STAGES
FIELDS = 5
LANES = 128
SUB = 8
HALF = LANES // 2
SLOTS = 2 * SUB
EXTRA = 2 * SUB
TALL = 32
ROWS = 3
PICKS = 4
VMEM_LIMIT = 32 * 1024 * 1024
PACK_LIMIT = 60 * 1024 * 1024

time_step = 0.08


def shift_bound(first_row, rows):
    d = rows - 1 - first_row
    return min(SMIN + (SMAX - SMIN - 1) * d * d // ((rows - 1) * (rows - 1)) + 1, SMAX)


def minmod(lower, upper):
    return jnp.maximum(jnp.minimum(lower, 0.0), jnp.minimum(upper, jnp.maximum(lower, 0.0)))


def physical(state):
    rho, mn, mt, bn, bt = state
    inverse = pltpu.reciprocal(rho, approx=True)
    vn = mn * inverse
    vt = mt * inverse
    bn_sq = bn * bn
    bt_sq = bt * bt
    ram = mn * vn + rho
    tension = bt_sq - bn_sq
    flux_t = mt * vn - bn * bt
    flux_b = bt * vn - bn * vt
    inside = (bn_sq + bt_sq) * inverse + 1.0
    speed = jnp.abs(vn) + inside * lax.rsqrt(inside)
    return ram, tension, flux_t, flux_b, speed


def face_twice(left, right):
    left_ram, left_tension, left_t, left_b, left_speed = physical(left)
    right_ram, right_tension, right_t, right_b, right_speed = physical(right)
    bound = jnp.maximum(left_speed, right_speed)
    jumps = [bound * (l - r) for l, r in zip(left, right)]
    return [
        (left[1] + right[1]) + jumps[0],
        ((left_ram + right_ram) + 0.5 * (left_tension + right_tension)) + jumps[1],
        (left_t + right_t) + jumps[2],
        jumps[3],
        (left_b + right_b) + jumps[4],
    ]


def swapped(five):
    return [five[0], five[2], five[1], five[4], five[3]]


def radial_faces(rows):
    halves = [[0.5 * x for x in r] for r in rows]
    jumps = [[b - a for a, b in zip(p, q)] for p, q in zip(halves[:-1], halves[1:])]
    slopes = [[minmod(a, b) for a, b in zip(p, q)] for p, q in zip(jumps[:-1], jumps[1:])]
    upper = [[x + s for x, s in zip(r, sl)] for r, sl in zip(rows[1:-1], slopes)]
    lower = [[x - s for x, s in zip(r, sl)] for r, sl in zip(rows[1:-1], slopes)]
    return [swapped(face_twice(swapped(u), swapped(l))) for u, l in zip(upper[:-1], lower[1:])]


def azimuth_change(fields):
    right_of = lambda x: pltpu.roll(x, LANES - 1, 1)
    left_of = lambda x: pltpu.roll(x, 1, 1)
    lower = []
    upper = []
    for x in fields:
        half = 0.5 * x
        jump = right_of(half) - half
        slope = minmod(left_of(jump), jump)
        upper.append(x + slope)
        lower.append(right_of(x - slope))
    return [x - left_of(x) for x in face_twice(upper, lower)]


def tile(i):
    return pl.ds(pl.multiple_of(i * SUB, SUB), SUB)


def run_stages(n, stages, spin, edges):
    half_dt = 0.5 * time_step
    low_mask, high_mask = edges
    first, last = REACH, REACH + n - 1

    def work(stage, i0, count, before):
        src, dst = stage, (stage & 1) + 1
        weight = jnp.where(stage == 0, 1.0, jnp.where(stage == 1, 0.25, 2.0 / 3.0))
        keep = jnp.where(stage == 0, 0.0, jnp.where(stage == 1, 0.75, 1.0 / 3.0))
        rows = [[stages[src, f, tile(i0 + k), :] for f in range(FIELDS)] for k in range(-1, count + 2)]
        starts = [[stages[0, f, tile(i0 + k), :] for f in range(FIELDS)] for k in range(count)]
        turns = [spin[tile(i0 + k), :] for k in range(count)]
        faces = [before] + radial_faces(rows)
        for k in range(count):
            fields = rows[k + 1]
            change = azimuth_change(fields)
            turn = turns[k]
            source = [
                None,
                (-0.5 * turn) * fields[2],
                (2.0 * turn) * fields[1],
                (-1.5 * turn) * fields[4],
                None,
            ]
            for f in range(FIELDS):
                new = fields[f] - half_dt * (change[f] + (faces[k + 1][f] - faces[k][f]))
                if source[f] is not None:
                    new = new + source[f]
                stages[dst, f, tile(i0 + k), :] = weight * new + keep * starts[k][f]
        return faces[-1]

    def run(stage, _):
        for f in range(FIELDS):
            inner = stages[stage, f, tile(first), :]
            outer = stages[stage, f, tile(last), :]
            for k in (1, 2):
                stages[stage, f, tile(first - k), :] = jnp.where(low_mask, inner, stages[stage, f, tile(first - k), :])
                stages[stage, f, tile(last + k), :] = jnp.where(high_mask, outer, stages[stage, f, tile(last + k), :])
        lo = 2 * stage + 1
        turns = lax.div(n + 2 * REACH - 3 - 4 * stage + ROWS - 1, ROWS)
        before = (jnp.zeros((SUB, LANES), jnp.float32),) * FIELDS
        lax.fori_loop(0, turns, lambda c, carried: tuple(work(stage, lo + c * ROWS, ROWS, list(carried))), before)
        return 0

    lax.fori_loop(0, STAGES, run, 0)


def spread(block, first, width):
    block = pltpu.roll(block, (LANES - first) % LANES, 1)
    lane = lax.broadcasted_iota(jnp.int32, block.shape, 1)
    while width < LANES:
        block = jnp.where(lane < width, block, pltpu.roll(block, width, 1))
        width *= 2
    return block


def pack_far(far, near, own_cells, spare):
    sublane = lax.broadcasted_iota(jnp.int32, (SUB, LANES), 0)

    def one(f, _):
        start = pl.multiple_of(f * own_cells, SUB)
        base = pl.multiple_of(f * (own_cells + SUB), SUB)
        low = near[pl.ds(start, own_cells), 0:LANES]
        high = near[pl.ds(start + own_cells - 2 * SUB, 2 * SUB), LANES : 2 * LANES]
        moved = pltpu.roll(high[0:SUB], spare, 0)
        far[pl.ds(base, SUB), :] = jnp.where(sublane < spare, moved, low[0:SUB])
        far[pl.ds(base + SUB, own_cells - SUB), :] = low[SUB:]
        far[pl.ds(base + own_cells, SUB), :] = high[SUB:]
        return 0

    lax.fori_loop(0, FIELDS, one, 0)


def pack_kernel(spare, levels, place, density, momentum, magnetic, rotation, shifts, *rest):
    nears, fars, rest = rest[:levels], rest[levels : 2 * levels], rest[2 * levels :]
    edge, spin_in, shift_in, arrived = rest
    own_cells, radius = density.shape[1:]
    on_low = place[0] == 0
    parts = radius // LANES
    copies = [
        pltpu.make_async_copy(rotation, spin_in, arrived.at[levels * FIELDS]),
        pltpu.make_async_copy(shifts, shift_in, arrived.at[levels * FIELDS + 1]),
    ]
    for level in range(levels):
        sources = [density.at[level]] + [x.at[k, level] for x in (momentum, magnetic) for k in range(2)]
        for f, x in enumerate(sources):
            at = nears[level].at[pl.ds(f * own_cells, own_cells), :]
            copies.append(pltpu.make_async_copy(x, at, arrived.at[level * FIELDS + f]))
    for copy in copies:
        copy.start()
    for copy in copies[:2]:
        copy.wait()
    wide = lambda ref: jnp.broadcast_to(
        jnp.where(on_low, ref[parts - 1 : parts, :], ref[0:1, :]).astype(jnp.float32), (own_cells, LANES)
    )
    turn = wide(spin_in) * time_step
    shift = wide(shift_in)
    zero = jnp.zeros((own_cells, LANES), jnp.float32)
    for copy in copies[2:]:
        copy.wait()
    for level in range(levels):
        near = nears[level]
        pack_far(fars[level], near, own_cells, spare)
        block = jnp.where(on_low, near[:, radius - LANES :], near[:, 0:LANES])
        split = 4 * own_cells
        for side, group in enumerate((block[0:split], jnp.concatenate([block[split:], turn, shift, zero], axis=0))):
            turned = group.T
            edge[level, :, side * LANES : (side + 1) * LANES] = jnp.where(on_low, turned[LANES - EXTRA :], turned[0:EXTRA])


class Blocks:
    def __init__(self, row, n, radius, total, moved):
        self.on_low = row == 0
        self.n = n
        self.own_at = pl.multiple_of(jnp.where(self.on_low, EXTRA, EXTRA + moved), SUB)
        self.edge_at = pl.multiple_of(jnp.where(self.on_low, EXTRA + radius, moved), SUB)
        bounds = [[shift_bound(r * radius - (moved if r else 0) + n * k, total) for k in range(SLOTS)] for r in range(2)]
        self.bounds = [jnp.where(self.on_low, a, b) for a, b in zip(*bounds)]

    def rows_of(self, k):
        start = EXTRA - REACH + self.n * k
        return slice(start, start + TALL)


def table_kernel(plans, place, side, rotation, shifts, *rest):
    outs, held = rest[:-1], rest[-1]
    lane = lax.broadcasted_iota(jnp.int32, (SUB, LANES), 1)
    sublane = lax.broadcasted_iota(jnp.int32, (SUB, LANES), 0)
    front = lax.broadcasted_iota(jnp.int32, (TALL, LANES), 1) < HALF
    more = side[0, :, LANES : 2 * LANES]
    for which, (n, radius, own_cells, total, spare, moved) in enumerate(plans):
        spin, pick = outs[2 * which : 2 * which + 2]
        blocks = Blocks(place[0], n, radius, total, moved)
        for part in range(radius // LANES):
            rows = pl.ds(blocks.own_at + part * LANES, LANES)
            along = lambda ref: jnp.broadcast_to(ref[part : part + 1, :].astype(jnp.float32), (LANES, LANES)).T
            held[0, rows, :] = along(rotation) * time_step
            held[1, rows, :] = along(shifts)
        held[0, pl.ds(blocks.edge_at, EXTRA), :] = spread(more, own_cells, own_cells)
        held[1, pl.ds(blocks.edge_at, EXTRA), :] = spread(more, 2 * own_cells, own_cells)
        bound = jnp.zeros((SUB, LANES), jnp.int32)
        for j in range(SUB):
            low, high = blocks.rows_of(j), blocks.rows_of(SUB + j)
            spin[pl.ds(j, TALL, stride=SUB), :] = jnp.where(front, held[0, low, :], held[0, high, :])
            pick[pl.ds(j, TALL, stride=SUB), :] = jnp.where(front, held[1, low, :], held[1, high, :]).astype(jnp.int32)
            bound = jnp.where(sublane == j, jnp.where(lane < HALF, blocks.bounds[j], blocks.bounds[SUB + j]), bound)

        def one(i, _):
            pick[tile(i), :] = (lane + (REACH + bound)) - pick[tile(i), :]
            return 0

        lax.fori_loop(0, TALL, one, 0)


def step_kernel(plan, refs, write, scratch):
    n, radius, own_cells, total, spare, moved = plan
    place, own, own_edge, near, near_edge, far, spin, pick = refs
    cells, stages, packed = scratch
    row = place[0]
    lane = lax.broadcasted_iota(jnp.int32, (SUB, LANES), 1)
    sublane = lax.broadcasted_iota(jnp.int32, (SUB, LANES), 0)
    blocks = Blocks(row, n, radius, total, moved)

    edge_lane = lax.broadcasted_iota(jnp.int32, (EXTRA, LANES), 1)
    parts = radius // LANES

    def gather(f, _):
        rows = pl.ds(pl.multiple_of(f * own_cells, SUB), own_cells)
        start = pl.multiple_of(f * (own_cells + SUB), SUB)
        for part in range(parts):
            columns = slice(part * LANES, (part + 1) * LANES)
            if part == 0:
                top = far[pl.ds(start, own_cells), :]
            else:
                top = jnp.concatenate(
                    [
                        jnp.zeros((own_cells - 2 * SUB, LANES), jnp.float32),
                        pltpu.roll(far[pl.ds(start, SUB), :], SUB - spare, 0),
                        far[pl.ds(start + own_cells, SUB), :],
                    ],
                    axis=0,
                )
            fill = jnp.zeros((own_cells, LANES), jnp.float32)
            block = jnp.concatenate([top, near[rows, columns], own[rows, columns], fill], axis=0)
            cells[f, pl.ds(blocks.own_at + part * LANES, LANES), :] = block.T
        columns = pl.ds(pl.multiple_of(lax.div(f, 4) * LANES, LANES), LANES)
        lanes_at = lax.rem(f, 4) * own_cells
        cells[f, pl.ds(blocks.edge_at, EXTRA), :] = jnp.where(
            edge_lane < 2 * own_cells,
            pltpu.roll(near_edge[:, columns], lax.rem(LANES + own_cells - lanes_at, LANES), 1),
            pltpu.roll(own_edge[:, columns], lax.rem(LANES + 2 * own_cells - lanes_at, LANES), 1),
        )
        return 0

    lax.fori_loop(0, FIELDS, gather, 0)

    front = lax.broadcasted_iota(jnp.int32, (TALL, LANES), 1) < HALF

    def deal(f, _):
        for j in range(SUB):
            low, high = j, SUB + j
            turn_low = (LANES - (2 * own_cells - REACH)) + blocks.bounds[low]
            turn_high = (HALF - (2 * own_cells - REACH)) + blocks.bounds[high]
            stages[0, f, pl.ds(j, TALL, stride=SUB), :] = jnp.where(
                front,
                pltpu.roll(cells[f, blocks.rows_of(low), :], turn_low, 1),
                pltpu.roll(cells[f, blocks.rows_of(high), :], turn_high, 1),
            )
        return 0

    lax.fori_loop(0, FIELDS, deal, 0)

    edges = (
        (sublane == 0) & (lane < HALF) & (row == 0),
        (sublane == SUB - 1) & (lane >= HALF) & (row == total // radius - 1),
    )
    run_stages(n, stages, spin, edges)

    even = (lane & own_cells) == 0

    def shift(turn, _):
        for k in range(PICKS):
            i = turn * PICKS + k
            rows = tile(REACH + i)
            source = pick[rows, :]
            picks = [source & (LANES - 1), (source - own_cells) & (LANES - 1)]
            turned = [
                jnp.take_along_axis(stages[1, f, rows, :], picks[f % 2], axis=1, mode="promise_in_bounds")
                for f in range(FIELDS)
            ]
            stages[2, 0, tile(i), :] = jnp.where(even, turned[0], turned[1])
            stages[2, 1, tile(i), :] = jnp.where(even, turned[2], turned[3])
            stages[2, 2, tile(i), :] = turned[4]
        return 0

    lax.fori_loop(0, (n + PICKS - 1) // PICKS, shift, 0)
    narrow = lax.broadcasted_iota(jnp.int32, (n, LANES), 1) < HALF
    for j in range(SUB):
        one, two, three = [stages[2, g, pl.ds(j, n, stride=SUB), :] for g in range(3)]
        low = slice(EXTRA + n * j, EXTRA + n * (j + 1))
        high = slice(EXTRA + n * (SUB + j), EXTRA + n * (SUB + j + 1))
        packed[0, low, :] = jnp.where(narrow, one, pltpu.roll(two, HALF, 1))
        packed[0, high, :] = jnp.where(narrow, pltpu.roll(one, HALF, 1), two)
        packed[1, low, :] = three
        packed[1, high, :] = pltpu.roll(three, HALF, 1)
    for part in range(parts):
        rows = pl.ds(blocks.own_at + part * LANES, LANES)
        write.fields(slice(part * LANES, (part + 1) * LANES), packed[0, rows, :].T, packed[1, rows, :].T)
    write.edge(packed[0, pl.ds(blocks.edge_at, EXTRA), :], packed[1, pl.ds(blocks.edge_at, EXTRA), :])
    write.end()


class ToMessage:
    def __init__(self, near, far, own_cells, spare):
        self.near, self.far, self.own_cells, self.spare = near, far, own_cells, spare

    def fields(self, columns, four, fifth):
        split = 4 * self.own_cells
        self.near[0:split, columns] = four
        self.near[split : split + self.own_cells, columns] = fifth[0 : self.own_cells]

    def edge(self, first, second):
        tail = FIELDS * self.own_cells
        self.near[tail : tail + EXTRA, 0:LANES] = first
        self.near[tail : tail + EXTRA, LANES : 2 * LANES] = second

    def end(self):
        pack_far(self.far, self.near, self.own_cells, self.spare)


class ToBuffer:
    def __init__(self, buffer):
        self.buffer = buffer

    def fields(self, columns, four, fifth):
        split = four.shape[0]
        self.buffer[0:split, columns] = four
        self.buffer[split:, columns] = fifth[0 : self.buffer.shape[0] - split]

    def edge(self, first, second):
        pass

    def end(self):
        pass


def copies_out(level, buffer, outs, sent):
    density, momentum, magnetic = outs
    cells = density.shape[1]
    targets = [density.at[level]] + [x.at[k, level] for x in (momentum, magnetic) for k in range(2)]
    return [
        pltpu.make_async_copy(buffer.at[pl.ds(f * cells, cells), :], x, sent.at[level * FIELDS + f])
        for f, x in enumerate(targets)
    ]


def tall_of(n):
    return EXTRA + SLOTS * n + 2 * SUB


def step_scratch(n):
    return [
        pltpu.VMEM((FIELDS, tall_of(n), LANES), jnp.float32),
        pltpu.VMEM((STAGES, FIELDS, TALL * SUB, LANES), jnp.float32),
        pltpu.VMEM((2, tall_of(n), LANES), jnp.float32),
    ]


vmem = pl.BlockSpec(memory_space=pltpu.VMEM)
smem = pl.BlockSpec(memory_space=pltpu.SMEM)
f32 = lambda *s: jax.ShapeDtypeStruct(s, jnp.float32)
params = pltpu.CompilerParams(vmem_limit_bytes=VMEM_LIMIT)
cost = pl.CostEstimate(flops=9_000_000_000, bytes_accessed=29_000_000, transcendentals=0)


def first_step(plan, level, operands):
    n, radius, own_cells, total, spare, moved = plan

    def kernel(place, own, near, far, side, corner, spin, pick, near_out, far_out, *scratch):
        refs = (place, own, side.at[level], near, corner.at[level], far, spin, pick)
        step_kernel(plan, refs, ToMessage(near_out, far_out, own_cells, spare), scratch)

    return pl.pallas_call(
        kernel,
        out_shape=[f32(FIELDS * own_cells + EXTRA, radius), f32(FIELDS * (own_cells + SUB), LANES)],
        in_specs=[smem] + [vmem] * 7,
        out_specs=[vmem] * 2,
        scratch_shapes=step_scratch(n),
        compiler_params=params,
        cost_estimate=cost,
        name="first_step",
    )(*operands)


def last_step(plan, level, operands, done, levels):
    n, radius, own_cells, total, spare, moved = plan
    tail = pl.ds(FIELDS * own_cells, EXTRA)
    final = level == levels - 1
    buffer = f32(FIELDS * own_cells, radius)

    def kernel(place, own, near, far, spin, pick, *rest):
        refs = (place, own, own.at[tail, :], near, near.at[tail, :], far, spin, pick)
        if not final:
            step_kernel(plan, refs, ToBuffer(rest[0]), rest[1:])
            return
        ready, outs, scratch = rest[: levels - 1], rest[levels - 1 : levels + 2], rest[levels + 2 :]
        last, sent = scratch[-2:]
        copies = []
        for k, x in enumerate(ready):
            copies += copies_out(k, x, outs, sent)
        for copy in copies:
            copy.start()
        step_kernel(plan, refs, ToBuffer(last), scratch[:-2])
        rest_of = copies_out(level, last, outs, sent)
        for copy in rest_of:
            copy.start()
        for copy in copies + rest_of:
            copy.wait()

    if final:
        out_shape = [f32(levels, own_cells, radius), f32(2, levels, own_cells, radius), f32(2, levels, own_cells, radius)]
        more = [pltpu.VMEM((FIELDS * own_cells, radius), jnp.float32), pltpu.SemaphoreType.DMA((levels * FIELDS,))]
    else:
        out_shape = buffer
        more = []
    return pl.pallas_call(
        kernel,
        out_shape=out_shape,
        in_specs=[smem] + [vmem] * (5 + len(done)),
        out_specs=[pl.BlockSpec(memory_space=pltpu.HBM)] * 3 if final else vmem,
        scratch_shapes=step_scratch(n) + more,
        compiler_params=params,
        cost_estimate=cost,
        name="last_step",
    )(*operands, *done)


def body(density, momentum, magnetic, rotation, shifts):
    phi_count = lax.axis_size("phi")
    row_count = lax.axis_size("row")
    levels, own_cells, radius = density.shape
    total = radius * row_count
    parts = radius // LANES
    n = radius // SLOTS
    need = [max(shift_bound(part * LANES, total) + REACH - own_cells, 0) for part in range(parts)]
    spare = own_cells - need[0]
    assert row_count == 2 and radius == 2 * LANES and own_cells == HALF // 2
    assert 0 < need[0] < own_cells and need[1] <= SUB + spare and spare <= SUB

    row = lax.axis_index("row")
    place = jnp.reshape(row, (1,)).astype(jnp.int32)
    here = lambda p, r: (p % phi_count) * row_count + r
    everyone = [(p, r) for p in range(phi_count) for r in range(row_count)]
    both = ("phi", "row")
    send_near = lambda x: lax.ppermute(x, "phi", [(p, (p + 1) % phi_count) for p in range(phi_count)])
    send_far = lambda x: lax.ppermute(x, "phi", [(p, (p + 2) % phi_count) for p in range(phi_count)])
    send_side = lambda x: lax.ppermute(x, "row", [(0, 1), (1, 0)])
    send_corner = lambda x: lax.ppermute(x, both, [(here(p, r), here(p + 1, 1 - r)) for p, r in everyone])

    spins, turns = rotation.reshape(parts, LANES), shifts.reshape(parts, LANES)
    near_message = f32(FIELDS * own_cells, radius)
    far_message = f32(FIELDS * (own_cells + SUB), LANES)
    packed = pl.pallas_call(
        lambda *refs: pack_kernel(spare, levels, *refs),
        out_shape=[near_message] * levels
        + [far_message] * levels
        + [f32(levels, EXTRA, 2 * LANES)],
        in_specs=[smem] + [pl.BlockSpec(memory_space=pltpu.HBM)] * 5,
        out_specs=[vmem] * (2 * levels + 1),
        scratch_shapes=[
            pltpu.VMEM((parts, LANES), jnp.float32),
            pltpu.VMEM((parts, LANES), jnp.int32),
            pltpu.SemaphoreType.DMA((levels * FIELDS + 2,)),
        ],
        compiler_params=pltpu.CompilerParams(vmem_limit_bytes=PACK_LIMIT),
        name="pack",
    )(place, density, momentum, magnetic, spins, turns)
    owns, fars, edge = packed[:levels], packed[levels : 2 * levels], packed[2 * levels]

    side = send_side(edge)
    corner = send_corner(edge)
    wide = (n + 1, radius, own_cells, total, spare, EXTRA)
    plain = (n, radius, own_cells, total, spare, 0)
    i32 = jax.ShapeDtypeStruct((TALL * SUB, LANES), jnp.int32)
    tables = pl.pallas_call(
        lambda *refs: table_kernel((wide, plain), *refs),
        out_shape=[f32(TALL * SUB, LANES), i32] * 2,
        in_specs=[smem] + [vmem] * 3,
        out_specs=[vmem] * 4,
        scratch_shapes=[pltpu.VMEM((2, tall_of(n + 1), LANES), jnp.float32)],
        compiler_params=params,
        name="tables",
    )(place, side, spins, turns)
    moved = [(send_near(own), send_far(far)) for own, far in zip(owns, fars)]
    states = []
    for level in range(levels):
        near, far = moved[level]
        states.append(first_step(wide, level, (place, owns[level], near, far, side, corner, *tables[:2])))
    moved = [(send_near(own), send_far(far)) for own, far in states]
    done = ()
    for level in range(levels):
        near, far = moved[level]
        operands = (place, states[level][0], near, far, *tables[2:])
        result = last_step(plain, level, operands, done if level == levels - 1 else (), levels)
        done += (result,)
    return tuple(result)


def solution(mesh):
    placed = (
        P(None, "phi", "row"),
        P(None, None, "phi", "row"),
        P(None, None, "phi", "row"),
        P("row"),
        P("row"),
    )
    return jax.shard_map(
        body,
        mesh=mesh,
        in_specs=placed,
        out_specs=(P(None, "phi", "row"), P(None, None, "phi", "row"), P(None, None, "phi", "row")),
        check_vma=False,
    )
```

```python
import jax
import jax.numpy as jnp
from jax import lax
from jax.experimental import pallas as pl
from jax.experimental.pallas import tpu as pltpu
from jax.sharding import PartitionSpec as P

STEPS = 2
SMIN = 8
SMAX = 56
STAGES = 3
REACH = 2 * STAGES
FIELDS = 5
LANES = 128
SUB = 8
HALF = LANES // 2
SLOTS = 2 * SUB
EXTRA = 2 * SUB
TALL = 32
ROWS = 4
PICKS = 4
VMEM_LIMIT = 32 * 1024 * 1024
EDGE_LIMIT = 60 * 1024 * 1024

time_step = 0.08


def shift_bound(first_row, rows):
    d = rows - 1 - first_row
    return min(SMIN + (SMAX - SMIN - 1) * d * d // ((rows - 1) * (rows - 1)) + 1, SMAX)


def minmod(lower, upper):
    return jnp.maximum(jnp.minimum(lower, 0.0), jnp.minimum(upper, jnp.maximum(lower, 0.0)))


def physical(state):
    rho, mn, mt, bn, bt = state
    inverse = pltpu.reciprocal(rho, approx=True)
    vn = mn * inverse
    vt = mt * inverse
    bn_sq = bn * bn
    bt_sq = bt * bt
    ram = mn * vn + rho
    tension = bt_sq - bn_sq
    flux_t = mt * vn - bn * bt
    flux_b = bt * vn - bn * vt
    inside = (bn_sq + bt_sq) * inverse + 1.0
    speed = jnp.abs(vn) + inside * lax.rsqrt(inside)
    return ram, tension, flux_t, flux_b, speed


def face_twice(left, right):
    left_ram, left_tension, left_t, left_b, left_speed = physical(left)
    right_ram, right_tension, right_t, right_b, right_speed = physical(right)
    bound = jnp.maximum(left_speed, right_speed)
    jumps = [bound * (l - r) for l, r in zip(left, right)]
    return [
        (left[1] + right[1]) + jumps[0],
        ((left_ram + right_ram) + 0.5 * (left_tension + right_tension)) + jumps[1],
        (left_t + right_t) + jumps[2],
        jumps[3],
        (left_b + right_b) + jumps[4],
    ]


def swapped(five):
    return [five[0], five[2], five[1], five[4], five[3]]


def radial_faces(rows):
    halves = [[0.5 * x for x in r] for r in rows]
    jumps = [[b - a for a, b in zip(p, q)] for p, q in zip(halves[:-1], halves[1:])]
    slopes = [[minmod(a, b) for a, b in zip(p, q)] for p, q in zip(jumps[:-1], jumps[1:])]
    upper = [[x + s for x, s in zip(r, sl)] for r, sl in zip(rows[1:-1], slopes)]
    lower = [[x - s for x, s in zip(r, sl)] for r, sl in zip(rows[1:-1], slopes)]
    return [swapped(face_twice(swapped(u), swapped(l))) for u, l in zip(upper[:-1], lower[1:])]


def azimuth_change(fields):
    right_of = lambda x: pltpu.roll(x, LANES - 1, 1)
    left_of = lambda x: pltpu.roll(x, 1, 1)
    lower = []
    upper = []
    for x in fields:
        half = 0.5 * x
        jump = right_of(half) - half
        slope = minmod(left_of(jump), jump)
        upper.append(x + slope)
        lower.append(right_of(x - slope))
    return [x - left_of(x) for x in face_twice(upper, lower)]


def tile(i):
    return pl.ds(pl.multiple_of(i * SUB, SUB), SUB)


def run_stages(n, stages, spin, edges):
    half_dt = 0.5 * time_step
    low_mask, high_mask = edges
    first, last = REACH, REACH + n - 1

    def work(stage, i0, count, before):
        src, dst = stage, (stage & 1) + 1
        weight = jnp.where(stage == 0, 1.0, jnp.where(stage == 1, 0.25, 2.0 / 3.0))
        keep = jnp.where(stage == 0, 0.0, jnp.where(stage == 1, 0.75, 1.0 / 3.0))
        rows = [[stages[src, f, tile(i0 + k), :] for f in range(FIELDS)] for k in range(-1, count + 2)]
        starts = [[stages[0, f, tile(i0 + k), :] for f in range(FIELDS)] for k in range(count)]
        turns = [spin[tile(i0 + k), :] for k in range(count)]
        faces = [before] + radial_faces(rows)
        for k in range(count):
            fields = rows[k + 1]
            change = azimuth_change(fields)
            turn = turns[k]
            source = [
                None,
                (-0.5 * turn) * fields[2],
                (2.0 * turn) * fields[1],
                (-1.5 * turn) * fields[4],
                None,
            ]
            for f in range(FIELDS):
                new = fields[f] - half_dt * (change[f] + (faces[k + 1][f] - faces[k][f]))
                if source[f] is not None:
                    new = new + source[f]
                stages[dst, f, tile(i0 + k), :] = weight * new + keep * starts[k][f]
        return faces[-1]

    def run(stage, _):
        for f in range(FIELDS):
            inner = stages[stage, f, tile(first), :]
            outer = stages[stage, f, tile(last), :]
            for k in (1, 2):
                stages[stage, f, tile(first - k), :] = jnp.where(low_mask, inner, stages[stage, f, tile(first - k), :])
                stages[stage, f, tile(last + k), :] = jnp.where(high_mask, outer, stages[stage, f, tile(last + k), :])
        count = n + 2 * REACH - 4 - 4 * stage
        if n % ROWS == 0:
            lo = 2 * stage + 2
            ahead = [[stages[stage, f, tile(lo + k), :] for f in range(FIELDS)] for k in range(-2, 2)]
            before = tuple(radial_faces(ahead)[0])
        else:
            lo = 2 * stage + 1
            count = count + 1
            before = (jnp.zeros((SUB, LANES), jnp.float32),) * FIELDS
        turns = lax.div(count + ROWS - 1, ROWS)
        lax.fori_loop(0, turns, lambda c, carried: tuple(work(stage, lo + c * ROWS, ROWS, list(carried))), before)
        return 0

    lax.fori_loop(0, STAGES, run, 0)


def spread(block, first, width):
    block = pltpu.roll(block, (LANES - first) % LANES, 1)
    lane = lax.broadcasted_iota(jnp.int32, block.shape, 1)
    while width < LANES:
        block = jnp.where(lane < width, block, pltpu.roll(block, width, 1))
        width *= 2
    return block


def pack_far(far, near, own_cells, spare):
    sublane = lax.broadcasted_iota(jnp.int32, (SUB, LANES), 0)

    def one(f, _):
        start = pl.multiple_of(f * own_cells, SUB)
        base = pl.multiple_of(f * (own_cells + SUB), SUB)
        low = near[pl.ds(start, own_cells), 0:LANES]
        high = near[pl.ds(start + own_cells - 2 * SUB, 2 * SUB), LANES : 2 * LANES]
        moved = pltpu.roll(high[0:SUB], spare, 0)
        far[pl.ds(base, SUB), :] = jnp.where(sublane < spare, moved, low[0:SUB])
        far[pl.ds(base + SUB, own_cells - SUB), :] = low[SUB:]
        far[pl.ds(base + own_cells, SUB), :] = high[SUB:]
        return 0

    lax.fori_loop(0, FIELDS, one, 0)


def edge_kernel(place, density, momentum, magnetic, rotation, shifts, edge, ends, spin_in, shift_in, arrived):
    levels, own_cells, radius = density.shape
    on_low = place[0] == 0
    parts = radius // LANES
    split = 4 * own_cells
    columns = pl.ds(pl.multiple_of(jnp.where(on_low, radius - LANES, 0), LANES), LANES)
    copies = [
        pltpu.make_async_copy(rotation, spin_in, arrived.at[levels * FIELDS]),
        pltpu.make_async_copy(shifts, shift_in, arrived.at[levels * FIELDS + 1]),
    ]
    for level in range(levels):
        sources = [density.at[level, :, columns]] + [x.at[k, level, :, columns] for x in (momentum, magnetic) for k in range(2)]
        for f, x in enumerate(sources):
            at = ends.at[level, pl.ds(f * own_cells, own_cells), :]
            copies.append(pltpu.make_async_copy(x, at, arrived.at[level * FIELDS + f]))
    for copy in copies:
        copy.start()
    for copy in copies:
        copy.wait()
    wide = lambda ref: jnp.broadcast_to(
        jnp.where(on_low, ref[parts - 1 : parts, :], ref[0:1, :]).astype(jnp.float32), (own_cells, LANES)
    )
    turn = wide(spin_in) * time_step
    shift = wide(shift_in)
    zero = jnp.zeros((own_cells, LANES), jnp.float32)
    for level in range(levels):
        last = jnp.concatenate([ends[level, split:, :], turn, shift, zero], axis=0)
        for side, group in enumerate((ends[level, 0:split, :], last)):
            turned = group.T
            edge[level, :, side * LANES : (side + 1) * LANES] = jnp.where(on_low, turned[LANES - EXTRA :], turned[0:EXTRA])


def pack_kernel(spare, levels, density, momentum, magnetic, side, *outs):
    nears, fars = outs[:levels], outs[levels:]
    own_cells = density.shape[1]
    for level in range(levels):
        sources = [density.at[level]] + [x.at[k, level] for x in (momentum, magnetic) for k in range(2)]
        for f, x in enumerate(sources):
            nears[level][f * own_cells : (f + 1) * own_cells, :] = x[...]
        nears[level][FIELDS * own_cells :, :] = side[level]
        pack_far(fars[level], nears[level], own_cells, spare)


class Blocks:
    def __init__(self, row, n, radius, total, moved):
        self.on_low = row == 0
        self.n = n
        self.own_at = pl.multiple_of(jnp.where(self.on_low, EXTRA, EXTRA + moved), SUB)
        self.edge_at = pl.multiple_of(jnp.where(self.on_low, EXTRA + radius, moved), SUB)
        bounds = [[shift_bound(r * radius - (moved if r else 0) + n * k, total) for k in range(SLOTS)] for r in range(2)]
        self.bounds = [jnp.where(self.on_low, a, b) for a, b in zip(*bounds)]

    def rows_of(self, k):
        start = EXTRA - REACH + self.n * k
        return slice(start, start + TALL)


def table_kernel(plans, place, side, rotation, shifts, *rest):
    outs, held = rest[:-1], rest[-1]
    lane = lax.broadcasted_iota(jnp.int32, (SUB, LANES), 1)
    sublane = lax.broadcasted_iota(jnp.int32, (SUB, LANES), 0)
    front = lax.broadcasted_iota(jnp.int32, (TALL, LANES), 1) < HALF
    more = side[0, :, LANES : 2 * LANES]
    for which, (n, radius, own_cells, total, spare, moved) in enumerate(plans):
        spin, pick = outs[2 * which : 2 * which + 2]
        blocks = Blocks(place[0], n, radius, total, moved)
        for part in range(radius // LANES):
            rows = pl.ds(blocks.own_at + part * LANES, LANES)
            along = lambda ref: jnp.broadcast_to(ref[part : part + 1, :].astype(jnp.float32), (LANES, LANES)).T
            held[0, rows, :] = along(rotation) * time_step
            held[1, rows, :] = along(shifts)
        held[0, pl.ds(blocks.edge_at, EXTRA), :] = spread(more, own_cells, own_cells)
        held[1, pl.ds(blocks.edge_at, EXTRA), :] = spread(more, 2 * own_cells, own_cells)
        bound = jnp.zeros((SUB, LANES), jnp.int32)
        for j in range(SUB):
            low, high = blocks.rows_of(j), blocks.rows_of(SUB + j)
            spin[pl.ds(j, TALL, stride=SUB), :] = jnp.where(front, held[0, low, :], held[0, high, :])
            pick[pl.ds(j, TALL, stride=SUB), :] = jnp.where(front, held[1, low, :], held[1, high, :]).astype(jnp.int32)
            bound = jnp.where(sublane == j, jnp.where(lane < HALF, blocks.bounds[j], blocks.bounds[SUB + j]), bound)

        def one(i, _):
            pick[tile(i), :] = (lane + (REACH + bound)) - pick[tile(i), :]
            return 0

        lax.fori_loop(0, TALL, one, 0)


def step_kernel(plan, refs, write, scratch):
    n, radius, own_cells, total, spare, moved = plan
    place, own, near, far, spin, pick = refs
    tail = slice(FIELDS * own_cells, FIELDS * own_cells + EXTRA)
    cells, stages, packed = scratch
    row = place[0]
    lane = lax.broadcasted_iota(jnp.int32, (SUB, LANES), 1)
    sublane = lax.broadcasted_iota(jnp.int32, (SUB, LANES), 0)
    blocks = Blocks(row, n, radius, total, moved)

    edge_lane = lax.broadcasted_iota(jnp.int32, (EXTRA, LANES), 1)
    parts = radius // LANES

    def gather(f, _):
        rows = pl.ds(pl.multiple_of(f * own_cells, SUB), own_cells)
        start = pl.multiple_of(f * (own_cells + SUB), SUB)
        for part in range(parts):
            columns = slice(part * LANES, (part + 1) * LANES)
            if part == 0:
                top = far[pl.ds(start, own_cells), :]
            else:
                top = jnp.concatenate(
                    [
                        jnp.zeros((own_cells - 2 * SUB, LANES), jnp.float32),
                        pltpu.roll(far[pl.ds(start, SUB), :], SUB - spare, 0),
                        far[pl.ds(start + own_cells, SUB), :],
                    ],
                    axis=0,
                )
            fill = jnp.zeros((own_cells, LANES), jnp.float32)
            block = jnp.concatenate([top, near[rows, columns], own[rows, columns], fill], axis=0)
            cells[f, pl.ds(blocks.own_at + part * LANES, LANES), :] = block.T
        columns = pl.ds(pl.multiple_of(lax.div(f, 4) * LANES, LANES), LANES)
        lanes_at = lax.rem(f, 4) * own_cells
        cells[f, pl.ds(blocks.edge_at, EXTRA), :] = jnp.where(
            edge_lane < 2 * own_cells,
            pltpu.roll(near[tail, columns], lax.rem(LANES + own_cells - lanes_at, LANES), 1),
            pltpu.roll(own[tail, columns], lax.rem(LANES + 2 * own_cells - lanes_at, LANES), 1),
        )
        return 0

    lax.fori_loop(0, FIELDS, gather, 0)

    front = lax.broadcasted_iota(jnp.int32, (TALL, LANES), 1) < HALF

    def deal(f, _):
        for j in range(SUB):
            low, high = j, SUB + j
            turn_low = (LANES - (2 * own_cells - REACH)) + blocks.bounds[low]
            turn_high = (HALF - (2 * own_cells - REACH)) + blocks.bounds[high]
            stages[0, f, pl.ds(j, TALL, stride=SUB), :] = jnp.where(
                front,
                pltpu.roll(cells[f, blocks.rows_of(low), :], turn_low, 1),
                pltpu.roll(cells[f, blocks.rows_of(high), :], turn_high, 1),
            )
        return 0

    lax.fori_loop(0, FIELDS, deal, 0)

    edges = (
        (sublane == 0) & (lane < HALF) & (row == 0),
        (sublane == SUB - 1) & (lane >= HALF) & (row == total // radius - 1),
    )
    run_stages(n, stages, spin, edges)

    even = (lane & own_cells) == 0

    def shift(turn, _):
        for k in range(PICKS):
            i = turn * PICKS + k
            rows = tile(REACH + i)
            source = pick[rows, :]
            picks = [source & (LANES - 1), (source - own_cells) & (LANES - 1)]
            turned = [
                jnp.take_along_axis(stages[1, f, rows, :], picks[f % 2], axis=1, mode="promise_in_bounds")
                for f in range(FIELDS)
            ]
            stages[2, 0, tile(i), :] = jnp.where(even, turned[0], turned[1])
            stages[2, 1, tile(i), :] = jnp.where(even, turned[2], turned[3])
            stages[2, 2, tile(i), :] = turned[4]
        return 0

    lax.fori_loop(0, (n + PICKS - 1) // PICKS, shift, 0)
    narrow = lax.broadcasted_iota(jnp.int32, (n, LANES), 1) < HALF
    for j in range(SUB):
        one, two, three = [stages[2, g, pl.ds(j, n, stride=SUB), :] for g in range(3)]
        low = slice(EXTRA + n * j, EXTRA + n * (j + 1))
        high = slice(EXTRA + n * (SUB + j), EXTRA + n * (SUB + j + 1))
        packed[0, low, :] = jnp.where(narrow, one, pltpu.roll(two, HALF, 1))
        packed[0, high, :] = jnp.where(narrow, pltpu.roll(one, HALF, 1), two)
        packed[1, low, :] = three
        packed[1, high, :] = pltpu.roll(three, HALF, 1)
    for part in range(parts):
        rows = pl.ds(blocks.own_at + part * LANES, LANES)
        write.fields(slice(part * LANES, (part + 1) * LANES), packed[0, rows, :].T, packed[1, rows, :].T)
    write.edge(packed[0, pl.ds(blocks.edge_at, EXTRA), :], packed[1, pl.ds(blocks.edge_at, EXTRA), :])
    write.end()


class ToMessage:
    def __init__(self, near, far, own_cells, spare):
        self.near, self.far, self.own_cells, self.spare = near, far, own_cells, spare

    def fields(self, columns, four, fifth):
        split = 4 * self.own_cells
        self.near[0:split, columns] = four
        self.near[split : split + self.own_cells, columns] = fifth[0 : self.own_cells]

    def edge(self, first, second):
        tail = FIELDS * self.own_cells
        self.near[tail : tail + EXTRA, 0:LANES] = first
        self.near[tail : tail + EXTRA, LANES : 2 * LANES] = second

    def end(self):
        pack_far(self.far, self.near, self.own_cells, self.spare)


class ToBuffer:
    def __init__(self, buffer):
        self.buffer = buffer

    def fields(self, columns, four, fifth):
        split = four.shape[0]
        self.buffer[0:split, columns] = four
        self.buffer[split:, columns] = fifth[0 : self.buffer.shape[0] - split]

    def edge(self, first, second):
        pass

    def end(self):
        pass


def copies_out(level, buffer, outs, sent):
    density, momentum, magnetic = outs
    cells = density.shape[1]
    targets = [density.at[level]] + [x.at[k, level] for x in (momentum, magnetic) for k in range(2)]
    return [
        pltpu.make_async_copy(buffer.at[pl.ds(f * cells, cells), :], x, sent.at[level * FIELDS + f])
        for f, x in enumerate(targets)
    ]


def tall_of(n):
    return EXTRA + SLOTS * n + 2 * SUB


def step_scratch(n):
    return [
        pltpu.VMEM((FIELDS, tall_of(n), LANES), jnp.float32),
        pltpu.VMEM((STAGES, FIELDS, TALL * SUB, LANES), jnp.float32),
        pltpu.VMEM((2, tall_of(n), LANES), jnp.float32),
    ]


vmem = pl.BlockSpec(memory_space=pltpu.VMEM)
smem = pl.BlockSpec(memory_space=pltpu.SMEM)
f32 = lambda *s: jax.ShapeDtypeStruct(s, jnp.float32)
params = pltpu.CompilerParams(vmem_limit_bytes=VMEM_LIMIT)
cost = pl.CostEstimate(flops=9_000_000_000, bytes_accessed=29_000_000, transcendentals=0)


def first_step(plan, operands):
    n, radius, own_cells, total, spare, moved = plan

    def kernel(place, own, near, far, spin, pick, near_out, far_out, *scratch):
        refs = (place, own, near, far, spin, pick)
        step_kernel(plan, refs, ToMessage(near_out, far_out, own_cells, spare), scratch)

    return pl.pallas_call(
        kernel,
        out_shape=[f32(FIELDS * own_cells + EXTRA, radius), f32(FIELDS * (own_cells + SUB), LANES)],
        in_specs=[smem] + [vmem] * 5,
        out_specs=[vmem] * 2,
        scratch_shapes=step_scratch(n),
        compiler_params=params,
        cost_estimate=cost,
        name="first_step",
    )(*operands)


def last_step(plan, level, operands, done, levels):
    n, radius, own_cells, total, spare, moved = plan
    final = level == levels - 1
    buffer = f32(FIELDS * own_cells, radius)

    def kernel(place, own, near, far, spin, pick, *rest):
        refs = (place, own, near, far, spin, pick)
        if not final:
            step_kernel(plan, refs, ToBuffer(rest[0]), rest[1:])
            return
        ready, outs, scratch = rest[: levels - 1], rest[levels - 1 : levels + 2], rest[levels + 2 :]
        last, sent = scratch[-2:]
        copies = []
        for k, x in enumerate(ready):
            copies += copies_out(k, x, outs, sent)
        for copy in copies:
            copy.start()
        step_kernel(plan, refs, ToBuffer(last), scratch[:-2])
        rest_of = copies_out(level, last, outs, sent)
        for copy in rest_of:
            copy.start()
        for copy in copies + rest_of:
            copy.wait()

    if final:
        out_shape = [f32(levels, own_cells, radius), f32(2, levels, own_cells, radius), f32(2, levels, own_cells, radius)]
        more = [pltpu.VMEM((FIELDS * own_cells, radius), jnp.float32), pltpu.SemaphoreType.DMA((levels * FIELDS,))]
    else:
        out_shape = buffer
        more = []
    return pl.pallas_call(
        kernel,
        out_shape=out_shape,
        in_specs=[smem] + [vmem] * (5 + len(done)),
        out_specs=[pl.BlockSpec(memory_space=pltpu.HBM)] * 3 if final else vmem,
        scratch_shapes=step_scratch(n) + more,
        compiler_params=params,
        cost_estimate=cost,
        name="last_step",
    )(*operands, *done)


def body(density, momentum, magnetic, rotation, shifts):
    phi_count = lax.axis_size("phi")
    row_count = lax.axis_size("row")
    levels, own_cells, radius = density.shape
    total = radius * row_count
    parts = radius // LANES
    n = radius // SLOTS
    need = [max(shift_bound(part * LANES, total) + REACH - own_cells, 0) for part in range(parts)]
    spare = own_cells - need[0]
    assert row_count == 2 and radius == 2 * LANES and own_cells == HALF // 2
    assert 0 < need[0] < own_cells and need[1] <= SUB + spare and spare <= SUB

    row = lax.axis_index("row")
    place = jnp.reshape(row, (1,)).astype(jnp.int32)
    send_near = lambda x: lax.ppermute(x, "phi", [(p, (p + 1) % phi_count) for p in range(phi_count)])
    send_far = lambda x: lax.ppermute(x, "phi", [(p, (p + 2) % phi_count) for p in range(phi_count)])
    send_side = lambda x: lax.ppermute(x, "row", [(0, 1), (1, 0)])

    spins, turns = rotation.reshape(parts, LANES), shifts.reshape(parts, LANES)
    near_message = f32(FIELDS * own_cells + EXTRA, radius)
    far_message = f32(FIELDS * (own_cells + SUB), LANES)
    edge = pl.pallas_call(
        edge_kernel,
        out_shape=f32(levels, EXTRA, 2 * LANES),
        in_specs=[smem] + [pl.BlockSpec(memory_space=pltpu.HBM)] * 5,
        out_specs=vmem,
        scratch_shapes=[
            pltpu.VMEM((levels, FIELDS * own_cells, LANES), jnp.float32),
            pltpu.VMEM((parts, LANES), jnp.float32),
            pltpu.VMEM((parts, LANES), jnp.int32),
            pltpu.SemaphoreType.DMA((levels * FIELDS + 2,)),
        ],
        compiler_params=pltpu.CompilerParams(vmem_limit_bytes=EDGE_LIMIT),
        name="edges",
    )(place, density, momentum, magnetic, spins, turns)
    side = send_side(edge)
    packed = pl.pallas_call(
        lambda *refs: pack_kernel(spare, levels, *refs),
        out_shape=[near_message] * levels + [far_message] * levels,
        in_specs=[vmem] * 4,
        out_specs=[vmem] * (2 * levels),
        compiler_params=params,
        cost_estimate=cost,
        name="pack",
    )(density, momentum, magnetic, side)
    owns, fars = packed[:levels], packed[levels:]
    wide = (n + 1, radius, own_cells, total, spare, EXTRA)
    plain = (n, radius, own_cells, total, spare, 0)
    i32 = jax.ShapeDtypeStruct((TALL * SUB, LANES), jnp.int32)
    tables = pl.pallas_call(
        lambda *refs: table_kernel((wide, plain), *refs),
        out_shape=[f32(TALL * SUB, LANES), i32] * 2,
        in_specs=[smem] + [vmem] * 3,
        out_specs=[vmem] * 4,
        scratch_shapes=[pltpu.VMEM((2, tall_of(n + 1), LANES), jnp.float32)],
        compiler_params=params,
        name="tables",
    )(place, side, spins, turns)
    moved = [(send_near(own), send_far(far)) for own, far in zip(owns, fars)]
    states = []
    for level in range(levels):
        near, far = moved[level]
        states.append(first_step(wide, (place, owns[level], near, far, *tables[:2])))
    moved = [(send_near(own), send_far(far)) for own, far in states]
    done = ()
    for level in range(levels):
        near, far = moved[level]
        operands = (place, states[level][0], near, far, *tables[2:])
        result = last_step(plain, level, operands, done if level == levels - 1 else (), levels)
        done += (result,)
    return tuple(result)


def solution(mesh):
    placed = (
        P(None, "phi", "row"),
        P(None, None, "phi", "row"),
        P(None, None, "phi", "row"),
        P("row"),
        P("row"),
    )
    return jax.shard_map(
        body,
        mesh=mesh,
        in_specs=placed,
        out_specs=(P(None, "phi", "row"), P(None, None, "phi", "row"), P(None, None, "phi", "row")),
        check_vma=False,
    )
```

```python
import jax
import jax.numpy as jnp
from jax import lax
from jax.experimental import pallas as pl
from jax.experimental.pallas import tpu as pltpu
from jax.sharding import PartitionSpec as P

STEPS = 2
SMIN = 8
SMAX = 56
STAGES = 3
REACH = 2 * STAGES
FIELDS = 5
LANES = 128
SUB = 8
HALF = LANES // 2
SLOTS = 2 * SUB
EXTRA = 2 * SUB
TALL = 32
ROWS = 4
PICKS = 4
VMEM_LIMIT = 32 * 1024 * 1024
EDGE_LIMIT = 60 * 1024 * 1024

time_step = 0.08


def shift_bound(first_row, rows):
    d = rows - 1 - first_row
    return min(SMIN + (SMAX - SMIN - 1) * d * d // ((rows - 1) * (rows - 1)) + 1, SMAX)


def minmod(lower, upper):
    return jnp.maximum(jnp.minimum(lower, 0.0), jnp.minimum(upper, jnp.maximum(lower, 0.0)))


def physical(state):
    rho, mn, mt, bn, bt = state
    inverse = pltpu.reciprocal(rho, approx=True)
    vn = mn * inverse
    vt = mt * inverse
    bn_sq = bn * bn
    bt_sq = bt * bt
    ram = mn * vn + rho
    tension = bt_sq - bn_sq
    flux_t = mt * vn - bn * bt
    flux_b = bt * vn - bn * vt
    inside = (bn_sq + bt_sq) * inverse + 1.0
    speed = jnp.abs(vn) + inside * lax.rsqrt(inside)
    return ram, tension, flux_t, flux_b, speed


def face_twice(left, right):
    left_ram, left_tension, left_t, left_b, left_speed = physical(left)
    right_ram, right_tension, right_t, right_b, right_speed = physical(right)
    bound = jnp.maximum(left_speed, right_speed)
    jumps = [bound * (l - r) for l, r in zip(left, right)]
    return [
        (left[1] + right[1]) + jumps[0],
        ((left_ram + right_ram) + 0.5 * (left_tension + right_tension)) + jumps[1],
        (left_t + right_t) + jumps[2],
        jumps[3],
        (left_b + right_b) + jumps[4],
    ]


def swapped(five):
    return [five[0], five[2], five[1], five[4], five[3]]


def radial_faces(rows):
    halves = [[0.5 * x for x in r] for r in rows]
    jumps = [[b - a for a, b in zip(p, q)] for p, q in zip(halves[:-1], halves[1:])]
    slopes = [[minmod(a, b) for a, b in zip(p, q)] for p, q in zip(jumps[:-1], jumps[1:])]
    upper = [[x + s for x, s in zip(r, sl)] for r, sl in zip(rows[1:-1], slopes)]
    lower = [[x - s for x, s in zip(r, sl)] for r, sl in zip(rows[1:-1], slopes)]
    return [swapped(face_twice(swapped(u), swapped(l))) for u, l in zip(upper[:-1], lower[1:])]


def azimuth_change(fields):
    right_of = lambda x: pltpu.roll(x, LANES - 1, 1)
    left_of = lambda x: pltpu.roll(x, 1, 1)
    lower = []
    upper = []
    for x in fields:
        half = 0.5 * x
        jump = right_of(half) - half
        slope = minmod(left_of(jump), jump)
        upper.append(x + slope)
        lower.append(right_of(x - slope))
    return [x - left_of(x) for x in face_twice(upper, lower)]


def tile(i):
    return pl.ds(pl.multiple_of(i * SUB, SUB), SUB)


def run_stages(n, stages, spin, edges, live):
    half_dt = 0.5 * time_step
    low_mask, high_mask = edges
    first, last = REACH, REACH + n - 1

    def work(stage, i0, count, before):
        src, dst = stage, (stage & 1) + 1
        weight = jnp.where(stage == 0, 1.0, jnp.where(stage == 1, 0.25, 2.0 / 3.0))
        keep = jnp.where(stage == 0, 0.0, jnp.where(stage == 1, 0.75, 1.0 / 3.0))
        rows = [[stages[src, f, tile(i0 + k), :] for f in range(FIELDS)] for k in range(-1, count + 2)]
        starts = [[stages[0, f, tile(i0 + k), :] for f in range(FIELDS)] for k in range(count)]
        turns = [spin[tile(i0 + k), :] for k in range(count)]
        faces = [before] + radial_faces(rows)
        for k in range(count):
            fields = rows[k + 1]
            change = azimuth_change(fields)
            turn = turns[k]
            source = [
                None,
                (-0.5 * turn) * fields[2],
                (2.0 * turn) * fields[1],
                (-1.5 * turn) * fields[4],
                None,
            ]
            for f in range(FIELDS):
                new = fields[f] - half_dt * (change[f] + (faces[k + 1][f] - faces[k][f]))
                if source[f] is not None:
                    new = new + source[f]
                stages[dst, f, tile(i0 + k), :] = weight * new + keep * starts[k][f]
        return faces[-1]

    def run(stage, _):
        for f in range(FIELDS):
            inner = stages[stage, f, tile(first), :]
            outer = stages[stage, f, tile(last), :]
            for k in (1, 2):
                stages[stage, f, tile(first - k), :] = jnp.where(low_mask, inner, stages[stage, f, tile(first - k), :])
                stages[stage, f, tile(last + k), :] = jnp.where(high_mask, outer, stages[stage, f, tile(last + k), :])
        count = n + 2 * REACH - 4 - 4 * stage
        if n % ROWS == 0:
            lo = 2 * stage + 2
            ahead = [[stages[stage, f, tile(lo + k), :] for f in range(FIELDS)] for k in range(-2, 2)]
            before = tuple(radial_faces(ahead)[0])
        else:
            lo = 2 * stage + 1
            count = count + 1
            before = (jnp.zeros((SUB, LANES), jnp.float32),) * FIELDS
        turns = jnp.where(live, lax.div(count + ROWS - 1, ROWS), 1)
        lax.fori_loop(0, turns, lambda c, carried: tuple(work(stage, lo + c * ROWS, ROWS, list(carried))), before)
        return 0

    lax.fori_loop(0, jnp.where(live, STAGES, 1), run, 0)


def spread(block, first, width):
    block = pltpu.roll(block, (LANES - first) % LANES, 1)
    lane = lax.broadcasted_iota(jnp.int32, block.shape, 1)
    while width < LANES:
        block = jnp.where(lane < width, block, pltpu.roll(block, width, 1))
        width *= 2
    return block


def pack_far(far, near, own_cells, spare):
    sublane = lax.broadcasted_iota(jnp.int32, (SUB, LANES), 0)

    def one(f, _):
        start = pl.multiple_of(f * own_cells, SUB)
        base = pl.multiple_of(f * (own_cells + SUB), SUB)
        low = near[pl.ds(start, own_cells), 0:LANES]
        high = near[pl.ds(start + own_cells - 2 * SUB, 2 * SUB), LANES : 2 * LANES]
        moved = pltpu.roll(high[0:SUB], spare, 0)
        far[pl.ds(base, SUB), :] = jnp.where(sublane < spare, moved, low[0:SUB])
        far[pl.ds(base + SUB, own_cells - SUB), :] = low[SUB:]
        far[pl.ds(base + own_cells, SUB), :] = high[SUB:]
        return 0

    lax.fori_loop(0, FIELDS, one, 0)


def edge_kernel(place, density, momentum, magnetic, rotation, shifts, edge, ends, spin_in, shift_in, arrived):
    levels, own_cells, radius = density.shape
    on_low = place[0] == 0
    parts = radius // LANES
    split = 4 * own_cells
    columns = pl.ds(pl.multiple_of(jnp.where(on_low, radius - LANES, 0), LANES), LANES)
    copies = [
        pltpu.make_async_copy(rotation, spin_in, arrived.at[levels * FIELDS]),
        pltpu.make_async_copy(shifts, shift_in, arrived.at[levels * FIELDS + 1]),
    ]
    for level in range(levels):
        sources = [density.at[level, :, columns]] + [x.at[k, level, :, columns] for x in (momentum, magnetic) for k in range(2)]
        for f, x in enumerate(sources):
            at = ends.at[level, pl.ds(f * own_cells, own_cells), :]
            copies.append(pltpu.make_async_copy(x, at, arrived.at[level * FIELDS + f]))
    for copy in copies:
        copy.start()
    for copy in copies:
        copy.wait()
    wide = lambda ref: jnp.broadcast_to(
        jnp.where(on_low, ref[parts - 1 : parts, :], ref[0:1, :]).astype(jnp.float32), (own_cells, LANES)
    )
    turn = wide(spin_in) * time_step
    shift = wide(shift_in)
    zero = jnp.zeros((own_cells, LANES), jnp.float32)
    for level in range(levels):
        last = jnp.concatenate([ends[level, split:, :], turn, shift, zero], axis=0)
        for side, group in enumerate((ends[level, 0:split, :], last)):
            turned = group.T
            edge[level, :, side * LANES : (side + 1) * LANES] = jnp.where(on_low, turned[LANES - EXTRA :], turned[0:EXTRA])


def pack_kernel(spare, levels, density, momentum, magnetic, side, *outs):
    nears, fars = outs[:levels], outs[levels:]
    own_cells = density.shape[1]
    for level in range(levels):
        sources = [density.at[level]] + [x.at[k, level] for x in (momentum, magnetic) for k in range(2)]
        for f, x in enumerate(sources):
            nears[level][f * own_cells : (f + 1) * own_cells, :] = x[...]
        nears[level][FIELDS * own_cells :, :] = side[level]
        pack_far(fars[level], nears[level], own_cells, spare)


class Blocks:
    def __init__(self, row, n, radius, total, moved):
        self.on_low = row == 0
        self.n = n
        self.own_at = pl.multiple_of(jnp.where(self.on_low, EXTRA, EXTRA + moved), SUB)
        self.edge_at = pl.multiple_of(jnp.where(self.on_low, EXTRA + radius, moved), SUB)
        bounds = [[shift_bound(r * radius - (moved if r else 0) + n * k, total) for k in range(SLOTS)] for r in range(2)]
        self.bounds = [jnp.where(self.on_low, a, b) for a, b in zip(*bounds)]

    def rows_of(self, k):
        start = EXTRA - REACH + self.n * k
        return slice(start, start + TALL)


def table_kernel(plans, place, side, rotation, shifts, *rest):
    outs, held = rest[:-1], rest[-1]
    lane = lax.broadcasted_iota(jnp.int32, (SUB, LANES), 1)
    sublane = lax.broadcasted_iota(jnp.int32, (SUB, LANES), 0)
    front = lax.broadcasted_iota(jnp.int32, (TALL, LANES), 1) < HALF
    more = side[0, :, LANES : 2 * LANES]
    for which, (n, radius, own_cells, total, spare, moved) in enumerate(plans):
        spin, pick = outs[2 * which : 2 * which + 2]
        blocks = Blocks(place[0], n, radius, total, moved)
        for part in range(radius // LANES):
            rows = pl.ds(blocks.own_at + part * LANES, LANES)
            along = lambda ref: jnp.broadcast_to(ref[part : part + 1, :].astype(jnp.float32), (LANES, LANES)).T
            held[0, rows, :] = along(rotation) * time_step
            held[1, rows, :] = along(shifts)
        held[0, pl.ds(blocks.edge_at, EXTRA), :] = spread(more, own_cells, own_cells)
        held[1, pl.ds(blocks.edge_at, EXTRA), :] = spread(more, 2 * own_cells, own_cells)
        bound = jnp.zeros((SUB, LANES), jnp.int32)
        for j in range(SUB):
            low, high = blocks.rows_of(j), blocks.rows_of(SUB + j)
            spin[pl.ds(j, TALL, stride=SUB), :] = jnp.where(front, held[0, low, :], held[0, high, :])
            pick[pl.ds(j, TALL, stride=SUB), :] = jnp.where(front, held[1, low, :], held[1, high, :]).astype(jnp.int32)
            bound = jnp.where(sublane == j, jnp.where(lane < HALF, blocks.bounds[j], blocks.bounds[SUB + j]), bound)

        def one(i, _):
            pick[tile(i), :] = (lane + (REACH + bound)) - pick[tile(i), :]
            return 0

        lax.fori_loop(0, TALL, one, 0)


def step_kernel(plan, refs, write, scratch):
    n, radius, own_cells, total, spare, moved = plan
    place, own, near, far, spin, pick = refs
    tail = slice(FIELDS * own_cells, FIELDS * own_cells + EXTRA)
    cells, stages, packed = scratch
    row = place[0]
    lane = lax.broadcasted_iota(jnp.int32, (SUB, LANES), 1)
    sublane = lax.broadcasted_iota(jnp.int32, (SUB, LANES), 0)
    blocks = Blocks(row, n, radius, total, moved)

    edge_lane = lax.broadcasted_iota(jnp.int32, (EXTRA, LANES), 1)
    parts = radius // LANES

    def gather(f, _):
        rows = pl.ds(pl.multiple_of(f * own_cells, SUB), own_cells)
        start = pl.multiple_of(f * (own_cells + SUB), SUB)
        for part in range(parts):
            columns = slice(part * LANES, (part + 1) * LANES)
            if part == 0:
                top = far[pl.ds(start, own_cells), :]
            else:
                top = jnp.concatenate(
                    [
                        jnp.zeros((own_cells - 2 * SUB, LANES), jnp.float32),
                        pltpu.roll(far[pl.ds(start, SUB), :], SUB - spare, 0),
                        far[pl.ds(start + own_cells, SUB), :],
                    ],
                    axis=0,
                )
            fill = jnp.zeros((own_cells, LANES), jnp.float32)
            block = jnp.concatenate([top, near[rows, columns], own[rows, columns], fill], axis=0)
            cells[f, pl.ds(blocks.own_at + part * LANES, LANES), :] = block.T
        columns = pl.ds(pl.multiple_of(lax.div(f, 4) * LANES, LANES), LANES)
        lanes_at = lax.rem(f, 4) * own_cells
        cells[f, pl.ds(blocks.edge_at, EXTRA), :] = jnp.where(
            edge_lane < 2 * own_cells,
            pltpu.roll(near[tail, columns], lax.rem(LANES + own_cells - lanes_at, LANES), 1),
            pltpu.roll(own[tail, columns], lax.rem(LANES + 2 * own_cells - lanes_at, LANES), 1),
        )
        return 0

    live = place[1] > 0
    lax.fori_loop(0, jnp.where(live, FIELDS, 1), gather, 0)

    front = lax.broadcasted_iota(jnp.int32, (TALL, LANES), 1) < HALF

    def deal(f, _):
        for j in range(SUB):
            low, high = j, SUB + j
            turn_low = (LANES - (2 * own_cells - REACH)) + blocks.bounds[low]
            turn_high = (HALF - (2 * own_cells - REACH)) + blocks.bounds[high]
            stages[0, f, pl.ds(j, TALL, stride=SUB), :] = jnp.where(
                front,
                pltpu.roll(cells[f, blocks.rows_of(low), :], turn_low, 1),
                pltpu.roll(cells[f, blocks.rows_of(high), :], turn_high, 1),
            )
        return 0

    lax.fori_loop(0, jnp.where(live, FIELDS, 1), deal, 0)

    edges = (
        (sublane == 0) & (lane < HALF) & (row == 0),
        (sublane == SUB - 1) & (lane >= HALF) & (row == total // radius - 1),
    )
    run_stages(n, stages, spin, edges, live)

    even = (lane & own_cells) == 0

    def shift(turn, _):
        for k in range(PICKS):
            i = turn * PICKS + k
            rows = tile(REACH + i)
            source = pick[rows, :]
            picks = [source & (LANES - 1), (source - own_cells) & (LANES - 1)]
            turned = [
                jnp.take_along_axis(stages[1, f, rows, :], picks[f % 2], axis=1, mode="promise_in_bounds")
                for f in range(FIELDS)
            ]
            stages[2, 0, tile(i), :] = jnp.where(even, turned[0], turned[1])
            stages[2, 1, tile(i), :] = jnp.where(even, turned[2], turned[3])
            stages[2, 2, tile(i), :] = turned[4]
        return 0

    lax.fori_loop(0, jnp.where(live, (n + PICKS - 1) // PICKS, 1), shift, 0)
    narrow = lax.broadcasted_iota(jnp.int32, (n, LANES), 1) < HALF
    for j in range(SUB):
        one, two, three = [stages[2, g, pl.ds(j, n, stride=SUB), :] for g in range(3)]
        low = slice(EXTRA + n * j, EXTRA + n * (j + 1))
        high = slice(EXTRA + n * (SUB + j), EXTRA + n * (SUB + j + 1))
        packed[0, low, :] = jnp.where(narrow, one, pltpu.roll(two, HALF, 1))
        packed[0, high, :] = jnp.where(narrow, pltpu.roll(one, HALF, 1), two)
        packed[1, low, :] = three
        packed[1, high, :] = pltpu.roll(three, HALF, 1)
    for part in range(parts):
        rows = pl.ds(blocks.own_at + part * LANES, LANES)
        write.fields(slice(part * LANES, (part + 1) * LANES), packed[0, rows, :].T, packed[1, rows, :].T)
    write.edge(packed[0, pl.ds(blocks.edge_at, EXTRA), :], packed[1, pl.ds(blocks.edge_at, EXTRA), :])
    write.end()


class ToMessage:
    def __init__(self, near, far, own_cells, spare):
        self.near, self.far, self.own_cells, self.spare = near, far, own_cells, spare

    def fields(self, columns, four, fifth):
        split = 4 * self.own_cells
        self.near[0:split, columns] = four
        self.near[split : split + self.own_cells, columns] = fifth[0 : self.own_cells]

    def edge(self, first, second):
        tail = FIELDS * self.own_cells
        self.near[tail : tail + EXTRA, 0:LANES] = first
        self.near[tail : tail + EXTRA, LANES : 2 * LANES] = second

    def end(self):
        pack_far(self.far, self.near, self.own_cells, self.spare)


def copies_out(level, buffer, outs, sent):
    density, momentum, magnetic = outs
    cells = density.shape[1]
    targets = [density.at[level]] + [x.at[k, level] for x in (momentum, magnetic) for k in range(2)]
    return [
        pltpu.make_async_copy(buffer.at[pl.ds(f * cells, cells), :], x, sent.at[level * FIELDS + f])
        for f, x in enumerate(targets)
    ]


def tall_of(n):
    return EXTRA + SLOTS * n + 2 * SUB


def step_scratch(n):
    return [
        pltpu.VMEM((FIELDS, tall_of(n), LANES), jnp.float32),
        pltpu.VMEM((STAGES, FIELDS, TALL * SUB, LANES), jnp.float32),
        pltpu.VMEM((2, tall_of(n), LANES), jnp.float32),
    ]


vmem = pl.BlockSpec(memory_space=pltpu.VMEM)
smem = pl.BlockSpec(memory_space=pltpu.SMEM)
f32 = lambda *s: jax.ShapeDtypeStruct(s, jnp.float32)
params = pltpu.CompilerParams(vmem_limit_bytes=VMEM_LIMIT)
cost = pl.CostEstimate(flops=9_000_000_000, bytes_accessed=29_000_000, transcendentals=0)


def step(plan, operands):
    n, radius, own_cells, total, spare, moved = plan

    def kernel(place, own, near, far, spin, pick, near_out, far_out, *scratch):
        refs = (place, own, near, far, spin, pick)
        step_kernel(plan, refs, ToMessage(near_out, far_out, own_cells, spare), scratch)

        @pl.when(place[1] == 0)
        def _():
            def hand(ref, out):
                def one(i, _):
                    out[tile(i), :] = ref[tile(i), :]
                    return 0

                lax.fori_loop(0, ref.shape[0] // SUB, one, 0)

            hand(own, near_out)
            hand(far, far_out)

    return pl.pallas_call(
        kernel,
        out_shape=[f32(FIELDS * own_cells + EXTRA, radius), f32(FIELDS * (own_cells + SUB), LANES)],
        in_specs=[smem] + [vmem] * 5,
        out_specs=[vmem] * 2,
        scratch_shapes=step_scratch(n),
        compiler_params=params,
        cost_estimate=cost,
        name="step",
    )(*operands)


def unpack(levels, own_cells, radius, states):
    def kernel(*refs):
        buffers, outs, sent = refs[:levels], refs[levels:-1], refs[-1]
        copies = [copy for level in range(levels) for copy in copies_out(level, buffers[level], outs, sent)]
        for copy in copies:
            copy.start()
        for copy in copies:
            copy.wait()

    return pl.pallas_call(
        kernel,
        out_shape=[f32(levels, own_cells, radius), f32(2, levels, own_cells, radius), f32(2, levels, own_cells, radius)],
        in_specs=[vmem] * levels,
        out_specs=[pl.BlockSpec(memory_space=pltpu.HBM)] * 3,
        scratch_shapes=[pltpu.SemaphoreType.DMA((levels * FIELDS,))],
        compiler_params=params,
        name="unpack",
    )(*states)


def body(density, momentum, magnetic, rotation, shifts):
    phi_count = lax.axis_size("phi")
    row_count = lax.axis_size("row")
    levels, own_cells, radius = density.shape
    total = radius * row_count
    parts = radius // LANES
    n = radius // SLOTS
    need = [max(shift_bound(part * LANES, total) + REACH - own_cells, 0) for part in range(parts)]
    spare = own_cells - need[0]
    assert row_count == 2 and radius == 2 * LANES and own_cells == HALF // 2
    assert 0 < need[0] < own_cells and need[1] <= SUB + spare and spare <= SUB

    row = lax.axis_index("row")
    place = jnp.reshape(row, (1,)).astype(jnp.int32)
    send_near = lambda x: lax.ppermute(x, "phi", [(p, (p + 1) % phi_count) for p in range(phi_count)])
    send_far = lambda x: lax.ppermute(x, "phi", [(p, (p + 2) % phi_count) for p in range(phi_count)])
    send_side = lambda x: lax.ppermute(x, "row", [(0, 1), (1, 0)])

    spins, turns = rotation.reshape(parts, LANES), shifts.reshape(parts, LANES)
    near_message = f32(FIELDS * own_cells + EXTRA, radius)
    far_message = f32(FIELDS * (own_cells + SUB), LANES)
    edge = pl.pallas_call(
        edge_kernel,
        out_shape=f32(levels, EXTRA, 2 * LANES),
        in_specs=[smem] + [pl.BlockSpec(memory_space=pltpu.HBM)] * 5,
        out_specs=vmem,
        scratch_shapes=[
            pltpu.VMEM((levels, FIELDS * own_cells, LANES), jnp.float32),
            pltpu.VMEM((parts, LANES), jnp.float32),
            pltpu.VMEM((parts, LANES), jnp.int32),
            pltpu.SemaphoreType.DMA((levels * FIELDS + 2,)),
        ],
        compiler_params=pltpu.CompilerParams(vmem_limit_bytes=EDGE_LIMIT),
        name="edges",
    )(place, density, momentum, magnetic, spins, turns)
    side = send_side(edge)
    packed = pl.pallas_call(
        lambda *refs: pack_kernel(spare, levels, *refs),
        out_shape=[near_message] * levels + [far_message] * levels,
        in_specs=[vmem] * 4,
        out_specs=[vmem] * (2 * levels),
        compiler_params=params,
        cost_estimate=cost,
        name="pack",
    )(density, momentum, magnetic, side)
    owns, fars = packed[:levels], packed[levels:]
    wide = (n + 1, radius, own_cells, total, spare, EXTRA)
    i32 = jax.ShapeDtypeStruct((TALL * SUB, LANES), jnp.int32)
    tables = pl.pallas_call(
        lambda *refs: table_kernel((wide,), *refs),
        out_shape=[f32(TALL * SUB, LANES), i32],
        in_specs=[smem] + [vmem] * 3,
        out_specs=[vmem] * 2,
        scratch_shapes=[pltpu.VMEM((2, tall_of(n + 1), LANES), jnp.float32)],
        compiler_params=params,
        name="tables",
    )(place, side, spins, turns)
    def turn(i, carried):
        send_own, send_beyond, own, near, far = carried
        where = jnp.stack([row, i]).astype(jnp.int32)
        sent = send_near(send_own), send_far(send_beyond)
        new = step(wide, (where, own, near, far, *tables))
        return (*new, send_own, *sent)

    assert levels == 2
    first = (owns[0], fars[0], owns[1], owns[1], fars[1])
    carried = lax.fori_loop(0, STEPS * levels + 1, turn, first)
    return tuple(unpack(levels, own_cells, radius, (carried[2], carried[0])))


def solution(mesh):
    placed = (
        P(None, "phi", "row"),
        P(None, None, "phi", "row"),
        P(None, None, "phi", "row"),
        P("row"),
        P("row"),
    )
    return jax.shard_map(
        body,
        mesh=mesh,
        in_specs=placed,
        out_specs=(P(None, "phi", "row"), P(None, None, "phi", "row"), P(None, None, "phi", "row")),
        check_vma=False,
    )
```

```python
import jax
import jax.numpy as jnp
from jax import lax
from jax.experimental import pallas as pl
from jax.experimental.pallas import tpu as pltpu
from jax.sharding import PartitionSpec as P

STEPS = 2
SMIN = 8
SMAX = 56
STAGES = 3
REACH = 2 * STAGES
FIELDS = 5
LANES = 128
SUB = 8
HALF = LANES // 2
SLOTS = 2 * SUB
EXTRA = 2 * SUB
TALL = 32
ROWS = 4
PICKS = 4
VMEM_LIMIT = 32 * 1024 * 1024
EDGE_LIMIT = 60 * 1024 * 1024

time_step = 0.08


def shift_bound(first_row, rows):
    d = rows - 1 - first_row
    return min(SMIN + (SMAX - SMIN - 1) * d * d // ((rows - 1) * (rows - 1)) + 1, SMAX)


def minmod(lower, upper):
    return jnp.maximum(jnp.minimum(lower, 0.0), jnp.minimum(upper, jnp.maximum(lower, 0.0)))


def physical(state):
    rho, mn, mt, bn, bt = state
    inverse = pltpu.reciprocal(rho, approx=True)
    vn = mn * inverse
    vt = mt * inverse
    bn_sq = bn * bn
    bt_sq = bt * bt
    ram = mn * vn + rho
    tension = bt_sq - bn_sq
    flux_t = mt * vn - bn * bt
    flux_b = bt * vn - bn * vt
    inside = (bn_sq + bt_sq) * inverse + 1.0
    speed = jnp.abs(vn) + inside * lax.rsqrt(inside)
    return ram, tension, flux_t, flux_b, speed


def face_twice(left, right):
    left_ram, left_tension, left_t, left_b, left_speed = physical(left)
    right_ram, right_tension, right_t, right_b, right_speed = physical(right)
    bound = jnp.maximum(left_speed, right_speed)
    jumps = [bound * (l - r) for l, r in zip(left, right)]
    return [
        (left[1] + right[1]) + jumps[0],
        ((left_ram + right_ram) + 0.5 * (left_tension + right_tension)) + jumps[1],
        (left_t + right_t) + jumps[2],
        jumps[3],
        (left_b + right_b) + jumps[4],
    ]


def swapped(five):
    return [five[0], five[2], five[1], five[4], five[3]]


def radial_faces(rows):
    halves = [[0.5 * x for x in r] for r in rows]
    jumps = [[b - a for a, b in zip(p, q)] for p, q in zip(halves[:-1], halves[1:])]
    slopes = [[minmod(a, b) for a, b in zip(p, q)] for p, q in zip(jumps[:-1], jumps[1:])]
    upper = [[x + s for x, s in zip(r, sl)] for r, sl in zip(rows[1:-1], slopes)]
    lower = [[x - s for x, s in zip(r, sl)] for r, sl in zip(rows[1:-1], slopes)]
    return [swapped(face_twice(swapped(u), swapped(l))) for u, l in zip(upper[:-1], lower[1:])]


def azimuth_change(fields):
    right_of = lambda x: pltpu.roll(x, LANES - 1, 1)
    left_of = lambda x: pltpu.roll(x, 1, 1)
    lower = []
    upper = []
    for x in fields:
        half = 0.5 * x
        jump = right_of(half) - half
        slope = minmod(left_of(jump), jump)
        upper.append(x + slope)
        lower.append(right_of(x - slope))
    return [x - left_of(x) for x in face_twice(upper, lower)]


def tile(i):
    return pl.ds(pl.multiple_of(i * SUB, SUB), SUB)


def run_stages(n, stages, spin, edges):
    half_dt = 0.5 * time_step
    low_mask, high_mask = edges
    first, last = REACH, REACH + n - 1

    def work(stage, i0, count, before):
        src, dst = stage, (stage & 1) + 1
        weight = jnp.where(stage == 0, 1.0, jnp.where(stage == 1, 0.25, 2.0 / 3.0))
        keep = jnp.where(stage == 0, 0.0, jnp.where(stage == 1, 0.75, 1.0 / 3.0))
        rows = [[stages[src, f, tile(i0 + k), :] for f in range(FIELDS)] for k in range(-1, count + 2)]
        starts = [[stages[0, f, tile(i0 + k), :] for f in range(FIELDS)] for k in range(count)]
        turns = [spin[tile(i0 + k), :] for k in range(count)]
        faces = [before] + radial_faces(rows)
        for k in range(count):
            fields = rows[k + 1]
            change = azimuth_change(fields)
            turn = turns[k]
            source = [
                None,
                (-0.5 * turn) * fields[2],
                (2.0 * turn) * fields[1],
                (-1.5 * turn) * fields[4],
                None,
            ]
            for f in range(FIELDS):
                new = fields[f] - half_dt * (change[f] + (faces[k + 1][f] - faces[k][f]))
                if source[f] is not None:
                    new = new + source[f]
                stages[dst, f, tile(i0 + k), :] = weight * new + keep * starts[k][f]
        return faces[-1]

    def run(stage, _):
        for f in range(FIELDS):
            inner = stages[stage, f, tile(first), :]
            outer = stages[stage, f, tile(last), :]
            for k in (1, 2):
                stages[stage, f, tile(first - k), :] = jnp.where(low_mask, inner, stages[stage, f, tile(first - k), :])
                stages[stage, f, tile(last + k), :] = jnp.where(high_mask, outer, stages[stage, f, tile(last + k), :])
        count = n + 2 * REACH - 4 - 4 * stage
        if n % ROWS == 0:
            lo = 2 * stage + 2
            ahead = [[stages[stage, f, tile(lo + k), :] for f in range(FIELDS)] for k in range(-2, 2)]
            before = tuple(radial_faces(ahead)[0])
        else:
            lo = 2 * stage + 1
            count = count + 1
            before = (jnp.zeros((SUB, LANES), jnp.float32),) * FIELDS
        turns = lax.div(count + ROWS - 1, ROWS)
        lax.fori_loop(0, turns, lambda c, carried: tuple(work(stage, lo + c * ROWS, ROWS, list(carried))), before)
        return 0

    lax.fori_loop(0, STAGES, run, 0)


def spread(block, first, width):
    block = pltpu.roll(block, (LANES - first) % LANES, 1)
    lane = lax.broadcasted_iota(jnp.int32, block.shape, 1)
    while width < LANES:
        block = jnp.where(lane < width, block, pltpu.roll(block, width, 1))
        width *= 2
    return block


def pack_far(far, near, own_cells, spare):
    sublane = lax.broadcasted_iota(jnp.int32, (SUB, LANES), 0)

    def one(f, _):
        start = pl.multiple_of(f * own_cells, SUB)
        base = pl.multiple_of(f * (own_cells + SUB), SUB)
        low = near[pl.ds(start, own_cells), 0:LANES]
        high = near[pl.ds(start + own_cells - 2 * SUB, 2 * SUB), LANES : 2 * LANES]
        moved = pltpu.roll(high[0:SUB], spare, 0)
        far[pl.ds(base, SUB), :] = jnp.where(sublane < spare, moved, low[0:SUB])
        far[pl.ds(base + SUB, own_cells - SUB), :] = low[SUB:]
        far[pl.ds(base + own_cells, SUB), :] = high[SUB:]
        return 0

    lax.fori_loop(0, FIELDS, one, 0)


def edge_kernel(place, density, momentum, magnetic, rotation, shifts, edge, ends, spin_in, shift_in, arrived):
    levels, own_cells, radius = density.shape
    on_low = place[0] == 0
    parts = radius // LANES
    split = 4 * own_cells
    columns = pl.ds(pl.multiple_of(jnp.where(on_low, radius - LANES, 0), LANES), LANES)
    copies = [
        pltpu.make_async_copy(rotation, spin_in, arrived.at[levels * FIELDS]),
        pltpu.make_async_copy(shifts, shift_in, arrived.at[levels * FIELDS + 1]),
    ]
    for level in range(levels):
        sources = [density.at[level, :, columns]] + [x.at[k, level, :, columns] for x in (momentum, magnetic) for k in range(2)]
        for f, x in enumerate(sources):
            at = ends.at[level, pl.ds(f * own_cells, own_cells), :]
            copies.append(pltpu.make_async_copy(x, at, arrived.at[level * FIELDS + f]))
    for copy in copies:
        copy.start()
    for copy in copies:
        copy.wait()
    wide = lambda ref: jnp.broadcast_to(
        jnp.where(on_low, ref[parts - 1 : parts, :], ref[0:1, :]).astype(jnp.float32), (own_cells, LANES)
    )
    turn = wide(spin_in) * time_step
    shift = wide(shift_in)
    zero = jnp.zeros((own_cells, LANES), jnp.float32)
    for level in range(levels):
        last = jnp.concatenate([ends[level, split:, :], turn, shift, zero], axis=0)
        for side, group in enumerate((ends[level, 0:split, :], last)):
            turned = group.T
            edge[level, :, side * LANES : (side + 1) * LANES] = jnp.where(on_low, turned[LANES - EXTRA :], turned[0:EXTRA])


def pack_kernel(spare, levels, density, momentum, magnetic, side, *outs):
    nears, fars = outs[:levels], outs[levels:]
    own_cells = density.shape[1]
    for level in range(levels):
        sources = [density.at[level]] + [x.at[k, level] for x in (momentum, magnetic) for k in range(2)]
        for f, x in enumerate(sources):
            nears[level][f * own_cells : (f + 1) * own_cells, :] = x[...]
        nears[level][FIELDS * own_cells :, :] = side[level]
        pack_far(fars[level], nears[level], own_cells, spare)


class Blocks:
    def __init__(self, row, n, radius, total, moved):
        self.on_low = row == 0
        self.n = n
        self.own_at = pl.multiple_of(jnp.where(self.on_low, EXTRA, EXTRA + moved), SUB)
        self.edge_at = pl.multiple_of(jnp.where(self.on_low, EXTRA + radius, moved), SUB)
        bounds = [[shift_bound(r * radius - (moved if r else 0) + n * k, total) for k in range(SLOTS)] for r in range(2)]
        self.bounds = [jnp.where(self.on_low, a, b) for a, b in zip(*bounds)]

    def rows_of(self, k):
        start = EXTRA - REACH + self.n * k
        return slice(start, start + TALL)


def table_kernel(plans, place, side, rotation, shifts, *rest):
    outs, held = rest[:-1], rest[-1]
    lane = lax.broadcasted_iota(jnp.int32, (SUB, LANES), 1)
    sublane = lax.broadcasted_iota(jnp.int32, (SUB, LANES), 0)
    front = lax.broadcasted_iota(jnp.int32, (TALL, LANES), 1) < HALF
    more = side[0, :, LANES : 2 * LANES]
    for which, (n, radius, own_cells, total, spare, moved) in enumerate(plans):
        spin, pick, frame = outs[3 * which : 3 * which + 3]
        blocks = Blocks(place[0], n, radius, total, moved)
        for part in range(radius // LANES):
            rows = pl.ds(blocks.own_at + part * LANES, LANES)
            along = lambda ref: jnp.broadcast_to(ref[part : part + 1, :].astype(jnp.float32), (LANES, LANES)).T
            held[0, rows, :] = along(rotation) * time_step
            held[1, rows, :] = along(shifts)
        held[0, pl.ds(blocks.edge_at, EXTRA), :] = spread(more, own_cells, own_cells)
        held[1, pl.ds(blocks.edge_at, EXTRA), :] = spread(more, 2 * own_cells, own_cells)
        bound = jnp.zeros((SUB, LANES), jnp.int32)
        for j in range(SUB):
            low, high = blocks.rows_of(j), blocks.rows_of(SUB + j)
            spin[pl.ds(j, TALL, stride=SUB), :] = jnp.where(front, held[0, low, :], held[0, high, :])
            pick[pl.ds(j, TALL, stride=SUB), :] = jnp.where(front, held[1, low, :], held[1, high, :]).astype(jnp.int32)
            bound = jnp.where(sublane == j, jnp.where(lane < HALF, blocks.bounds[j], blocks.bounds[SUB + j]), bound)

        first = lane + (2 * own_cells - REACH) - bound
        frame[0] = first & (LANES - 1)
        frame[1] = (first + HALF) & (LANES - 1)

        def one(i, _):
            pick[tile(i), :] = (lane + (REACH + bound)) - pick[tile(i), :]
            return 0

        lax.fori_loop(0, TALL, one, 0)


def lanes_of(x, index):
    return jnp.take_along_axis(x, index, axis=1, mode="promise_in_bounds")


def step_kernel(plan, refs, write, scratch):
    n, radius, own_cells, total, spare, moved = plan
    place, own, near, far, spin, pick, frame = refs
    tail = slice(FIELDS * own_cells, FIELDS * own_cells + EXTRA)
    cells, stages, packed = scratch
    row = place[0]
    lane = lax.broadcasted_iota(jnp.int32, (SUB, LANES), 1)
    sublane = lax.broadcasted_iota(jnp.int32, (SUB, LANES), 0)
    blocks = Blocks(row, n, radius, total, moved)

    edge_lane = lax.broadcasted_iota(jnp.int32, (EXTRA, LANES), 1)
    parts = radius // LANES

    def gather(f, _):
        rows = pl.ds(pl.multiple_of(f * own_cells, SUB), own_cells)
        start = pl.multiple_of(f * (own_cells + SUB), SUB)
        for part in range(parts):
            columns = slice(part * LANES, (part + 1) * LANES)
            if part == 0:
                top = far[pl.ds(start, own_cells), :]
            else:
                top = jnp.concatenate(
                    [
                        jnp.zeros((own_cells - 2 * SUB, LANES), jnp.float32),
                        pltpu.roll(far[pl.ds(start, SUB), :], SUB - spare, 0),
                        far[pl.ds(start + own_cells, SUB), :],
                    ],
                    axis=0,
                )
            block = jnp.concatenate([top, near[rows, columns], own[rows, columns]], axis=0)
            cells[f, pl.ds(blocks.own_at + part * LANES, LANES), 0 : 3 * own_cells] = block.T
        columns = pl.ds(pl.multiple_of(lax.div(f, 4) * LANES, LANES), LANES)
        lanes_at = lax.rem(f, 4) * own_cells
        cells[f, pl.ds(blocks.edge_at, EXTRA), :] = jnp.where(
            edge_lane < 2 * own_cells,
            pltpu.roll(near[tail, columns], lax.rem(LANES + own_cells - lanes_at, LANES), 1),
            pltpu.roll(own[tail, columns], lax.rem(LANES + 2 * own_cells - lanes_at, LANES), 1),
        )
        return 0

    lax.fori_loop(0, FIELDS, gather, 0)

    front = lane < HALF

    def deal(turn, _):
        low, high = frame[0], frame[1]
        for k in range(PICKS):
            i = turn * PICKS + k
            at = EXTRA - REACH + i
            for f in range(FIELDS):
                one = cells[f, pl.ds(at, SUB, stride=n), :]
                two = cells[f, pl.ds(at + SUB * n, SUB, stride=n), :]
                stages[0, f, tile(i), :] = jnp.where(front, lanes_of(one, low), lanes_of(two, high))
        return 0

    lax.fori_loop(0, (n + 2 * REACH + PICKS - 1) // PICKS, deal, 0)

    edges = (
        (sublane == 0) & (lane < HALF) & (row == 0),
        (sublane == SUB - 1) & (lane >= HALF) & (row == total // radius - 1),
    )
    run_stages(n, stages, spin, edges)

    even = (lane & own_cells) == 0

    count = (n + PICKS - 1) // PICKS

    def shift(turn, _):
        for k in range(PICKS):
            i = (count - turn) * PICKS - 1 - k
            rows = tile(REACH + i)
            source = pick[rows, :]
            picks = [source & (LANES - 1), (source - own_cells) & (LANES - 1)]
            turned = [lanes_of(stages[1, f, rows, :], picks[f % 2]) for f in range(FIELDS)]
            one = jnp.where(even, turned[0], turned[1])
            two = jnp.where(even, turned[2], turned[3])
            low = pl.ds(EXTRA + i, SUB, stride=n)
            high = pl.ds(EXTRA + SUB * n + i, SUB, stride=n)
            packed[0, low, :] = jnp.where(front, one, pltpu.roll(two, HALF, 1))
            packed[0, high, :] = jnp.where(front, pltpu.roll(one, HALF, 1), two)
            packed[1, low, :] = turned[4]
            packed[1, high, :] = pltpu.roll(turned[4], HALF, 1)
        return 0

    lax.fori_loop(0, count, shift, 0)
    for part in range(parts):
        rows = pl.ds(blocks.own_at + part * LANES, LANES)
        write.fields(slice(part * LANES, (part + 1) * LANES), packed[0, rows, :].T, packed[1, rows, :].T)
    write.edge(packed[0, pl.ds(blocks.edge_at, EXTRA), :], packed[1, pl.ds(blocks.edge_at, EXTRA), :])
    write.end()


class ToMessage:
    def __init__(self, near, far, own_cells, spare):
        self.near, self.far, self.own_cells, self.spare = near, far, own_cells, spare

    def fields(self, columns, four, fifth):
        split = 4 * self.own_cells
        self.near[0:split, columns] = four
        self.near[split : split + self.own_cells, columns] = fifth[0 : self.own_cells]

    def edge(self, first, second):
        tail = FIELDS * self.own_cells
        self.near[tail : tail + EXTRA, 0:LANES] = first
        self.near[tail : tail + EXTRA, LANES : 2 * LANES] = second

    def end(self):
        pack_far(self.far, self.near, self.own_cells, self.spare)


class ToBuffer:
    def __init__(self, buffer):
        self.buffer = buffer

    def fields(self, columns, four, fifth):
        split = four.shape[0]
        self.buffer[0:split, columns] = four
        self.buffer[split:, columns] = fifth[0 : self.buffer.shape[0] - split]

    def edge(self, first, second):
        pass

    def end(self):
        pass


def copies_out(level, buffer, outs, sent):
    density, momentum, magnetic = outs
    cells = density.shape[1]
    targets = [density.at[level]] + [x.at[k, level] for x in (momentum, magnetic) for k in range(2)]
    return [
        pltpu.make_async_copy(buffer.at[pl.ds(f * cells, cells), :], x, sent.at[level * FIELDS + f])
        for f, x in enumerate(targets)
    ]


def tall_of(n):
    return EXTRA + SLOTS * n + 2 * SUB


def step_scratch(n):
    return [
        pltpu.VMEM((FIELDS, tall_of(n), LANES), jnp.float32),
        pltpu.VMEM((STAGES, FIELDS, TALL * SUB, LANES), jnp.float32),
        pltpu.VMEM((2, tall_of(n), LANES), jnp.float32),
    ]


vmem = pl.BlockSpec(memory_space=pltpu.VMEM)
smem = pl.BlockSpec(memory_space=pltpu.SMEM)
f32 = lambda *s: jax.ShapeDtypeStruct(s, jnp.float32)
params = pltpu.CompilerParams(vmem_limit_bytes=VMEM_LIMIT)
cost = pl.CostEstimate(flops=9_000_000_000, bytes_accessed=29_000_000, transcendentals=0)


def first_step(plan, operands):
    n, radius, own_cells, total, spare, moved = plan

    def kernel(place, own, near, far, spin, pick, frame, near_out, far_out, *scratch):
        refs = (place, own, near, far, spin, pick, frame)
        step_kernel(plan, refs, ToMessage(near_out, far_out, own_cells, spare), scratch)

    return pl.pallas_call(
        kernel,
        out_shape=[f32(FIELDS * own_cells + EXTRA, radius), f32(FIELDS * (own_cells + SUB), LANES)],
        in_specs=[smem] + [vmem] * 6,
        out_specs=[vmem] * 2,
        scratch_shapes=step_scratch(n),
        compiler_params=params,
        cost_estimate=cost,
        name="first_step",
    )(*operands)


def last_step(plan, level, operands, done, levels):
    n, radius, own_cells, total, spare, moved = plan
    final = level == levels - 1
    buffer = f32(FIELDS * own_cells, radius)

    def kernel(place, own, near, far, spin, pick, frame, *rest):
        refs = (place, own, near, far, spin, pick, frame)
        if not final:
            step_kernel(plan, refs, ToBuffer(rest[0]), rest[1:])
            return
        ready, outs, scratch = rest[: levels - 1], rest[levels - 1 : levels + 2], rest[levels + 2 :]
        last, sent = scratch[-2:]
        copies = []
        for k, x in enumerate(ready):
            copies += copies_out(k, x, outs, sent)
        for copy in copies:
            copy.start()
        step_kernel(plan, refs, ToBuffer(last), scratch[:-2])
        rest_of = copies_out(level, last, outs, sent)
        for copy in rest_of:
            copy.start()
        for copy in copies + rest_of:
            copy.wait()

    if final:
        out_shape = [f32(levels, own_cells, radius), f32(2, levels, own_cells, radius), f32(2, levels, own_cells, radius)]
        more = [pltpu.VMEM((FIELDS * own_cells, radius), jnp.float32), pltpu.SemaphoreType.DMA((levels * FIELDS,))]
    else:
        out_shape = buffer
        more = []
    return pl.pallas_call(
        kernel,
        out_shape=out_shape,
        in_specs=[smem] + [vmem] * (6 + len(done)),
        out_specs=[pl.BlockSpec(memory_space=pltpu.HBM)] * 3 if final else vmem,
        scratch_shapes=step_scratch(n) + more,
        compiler_params=params,
        cost_estimate=cost,
        name="last_step",
    )(*operands, *done)


def body(density, momentum, magnetic, rotation, shifts):
    phi_count = lax.axis_size("phi")
    row_count = lax.axis_size("row")
    levels, own_cells, radius = density.shape
    total = radius * row_count
    parts = radius // LANES
    n = radius // SLOTS
    need = [max(shift_bound(part * LANES, total) + REACH - own_cells, 0) for part in range(parts)]
    spare = own_cells - need[0]
    assert row_count == 2 and radius == 2 * LANES and own_cells == HALF // 2
    assert 0 < need[0] < own_cells and need[1] <= SUB + spare and spare <= SUB

    row = lax.axis_index("row")
    place = jnp.reshape(row, (1,)).astype(jnp.int32)
    send_near = lambda x: lax.ppermute(x, "phi", [(p, (p + 1) % phi_count) for p in range(phi_count)])
    send_far = lambda x: lax.ppermute(x, "phi", [(p, (p + 2) % phi_count) for p in range(phi_count)])
    send_side = lambda x: lax.ppermute(x, "row", [(0, 1), (1, 0)])

    spins, turns = rotation.reshape(parts, LANES), shifts.reshape(parts, LANES)
    near_message = f32(FIELDS * own_cells + EXTRA, radius)
    far_message = f32(FIELDS * (own_cells + SUB), LANES)
    edge = pl.pallas_call(
        edge_kernel,
        out_shape=f32(levels, EXTRA, 2 * LANES),
        in_specs=[smem] + [pl.BlockSpec(memory_space=pltpu.HBM)] * 5,
        out_specs=vmem,
        scratch_shapes=[
            pltpu.VMEM((levels, FIELDS * own_cells, LANES), jnp.float32),
            pltpu.VMEM((parts, LANES), jnp.float32),
            pltpu.VMEM((parts, LANES), jnp.int32),
            pltpu.SemaphoreType.DMA((levels * FIELDS + 2,)),
        ],
        compiler_params=pltpu.CompilerParams(vmem_limit_bytes=EDGE_LIMIT),
        name="edges",
    )(place, density, momentum, magnetic, spins, turns)
    side = send_side(edge)
    packed = pl.pallas_call(
        lambda *refs: pack_kernel(spare, levels, *refs),
        out_shape=[near_message] * levels + [far_message] * levels,
        in_specs=[vmem] * 4,
        out_specs=[vmem] * (2 * levels),
        compiler_params=params,
        cost_estimate=cost,
        name="pack",
    )(density, momentum, magnetic, side)
    owns, fars = packed[:levels], packed[levels:]
    wide = (n + 1, radius, own_cells, total, spare, EXTRA)
    plain = (n, radius, own_cells, total, spare, 0)
    i32 = jax.ShapeDtypeStruct((TALL * SUB, LANES), jnp.int32)
    frames = jax.ShapeDtypeStruct((2, SUB, LANES), jnp.int32)
    tables = pl.pallas_call(
        lambda *refs: table_kernel((wide, plain), *refs),
        out_shape=[f32(TALL * SUB, LANES), i32, frames] * 2,
        in_specs=[smem] + [vmem] * 3,
        out_specs=[vmem] * 6,
        scratch_shapes=[pltpu.VMEM((2, tall_of(n + 1), LANES), jnp.float32)],
        compiler_params=params,
        name="tables",
    )(place, side, spins, turns)
    moved = [(send_near(own), send_far(far)) for own, far in zip(owns, fars)]
    states = []
    for level in range(levels):
        near, far = moved[level]
        states.append(first_step(wide, (place, owns[level], near, far, *tables[:3])))
    moved = [(send_near(own), send_far(far)) for own, far in states]
    done = ()
    for level in range(levels):
        near, far = moved[level]
        operands = (place, states[level][0], near, far, *tables[3:])
        result = last_step(plain, level, operands, done if level == levels - 1 else (), levels)
        done += (result,)
    return tuple(result)


def solution(mesh):
    placed = (
        P(None, "phi", "row"),
        P(None, None, "phi", "row"),
        P(None, None, "phi", "row"),
        P("row"),
        P("row"),
    )
    return jax.shard_map(
        body,
        mesh=mesh,
        in_specs=placed,
        out_specs=(P(None, "phi", "row"), P(None, None, "phi", "row"), P(None, None, "phi", "row")),
        check_vma=False,
    )
```

```python
import jax
import jax.numpy as jnp
from jax import lax
from jax.experimental import pallas as pl
from jax.experimental.pallas import tpu as pltpu
from jax.sharding import PartitionSpec as P

STEPS = 2
SMIN = 8
SMAX = 56
STAGES = 3
REACH = 2 * STAGES
FIELDS = 5
LANES = 128
SUB = 8
HALF = LANES // 2
SLOTS = 2 * SUB
EXTRA = 2 * SUB
TALL = 32
ROWS = 4
PICKS = 4
VMEM_LIMIT = 32 * 1024 * 1024
EDGE_LIMIT = 60 * 1024 * 1024

time_step = 0.08


def shift_bound(first_row, rows):
    d = rows - 1 - first_row
    return min(SMIN + (SMAX - SMIN - 1) * d * d // ((rows - 1) * (rows - 1)) + 1, SMAX)


def minmod(lower, upper):
    return jnp.maximum(jnp.minimum(lower, 0.0), jnp.minimum(upper, jnp.maximum(lower, 0.0)))


def physical(state):
    rho, mn, mt, bn, bt = state
    inverse = pltpu.reciprocal(rho, approx=True)
    bn_sq = bn * bn
    bt_sq = bt * bt
    vn = mn * inverse
    vt = mt * inverse
    inside = (bn_sq + bt_sq) * inverse + 1.0
    root = lax.rsqrt(inside)
    ram = mn * vn + rho
    tension = bt_sq - bn_sq
    flux_t = mt * vn - bn * bt
    flux_b = bt * vn - bn * vt
    speed = jnp.abs(vn) + inside * root
    return ram, tension, flux_t, flux_b, speed


def face_twice(left, right, of_left, of_right):
    left_ram, left_tension, left_t, left_b, left_speed = of_left
    right_ram, right_tension, right_t, right_b, right_speed = of_right
    bound = jnp.maximum(left_speed, right_speed)
    jumps = [bound * (l - r) for l, r in zip(left, right)]
    return [
        (left[1] + right[1]) + jumps[0],
        ((left_ram + right_ram) + 0.5 * (left_tension + right_tension)) + jumps[1],
        (left_t + right_t) + jumps[2],
        jumps[3],
        (left_b + right_b) + jumps[4],
    ]


def swapped(five):
    return [five[0], five[2], five[1], five[4], five[3]]


def tile(i):
    return pl.ds(pl.multiple_of(i * SUB, SUB), SUB)


def run_stages(n, stages, spin, edges):
    half_dt = 0.5 * time_step
    low_mask, high_mask = edges
    first, last = REACH, REACH + n - 1

    right_of = lambda x: pltpu.roll(x, LANES - 1, 1)
    left_of = lambda x: pltpu.roll(x, 1, 1)

    def radial_states(halves, centres):
        jumps = [h[SUB:] - h[:-SUB] for h in halves]
        slopes = [minmod(d[:-SUB], d[SUB:]) for d in jumps]
        lower = [x - g for x, g in zip(centres, slopes)]
        upper = [x + g for x, g in zip(centres, slopes)]
        return swapped([x[:-SUB] for x in upper]), swapped([x[SUB:] for x in lower])

    def work(stage, i0, before):
        src, dst = stage, (stage & 1) + 1
        weight = jnp.where(stage == 0, 1.0, jnp.where(stage == 1, 0.25, 2.0 / 3.0))
        keep = jnp.where(stage == 0, 0.0, jnp.where(stage == 1, 0.75, 1.0 / 3.0))
        some = lambda first, count: pl.ds(pl.multiple_of((i0 + first) * SUB, SUB), count * SUB)
        here = some(0, ROWS)
        size = ROWS * SUB
        rows = [stages[src, f, some(-1, ROWS + 3), :] for f in range(FIELDS)]
        halves = [0.5 * x for x in rows]
        own = [x[SUB : SUB + size] for x in rows]
        half = [x[SUB : SUB + size] for x in halves]
        after = [right_of(x) for x in half]
        left, right = radial_states(halves, [x[SUB:-SUB] for x in rows])
        jump = [x - y for x, y in zip(after, half)]
        behind = [left_of(x) for x in jump]
        of_left = physical(left)
        of_right = physical(right)
        slopes = [minmod(x, y) for x, y in zip(behind, jump)]
        lower = [right_of(x - y) for x, y in zip(own, slopes)]
        upper = [x + y for x, y in zip(own, slopes)]
        of_upper = physical(upper)
        faces = swapped(face_twice(left, right, of_left, of_right))
        of_lower = physical(lower)
        azimuth = face_twice(upper, lower, of_upper, of_lower)
        shifted = [left_of(x) for x in azimuth]
        change = [x - jnp.concatenate([y, x[:-SUB]], axis=0) for x, y in zip(faces, before)]
        turn = spin[here, :]
        source = [None, (-0.5 * turn) * own[2], (2.0 * turn) * own[1], (-1.5 * turn) * own[4], None]
        partial = [x if y is None else x + y for x, y in zip(own, source)]
        starts = [keep * stages[0, f, here, :] for f in range(FIELDS)]
        for f in range(FIELDS):
            new = partial[f] - half_dt * ((azimuth[f] - shifted[f]) + change[f])
            stages[dst, f, here, :] = weight * new + starts[f]
        return [x[-SUB:] for x in faces]

    def run(stage, _):
        for f in range(FIELDS):
            inner = stages[stage, f, tile(first), :]
            outer = stages[stage, f, tile(last), :]
            for k in (1, 2):
                stages[stage, f, tile(first - k), :] = jnp.where(low_mask, inner, stages[stage, f, tile(first - k), :])
                stages[stage, f, tile(last + k), :] = jnp.where(high_mask, outer, stages[stage, f, tile(last + k), :])
        count = n + 2 * REACH - 4 - 4 * stage
        if n % ROWS == 0:
            lo = 2 * stage + 2
            rows = [stages[stage, f, pl.ds(pl.multiple_of((lo - 2) * SUB, SUB), 4 * SUB), :] for f in range(FIELDS)]
            left, right = radial_states([0.5 * x for x in rows], [x[SUB:-SUB] for x in rows])
            before = tuple(swapped(face_twice(left, right, physical(left), physical(right))))
        else:
            lo = 2 * stage + 1
            count = count + 1
            before = (jnp.zeros((SUB, LANES), jnp.float32),) * FIELDS
        turns = lax.div(count + ROWS - 1, ROWS)
        lax.fori_loop(0, turns, lambda c, carried: tuple(work(stage, lo + c * ROWS, list(carried))), before)
        return 0

    lax.fori_loop(0, STAGES, run, 0)


def spread(block, first, width):
    block = pltpu.roll(block, (LANES - first) % LANES, 1)
    lane = lax.broadcasted_iota(jnp.int32, block.shape, 1)
    while width < LANES:
        block = jnp.where(lane < width, block, pltpu.roll(block, width, 1))
        width *= 2
    return block


def pack_far(far, near, own_cells, spare):
    sublane = lax.broadcasted_iota(jnp.int32, (SUB, LANES), 0)

    def one(f, _):
        start = pl.multiple_of(f * own_cells, SUB)
        base = pl.multiple_of(f * (own_cells + SUB), SUB)
        low = near[pl.ds(start, own_cells), 0:LANES]
        high = near[pl.ds(start + own_cells - 2 * SUB, 2 * SUB), LANES : 2 * LANES]
        moved = pltpu.roll(high[0:SUB], spare, 0)
        far[pl.ds(base, SUB), :] = jnp.where(sublane < spare, moved, low[0:SUB])
        far[pl.ds(base + SUB, own_cells - SUB), :] = low[SUB:]
        far[pl.ds(base + own_cells, SUB), :] = high[SUB:]
        return 0

    lax.fori_loop(0, FIELDS, one, 0)


def edge_kernel(place, density, momentum, magnetic, rotation, shifts, edge, ends, spin_in, shift_in, arrived):
    levels, own_cells, radius = density.shape
    on_low = place[0] == 0
    parts = radius // LANES
    split = 4 * own_cells
    columns = pl.ds(pl.multiple_of(jnp.where(on_low, radius - LANES, 0), LANES), LANES)
    copies = [
        pltpu.make_async_copy(rotation, spin_in, arrived.at[levels * FIELDS]),
        pltpu.make_async_copy(shifts, shift_in, arrived.at[levels * FIELDS + 1]),
    ]
    for level in range(levels):
        sources = [density.at[level, :, columns]] + [x.at[k, level, :, columns] for x in (momentum, magnetic) for k in range(2)]
        for f, x in enumerate(sources):
            at = ends.at[level, pl.ds(f * own_cells, own_cells), :]
            copies.append(pltpu.make_async_copy(x, at, arrived.at[level * FIELDS + f]))
    for copy in copies:
        copy.start()
    for copy in copies:
        copy.wait()
    wide = lambda ref: jnp.broadcast_to(
        jnp.where(on_low, ref[parts - 1 : parts, :], ref[0:1, :]).astype(jnp.float32), (own_cells, LANES)
    )
    turn = wide(spin_in) * time_step
    shift = wide(shift_in)
    zero = jnp.zeros((own_cells, LANES), jnp.float32)
    for level in range(levels):
        last = jnp.concatenate([ends[level, split:, :], turn, shift, zero], axis=0)
        for side, group in enumerate((ends[level, 0:split, :], last)):
            turned = group.T
            edge[level, :, side * LANES : (side + 1) * LANES] = jnp.where(on_low, turned[LANES - EXTRA :], turned[0:EXTRA])


def pack_kernel(spare, levels, density, momentum, magnetic, side, *outs):
    nears, fars = outs[:levels], outs[levels:]
    own_cells = density.shape[1]
    for level in range(levels):
        sources = [density.at[level]] + [x.at[k, level] for x in (momentum, magnetic) for k in range(2)]
        for f, x in enumerate(sources):
            nears[level][f * own_cells : (f + 1) * own_cells, :] = x[...]
        nears[level][FIELDS * own_cells :, :] = side[level]
        pack_far(fars[level], nears[level], own_cells, spare)


class Blocks:
    def __init__(self, row, n, radius, total, moved):
        self.on_low = row == 0
        self.n = n
        self.own_at = pl.multiple_of(jnp.where(self.on_low, EXTRA, EXTRA + moved), SUB)
        self.edge_at = pl.multiple_of(jnp.where(self.on_low, EXTRA + radius, moved), SUB)
        bounds = [[shift_bound(r * radius - (moved if r else 0) + n * k, total) for k in range(SLOTS)] for r in range(2)]
        self.bounds = [jnp.where(self.on_low, a, b) for a, b in zip(*bounds)]

    def rows_of(self, k):
        start = EXTRA - REACH + self.n * k
        return slice(start, start + TALL)


def table_kernel(plans, place, side, rotation, shifts, *rest):
    outs, held = rest[:-1], rest[-1]
    lane = lax.broadcasted_iota(jnp.int32, (SUB, LANES), 1)
    sublane = lax.broadcasted_iota(jnp.int32, (SUB, LANES), 0)
    front = lax.broadcasted_iota(jnp.int32, (TALL, LANES), 1) < HALF
    more = side[0, :, LANES : 2 * LANES]
    for which, (n, radius, own_cells, total, spare, moved) in enumerate(plans):
        spin, pick = outs[2 * which : 2 * which + 2]
        blocks = Blocks(place[0], n, radius, total, moved)
        for part in range(radius // LANES):
            rows = pl.ds(blocks.own_at + part * LANES, LANES)
            along = lambda ref: jnp.broadcast_to(ref[part : part + 1, :].astype(jnp.float32), (LANES, LANES)).T
            held[0, rows, :] = along(rotation) * time_step
            held[1, rows, :] = along(shifts)
        held[0, pl.ds(blocks.edge_at, EXTRA), :] = spread(more, own_cells, own_cells)
        held[1, pl.ds(blocks.edge_at, EXTRA), :] = spread(more, 2 * own_cells, own_cells)
        bound = jnp.zeros((SUB, LANES), jnp.int32)
        for j in range(SUB):
            low, high = blocks.rows_of(j), blocks.rows_of(SUB + j)
            spin[pl.ds(j, TALL, stride=SUB), :] = jnp.where(front, held[0, low, :], held[0, high, :])
            pick[pl.ds(j, TALL, stride=SUB), :] = jnp.where(front, held[1, low, :], held[1, high, :]).astype(jnp.int32)
            bound = jnp.where(sublane == j, jnp.where(lane < HALF, blocks.bounds[j], blocks.bounds[SUB + j]), bound)

        def one(i, _):
            pick[tile(i), :] = (lane + (REACH + bound)) - pick[tile(i), :]
            return 0

        lax.fori_loop(0, TALL, one, 0)


def step_kernel(plan, refs, write, scratch):
    n, radius, own_cells, total, spare, moved = plan
    place, own, near, far, spin, pick = refs
    tail = slice(FIELDS * own_cells, FIELDS * own_cells + EXTRA)
    cells, stages, packed = scratch
    row = place[0]
    lane = lax.broadcasted_iota(jnp.int32, (SUB, LANES), 1)
    sublane = lax.broadcasted_iota(jnp.int32, (SUB, LANES), 0)
    blocks = Blocks(row, n, radius, total, moved)

    edge_lane = lax.broadcasted_iota(jnp.int32, (EXTRA, LANES), 1)
    parts = radius // LANES

    def gather(f, _):
        rows = pl.ds(pl.multiple_of(f * own_cells, SUB), own_cells)
        start = pl.multiple_of(f * (own_cells + SUB), SUB)
        for part in range(parts):
            columns = slice(part * LANES, (part + 1) * LANES)
            if part == 0:
                top = far[pl.ds(start, own_cells), :]
            else:
                top = jnp.concatenate(
                    [
                        jnp.zeros((own_cells - 2 * SUB, LANES), jnp.float32),
                        pltpu.roll(far[pl.ds(start, SUB), :], SUB - spare, 0),
                        far[pl.ds(start + own_cells, SUB), :],
                    ],
                    axis=0,
                )
            fill = jnp.zeros((own_cells, LANES), jnp.float32)
            block = jnp.concatenate([top, near[rows, columns], own[rows, columns], fill], axis=0)
            cells[f, pl.ds(blocks.own_at + part * LANES, LANES), :] = block.T
        columns = pl.ds(pl.multiple_of(lax.div(f, 4) * LANES, LANES), LANES)
        lanes_at = lax.rem(f, 4) * own_cells
        cells[f, pl.ds(blocks.edge_at, EXTRA), :] = jnp.where(
            edge_lane < 2 * own_cells,
            pltpu.roll(near[tail, columns], lax.rem(LANES + own_cells - lanes_at, LANES), 1),
            pltpu.roll(own[tail, columns], lax.rem(LANES + 2 * own_cells - lanes_at, LANES), 1),
        )
        return 0

    lax.fori_loop(0, FIELDS, gather, 0)

    front = lax.broadcasted_iota(jnp.int32, (TALL, LANES), 1) < HALF

    def deal(f, _):
        for j in range(SUB):
            low, high = j, SUB + j
            turn_low = (LANES - (2 * own_cells - REACH)) + blocks.bounds[low]
            turn_high = (HALF - (2 * own_cells - REACH)) + blocks.bounds[high]
            stages[0, f, pl.ds(j, TALL, stride=SUB), :] = jnp.where(
                front,
                pltpu.roll(cells[f, blocks.rows_of(low), :], turn_low, 1),
                pltpu.roll(cells[f, blocks.rows_of(high), :], turn_high, 1),
            )
        return 0

    lax.fori_loop(0, FIELDS, deal, 0)

    edges = (
        (sublane == 0) & (lane < HALF) & (row == 0),
        (sublane == SUB - 1) & (lane >= HALF) & (row == total // radius - 1),
    )
    run_stages(n, stages, spin, edges)

    even = (lane & own_cells) == 0

    def shift(turn, _):
        for k in range(PICKS):
            i = turn * PICKS + k
            rows = tile(REACH + i)
            source = pick[rows, :]
            picks = [source & (LANES - 1), (source - own_cells) & (LANES - 1)]
            turned = [
                jnp.take_along_axis(stages[1, f, rows, :], picks[f % 2], axis=1, mode="promise_in_bounds")
                for f in range(FIELDS)
            ]
            stages[2, 0, tile(i), :] = jnp.where(even, turned[0], turned[1])
            stages[2, 1, tile(i), :] = jnp.where(even, turned[2], turned[3])
            stages[2, 2, tile(i), :] = turned[4]
        return 0

    lax.fori_loop(0, (n + PICKS - 1) // PICKS, shift, 0)
    narrow = lax.broadcasted_iota(jnp.int32, (n, LANES), 1) < HALF
    for j in range(SUB):
        one, two, three = [stages[2, g, pl.ds(j, n, stride=SUB), :] for g in range(3)]
        low = slice(EXTRA + n * j, EXTRA + n * (j + 1))
        high = slice(EXTRA + n * (SUB + j), EXTRA + n * (SUB + j + 1))
        packed[0, low, :] = jnp.where(narrow, one, pltpu.roll(two, HALF, 1))
        packed[0, high, :] = jnp.where(narrow, pltpu.roll(one, HALF, 1), two)
        packed[1, low, :] = three
        packed[1, high, :] = pltpu.roll(three, HALF, 1)
    for part in range(parts):
        rows = pl.ds(blocks.own_at + part * LANES, LANES)
        write.fields(slice(part * LANES, (part + 1) * LANES), packed[0, rows, :].T, packed[1, rows, :].T)
    write.edge(packed[0, pl.ds(blocks.edge_at, EXTRA), :], packed[1, pl.ds(blocks.edge_at, EXTRA), :])
    write.end()


class ToMessage:
    def __init__(self, near, far, own_cells, spare):
        self.near, self.far, self.own_cells, self.spare = near, far, own_cells, spare

    def fields(self, columns, four, fifth):
        split = 4 * self.own_cells
        self.near[0:split, columns] = four
        self.near[split : split + self.own_cells, columns] = fifth[0 : self.own_cells]

    def edge(self, first, second):
        tail = FIELDS * self.own_cells
        self.near[tail : tail + EXTRA, 0:LANES] = first
        self.near[tail : tail + EXTRA, LANES : 2 * LANES] = second

    def end(self):
        pack_far(self.far, self.near, self.own_cells, self.spare)


class ToBuffer:
    def __init__(self, buffer):
        self.buffer = buffer

    def fields(self, columns, four, fifth):
        split = four.shape[0]
        self.buffer[0:split, columns] = four
        self.buffer[split:, columns] = fifth[0 : self.buffer.shape[0] - split]

    def edge(self, first, second):
        pass

    def end(self):
        pass


def copies_out(level, buffer, outs, sent):
    density, momentum, magnetic = outs
    cells = density.shape[1]
    targets = [density.at[level]] + [x.at[k, level] for x in (momentum, magnetic) for k in range(2)]
    return [
        pltpu.make_async_copy(buffer.at[pl.ds(f * cells, cells), :], x, sent.at[level * FIELDS + f])
        for f, x in enumerate(targets)
    ]


def tall_of(n):
    return EXTRA + SLOTS * n + 2 * SUB


def step_scratch(n):
    return [
        pltpu.VMEM((FIELDS, tall_of(n), LANES), jnp.float32),
        pltpu.VMEM((STAGES, FIELDS, TALL * SUB, LANES), jnp.float32),
        pltpu.VMEM((2, tall_of(n), LANES), jnp.float32),
    ]


vmem = pl.BlockSpec(memory_space=pltpu.VMEM)
smem = pl.BlockSpec(memory_space=pltpu.SMEM)
f32 = lambda *s: jax.ShapeDtypeStruct(s, jnp.float32)
params = pltpu.CompilerParams(vmem_limit_bytes=VMEM_LIMIT)
cost = pl.CostEstimate(flops=9_000_000_000, bytes_accessed=29_000_000, transcendentals=0)


def first_step(plan, operands):
    n, radius, own_cells, total, spare, moved = plan

    def kernel(place, own, near, far, spin, pick, near_out, far_out, *scratch):
        refs = (place, own, near, far, spin, pick)
        step_kernel(plan, refs, ToMessage(near_out, far_out, own_cells, spare), scratch)

    return pl.pallas_call(
        kernel,
        out_shape=[f32(FIELDS * own_cells + EXTRA, radius), f32(FIELDS * (own_cells + SUB), LANES)],
        in_specs=[smem] + [vmem] * 5,
        out_specs=[vmem] * 2,
        scratch_shapes=step_scratch(n),
        compiler_params=params,
        cost_estimate=cost,
        name="first_step",
    )(*operands)


def last_step(plan, level, operands, done, levels):
    n, radius, own_cells, total, spare, moved = plan
    final = level == levels - 1
    buffer = f32(FIELDS * own_cells, radius)

    def kernel(place, own, near, far, spin, pick, *rest):
        refs = (place, own, near, far, spin, pick)
        if not final:
            step_kernel(plan, refs, ToBuffer(rest[0]), rest[1:])
            return
        ready, outs, scratch = rest[: levels - 1], rest[levels - 1 : levels + 2], rest[levels + 2 :]
        last, sent = scratch[-2:]
        copies = []
        for k, x in enumerate(ready):
            copies += copies_out(k, x, outs, sent)
        for copy in copies:
            copy.start()
        step_kernel(plan, refs, ToBuffer(last), scratch[:-2])
        rest_of = copies_out(level, last, outs, sent)
        for copy in rest_of:
            copy.start()
        for copy in copies + rest_of:
            copy.wait()

    if final:
        out_shape = [f32(levels, own_cells, radius), f32(2, levels, own_cells, radius), f32(2, levels, own_cells, radius)]
        more = [pltpu.VMEM((FIELDS * own_cells, radius), jnp.float32), pltpu.SemaphoreType.DMA((levels * FIELDS,))]
    else:
        out_shape = buffer
        more = []
    return pl.pallas_call(
        kernel,
        out_shape=out_shape,
        in_specs=[smem] + [vmem] * (5 + len(done)),
        out_specs=[pl.BlockSpec(memory_space=pltpu.HBM)] * 3 if final else vmem,
        scratch_shapes=step_scratch(n) + more,
        compiler_params=params,
        cost_estimate=cost,
        name="last_step",
    )(*operands, *done)


def body(density, momentum, magnetic, rotation, shifts):
    phi_count = lax.axis_size("phi")
    row_count = lax.axis_size("row")
    levels, own_cells, radius = density.shape
    total = radius * row_count
    parts = radius // LANES
    n = radius // SLOTS
    need = [max(shift_bound(part * LANES, total) + REACH - own_cells, 0) for part in range(parts)]
    spare = own_cells - need[0]
    assert row_count == 2 and radius == 2 * LANES and own_cells == HALF // 2
    assert 0 < need[0] < own_cells and need[1] <= SUB + spare and spare <= SUB

    row = lax.axis_index("row")
    place = jnp.reshape(row, (1,)).astype(jnp.int32)
    send_near = lambda x: lax.ppermute(x, "phi", [(p, (p + 1) % phi_count) for p in range(phi_count)])
    send_far = lambda x: lax.ppermute(x, "phi", [(p, (p + 2) % phi_count) for p in range(phi_count)])
    send_side = lambda x: lax.ppermute(x, "row", [(0, 1), (1, 0)])

    spins, turns = rotation.reshape(parts, LANES), shifts.reshape(parts, LANES)
    near_message = f32(FIELDS * own_cells + EXTRA, radius)
    far_message = f32(FIELDS * (own_cells + SUB), LANES)
    edge = pl.pallas_call(
        edge_kernel,
        out_shape=f32(levels, EXTRA, 2 * LANES),
        in_specs=[smem] + [pl.BlockSpec(memory_space=pltpu.HBM)] * 5,
        out_specs=vmem,
        scratch_shapes=[
            pltpu.VMEM((levels, FIELDS * own_cells, LANES), jnp.float32),
            pltpu.VMEM((parts, LANES), jnp.float32),
            pltpu.VMEM((parts, LANES), jnp.int32),
            pltpu.SemaphoreType.DMA((levels * FIELDS + 2,)),
        ],
        compiler_params=pltpu.CompilerParams(vmem_limit_bytes=EDGE_LIMIT),
        name="edges",
    )(place, density, momentum, magnetic, spins, turns)
    side = send_side(edge)
    packed = pl.pallas_call(
        lambda *refs: pack_kernel(spare, levels, *refs),
        out_shape=[near_message] * levels + [far_message] * levels,
        in_specs=[vmem] * 4,
        out_specs=[vmem] * (2 * levels),
        compiler_params=params,
        cost_estimate=cost,
        name="pack",
    )(density, momentum, magnetic, side)
    owns, fars = packed[:levels], packed[levels:]
    wide = (n + 1, radius, own_cells, total, spare, EXTRA)
    plain = (n, radius, own_cells, total, spare, 0)
    i32 = jax.ShapeDtypeStruct((TALL * SUB, LANES), jnp.int32)
    tables = pl.pallas_call(
        lambda *refs: table_kernel((wide, plain), *refs),
        out_shape=[f32(TALL * SUB, LANES), i32] * 2,
        in_specs=[smem] + [vmem] * 3,
        out_specs=[vmem] * 4,
        scratch_shapes=[pltpu.VMEM((2, tall_of(n + 1), LANES), jnp.float32)],
        compiler_params=params,
        name="tables",
    )(place, side, spins, turns)
    moved = [(send_near(own), send_far(far)) for own, far in zip(owns, fars)]
    states = []
    for level in range(levels):
        near, far = moved[level]
        states.append(first_step(wide, (place, owns[level], near, far, *tables[:2])))
    moved = [(send_near(own), send_far(far)) for own, far in states]
    done = ()
    for level in range(levels):
        near, far = moved[level]
        operands = (place, states[level][0], near, far, *tables[2:])
        result = last_step(plain, level, operands, done if level == levels - 1 else (), levels)
        done += (result,)
    return tuple(result)


def solution(mesh):
    placed = (
        P(None, "phi", "row"),
        P(None, None, "phi", "row"),
        P(None, None, "phi", "row"),
        P("row"),
        P("row"),
    )
    return jax.shard_map(
        body,
        mesh=mesh,
        in_specs=placed,
        out_specs=(P(None, "phi", "row"), P(None, None, "phi", "row"), P(None, None, "phi", "row")),
        check_vma=False,
    )
```

```python
import jax
import jax.numpy as jnp
from jax import lax
from jax.experimental import pallas as pl
from jax.experimental.pallas import tpu as pltpu
from jax.sharding import PartitionSpec as P

STEPS = 2
SMIN = 8
SMAX = 56
STAGES = 3
REACH = 2 * STAGES
FIELDS = 5
LANES = 128
SUB = 8
HALF = LANES // 2
SLOTS = 2 * SUB
EXTRA = 2 * SUB
DEALT = 32
TALL = 40
ROWS = 8
PICKS = 4
VMEM_LIMIT = 32 * 1024 * 1024
EDGE_LIMIT = 60 * 1024 * 1024

time_step = 0.08


def shift_bound(first_row, rows):
    d = rows - 1 - first_row
    return min(SMIN + (SMAX - SMIN - 1) * d * d // ((rows - 1) * (rows - 1)) + 1, SMAX)


def minmod(lower, upper):
    return jnp.maximum(jnp.minimum(lower, 0.0), jnp.minimum(upper, jnp.maximum(lower, 0.0)))


def physical(state):
    rho, mn, mt, bn, bt = state
    inverse = pltpu.reciprocal(rho, approx=True)
    bn_sq = bn * bn
    bt_sq = bt * bt
    vn = mn * inverse
    vt = mt * inverse
    inside = (bn_sq + bt_sq) * inverse + 1.0
    root = lax.rsqrt(inside)
    ram = mn * vn + rho
    tension = bt_sq - bn_sq
    flux_t = mt * vn - bn * bt
    flux_b = bt * vn - bn * vt
    speed = jnp.abs(vn) + inside * root
    return ram, tension, flux_t, flux_b, speed


def face_twice(left, right, of_left, of_right):
    left_ram, left_tension, left_t, left_b, left_speed = of_left
    right_ram, right_tension, right_t, right_b, right_speed = of_right
    bound = jnp.maximum(left_speed, right_speed)
    jumps = [bound * (l - r) for l, r in zip(left, right)]
    return [
        (left[1] + right[1]) + jumps[0],
        ((left_ram + right_ram) + 0.5 * (left_tension + right_tension)) + jumps[1],
        (left_t + right_t) + jumps[2],
        jumps[3],
        (left_b + right_b) + jumps[4],
    ]


def swapped(five):
    return [five[0], five[2], five[1], five[4], five[3]]


def tile(i):
    return pl.ds(pl.multiple_of(i * SUB, SUB), SUB)


def run_stages(n, stages, spin, edges):
    half_dt = 0.5 * time_step
    low_mask, high_mask = edges
    first, last = REACH, REACH + n - 1

    right_of = lambda x: pltpu.roll(x, LANES - 1, 1)
    left_of = lambda x: pltpu.roll(x, 1, 1)

    def radial_states(halves, centres):
        jumps = [h[SUB:] - h[:-SUB] for h in halves]
        slopes = [minmod(d[:-SUB], d[SUB:]) for d in jumps]
        lower = [x - g for x, g in zip(centres, slopes)]
        upper = [x + g for x, g in zip(centres, slopes)]
        return swapped([x[:-SUB] for x in upper]), swapped([x[SUB:] for x in lower])

    def work(stage, i0, before):
        src, dst = stage, (stage & 1) + 1
        weight = jnp.where(stage == 0, 1.0, jnp.where(stage == 1, 0.25, 2.0 / 3.0))
        keep = jnp.where(stage == 0, 0.0, jnp.where(stage == 1, 0.75, 1.0 / 3.0))
        some = lambda first, count: pl.ds(pl.multiple_of((i0 + first) * SUB, SUB), count * SUB)
        here = some(0, ROWS)
        size = ROWS * SUB
        rows = [stages[src, f, some(-1, ROWS + 3), :] for f in range(FIELDS)]
        halves = [0.5 * x for x in rows]
        own = [x[SUB : SUB + size] for x in rows]
        half = [x[SUB : SUB + size] for x in halves]
        after = [right_of(x) for x in half]
        left, right = radial_states(halves, [x[SUB:-SUB] for x in rows])
        jump = [x - y for x, y in zip(after, half)]
        behind = [left_of(x) for x in jump]
        of_left = physical(left)
        of_right = physical(right)
        slopes = [minmod(x, y) for x, y in zip(behind, jump)]
        lower = [right_of(x - y) for x, y in zip(own, slopes)]
        upper = [x + y for x, y in zip(own, slopes)]
        of_upper = physical(upper)
        faces = swapped(face_twice(left, right, of_left, of_right))
        of_lower = physical(lower)
        azimuth = face_twice(upper, lower, of_upper, of_lower)
        shifted = [left_of(x) for x in azimuth]
        change = [x - jnp.concatenate([y, x[:-SUB]], axis=0) for x, y in zip(faces, before)]
        turn = spin[here, :]
        source = [None, (-0.5 * turn) * own[2], (2.0 * turn) * own[1], (-1.5 * turn) * own[4], None]
        partial = [x if y is None else x + y for x, y in zip(own, source)]
        starts = [keep * stages[0, f, here, :] for f in range(FIELDS)]
        for f in range(FIELDS):
            new = partial[f] - half_dt * ((azimuth[f] - shifted[f]) + change[f])
            stages[dst, f, here, :] = weight * new + starts[f]
        return [x[-SUB:] for x in faces]

    def run(stage, _):
        for f in range(FIELDS):
            inner = stages[stage, f, tile(first), :]
            outer = stages[stage, f, tile(last), :]
            for k in (1, 2):
                stages[stage, f, tile(first - k), :] = jnp.where(low_mask, inner, stages[stage, f, tile(first - k), :])
                stages[stage, f, tile(last + k), :] = jnp.where(high_mask, outer, stages[stage, f, tile(last + k), :])
        count = n + 2 * REACH - 4 - 4 * stage
        if n % ROWS == 0:
            lo = 2 * stage + 2
            rows = [stages[stage, f, pl.ds(pl.multiple_of((lo - 2) * SUB, SUB), 4 * SUB), :] for f in range(FIELDS)]
            left, right = radial_states([0.5 * x for x in rows], [x[SUB:-SUB] for x in rows])
            before = tuple(swapped(face_twice(left, right, physical(left), physical(right))))
        else:
            lo = 2 * stage + 1
            count = count + 1
            before = (jnp.zeros((SUB, LANES), jnp.float32),) * FIELDS
        turns = lax.div(count + ROWS - 1, ROWS)
        lax.fori_loop(0, turns, lambda c, carried: tuple(work(stage, lo + c * ROWS, list(carried))), before)
        return 0

    lax.fori_loop(0, STAGES, run, 0)


def spread(block, first, width):
    block = pltpu.roll(block, (LANES - first) % LANES, 1)
    lane = lax.broadcasted_iota(jnp.int32, block.shape, 1)
    while width < LANES:
        block = jnp.where(lane < width, block, pltpu.roll(block, width, 1))
        width *= 2
    return block


def pack_far(far, near, own_cells, spare):
    sublane = lax.broadcasted_iota(jnp.int32, (SUB, LANES), 0)

    def one(f, _):
        start = pl.multiple_of(f * own_cells, SUB)
        base = pl.multiple_of(f * (own_cells + SUB), SUB)
        low = near[pl.ds(start, own_cells), 0:LANES]
        high = near[pl.ds(start + own_cells - 2 * SUB, 2 * SUB), LANES : 2 * LANES]
        moved = pltpu.roll(high[0:SUB], spare, 0)
        far[pl.ds(base, SUB), :] = jnp.where(sublane < spare, moved, low[0:SUB])
        far[pl.ds(base + SUB, own_cells - SUB), :] = low[SUB:]
        far[pl.ds(base + own_cells, SUB), :] = high[SUB:]
        return 0

    lax.fori_loop(0, FIELDS, one, 0)


def edge_kernel(place, density, momentum, magnetic, rotation, shifts, edge, ends, spin_in, shift_in, arrived):
    levels, own_cells, radius = density.shape
    on_low = place[0] == 0
    parts = radius // LANES
    split = 4 * own_cells
    columns = pl.ds(pl.multiple_of(jnp.where(on_low, radius - LANES, 0), LANES), LANES)
    copies = [
        pltpu.make_async_copy(rotation, spin_in, arrived.at[levels * FIELDS]),
        pltpu.make_async_copy(shifts, shift_in, arrived.at[levels * FIELDS + 1]),
    ]
    for level in range(levels):
        sources = [density.at[level, :, columns]] + [x.at[k, level, :, columns] for x in (momentum, magnetic) for k in range(2)]
        for f, x in enumerate(sources):
            at = ends.at[level, pl.ds(f * own_cells, own_cells), :]
            copies.append(pltpu.make_async_copy(x, at, arrived.at[level * FIELDS + f]))
    for copy in copies:
        copy.start()
    for copy in copies:
        copy.wait()
    wide = lambda ref: jnp.broadcast_to(
        jnp.where(on_low, ref[parts - 1 : parts, :], ref[0:1, :]).astype(jnp.float32), (own_cells, LANES)
    )
    turn = wide(spin_in) * time_step
    shift = wide(shift_in)
    zero = jnp.zeros((own_cells, LANES), jnp.float32)
    for level in range(levels):
        last = jnp.concatenate([ends[level, split:, :], turn, shift, zero], axis=0)
        for side, group in enumerate((ends[level, 0:split, :], last)):
            turned = group.T
            edge[level, :, side * LANES : (side + 1) * LANES] = jnp.where(on_low, turned[LANES - EXTRA :], turned[0:EXTRA])


def pack_kernel(spare, levels, density, momentum, magnetic, side, *outs):
    nears, fars = outs[:levels], outs[levels:]
    own_cells = density.shape[1]
    for level in range(levels):
        sources = [density.at[level]] + [x.at[k, level] for x in (momentum, magnetic) for k in range(2)]
        for f, x in enumerate(sources):
            nears[level][f * own_cells : (f + 1) * own_cells, :] = x[...]
        nears[level][FIELDS * own_cells :, :] = side[level]
        pack_far(fars[level], nears[level], own_cells, spare)


class Blocks:
    def __init__(self, row, n, radius, total, moved):
        self.on_low = row == 0
        self.n = n
        self.own_at = pl.multiple_of(jnp.where(self.on_low, EXTRA, EXTRA + moved), SUB)
        self.edge_at = pl.multiple_of(jnp.where(self.on_low, EXTRA + radius, moved), SUB)
        bounds = [[shift_bound(r * radius - (moved if r else 0) + n * k, total) for k in range(SLOTS)] for r in range(2)]
        self.bounds = [jnp.where(self.on_low, a, b) for a, b in zip(*bounds)]

    def rows_of(self, k):
        start = EXTRA - REACH + self.n * k
        return slice(start, start + DEALT)


def table_kernel(plans, place, side, rotation, shifts, *rest):
    outs, held = rest[:-1], rest[-1]
    lane = lax.broadcasted_iota(jnp.int32, (SUB, LANES), 1)
    sublane = lax.broadcasted_iota(jnp.int32, (SUB, LANES), 0)
    front = lax.broadcasted_iota(jnp.int32, (DEALT, LANES), 1) < HALF
    more = side[0, :, LANES : 2 * LANES]
    for which, (n, radius, own_cells, total, spare, moved) in enumerate(plans):
        spin, pick = outs[2 * which : 2 * which + 2]
        blocks = Blocks(place[0], n, radius, total, moved)
        for part in range(radius // LANES):
            rows = pl.ds(blocks.own_at + part * LANES, LANES)
            along = lambda ref: jnp.broadcast_to(ref[part : part + 1, :].astype(jnp.float32), (LANES, LANES)).T
            held[0, rows, :] = along(rotation) * time_step
            held[1, rows, :] = along(shifts)
        held[0, pl.ds(blocks.edge_at, EXTRA), :] = spread(more, own_cells, own_cells)
        held[1, pl.ds(blocks.edge_at, EXTRA), :] = spread(more, 2 * own_cells, own_cells)
        bound = jnp.zeros((SUB, LANES), jnp.int32)
        for j in range(SUB):
            low, high = blocks.rows_of(j), blocks.rows_of(SUB + j)
            spin[pl.ds(j, DEALT, stride=SUB), :] = jnp.where(front, held[0, low, :], held[0, high, :])
            pick[pl.ds(j, DEALT, stride=SUB), :] = jnp.where(front, held[1, low, :], held[1, high, :]).astype(jnp.int32)
            bound = jnp.where(sublane == j, jnp.where(lane < HALF, blocks.bounds[j], blocks.bounds[SUB + j]), bound)

        def one(i, _):
            pick[tile(i), :] = (lane + (REACH + bound)) - pick[tile(i), :]
            return 0

        lax.fori_loop(0, TALL, one, 0)


def step_kernel(plan, refs, write, scratch):
    n, radius, own_cells, total, spare, moved = plan
    place, own, near, far, spin, pick = refs
    tail = slice(FIELDS * own_cells, FIELDS * own_cells + EXTRA)
    cells, stages, packed = scratch
    row = place[0]
    lane = lax.broadcasted_iota(jnp.int32, (SUB, LANES), 1)
    sublane = lax.broadcasted_iota(jnp.int32, (SUB, LANES), 0)
    blocks = Blocks(row, n, radius, total, moved)

    edge_lane = lax.broadcasted_iota(jnp.int32, (EXTRA, LANES), 1)
    parts = radius // LANES

    def gather(f, _):
        rows = pl.ds(pl.multiple_of(f * own_cells, SUB), own_cells)
        start = pl.multiple_of(f * (own_cells + SUB), SUB)
        for part in range(parts):
            columns = slice(part * LANES, (part + 1) * LANES)
            if part == 0:
                top = far[pl.ds(start, own_cells), :]
            else:
                top = jnp.concatenate(
                    [
                        jnp.zeros((own_cells - 2 * SUB, LANES), jnp.float32),
                        pltpu.roll(far[pl.ds(start, SUB), :], SUB - spare, 0),
                        far[pl.ds(start + own_cells, SUB), :],
                    ],
                    axis=0,
                )
            fill = jnp.zeros((own_cells, LANES), jnp.float32)
            block = jnp.concatenate([top, near[rows, columns], own[rows, columns], fill], axis=0)
            cells[f, pl.ds(blocks.own_at + part * LANES, LANES), :] = block.T
        columns = pl.ds(pl.multiple_of(lax.div(f, 4) * LANES, LANES), LANES)
        lanes_at = lax.rem(f, 4) * own_cells
        cells[f, pl.ds(blocks.edge_at, EXTRA), :] = jnp.where(
            edge_lane < 2 * own_cells,
            pltpu.roll(near[tail, columns], lax.rem(LANES + own_cells - lanes_at, LANES), 1),
            pltpu.roll(own[tail, columns], lax.rem(LANES + 2 * own_cells - lanes_at, LANES), 1),
        )
        return 0

    lax.fori_loop(0, FIELDS, gather, 0)

    front = lax.broadcasted_iota(jnp.int32, (DEALT, LANES), 1) < HALF

    def deal(f, _):
        for j in range(SUB):
            low, high = j, SUB + j
            turn_low = (LANES - (2 * own_cells - REACH)) + blocks.bounds[low]
            turn_high = (HALF - (2 * own_cells - REACH)) + blocks.bounds[high]
            stages[0, f, pl.ds(j, DEALT, stride=SUB), :] = jnp.where(
                front,
                pltpu.roll(cells[f, blocks.rows_of(low), :], turn_low, 1),
                pltpu.roll(cells[f, blocks.rows_of(high), :], turn_high, 1),
            )
        return 0

    lax.fori_loop(0, FIELDS, deal, 0)

    edges = (
        (sublane == 0) & (lane < HALF) & (row == 0),
        (sublane == SUB - 1) & (lane >= HALF) & (row == total // radius - 1),
    )
    run_stages(n, stages, spin, edges)

    even = (lane & own_cells) == 0

    def shift(turn, _):
        for k in range(PICKS):
            i = turn * PICKS + k
            rows = tile(REACH + i)
            source = pick[rows, :]
            picks = [source & (LANES - 1), (source - own_cells) & (LANES - 1)]
            turned = [
                jnp.take_along_axis(stages[1, f, rows, :], picks[f % 2], axis=1, mode="promise_in_bounds")
                for f in range(FIELDS)
            ]
            stages[2, 0, tile(i), :] = jnp.where(even, turned[0], turned[1])
            stages[2, 1, tile(i), :] = jnp.where(even, turned[2], turned[3])
            stages[2, 2, tile(i), :] = turned[4]
        return 0

    lax.fori_loop(0, (n + PICKS - 1) // PICKS, shift, 0)
    narrow = lax.broadcasted_iota(jnp.int32, (n, LANES), 1) < HALF
    for j in range(SUB):
        one, two, three = [stages[2, g, pl.ds(j, n, stride=SUB), :] for g in range(3)]
        low = slice(EXTRA + n * j, EXTRA + n * (j + 1))
        high = slice(EXTRA + n * (SUB + j), EXTRA + n * (SUB + j + 1))
        packed[0, low, :] = jnp.where(narrow, one, pltpu.roll(two, HALF, 1))
        packed[0, high, :] = jnp.where(narrow, pltpu.roll(one, HALF, 1), two)
        packed[1, low, :] = three
        packed[1, high, :] = pltpu.roll(three, HALF, 1)
    for part in range(parts):
        rows = pl.ds(blocks.own_at + part * LANES, LANES)
        write.fields(slice(part * LANES, (part + 1) * LANES), packed[0, rows, :].T, packed[1, rows, :].T)
    write.edge(packed[0, pl.ds(blocks.edge_at, EXTRA), :], packed[1, pl.ds(blocks.edge_at, EXTRA), :])
    write.end()


class ToMessage:
    def __init__(self, near, far, own_cells, spare):
        self.near, self.far, self.own_cells, self.spare = near, far, own_cells, spare

    def fields(self, columns, four, fifth):
        split = 4 * self.own_cells
        self.near[0:split, columns] = four
        self.near[split : split + self.own_cells, columns] = fifth[0 : self.own_cells]

    def edge(self, first, second):
        tail = FIELDS * self.own_cells
        self.near[tail : tail + EXTRA, 0:LANES] = first
        self.near[tail : tail + EXTRA, LANES : 2 * LANES] = second

    def end(self):
        pack_far(self.far, self.near, self.own_cells, self.spare)


class ToBuffer:
    def __init__(self, buffer):
        self.buffer = buffer

    def fields(self, columns, four, fifth):
        split = four.shape[0]
        self.buffer[0:split, columns] = four
        self.buffer[split:, columns] = fifth[0 : self.buffer.shape[0] - split]

    def edge(self, first, second):
        pass

    def end(self):
        pass


def copies_out(level, buffer, outs, sent):
    density, momentum, magnetic = outs
    cells = density.shape[1]
    targets = [density.at[level]] + [x.at[k, level] for x in (momentum, magnetic) for k in range(2)]
    return [
        pltpu.make_async_copy(buffer.at[pl.ds(f * cells, cells), :], x, sent.at[level * FIELDS + f])
        for f, x in enumerate(targets)
    ]


def tall_of(n):
    return EXTRA + SLOTS * n + 2 * SUB


def step_scratch(n):
    return [
        pltpu.VMEM((FIELDS, tall_of(n), LANES), jnp.float32),
        pltpu.VMEM((STAGES, FIELDS, TALL * SUB, LANES), jnp.float32),
        pltpu.VMEM((2, tall_of(n), LANES), jnp.float32),
    ]


vmem = pl.BlockSpec(memory_space=pltpu.VMEM)
smem = pl.BlockSpec(memory_space=pltpu.SMEM)
f32 = lambda *s: jax.ShapeDtypeStruct(s, jnp.float32)
params = pltpu.CompilerParams(vmem_limit_bytes=VMEM_LIMIT)
cost = pl.CostEstimate(flops=9_000_000_000, bytes_accessed=29_000_000, transcendentals=0)


def first_step(plan, operands):
    n, radius, own_cells, total, spare, moved = plan

    def kernel(place, own, near, far, spin, pick, near_out, far_out, *scratch):
        refs = (place, own, near, far, spin, pick)
        step_kernel(plan, refs, ToMessage(near_out, far_out, own_cells, spare), scratch)

    return pl.pallas_call(
        kernel,
        out_shape=[f32(FIELDS * own_cells + EXTRA, radius), f32(FIELDS * (own_cells + SUB), LANES)],
        in_specs=[smem] + [vmem] * 5,
        out_specs=[vmem] * 2,
        scratch_shapes=step_scratch(n),
        compiler_params=params,
        cost_estimate=cost,
        name="first_step",
    )(*operands)


def last_step(plan, level, operands, done, levels):
    n, radius, own_cells, total, spare, moved = plan
    final = level == levels - 1
    buffer = f32(FIELDS * own_cells, radius)

    def kernel(place, own, near, far, spin, pick, *rest):
        refs = (place, own, near, far, spin, pick)
        if not final:
            step_kernel(plan, refs, ToBuffer(rest[0]), rest[1:])
            return
        ready, outs, scratch = rest[: levels - 1], rest[levels - 1 : levels + 2], rest[levels + 2 :]
        last, sent = scratch[-2:]
        copies = []
        for k, x in enumerate(ready):
            copies += copies_out(k, x, outs, sent)
        for copy in copies:
            copy.start()
        step_kernel(plan, refs, ToBuffer(last), scratch[:-2])
        rest_of = copies_out(level, last, outs, sent)
        for copy in rest_of:
            copy.start()
        for copy in copies + rest_of:
            copy.wait()

    if final:
        out_shape = [f32(levels, own_cells, radius), f32(2, levels, own_cells, radius), f32(2, levels, own_cells, radius)]
        more = [pltpu.VMEM((FIELDS * own_cells, radius), jnp.float32), pltpu.SemaphoreType.DMA((levels * FIELDS,))]
    else:
        out_shape = buffer
        more = []
    return pl.pallas_call(
        kernel,
        out_shape=out_shape,
        in_specs=[smem] + [vmem] * (5 + len(done)),
        out_specs=[pl.BlockSpec(memory_space=pltpu.HBM)] * 3 if final else vmem,
        scratch_shapes=step_scratch(n) + more,
        compiler_params=params,
        cost_estimate=cost,
        name="last_step",
    )(*operands, *done)


def body(density, momentum, magnetic, rotation, shifts):
    phi_count = lax.axis_size("phi")
    row_count = lax.axis_size("row")
    levels, own_cells, radius = density.shape
    total = radius * row_count
    parts = radius // LANES
    n = radius // SLOTS
    need = [max(shift_bound(part * LANES, total) + REACH - own_cells, 0) for part in range(parts)]
    spare = own_cells - need[0]
    assert row_count == 2 and radius == 2 * LANES and own_cells == HALF // 2
    assert 0 < need[0] < own_cells and need[1] <= SUB + spare and spare <= SUB

    row = lax.axis_index("row")
    place = jnp.reshape(row, (1,)).astype(jnp.int32)
    send_near = lambda x: lax.ppermute(x, "phi", [(p, (p + 1) % phi_count) for p in range(phi_count)])
    send_far = lambda x: lax.ppermute(x, "phi", [(p, (p + 2) % phi_count) for p in range(phi_count)])
    send_side = lambda x: lax.ppermute(x, "row", [(0, 1), (1, 0)])

    spins, turns = rotation.reshape(parts, LANES), shifts.reshape(parts, LANES)
    near_message = f32(FIELDS * own_cells + EXTRA, radius)
    far_message = f32(FIELDS * (own_cells + SUB), LANES)
    edge = pl.pallas_call(
        edge_kernel,
        out_shape=f32(levels, EXTRA, 2 * LANES),
        in_specs=[smem] + [pl.BlockSpec(memory_space=pltpu.HBM)] * 5,
        out_specs=vmem,
        scratch_shapes=[
            pltpu.VMEM((levels, FIELDS * own_cells, LANES), jnp.float32),
            pltpu.VMEM((parts, LANES), jnp.float32),
            pltpu.VMEM((parts, LANES), jnp.int32),
            pltpu.SemaphoreType.DMA((levels * FIELDS + 2,)),
        ],
        compiler_params=pltpu.CompilerParams(vmem_limit_bytes=EDGE_LIMIT),
        name="edges",
    )(place, density, momentum, magnetic, spins, turns)
    side = send_side(edge)
    packed = pl.pallas_call(
        lambda *refs: pack_kernel(spare, levels, *refs),
        out_shape=[near_message] * levels + [far_message] * levels,
        in_specs=[vmem] * 4,
        out_specs=[vmem] * (2 * levels),
        compiler_params=params,
        cost_estimate=cost,
        name="pack",
    )(density, momentum, magnetic, side)
    owns, fars = packed[:levels], packed[levels:]
    wide = (n + 1, radius, own_cells, total, spare, EXTRA)
    plain = (n, radius, own_cells, total, spare, 0)
    i32 = jax.ShapeDtypeStruct((TALL * SUB, LANES), jnp.int32)
    tables = pl.pallas_call(
        lambda *refs: table_kernel((wide, plain), *refs),
        out_shape=[f32(TALL * SUB, LANES), i32] * 2,
        in_specs=[smem] + [vmem] * 3,
        out_specs=[vmem] * 4,
        scratch_shapes=[pltpu.VMEM((2, tall_of(n + 1), LANES), jnp.float32)],
        compiler_params=params,
        name="tables",
    )(place, side, spins, turns)
    moved = [(send_near(own), send_far(far)) for own, far in zip(owns, fars)]
    states = []
    for level in range(levels):
        near, far = moved[level]
        states.append(first_step(wide, (place, owns[level], near, far, *tables[:2])))
    moved = [(send_near(own), send_far(far)) for own, far in states]
    done = ()
    for level in range(levels):
        near, far = moved[level]
        operands = (place, states[level][0], near, far, *tables[2:])
        result = last_step(plain, level, operands, done if level == levels - 1 else (), levels)
        done += (result,)
    return tuple(result)


def solution(mesh):
    placed = (
        P(None, "phi", "row"),
        P(None, None, "phi", "row"),
        P(None, None, "phi", "row"),
        P("row"),
        P("row"),
    )
    return jax.shard_map(
        body,
        mesh=mesh,
        in_specs=placed,
        out_specs=(P(None, "phi", "row"), P(None, None, "phi", "row"), P(None, None, "phi", "row")),
        check_vma=False,
    )
```

```python
import jax
import jax.numpy as jnp
from jax import lax
from jax.experimental import pallas as pl
from jax.experimental.pallas import tpu as pltpu
from jax.sharding import PartitionSpec as P

STEPS = 2
SMIN = 8
SMAX = 56
STAGES = 3
REACH = 2 * STAGES
FIELDS = 5
LANES = 128
SUB = 8
HALF = LANES // 2
SLOTS = 2 * SUB
EXTRA = 2 * SUB
DEALT = 32
TALL = 40
ROWS = 8
PICKS = 4
VMEM_LIMIT = 32 * 1024 * 1024
EDGE_LIMIT = 60 * 1024 * 1024

time_step = 0.08


def shift_bound(first_row, rows):
    d = rows - 1 - first_row
    return min(SMIN + (SMAX - SMIN - 1) * d * d // ((rows - 1) * (rows - 1)) + 1, SMAX)


def minmod(lower, upper):
    return jnp.maximum(jnp.minimum(lower, 0.0), jnp.minimum(upper, jnp.maximum(lower, 0.0)))


def physical(state):
    rho, mn, mt, bn, bt = state
    inverse = pltpu.reciprocal(rho, approx=True)
    bn_sq = bn * bn
    bt_sq = bt * bt
    vn = mn * inverse
    vt = mt * inverse
    inside = (bn_sq + bt_sq) * inverse + 1.0
    root = lax.rsqrt(inside)
    ram = mn * vn + rho
    tension = bt_sq - bn_sq
    flux_t = mt * vn - bn * bt
    flux_b = bt * vn - bn * vt
    speed = jnp.abs(vn) + inside * root
    return ram, tension, flux_t, flux_b, speed


def face_twice(left, right, of_left, of_right):
    left_ram, left_tension, left_t, left_b, left_speed = of_left
    right_ram, right_tension, right_t, right_b, right_speed = of_right
    bound = jnp.maximum(left_speed, right_speed)
    jumps = [bound * (l - r) for l, r in zip(left, right)]
    return [
        (left[1] + right[1]) + jumps[0],
        ((left_ram + right_ram) + 0.5 * (left_tension + right_tension)) + jumps[1],
        (left_t + right_t) + jumps[2],
        jumps[3],
        (left_b + right_b) + jumps[4],
    ]


def swapped(five):
    return [five[0], five[2], five[1], five[4], five[3]]


def tile(i):
    return pl.ds(pl.multiple_of(i * SUB, SUB), SUB)


def run_stages(n, stages, spin, edges):
    half_dt = 0.5 * time_step
    low_mask, high_mask = edges
    first, last = REACH, REACH + n - 1

    right_of = lambda x: pltpu.roll(x, LANES - 1, 1)
    left_of = lambda x: pltpu.roll(x, 1, 1)

    def radial_states(halves, centres):
        jumps = [h[SUB:] - h[:-SUB] for h in halves]
        slopes = [minmod(d[:-SUB], d[SUB:]) for d in jumps]
        lower = [x - g for x, g in zip(centres, slopes)]
        upper = [x + g for x, g in zip(centres, slopes)]
        return swapped([x[:-SUB] for x in upper]), swapped([x[SUB:] for x in lower])

    def work(stage, i0, before):
        src, dst = stage, (stage & 1) + 1
        weight = jnp.where(stage == 0, 1.0, jnp.where(stage == 1, 0.25, 2.0 / 3.0))
        keep = jnp.where(stage == 0, 0.0, jnp.where(stage == 1, 0.75, 1.0 / 3.0))
        some = lambda first, count: pl.ds(pl.multiple_of((i0 + first) * SUB, SUB), count * SUB)
        here = some(0, ROWS)
        size = ROWS * SUB
        rows = [stages[src, f, some(-1, ROWS + 3), :] for f in range(FIELDS)]
        halves = [0.5 * x for x in rows]
        own = [x[SUB : SUB + size] for x in rows]
        half = [x[SUB : SUB + size] for x in halves]
        before_half = [left_of(x) for x in half]
        after_half = [right_of(x) for x in half]
        second_half = [pltpu.roll(x, LANES - 2, 1) for x in half]
        left, right = radial_states(halves, [x[SUB:-SUB] for x in rows])
        of_left = physical(left)
        of_right = physical(right)
        behind = [x - y for x, y in zip(half, before_half)]
        jump = [x - y for x, y in zip(after_half, half)]
        ahead = [x - y for x, y in zip(second_half, after_half)]
        upper = [x + minmod(p, q) for x, p, q in zip(own, behind, jump)]
        lower = [(x + x) - minmod(p, q) for x, p, q in zip(after_half, jump, ahead)]
        of_upper = physical(upper)
        faces = swapped(face_twice(left, right, of_left, of_right))
        of_lower = physical(lower)
        azimuth = face_twice(upper, lower, of_upper, of_lower)
        shifted = [left_of(x) for x in azimuth]
        change = [x - jnp.concatenate([y, x[:-SUB]], axis=0) for x, y in zip(faces, before)]
        turn = spin[here, :]
        source = [None, (-0.5 * turn) * own[2], (2.0 * turn) * own[1], (-1.5 * turn) * own[4], None]
        partial = [x if y is None else x + y for x, y in zip(own, source)]
        starts = [keep * stages[0, f, here, :] for f in range(FIELDS)]
        for f in range(FIELDS):
            new = partial[f] - half_dt * ((azimuth[f] - shifted[f]) + change[f])
            stages[dst, f, here, :] = weight * new + starts[f]
        return [x[-SUB:] for x in faces]

    def run(stage, _):
        for f in range(FIELDS):
            inner = stages[stage, f, tile(first), :]
            outer = stages[stage, f, tile(last), :]
            for k in (1, 2):
                stages[stage, f, tile(first - k), :] = jnp.where(low_mask, inner, stages[stage, f, tile(first - k), :])
                stages[stage, f, tile(last + k), :] = jnp.where(high_mask, outer, stages[stage, f, tile(last + k), :])
        count = n + 2 * REACH - 4 - 4 * stage
        if n % ROWS == 0:
            lo = 2 * stage + 2
            rows = [stages[stage, f, pl.ds(pl.multiple_of((lo - 2) * SUB, SUB), 4 * SUB), :] for f in range(FIELDS)]
            left, right = radial_states([0.5 * x for x in rows], [x[SUB:-SUB] for x in rows])
            before = tuple(swapped(face_twice(left, right, physical(left), physical(right))))
        else:
            lo = 2 * stage + 1
            count = count + 1
            before = (jnp.zeros((SUB, LANES), jnp.float32),) * FIELDS
        turns = lax.div(count + ROWS - 1, ROWS)
        lax.fori_loop(0, turns, lambda c, carried: tuple(work(stage, lo + c * ROWS, list(carried))), before)
        return 0

    lax.fori_loop(0, STAGES, run, 0)


def spread(block, first, width):
    block = pltpu.roll(block, (LANES - first) % LANES, 1)
    lane = lax.broadcasted_iota(jnp.int32, block.shape, 1)
    while width < LANES:
        block = jnp.where(lane < width, block, pltpu.roll(block, width, 1))
        width *= 2
    return block


def pack_far(far, near, own_cells, spare):
    sublane = lax.broadcasted_iota(jnp.int32, (SUB, LANES), 0)

    def one(f, _):
        start = pl.multiple_of(f * own_cells, SUB)
        base = pl.multiple_of(f * (own_cells + SUB), SUB)
        low = near[pl.ds(start, own_cells), 0:LANES]
        high = near[pl.ds(start + own_cells - 2 * SUB, 2 * SUB), LANES : 2 * LANES]
        moved = pltpu.roll(high[0:SUB], spare, 0)
        far[pl.ds(base, SUB), :] = jnp.where(sublane < spare, moved, low[0:SUB])
        far[pl.ds(base + SUB, own_cells - SUB), :] = low[SUB:]
        far[pl.ds(base + own_cells, SUB), :] = high[SUB:]
        return 0

    lax.fori_loop(0, FIELDS, one, 0)


def edge_kernel(place, density, momentum, magnetic, rotation, shifts, edge, ends, spin_in, shift_in, arrived):
    levels, own_cells, radius = density.shape
    on_low = place[0] == 0
    parts = radius // LANES
    split = 4 * own_cells
    columns = pl.ds(pl.multiple_of(jnp.where(on_low, radius - LANES, 0), LANES), LANES)
    copies = [
        pltpu.make_async_copy(rotation, spin_in, arrived.at[levels * FIELDS]),
        pltpu.make_async_copy(shifts, shift_in, arrived.at[levels * FIELDS + 1]),
    ]
    for level in range(levels):
        sources = [density.at[level, :, columns]] + [x.at[k, level, :, columns] for x in (momentum, magnetic) for k in range(2)]
        for f, x in enumerate(sources):
            at = ends.at[level, pl.ds(f * own_cells, own_cells), :]
            copies.append(pltpu.make_async_copy(x, at, arrived.at[level * FIELDS + f]))
    for copy in copies:
        copy.start()
    for copy in copies:
        copy.wait()
    wide = lambda ref: jnp.broadcast_to(
        jnp.where(on_low, ref[parts - 1 : parts, :], ref[0:1, :]).astype(jnp.float32), (own_cells, LANES)
    )
    turn = wide(spin_in) * time_step
    shift = wide(shift_in)
    zero = jnp.zeros((own_cells, LANES), jnp.float32)
    for level in range(levels):
        last = jnp.concatenate([ends[level, split:, :], turn, shift, zero], axis=0)
        for side, group in enumerate((ends[level, 0:split, :], last)):
            turned = group.T
            edge[level, :, side * LANES : (side + 1) * LANES] = jnp.where(on_low, turned[LANES - EXTRA :], turned[0:EXTRA])


def pack_kernel(spare, levels, density, momentum, magnetic, side, *outs):
    nears, fars = outs[:levels], outs[levels:]
    own_cells = density.shape[1]
    for level in range(levels):
        sources = [density.at[level]] + [x.at[k, level] for x in (momentum, magnetic) for k in range(2)]
        for f, x in enumerate(sources):
            nears[level][f * own_cells : (f + 1) * own_cells, :] = x[...]
        nears[level][FIELDS * own_cells :, :] = side[level]
        pack_far(fars[level], nears[level], own_cells, spare)


class Blocks:
    def __init__(self, row, n, radius, total, moved):
        self.on_low = row == 0
        self.n = n
        self.own_at = pl.multiple_of(jnp.where(self.on_low, EXTRA, EXTRA + moved), SUB)
        self.edge_at = pl.multiple_of(jnp.where(self.on_low, EXTRA + radius, moved), SUB)
        bounds = [[shift_bound(r * radius - (moved if r else 0) + n * k, total) for k in range(SLOTS)] for r in range(2)]
        self.bounds = [jnp.where(self.on_low, a, b) for a, b in zip(*bounds)]

    def rows_of(self, k):
        start = EXTRA - REACH + self.n * k
        return slice(start, start + DEALT)


def table_kernel(plans, place, side, rotation, shifts, *rest):
    outs, held = rest[:-1], rest[-1]
    lane = lax.broadcasted_iota(jnp.int32, (SUB, LANES), 1)
    sublane = lax.broadcasted_iota(jnp.int32, (SUB, LANES), 0)
    front = lax.broadcasted_iota(jnp.int32, (DEALT, LANES), 1) < HALF
    more = side[0, :, LANES : 2 * LANES]
    for which, (n, radius, own_cells, total, spare, moved) in enumerate(plans):
        spin, pick = outs[2 * which : 2 * which + 2]
        blocks = Blocks(place[0], n, radius, total, moved)
        for part in range(radius // LANES):
            rows = pl.ds(blocks.own_at + part * LANES, LANES)
            along = lambda ref: jnp.broadcast_to(ref[part : part + 1, :].astype(jnp.float32), (LANES, LANES)).T
            held[0, rows, :] = along(rotation) * time_step
            held[1, rows, :] = along(shifts)
        held[0, pl.ds(blocks.edge_at, EXTRA), :] = spread(more, own_cells, own_cells)
        held[1, pl.ds(blocks.edge_at, EXTRA), :] = spread(more, 2 * own_cells, own_cells)
        bound = jnp.zeros((SUB, LANES), jnp.int32)
        for j in range(SUB):
            low, high = blocks.rows_of(j), blocks.rows_of(SUB + j)
            spin[pl.ds(j, DEALT, stride=SUB), :] = jnp.where(front, held[0, low, :], held[0, high, :])
            pick[pl.ds(j, DEALT, stride=SUB), :] = jnp.where(front, held[1, low, :], held[1, high, :]).astype(jnp.int32)
            bound = jnp.where(sublane == j, jnp.where(lane < HALF, blocks.bounds[j], blocks.bounds[SUB + j]), bound)

        def one(i, _):
            pick[tile(i), :] = (lane + (REACH + bound)) - pick[tile(i), :]
            return 0

        lax.fori_loop(0, TALL, one, 0)


def step_kernel(plan, refs, write, scratch):
    n, radius, own_cells, total, spare, moved = plan
    place, own, near, far, spin, pick = refs
    tail = slice(FIELDS * own_cells, FIELDS * own_cells + EXTRA)
    cells, stages, packed = scratch
    row = place[0]
    lane = lax.broadcasted_iota(jnp.int32, (SUB, LANES), 1)
    sublane = lax.broadcasted_iota(jnp.int32, (SUB, LANES), 0)
    blocks = Blocks(row, n, radius, total, moved)

    edge_lane = lax.broadcasted_iota(jnp.int32, (EXTRA, LANES), 1)
    parts = radius // LANES

    def gather(f, _):
        rows = pl.ds(pl.multiple_of(f * own_cells, SUB), own_cells)
        start = pl.multiple_of(f * (own_cells + SUB), SUB)
        for part in range(parts):
            columns = slice(part * LANES, (part + 1) * LANES)
            if part == 0:
                top = far[pl.ds(start, own_cells), :]
            else:
                top = jnp.concatenate(
                    [
                        jnp.zeros((own_cells - 2 * SUB, LANES), jnp.float32),
                        pltpu.roll(far[pl.ds(start, SUB), :], SUB - spare, 0),
                        far[pl.ds(start + own_cells, SUB), :],
                    ],
                    axis=0,
                )
            fill = jnp.zeros((own_cells, LANES), jnp.float32)
            block = jnp.concatenate([top, near[rows, columns], own[rows, columns], fill], axis=0)
            cells[f, pl.ds(blocks.own_at + part * LANES, LANES), :] = block.T
        columns = pl.ds(pl.multiple_of(lax.div(f, 4) * LANES, LANES), LANES)
        lanes_at = lax.rem(f, 4) * own_cells
        cells[f, pl.ds(blocks.edge_at, EXTRA), :] = jnp.where(
            edge_lane < 2 * own_cells,
            pltpu.roll(near[tail, columns], lax.rem(LANES + own_cells - lanes_at, LANES), 1),
            pltpu.roll(own[tail, columns], lax.rem(LANES + 2 * own_cells - lanes_at, LANES), 1),
        )
        return 0

    lax.fori_loop(0, FIELDS, gather, 0)

    front = lax.broadcasted_iota(jnp.int32, (DEALT, LANES), 1) < HALF

    def deal(f, _):
        for j in range(SUB):
            low, high = j, SUB + j
            turn_low = (LANES - (2 * own_cells - REACH)) + blocks.bounds[low]
            turn_high = (HALF - (2 * own_cells - REACH)) + blocks.bounds[high]
            stages[0, f, pl.ds(j, DEALT, stride=SUB), :] = jnp.where(
                front,
                pltpu.roll(cells[f, blocks.rows_of(low), :], turn_low, 1),
                pltpu.roll(cells[f, blocks.rows_of(high), :], turn_high, 1),
            )
        return 0

    lax.fori_loop(0, FIELDS, deal, 0)

    edges = (
        (sublane == 0) & (lane < HALF) & (row == 0),
        (sublane == SUB - 1) & (lane >= HALF) & (row == total // radius - 1),
    )
    run_stages(n, stages, spin, edges)

    even = (lane & own_cells) == 0

    def shift(turn, _):
        for k in range(PICKS):
            i = turn * PICKS + k
            rows = tile(REACH + i)
            source = pick[rows, :]
            picks = [source & (LANES - 1), (source - own_cells) & (LANES - 1)]
            turned = [
                jnp.take_along_axis(stages[1, f, rows, :], picks[f % 2], axis=1, mode="promise_in_bounds")
                for f in range(FIELDS)
            ]
            stages[2, 0, tile(i), :] = jnp.where(even, turned[0], turned[1])
            stages[2, 1, tile(i), :] = jnp.where(even, turned[2], turned[3])
            stages[2, 2, tile(i), :] = turned[4]
        return 0

    lax.fori_loop(0, (n + PICKS - 1) // PICKS, shift, 0)
    narrow = lax.broadcasted_iota(jnp.int32, (n, LANES), 1) < HALF
    for j in range(SUB):
        one, two, three = [stages[2, g, pl.ds(j, n, stride=SUB), :] for g in range(3)]
        low = slice(EXTRA + n * j, EXTRA + n * (j + 1))
        high = slice(EXTRA + n * (SUB + j), EXTRA + n * (SUB + j + 1))
        packed[0, low, :] = jnp.where(narrow, one, pltpu.roll(two, HALF, 1))
        packed[0, high, :] = jnp.where(narrow, pltpu.roll(one, HALF, 1), two)
        packed[1, low, :] = three
        packed[1, high, :] = pltpu.roll(three, HALF, 1)
    for part in range(parts):
        rows = pl.ds(blocks.own_at + part * LANES, LANES)
        write.fields(slice(part * LANES, (part + 1) * LANES), packed[0, rows, :].T, packed[1, rows, :].T)
    write.edge(packed[0, pl.ds(blocks.edge_at, EXTRA), :], packed[1, pl.ds(blocks.edge_at, EXTRA), :])
    write.end()


class ToMessage:
    def __init__(self, near, far, own_cells, spare):
        self.near, self.far, self.own_cells, self.spare = near, far, own_cells, spare

    def fields(self, columns, four, fifth):
        split = 4 * self.own_cells
        self.near[0:split, columns] = four
        self.near[split : split + self.own_cells, columns] = fifth[0 : self.own_cells]

    def edge(self, first, second):
        tail = FIELDS * self.own_cells
        self.near[tail : tail + EXTRA, 0:LANES] = first
        self.near[tail : tail + EXTRA, LANES : 2 * LANES] = second

    def end(self):
        pack_far(self.far, self.near, self.own_cells, self.spare)


class ToBuffer:
    def __init__(self, buffer):
        self.buffer = buffer

    def fields(self, columns, four, fifth):
        split = four.shape[0]
        self.buffer[0:split, columns] = four
        self.buffer[split:, columns] = fifth[0 : self.buffer.shape[0] - split]

    def edge(self, first, second):
        pass

    def end(self):
        pass


def copies_out(level, buffer, outs, sent):
    density, momentum, magnetic = outs
    cells = density.shape[1]
    targets = [density.at[level]] + [x.at[k, level] for x in (momentum, magnetic) for k in range(2)]
    return [
        pltpu.make_async_copy(buffer.at[pl.ds(f * cells, cells), :], x, sent.at[level * FIELDS + f])
        for f, x in enumerate(targets)
    ]


def tall_of(n):
    return EXTRA + SLOTS * n + 2 * SUB


def step_scratch(n):
    return [
        pltpu.VMEM((FIELDS, tall_of(n), LANES), jnp.float32),
        pltpu.VMEM((STAGES, FIELDS, TALL * SUB, LANES), jnp.float32),
        pltpu.VMEM((2, tall_of(n), LANES), jnp.float32),
    ]


vmem = pl.BlockSpec(memory_space=pltpu.VMEM)
smem = pl.BlockSpec(memory_space=pltpu.SMEM)
f32 = lambda *s: jax.ShapeDtypeStruct(s, jnp.float32)
params = pltpu.CompilerParams(vmem_limit_bytes=VMEM_LIMIT)
cost = pl.CostEstimate(flops=9_000_000_000, bytes_accessed=29_000_000, transcendentals=0)


def first_step(plan, operands):
    n, radius, own_cells, total, spare, moved = plan

    def kernel(place, own, near, far, spin, pick, near_out, far_out, *scratch):
        refs = (place, own, near, far, spin, pick)
        step_kernel(plan, refs, ToMessage(near_out, far_out, own_cells, spare), scratch)

    return pl.pallas_call(
        kernel,
        out_shape=[f32(FIELDS * own_cells + EXTRA, radius), f32(FIELDS * (own_cells + SUB), LANES)],
        in_specs=[smem] + [vmem] * 5,
        out_specs=[vmem] * 2,
        scratch_shapes=step_scratch(n),
        compiler_params=params,
        cost_estimate=cost,
        name="first_step",
    )(*operands)


def last_step(plan, level, operands, done, levels):
    n, radius, own_cells, total, spare, moved = plan
    final = level == levels - 1
    buffer = f32(FIELDS * own_cells, radius)

    def kernel(place, own, near, far, spin, pick, *rest):
        refs = (place, own, near, far, spin, pick)
        if not final:
            step_kernel(plan, refs, ToBuffer(rest[0]), rest[1:])
            return
        ready, outs, scratch = rest[: levels - 1], rest[levels - 1 : levels + 2], rest[levels + 2 :]
        last, sent = scratch[-2:]
        copies = []
        for k, x in enumerate(ready):
            copies += copies_out(k, x, outs, sent)
        for copy in copies:
            copy.start()
        step_kernel(plan, refs, ToBuffer(last), scratch[:-2])
        rest_of = copies_out(level, last, outs, sent)
        for copy in rest_of:
            copy.start()
        for copy in copies + rest_of:
            copy.wait()

    if final:
        out_shape = [f32(levels, own_cells, radius), f32(2, levels, own_cells, radius), f32(2, levels, own_cells, radius)]
        more = [pltpu.VMEM((FIELDS * own_cells, radius), jnp.float32), pltpu.SemaphoreType.DMA((levels * FIELDS,))]
    else:
        out_shape = buffer
        more = []
    return pl.pallas_call(
        kernel,
        out_shape=out_shape,
        in_specs=[smem] + [vmem] * (5 + len(done)),
        out_specs=[pl.BlockSpec(memory_space=pltpu.HBM)] * 3 if final else vmem,
        scratch_shapes=step_scratch(n) + more,
        compiler_params=params,
        cost_estimate=cost,
        name="last_step",
    )(*operands, *done)


def body(density, momentum, magnetic, rotation, shifts):
    phi_count = lax.axis_size("phi")
    row_count = lax.axis_size("row")
    levels, own_cells, radius = density.shape
    total = radius * row_count
    parts = radius // LANES
    n = radius // SLOTS
    need = [max(shift_bound(part * LANES, total) + REACH - own_cells, 0) for part in range(parts)]
    spare = own_cells - need[0]
    assert row_count == 2 and radius == 2 * LANES and own_cells == HALF // 2
    assert 0 < need[0] < own_cells and need[1] <= SUB + spare and spare <= SUB

    row = lax.axis_index("row")
    place = jnp.reshape(row, (1,)).astype(jnp.int32)
    send_near = lambda x: lax.ppermute(x, "phi", [(p, (p + 1) % phi_count) for p in range(phi_count)])
    send_far = lambda x: lax.ppermute(x, "phi", [(p, (p + 2) % phi_count) for p in range(phi_count)])
    send_side = lambda x: lax.ppermute(x, "row", [(0, 1), (1, 0)])

    spins, turns = rotation.reshape(parts, LANES), shifts.reshape(parts, LANES)
    near_message = f32(FIELDS * own_cells + EXTRA, radius)
    far_message = f32(FIELDS * (own_cells + SUB), LANES)
    edge = pl.pallas_call(
        edge_kernel,
        out_shape=f32(levels, EXTRA, 2 * LANES),
        in_specs=[smem] + [pl.BlockSpec(memory_space=pltpu.HBM)] * 5,
        out_specs=vmem,
        scratch_shapes=[
            pltpu.VMEM((levels, FIELDS * own_cells, LANES), jnp.float32),
            pltpu.VMEM((parts, LANES), jnp.float32),
            pltpu.VMEM((parts, LANES), jnp.int32),
            pltpu.SemaphoreType.DMA((levels * FIELDS + 2,)),
        ],
        compiler_params=pltpu.CompilerParams(vmem_limit_bytes=EDGE_LIMIT),
        name="edges",
    )(place, density, momentum, magnetic, spins, turns)
    side = send_side(edge)
    packed = pl.pallas_call(
        lambda *refs: pack_kernel(spare, levels, *refs),
        out_shape=[near_message] * levels + [far_message] * levels,
        in_specs=[vmem] * 4,
        out_specs=[vmem] * (2 * levels),
        compiler_params=params,
        cost_estimate=cost,
        name="pack",
    )(density, momentum, magnetic, side)
    owns, fars = packed[:levels], packed[levels:]
    wide = (n + 1, radius, own_cells, total, spare, EXTRA)
    plain = (n, radius, own_cells, total, spare, 0)
    i32 = jax.ShapeDtypeStruct((TALL * SUB, LANES), jnp.int32)
    tables = pl.pallas_call(
        lambda *refs: table_kernel((wide, plain), *refs),
        out_shape=[f32(TALL * SUB, LANES), i32] * 2,
        in_specs=[smem] + [vmem] * 3,
        out_specs=[vmem] * 4,
        scratch_shapes=[pltpu.VMEM((2, tall_of(n + 1), LANES), jnp.float32)],
        compiler_params=params,
        name="tables",
    )(place, side, spins, turns)
    moved = [(send_near(own), send_far(far)) for own, far in zip(owns, fars)]
    states = []
    for level in range(levels):
        near, far = moved[level]
        states.append(first_step(wide, (place, owns[level], near, far, *tables[:2])))
    moved = [(send_near(own), send_far(far)) for own, far in states]
    done = ()
    for level in range(levels):
        near, far = moved[level]
        operands = (place, states[level][0], near, far, *tables[2:])
        result = last_step(plain, level, operands, done if level == levels - 1 else (), levels)
        done += (result,)
    return tuple(result)


def solution(mesh):
    placed = (
        P(None, "phi", "row"),
        P(None, None, "phi", "row"),
        P(None, None, "phi", "row"),
        P("row"),
        P("row"),
    )
    return jax.shard_map(
        body,
        mesh=mesh,
        in_specs=placed,
        out_specs=(P(None, "phi", "row"), P(None, None, "phi", "row"), P(None, None, "phi", "row")),
        check_vma=False,
    )
```

```python
import jax
import jax.numpy as jnp
from jax import lax
from jax.experimental import pallas as pl
from jax.experimental.pallas import tpu as pltpu
from jax.sharding import PartitionSpec as P

STEPS = 2
SMIN = 8
SMAX = 56
STAGES = 3
REACH = 2 * STAGES
FIELDS = 5
LANES = 128
SUB = 8
HALF = LANES // 2
SLOTS = 2 * SUB
EXTRA = 2 * SUB
DEALT = 32
TALL = 40
ROWS = 8
PICKS = 4
VMEM_LIMIT = 32 * 1024 * 1024
EDGE_LIMIT = 60 * 1024 * 1024

time_step = 0.08


def shift_bound(first_row, rows):
    d = rows - 1 - first_row
    return min(SMIN + (SMAX - SMIN - 1) * d * d // ((rows - 1) * (rows - 1)) + 1, SMAX)


def minmod(lower, upper):
    return jnp.maximum(jnp.minimum(lower, 0.0), jnp.minimum(upper, jnp.maximum(lower, 0.0)))


def physical(state):
    rho, mn, mt, bn, bt = state
    inverse = pltpu.reciprocal(rho, approx=True)
    bn_sq = bn * bn
    bt_sq = bt * bt
    vn = mn * inverse
    vt = mt * inverse
    inside = (bn_sq + bt_sq) * inverse + 1.0
    root = lax.rsqrt(inside)
    ram = mn * vn + rho
    tension = bt_sq - bn_sq
    flux_t = mt * vn - bn * bt
    flux_b = bt * vn - bn * vt
    speed = jnp.abs(vn) + inside * root
    return ram, tension, flux_t, flux_b, speed


def face_twice(left, right, of_left, of_right):
    left_ram, left_tension, left_t, left_b, left_speed = of_left
    right_ram, right_tension, right_t, right_b, right_speed = of_right
    bound = jnp.maximum(left_speed, right_speed)
    jumps = [bound * (l - r) for l, r in zip(left, right)]
    return [
        (left[1] + right[1]) + jumps[0],
        ((left_ram + right_ram) + 0.5 * (left_tension + right_tension)) + jumps[1],
        (left_t + right_t) + jumps[2],
        jumps[3],
        (left_b + right_b) + jumps[4],
    ]


def swapped(five):
    return [five[0], five[2], five[1], five[4], five[3]]


def tile(i):
    return pl.ds(pl.multiple_of(i * SUB, SUB), SUB)


def run_stages(n, stages, spin, edges):
    half_dt = 0.5 * time_step
    low_mask, high_mask = edges
    first, last = REACH, REACH + n - 1

    right_of = lambda x: pltpu.roll(x, LANES - 1, 1)
    left_of = lambda x: pltpu.roll(x, 1, 1)

    def radial_states(halves, centres):
        jumps = [h[SUB:] - h[:-SUB] for h in halves]
        slopes = [minmod(d[:-SUB], d[SUB:]) for d in jumps]
        lower = [x - g for x, g in zip(centres, slopes)]
        upper = [x + g for x, g in zip(centres, slopes)]
        return swapped([x[:-SUB] for x in upper]), swapped([x[SUB:] for x in lower])

    def work(stage, i0, before):
        src, dst = stage, (stage & 1) + 1
        weight = jnp.where(stage == 0, 1.0, jnp.where(stage == 1, 0.25, 2.0 / 3.0))
        keep = jnp.where(stage == 0, 0.0, jnp.where(stage == 1, 0.75, 1.0 / 3.0))
        some = lambda first, count: pl.ds(pl.multiple_of((i0 + first) * SUB, SUB), count * SUB)
        here = some(0, ROWS)
        size = ROWS * SUB
        rows = [stages[src, f, some(-1, ROWS + 3), :] for f in range(FIELDS)]
        halves = [0.5 * x for x in rows]
        own = [x[SUB : SUB + size] for x in rows]
        half = [x[SUB : SUB + size] for x in halves]
        after = [right_of(x) for x in half]
        left, right = radial_states(halves, [x[SUB:-SUB] for x in rows])
        jump = [x - y for x, y in zip(after, half)]
        behind = [left_of(x) for x in jump]
        of_left = physical(left)
        of_right = physical(right)
        slopes = [minmod(x, y) for x, y in zip(behind, jump)]
        lower = [right_of(x - y) for x, y in zip(own, slopes)]
        upper = [x + y for x, y in zip(own, slopes)]
        of_upper = physical(upper)
        faces = swapped(face_twice(left, right, of_left, of_right))
        of_lower = physical(lower)
        azimuth = face_twice(upper, lower, of_upper, of_lower)
        shifted = [left_of(x) for x in azimuth]
        change = [x - jnp.concatenate([y, x[:-SUB]], axis=0) for x, y in zip(faces, before)]
        turn = spin[here, :]
        source = [None, (-0.5 * turn) * own[2], (2.0 * turn) * own[1], (-1.5 * turn) * own[4], None]
        partial = [x if y is None else x + y for x, y in zip(own, source)]
        starts = [keep * stages[0, f, here, :] for f in range(FIELDS)]
        for f in range(FIELDS):
            new = partial[f] - half_dt * ((azimuth[f] - shifted[f]) + change[f])
            stages[dst, f, here, :] = weight * new + starts[f]
        return [x[-SUB:] for x in faces]

    def run(stage, _):
        for f in range(FIELDS):
            inner = stages[stage, f, tile(first), :]
            outer = stages[stage, f, tile(last), :]
            for k in (1, 2):
                stages[stage, f, tile(first - k), :] = jnp.where(low_mask, inner, stages[stage, f, tile(first - k), :])
                stages[stage, f, tile(last + k), :] = jnp.where(high_mask, outer, stages[stage, f, tile(last + k), :])
        count = n + 2 * REACH - 4 - 4 * stage
        if n % ROWS == 0:
            lo = 2 * stage + 2
            rows = [stages[stage, f, pl.ds(pl.multiple_of((lo - 2) * SUB, SUB), 4 * SUB), :] for f in range(FIELDS)]
            left, right = radial_states([0.5 * x for x in rows], [x[SUB:-SUB] for x in rows])
            before = tuple(swapped(face_twice(left, right, physical(left), physical(right))))
        else:
            lo = 2 * stage + 1
            count = count + 1
            before = (jnp.zeros((SUB, LANES), jnp.float32),) * FIELDS
        turns = lax.div(count + ROWS - 1, ROWS)
        lax.fori_loop(0, turns, lambda c, carried: tuple(work(stage, lo + c * ROWS, list(carried))), before)
        return 0

    lax.fori_loop(0, STAGES, run, 0)


def spread(block, first, width):
    block = pltpu.roll(block, (LANES - first) % LANES, 1)
    lane = lax.broadcasted_iota(jnp.int32, block.shape, 1)
    while width < LANES:
        block = jnp.where(lane < width, block, pltpu.roll(block, width, 1))
        width *= 2
    return block


def pack_far(far, near, own_cells, spare):
    sublane = lax.broadcasted_iota(jnp.int32, (SUB, LANES), 0)

    def one(f, _):
        start = pl.multiple_of(f * own_cells, SUB)
        base = pl.multiple_of(f * (own_cells + SUB), SUB)
        low = near[pl.ds(start, own_cells), 0:LANES]
        high = near[pl.ds(start + own_cells - 2 * SUB, 2 * SUB), LANES : 2 * LANES]
        moved = pltpu.roll(high[0:SUB], spare, 0)
        far[pl.ds(base, SUB), :] = jnp.where(sublane < spare, moved, low[0:SUB])
        far[pl.ds(base + SUB, own_cells - SUB), :] = low[SUB:]
        far[pl.ds(base + own_cells, SUB), :] = high[SUB:]
        return 0

    lax.fori_loop(0, FIELDS, one, 0)


def edge_kernel(place, density, momentum, magnetic, rotation, shifts, edge, ends, spin_in, shift_in, arrived):
    levels, own_cells, radius = density.shape
    on_low = place[0] == 0
    parts = radius // LANES
    split = 4 * own_cells
    columns = pl.ds(pl.multiple_of(jnp.where(on_low, radius - LANES, 0), LANES), LANES)
    copies = [
        pltpu.make_async_copy(rotation, spin_in, arrived.at[levels * FIELDS]),
        pltpu.make_async_copy(shifts, shift_in, arrived.at[levels * FIELDS + 1]),
    ]
    for level in range(levels):
        sources = [density.at[level, :, columns]] + [x.at[k, level, :, columns] for x in (momentum, magnetic) for k in range(2)]
        for f, x in enumerate(sources):
            at = ends.at[level, pl.ds(f * own_cells, own_cells), :]
            copies.append(pltpu.make_async_copy(x, at, arrived.at[level * FIELDS + f]))
    for copy in copies:
        copy.start()
    for copy in copies:
        copy.wait()
    wide = lambda ref: jnp.broadcast_to(
        jnp.where(on_low, ref[parts - 1 : parts, :], ref[0:1, :]).astype(jnp.float32), (own_cells, LANES)
    )
    turn = wide(spin_in) * time_step
    shift = wide(shift_in)
    zero = jnp.zeros((own_cells, LANES), jnp.float32)
    for level in range(levels):
        last = jnp.concatenate([ends[level, split:, :], turn, shift, zero], axis=0)
        for side, group in enumerate((ends[level, 0:split, :], last)):
            turned = group.T
            edge[level, :, side * LANES : (side + 1) * LANES] = jnp.where(on_low, turned[LANES - EXTRA :], turned[0:EXTRA])


def pack_kernel(spare, levels, density, momentum, magnetic, edge, *outs):
    del edge
    nears, fars = outs[:levels], outs[levels:]
    own_cells = density.shape[1]
    for level in range(levels):
        sources = [density.at[level]] + [x.at[k, level] for x in (momentum, magnetic) for k in range(2)]
        for f, x in enumerate(sources):
            nears[level][f * own_cells : (f + 1) * own_cells, :] = x[...]
        pack_far(fars[level], nears[level], own_cells, spare)


class Blocks:
    def __init__(self, row, n, radius, total, moved):
        self.on_low = row == 0
        self.n = n
        self.own_at = pl.multiple_of(jnp.where(self.on_low, EXTRA, EXTRA + moved), SUB)
        self.edge_at = pl.multiple_of(jnp.where(self.on_low, EXTRA + radius, moved), SUB)
        bounds = [[shift_bound(r * radius - (moved if r else 0) + n * k, total) for k in range(SLOTS)] for r in range(2)]
        self.bounds = [jnp.where(self.on_low, a, b) for a, b in zip(*bounds)]

    def rows_of(self, k):
        start = EXTRA - REACH + self.n * k
        return slice(start, start + DEALT)


def table_kernel(plans, place, side, rotation, shifts, *rest):
    outs, held = rest[:-1], rest[-1]
    lane = lax.broadcasted_iota(jnp.int32, (SUB, LANES), 1)
    sublane = lax.broadcasted_iota(jnp.int32, (SUB, LANES), 0)
    front = lax.broadcasted_iota(jnp.int32, (DEALT, LANES), 1) < HALF
    more = side[0, :, LANES : 2 * LANES]
    for which, (n, radius, own_cells, total, spare, moved) in enumerate(plans):
        spin, pick = outs[2 * which : 2 * which + 2]
        blocks = Blocks(place[0], n, radius, total, moved)
        for part in range(radius // LANES):
            rows = pl.ds(blocks.own_at + part * LANES, LANES)
            along = lambda ref: jnp.broadcast_to(ref[part : part + 1, :].astype(jnp.float32), (LANES, LANES)).T
            held[0, rows, :] = along(rotation) * time_step
            held[1, rows, :] = along(shifts)
        held[0, pl.ds(blocks.edge_at, EXTRA), :] = spread(more, own_cells, own_cells)
        held[1, pl.ds(blocks.edge_at, EXTRA), :] = spread(more, 2 * own_cells, own_cells)
        bound = jnp.zeros((SUB, LANES), jnp.int32)
        for j in range(SUB):
            low, high = blocks.rows_of(j), blocks.rows_of(SUB + j)
            spin[pl.ds(j, DEALT, stride=SUB), :] = jnp.where(front, held[0, low, :], held[0, high, :])
            pick[pl.ds(j, DEALT, stride=SUB), :] = jnp.where(front, held[1, low, :], held[1, high, :]).astype(jnp.int32)
            bound = jnp.where(sublane == j, jnp.where(lane < HALF, blocks.bounds[j], blocks.bounds[SUB + j]), bound)

        def one(i, _):
            pick[tile(i), :] = (lane + (REACH + bound)) - pick[tile(i), :]
            return 0

        lax.fori_loop(0, TALL, one, 0)


def step_kernel(plan, refs, write, scratch):
    n, radius, own_cells, total, spare, moved = plan
    place, own, own_edge, near, near_edge, far, spin, pick = refs
    cells, stages, packed = scratch
    row = place[0]
    lane = lax.broadcasted_iota(jnp.int32, (SUB, LANES), 1)
    sublane = lax.broadcasted_iota(jnp.int32, (SUB, LANES), 0)
    blocks = Blocks(row, n, radius, total, moved)

    edge_lane = lax.broadcasted_iota(jnp.int32, (EXTRA, LANES), 1)
    parts = radius // LANES

    def gather(f, _):
        rows = pl.ds(pl.multiple_of(f * own_cells, SUB), own_cells)
        start = pl.multiple_of(f * (own_cells + SUB), SUB)
        for part in range(parts):
            columns = slice(part * LANES, (part + 1) * LANES)
            if part == 0:
                top = far[pl.ds(start, own_cells), :]
            else:
                top = jnp.concatenate(
                    [
                        jnp.zeros((own_cells - 2 * SUB, LANES), jnp.float32),
                        pltpu.roll(far[pl.ds(start, SUB), :], SUB - spare, 0),
                        far[pl.ds(start + own_cells, SUB), :],
                    ],
                    axis=0,
                )
            fill = jnp.zeros((own_cells, LANES), jnp.float32)
            block = jnp.concatenate([top, near[rows, columns], own[rows, columns], fill], axis=0)
            cells[f, pl.ds(blocks.own_at + part * LANES, LANES), :] = block.T
        columns = pl.ds(pl.multiple_of(lax.div(f, 4) * LANES, LANES), LANES)
        lanes_at = lax.rem(f, 4) * own_cells
        cells[f, pl.ds(blocks.edge_at, EXTRA), :] = jnp.where(
            edge_lane < 2 * own_cells,
            pltpu.roll(near_edge[:, columns], lax.rem(LANES + own_cells - lanes_at, LANES), 1),
            pltpu.roll(own_edge[:, columns], lax.rem(LANES + 2 * own_cells - lanes_at, LANES), 1),
        )
        return 0

    lax.fori_loop(0, FIELDS, gather, 0)

    front = lax.broadcasted_iota(jnp.int32, (DEALT, LANES), 1) < HALF

    def deal(f, _):
        for j in range(SUB):
            low, high = j, SUB + j
            turn_low = (LANES - (2 * own_cells - REACH)) + blocks.bounds[low]
            turn_high = (HALF - (2 * own_cells - REACH)) + blocks.bounds[high]
            stages[0, f, pl.ds(j, DEALT, stride=SUB), :] = jnp.where(
                front,
                pltpu.roll(cells[f, blocks.rows_of(low), :], turn_low, 1),
                pltpu.roll(cells[f, blocks.rows_of(high), :], turn_high, 1),
            )
        return 0

    lax.fori_loop(0, FIELDS, deal, 0)

    edges = (
        (sublane == 0) & (lane < HALF) & (row == 0),
        (sublane == SUB - 1) & (lane >= HALF) & (row == total // radius - 1),
    )
    run_stages(n, stages, spin, edges)

    even = (lane & own_cells) == 0

    def shift(turn, _):
        for k in range(PICKS):
            i = turn * PICKS + k
            rows = tile(REACH + i)
            source = pick[rows, :]
            picks = [source & (LANES - 1), (source - own_cells) & (LANES - 1)]
            turned = [
                jnp.take_along_axis(stages[1, f, rows, :], picks[f % 2], axis=1, mode="promise_in_bounds")
                for f in range(FIELDS)
            ]
            stages[2, 0, tile(i), :] = jnp.where(even, turned[0], turned[1])
            stages[2, 1, tile(i), :] = jnp.where(even, turned[2], turned[3])
            stages[2, 2, tile(i), :] = turned[4]
        return 0

    lax.fori_loop(0, (n + PICKS - 1) // PICKS, shift, 0)
    narrow = lax.broadcasted_iota(jnp.int32, (n, LANES), 1) < HALF
    for j in range(SUB):
        one, two, three = [stages[2, g, pl.ds(j, n, stride=SUB), :] for g in range(3)]
        low = slice(EXTRA + n * j, EXTRA + n * (j + 1))
        high = slice(EXTRA + n * (SUB + j), EXTRA + n * (SUB + j + 1))
        packed[0, low, :] = jnp.where(narrow, one, pltpu.roll(two, HALF, 1))
        packed[0, high, :] = jnp.where(narrow, pltpu.roll(one, HALF, 1), two)
        packed[1, low, :] = three
        packed[1, high, :] = pltpu.roll(three, HALF, 1)
    for part in range(parts):
        rows = pl.ds(blocks.own_at + part * LANES, LANES)
        write.fields(slice(part * LANES, (part + 1) * LANES), packed[0, rows, :].T, packed[1, rows, :].T)
    write.edge(packed[0, pl.ds(blocks.edge_at, EXTRA), :], packed[1, pl.ds(blocks.edge_at, EXTRA), :])
    write.end()


class ToMessage:
    def __init__(self, near, far, own_cells, spare):
        self.near, self.far, self.own_cells, self.spare = near, far, own_cells, spare

    def fields(self, columns, four, fifth):
        split = 4 * self.own_cells
        self.near[0:split, columns] = four
        self.near[split : split + self.own_cells, columns] = fifth[0 : self.own_cells]

    def edge(self, first, second):
        tail = FIELDS * self.own_cells
        self.near[tail : tail + EXTRA, 0:LANES] = first
        self.near[tail : tail + EXTRA, LANES : 2 * LANES] = second

    def end(self):
        pack_far(self.far, self.near, self.own_cells, self.spare)


class ToBuffer:
    def __init__(self, buffer):
        self.buffer = buffer

    def fields(self, columns, four, fifth):
        split = four.shape[0]
        self.buffer[0:split, columns] = four
        self.buffer[split:, columns] = fifth[0 : self.buffer.shape[0] - split]

    def edge(self, first, second):
        pass

    def end(self):
        pass


def copies_out(level, buffer, outs, sent):
    density, momentum, magnetic = outs
    cells = density.shape[1]
    targets = [density.at[level]] + [x.at[k, level] for x in (momentum, magnetic) for k in range(2)]
    return [
        pltpu.make_async_copy(buffer.at[pl.ds(f * cells, cells), :], x, sent.at[level * FIELDS + f])
        for f, x in enumerate(targets)
    ]


def tall_of(n):
    return EXTRA + SLOTS * n + 2 * SUB


def step_scratch(n):
    return [
        pltpu.VMEM((FIELDS, tall_of(n), LANES), jnp.float32),
        pltpu.VMEM((STAGES, FIELDS, TALL * SUB, LANES), jnp.float32),
        pltpu.VMEM((2, tall_of(n), LANES), jnp.float32),
    ]


vmem = pl.BlockSpec(memory_space=pltpu.VMEM)
smem = pl.BlockSpec(memory_space=pltpu.SMEM)
f32 = lambda *s: jax.ShapeDtypeStruct(s, jnp.float32)
params = pltpu.CompilerParams(vmem_limit_bytes=VMEM_LIMIT)
cost = pl.CostEstimate(flops=9_000_000_000, bytes_accessed=29_000_000, transcendentals=0)


def first_step(plan, level, operands):
    n, radius, own_cells, total, spare, moved = plan

    def kernel(place, own, near, far, side, corner, spin, pick, near_out, far_out, *scratch):
        refs = (place, own, side.at[level], near, corner.at[level], far, spin, pick)
        step_kernel(plan, refs, ToMessage(near_out, far_out, own_cells, spare), scratch)

    return pl.pallas_call(
        kernel,
        out_shape=[f32(FIELDS * own_cells + EXTRA, radius), f32(FIELDS * (own_cells + SUB), LANES)],
        in_specs=[smem] + [vmem] * 7,
        out_specs=[vmem] * 2,
        scratch_shapes=step_scratch(n),
        compiler_params=params,
        cost_estimate=cost,
        name="first_step",
    )(*operands)


def last_step(plan, level, operands, done, levels):
    n, radius, own_cells, total, spare, moved = plan
    final = level == levels - 1
    tail = pl.ds(FIELDS * own_cells, EXTRA)
    buffer = f32(FIELDS * own_cells, radius)

    def kernel(place, own, near, far, spin, pick, *rest):
        refs = (place, own, own.at[tail, :], near, near.at[tail, :], far, spin, pick)
        if not final:
            step_kernel(plan, refs, ToBuffer(rest[0]), rest[1:])
            return
        ready, outs, scratch = rest[: levels - 1], rest[levels - 1 : levels + 2], rest[levels + 2 :]
        last, sent = scratch[-2:]
        copies = []
        for k, x in enumerate(ready):
            copies += copies_out(k, x, outs, sent)
        for copy in copies:
            copy.start()
        step_kernel(plan, refs, ToBuffer(last), scratch[:-2])
        rest_of = copies_out(level, last, outs, sent)
        for copy in rest_of:
            copy.start()
        for copy in copies + rest_of:
            copy.wait()

    if final:
        out_shape = [f32(levels, own_cells, radius), f32(2, levels, own_cells, radius), f32(2, levels, own_cells, radius)]
        more = [pltpu.VMEM((FIELDS * own_cells, radius), jnp.float32), pltpu.SemaphoreType.DMA((levels * FIELDS,))]
    else:
        out_shape = buffer
        more = []
    return pl.pallas_call(
        kernel,
        out_shape=out_shape,
        in_specs=[smem] + [vmem] * (5 + len(done)),
        out_specs=[pl.BlockSpec(memory_space=pltpu.HBM)] * 3 if final else vmem,
        scratch_shapes=step_scratch(n) + more,
        compiler_params=params,
        cost_estimate=cost,
        name="last_step",
    )(*operands, *done)


def body(density, momentum, magnetic, rotation, shifts):
    phi_count = lax.axis_size("phi")
    row_count = lax.axis_size("row")
    levels, own_cells, radius = density.shape
    total = radius * row_count
    parts = radius // LANES
    n = radius // SLOTS
    need = [max(shift_bound(part * LANES, total) + REACH - own_cells, 0) for part in range(parts)]
    spare = own_cells - need[0]
    assert row_count == 2 and radius == 2 * LANES and own_cells == HALF // 2
    assert 0 < need[0] < own_cells and need[1] <= SUB + spare and spare <= SUB

    row = lax.axis_index("row")
    place = jnp.reshape(row, (1,)).astype(jnp.int32)
    send_near = lambda x: lax.ppermute(x, "phi", [(p, (p + 1) % phi_count) for p in range(phi_count)])
    send_far = lambda x: lax.ppermute(x, "phi", [(p, (p + 2) % phi_count) for p in range(phi_count)])
    send_side = lambda x: lax.ppermute(x, "row", [(0, 1), (1, 0)])

    spins, turns = rotation.reshape(parts, LANES), shifts.reshape(parts, LANES)
    near_message = f32(FIELDS * own_cells, radius)
    far_message = f32(FIELDS * (own_cells + SUB), LANES)
    edge = pl.pallas_call(
        edge_kernel,
        out_shape=f32(levels, EXTRA, 2 * LANES),
        in_specs=[smem] + [pl.BlockSpec(memory_space=pltpu.HBM)] * 5,
        out_specs=vmem,
        scratch_shapes=[
            pltpu.VMEM((levels, FIELDS * own_cells, LANES), jnp.float32),
            pltpu.VMEM((parts, LANES), jnp.float32),
            pltpu.VMEM((parts, LANES), jnp.int32),
            pltpu.SemaphoreType.DMA((levels * FIELDS + 2,)),
        ],
        compiler_params=pltpu.CompilerParams(vmem_limit_bytes=EDGE_LIMIT),
        name="edges",
    )(place, density, momentum, magnetic, spins, turns)
    packed = pl.pallas_call(
        lambda *refs: pack_kernel(spare, levels, *refs),
        out_shape=[near_message] * levels + [far_message] * levels,
        in_specs=[vmem] * 3 + [pl.BlockSpec(memory_space=pl.ANY)],
        out_specs=[vmem] * (2 * levels),
        compiler_params=params,
        cost_estimate=cost,
        name="pack",
    )(density, momentum, magnetic, edge)
    owns, fars = packed[:levels], packed[levels:]
    side = send_side(edge)
    corner = send_near(side)
    wide = (n + 1, radius, own_cells, total, spare, EXTRA)
    plain = (n, radius, own_cells, total, spare, 0)
    i32 = jax.ShapeDtypeStruct((TALL * SUB, LANES), jnp.int32)
    tables = pl.pallas_call(
        lambda *refs: table_kernel((wide, plain), *refs),
        out_shape=[f32(TALL * SUB, LANES), i32] * 2,
        in_specs=[smem] + [vmem] * 3,
        out_specs=[vmem] * 4,
        scratch_shapes=[pltpu.VMEM((2, tall_of(n + 1), LANES), jnp.float32)],
        compiler_params=params,
        name="tables",
    )(place, side, spins, turns)
    moved = []
    for own, far in zip(owns, fars):
        if moved:
            own, far, _ = lax.optimization_barrier((own, far, tables[0]))
        moved.append((send_near(own), send_far(far)))
    states = []
    for level in range(levels):
        near, far = moved[level]
        states.append(first_step(wide, level, (place, owns[level], near, far, side, corner, *tables[:2])))
    moved = [(send_near(own), send_far(far)) for own, far in states]
    done = ()
    for level in range(levels):
        near, far = moved[level]
        operands = (place, states[level][0], near, far, *tables[2:])
        result = last_step(plain, level, operands, done if level == levels - 1 else (), levels)
        done += (result,)
    return tuple(result)


def solution(mesh):
    placed = (
        P(None, "phi", "row"),
        P(None, None, "phi", "row"),
        P(None, None, "phi", "row"),
        P("row"),
        P("row"),
    )
    return jax.shard_map(
        body,
        mesh=mesh,
        in_specs=placed,
        out_specs=(P(None, "phi", "row"), P(None, None, "phi", "row"), P(None, None, "phi", "row")),
        check_vma=False,
    )
```

```python
import jax
import jax.numpy as jnp
from jax import lax
from jax.experimental import pallas as pl
from jax.experimental.pallas import tpu as pltpu
from jax.sharding import PartitionSpec as P

STEPS = 2
SMIN = 8
SMAX = 56
STAGES = 3
REACH = 2 * STAGES
FIELDS = 5
LANES = 128
SUB = 8
HALF = LANES // 2
SLOTS = 2 * SUB
EXTRA = 2 * SUB
DEALT = 32
TALL = 40
ROWS = 8
PICKS = 4
VMEM_LIMIT = 32 * 1024 * 1024
EDGE_LIMIT = 60 * 1024 * 1024

time_step = 0.08


def shift_bound(first_row, rows):
    d = rows - 1 - first_row
    return min(SMIN + (SMAX - SMIN - 1) * d * d // ((rows - 1) * (rows - 1)) + 1, SMAX)


def minmod(lower, upper):
    return jnp.maximum(jnp.minimum(lower, 0.0), jnp.minimum(upper, jnp.maximum(lower, 0.0)))


def physical(state):
    rho, mn, mt, bn, bt = state
    inverse = pltpu.reciprocal(rho, approx=True)
    bn_sq = bn * bn
    bt_sq = bt * bt
    vn = mn * inverse
    vt = mt * inverse
    inside = (bn_sq + bt_sq) * inverse + 1.0
    root = lax.rsqrt(inside)
    ram = mn * vn + rho
    tension = bt_sq - bn_sq
    flux_t = mt * vn - bn * bt
    flux_b = bt * vn - bn * vt
    speed = jnp.abs(vn) + inside * root
    return ram, tension, flux_t, flux_b, speed


def face_twice(left, right, of_left, of_right):
    left_ram, left_tension, left_t, left_b, left_speed = of_left
    right_ram, right_tension, right_t, right_b, right_speed = of_right
    bound = jnp.maximum(left_speed, right_speed)
    jumps = [bound * (l - r) for l, r in zip(left, right)]
    return [
        (left[1] + right[1]) + jumps[0],
        ((left_ram + right_ram) + 0.5 * (left_tension + right_tension)) + jumps[1],
        (left_t + right_t) + jumps[2],
        jumps[3],
        (left_b + right_b) + jumps[4],
    ]


def swapped(five):
    return [five[0], five[2], five[1], five[4], five[3]]


def tile(i):
    return pl.ds(pl.multiple_of(i * SUB, SUB), SUB)


def run_stages(n, stages, spin, edges):
    half_dt = 0.5 * time_step
    low_mask, high_mask = edges
    first, last = REACH, REACH + n - 1

    right_of = lambda x: pltpu.roll(x, LANES - 1, 1)
    left_of = lambda x: pltpu.roll(x, 1, 1)

    def radial_states(halves, centres):
        jumps = [h[SUB:] - h[:-SUB] for h in halves]
        slopes = [minmod(d[:-SUB], d[SUB:]) for d in jumps]
        lower = [x - g for x, g in zip(centres, slopes)]
        upper = [x + g for x, g in zip(centres, slopes)]
        return swapped([x[:-SUB] for x in upper]), swapped([x[SUB:] for x in lower])

    def work(stage, i0, before):
        src, dst = stage, (stage & 1) + 1
        weight = jnp.where(stage == 0, 1.0, jnp.where(stage == 1, 0.25, 2.0 / 3.0))
        keep = jnp.where(stage == 0, 0.0, jnp.where(stage == 1, 0.75, 1.0 / 3.0))
        some = lambda first, count: pl.ds(pl.multiple_of((i0 + first) * SUB, SUB), count * SUB)
        here = some(0, ROWS)
        size = ROWS * SUB
        rows = [stages[src, f, some(-1, ROWS + 3), :] for f in range(FIELDS)]
        halves = [0.5 * x for x in rows]
        own = [x[SUB : SUB + size] for x in rows]
        half = [x[SUB : SUB + size] for x in halves]
        after = [right_of(x) for x in half]
        left, right = radial_states(halves, [x[SUB:-SUB] for x in rows])
        jump = [x - y for x, y in zip(after, half)]
        behind = [left_of(x) for x in jump]
        of_left = physical(left)
        of_right = physical(right)
        slopes = [minmod(x, y) for x, y in zip(behind, jump)]
        lower = [right_of(x - y) for x, y in zip(own, slopes)]
        upper = [x + y for x, y in zip(own, slopes)]
        of_upper = physical(upper)
        faces = swapped(face_twice(left, right, of_left, of_right))
        of_lower = physical(lower)
        azimuth = face_twice(upper, lower, of_upper, of_lower)
        shifted = [left_of(x) for x in azimuth]
        change = [x - jnp.concatenate([y, x[:-SUB]], axis=0) for x, y in zip(faces, before)]
        turn = spin[here, :]
        source = [None, (-0.5 * turn) * own[2], (2.0 * turn) * own[1], (-1.5 * turn) * own[4], None]
        partial = [x if y is None else x + y for x, y in zip(own, source)]
        starts = [keep * stages[0, f, here, :] for f in range(FIELDS)]
        for f in range(FIELDS):
            new = partial[f] - half_dt * ((azimuth[f] - shifted[f]) + change[f])
            stages[dst, f, here, :] = weight * new + starts[f]
        return [x[-SUB:] for x in faces]

    def run(stage, _):
        for f in range(FIELDS):
            inner = stages[stage, f, tile(first), :]
            outer = stages[stage, f, tile(last), :]
            for k in (1, 2):
                stages[stage, f, tile(first - k), :] = jnp.where(low_mask, inner, stages[stage, f, tile(first - k), :])
                stages[stage, f, tile(last + k), :] = jnp.where(high_mask, outer, stages[stage, f, tile(last + k), :])
        count = n + 2 * REACH - 4 - 4 * stage
        if n % ROWS == 0:
            lo = 2 * stage + 2
            rows = [stages[stage, f, pl.ds(pl.multiple_of((lo - 2) * SUB, SUB), 4 * SUB), :] for f in range(FIELDS)]
            left, right = radial_states([0.5 * x for x in rows], [x[SUB:-SUB] for x in rows])
            before = tuple(swapped(face_twice(left, right, physical(left), physical(right))))
        else:
            lo = 2 * stage + 1
            count = count + 1
            before = (jnp.zeros((SUB, LANES), jnp.float32),) * FIELDS
        turns = lax.div(count + ROWS - 1, ROWS)
        lax.fori_loop(0, turns, lambda c, carried: tuple(work(stage, lo + c * ROWS, list(carried))), before)
        return 0

    lax.fori_loop(0, STAGES, run, 0)


def spread(block, first, width):
    block = pltpu.roll(block, (LANES - first) % LANES, 1)
    lane = lax.broadcasted_iota(jnp.int32, block.shape, 1)
    while width < LANES:
        block = jnp.where(lane < width, block, pltpu.roll(block, width, 1))
        width *= 2
    return block


def pack_far(far, near, own_cells, spare):
    sublane = lax.broadcasted_iota(jnp.int32, (SUB, LANES), 0)

    def one(f, _):
        start = pl.multiple_of(f * own_cells, SUB)
        base = pl.multiple_of(f * (own_cells + SUB), SUB)
        low = near[pl.ds(start, own_cells), 0:LANES]
        high = near[pl.ds(start + own_cells - 2 * SUB, 2 * SUB), LANES : 2 * LANES]
        moved = pltpu.roll(high[0:SUB], spare, 0)
        far[pl.ds(base, SUB), :] = jnp.where(sublane < spare, moved, low[0:SUB])
        far[pl.ds(base + SUB, own_cells - SUB), :] = low[SUB:]
        far[pl.ds(base + own_cells, SUB), :] = high[SUB:]
        return 0

    lax.fori_loop(0, FIELDS, one, 0)


def edge_kernel(place, density, momentum, magnetic, rotation, shifts, edge, ends, spin_in, shift_in, arrived):
    levels, own_cells, radius = density.shape
    on_low = place[0] == 0
    parts = radius // LANES
    split = 4 * own_cells
    columns = pl.ds(pl.multiple_of(jnp.where(on_low, radius - LANES, 0), LANES), LANES)
    copies = [
        pltpu.make_async_copy(rotation, spin_in, arrived.at[levels * FIELDS]),
        pltpu.make_async_copy(shifts, shift_in, arrived.at[levels * FIELDS + 1]),
    ]
    for level in range(levels):
        sources = [density.at[level, :, columns]] + [x.at[k, level, :, columns] for x in (momentum, magnetic) for k in range(2)]
        for f, x in enumerate(sources):
            at = ends.at[level, pl.ds(f * own_cells, own_cells), :]
            copies.append(pltpu.make_async_copy(x, at, arrived.at[level * FIELDS + f]))
    for copy in copies:
        copy.start()
    for copy in copies:
        copy.wait()
    wide = lambda ref: jnp.broadcast_to(
        jnp.where(on_low, ref[parts - 1 : parts, :], ref[0:1, :]).astype(jnp.float32), (own_cells, LANES)
    )
    turn = wide(spin_in) * time_step
    shift = wide(shift_in)
    zero = jnp.zeros((own_cells, LANES), jnp.float32)
    for level in range(levels):
        last = jnp.concatenate([ends[level, split:, :], turn, shift, zero], axis=0)
        for side, group in enumerate((ends[level, 0:split, :], last)):
            turned = group.T
            edge[level, :, side * LANES : (side + 1) * LANES] = jnp.where(on_low, turned[LANES - EXTRA :], turned[0:EXTRA])


def pack_kernel(spare, levels, density, momentum, magnetic, edge, *outs):
    del edge
    nears, fars = outs[:levels], outs[levels:]
    own_cells = density.shape[1]
    for level in range(levels):
        sources = [density.at[level]] + [x.at[k, level] for x in (momentum, magnetic) for k in range(2)]
        for f, x in enumerate(sources):
            nears[level][f * own_cells : (f + 1) * own_cells, :] = x[...]
        pack_far(fars[level], nears[level], own_cells, spare)


class Blocks:
    def __init__(self, row, n, radius, total, moved):
        self.on_low = row == 0
        self.n = n
        self.own_at = pl.multiple_of(jnp.where(self.on_low, EXTRA, EXTRA + moved), SUB)
        self.edge_at = pl.multiple_of(jnp.where(self.on_low, EXTRA + radius, moved), SUB)
        bounds = [[shift_bound(r * radius - (moved if r else 0) + n * k, total) for k in range(SLOTS)] for r in range(2)]
        self.bounds = [jnp.where(self.on_low, a, b) for a, b in zip(*bounds)]

    def rows_of(self, k):
        start = EXTRA - REACH + self.n * k
        return slice(start, start + DEALT)


def table_kernel(plans, place, side, rotation, shifts, *rest):
    outs, held = rest[:-1], rest[-1]
    lane = lax.broadcasted_iota(jnp.int32, (SUB, LANES), 1)
    sublane = lax.broadcasted_iota(jnp.int32, (SUB, LANES), 0)
    front = lax.broadcasted_iota(jnp.int32, (DEALT, LANES), 1) < HALF
    more = side[0, :, LANES : 2 * LANES]
    for which, (n, radius, own_cells, total, spare, moved) in enumerate(plans):
        spin, pick = outs[2 * which : 2 * which + 2]
        blocks = Blocks(place[0], n, radius, total, moved)
        for part in range(radius // LANES):
            rows = pl.ds(blocks.own_at + part * LANES, LANES)
            along = lambda ref: jnp.broadcast_to(ref[part : part + 1, :].astype(jnp.float32), (LANES, LANES)).T
            held[0, rows, :] = along(rotation) * time_step
            held[1, rows, :] = along(shifts)
        held[0, pl.ds(blocks.edge_at, EXTRA), :] = spread(more, own_cells, own_cells)
        held[1, pl.ds(blocks.edge_at, EXTRA), :] = spread(more, 2 * own_cells, own_cells)
        bound = jnp.zeros((SUB, LANES), jnp.int32)
        for j in range(SUB):
            low, high = blocks.rows_of(j), blocks.rows_of(SUB + j)
            spin[pl.ds(j, DEALT, stride=SUB), :] = jnp.where(front, held[0, low, :], held[0, high, :])
            pick[pl.ds(j, DEALT, stride=SUB), :] = jnp.where(front, held[1, low, :], held[1, high, :]).astype(jnp.int32)
            bound = jnp.where(sublane == j, jnp.where(lane < HALF, blocks.bounds[j], blocks.bounds[SUB + j]), bound)

        def one(i, _):
            pick[tile(i), :] = (lane + (REACH + bound)) - pick[tile(i), :]
            return 0

        lax.fori_loop(0, TALL, one, 0)


def step_kernel(plan, refs, write, scratch):
    n, radius, own_cells, total, spare, moved = plan
    place, own, own_edge, near, near_edge, far, spin, pick = refs
    cells, stages, packed = scratch
    row = place[0]
    lane = lax.broadcasted_iota(jnp.int32, (SUB, LANES), 1)
    sublane = lax.broadcasted_iota(jnp.int32, (SUB, LANES), 0)
    blocks = Blocks(row, n, radius, total, moved)

    edge_lane = lax.broadcasted_iota(jnp.int32, (EXTRA, LANES), 1)
    parts = radius // LANES

    def gather(f, _):
        rows = pl.ds(pl.multiple_of(f * own_cells, SUB), own_cells)
        start = pl.multiple_of(f * (own_cells + SUB), SUB)
        for part in range(parts):
            columns = slice(part * LANES, (part + 1) * LANES)
            if part == 0:
                top = far[pl.ds(start, own_cells), :]
            else:
                top = jnp.concatenate(
                    [
                        jnp.zeros((own_cells - 2 * SUB, LANES), jnp.float32),
                        pltpu.roll(far[pl.ds(start, SUB), :], SUB - spare, 0),
                        far[pl.ds(start + own_cells, SUB), :],
                    ],
                    axis=0,
                )
            fill = jnp.zeros((own_cells, LANES), jnp.float32)
            block = jnp.concatenate([top, near[rows, columns], own[rows, columns], fill], axis=0)
            cells[f, pl.ds(blocks.own_at + part * LANES, LANES), :] = block.T
        columns = pl.ds(pl.multiple_of(lax.div(f, 4) * LANES, LANES), LANES)
        lanes_at = lax.rem(f, 4) * own_cells
        cells[f, pl.ds(blocks.edge_at, EXTRA), :] = jnp.where(
            edge_lane < 2 * own_cells,
            pltpu.roll(near_edge[:, columns], lax.rem(LANES + own_cells - lanes_at, LANES), 1),
            pltpu.roll(own_edge[:, columns], lax.rem(LANES + 2 * own_cells - lanes_at, LANES), 1),
        )
        return 0

    lax.fori_loop(0, FIELDS, gather, 0)

    front = lax.broadcasted_iota(jnp.int32, (DEALT, LANES), 1) < HALF

    def deal(f, _):
        for j in range(SUB):
            low, high = j, SUB + j
            turn_low = (LANES - (2 * own_cells - REACH)) + blocks.bounds[low]
            turn_high = (HALF - (2 * own_cells - REACH)) + blocks.bounds[high]
            stages[0, f, pl.ds(j, DEALT, stride=SUB), :] = jnp.where(
                front,
                pltpu.roll(cells[f, blocks.rows_of(low), :], turn_low, 1),
                pltpu.roll(cells[f, blocks.rows_of(high), :], turn_high, 1),
            )
        return 0

    lax.fori_loop(0, FIELDS, deal, 0)

    edges = (
        (sublane == 0) & (lane < HALF) & (row == 0),
        (sublane == SUB - 1) & (lane >= HALF) & (row == total // radius - 1),
    )
    run_stages(n, stages, spin, edges)

    even = (lane & own_cells) == 0

    def shift(turn, _):
        for k in range(PICKS):
            i = turn * PICKS + k
            rows = tile(REACH + i)
            source = pick[rows, :]
            picks = [source & (LANES - 1), (source - own_cells) & (LANES - 1)]
            turned = [
                jnp.take_along_axis(stages[1, f, rows, :], picks[f % 2], axis=1, mode="promise_in_bounds")
                for f in range(FIELDS)
            ]
            stages[2, 0, tile(i), :] = jnp.where(even, turned[0], turned[1])
            stages[2, 1, tile(i), :] = jnp.where(even, turned[2], turned[3])
            stages[2, 2, tile(i), :] = turned[4]
        return 0

    lax.fori_loop(0, (n + PICKS - 1) // PICKS, shift, 0)
    narrow = lax.broadcasted_iota(jnp.int32, (n, LANES), 1) < HALF
    for j in range(SUB):
        one, two, three = [stages[2, g, pl.ds(j, n, stride=SUB), :] for g in range(3)]
        low = slice(EXTRA + n * j, EXTRA + n * (j + 1))
        high = slice(EXTRA + n * (SUB + j), EXTRA + n * (SUB + j + 1))
        packed[0, low, :] = jnp.where(narrow, one, pltpu.roll(two, HALF, 1))
        packed[0, high, :] = jnp.where(narrow, pltpu.roll(one, HALF, 1), two)
        packed[1, low, :] = three
        packed[1, high, :] = pltpu.roll(three, HALF, 1)
    for part in range(parts):
        rows = pl.ds(blocks.own_at + part * LANES, LANES)
        write.fields(slice(part * LANES, (part + 1) * LANES), packed[0, rows, :].T, packed[1, rows, :].T)
    write.edge(packed[0, pl.ds(blocks.edge_at, EXTRA), :], packed[1, pl.ds(blocks.edge_at, EXTRA), :])
    write.end()


class ToMessage:
    def __init__(self, near, far, own_cells, spare):
        self.near, self.far, self.own_cells, self.spare = near, far, own_cells, spare

    def fields(self, columns, four, fifth):
        split = 4 * self.own_cells
        self.near[0:split, columns] = four
        self.near[split : split + self.own_cells, columns] = fifth[0 : self.own_cells]

    def edge(self, first, second):
        tail = FIELDS * self.own_cells
        self.near[tail : tail + EXTRA, 0:LANES] = first
        self.near[tail : tail + EXTRA, LANES : 2 * LANES] = second

    def end(self):
        pack_far(self.far, self.near, self.own_cells, self.spare)


class ToBuffer:
    def __init__(self, buffer):
        self.buffer = buffer

    def fields(self, columns, four, fifth):
        split = four.shape[0]
        self.buffer[0:split, columns] = four
        self.buffer[split:, columns] = fifth[0 : self.buffer.shape[0] - split]

    def edge(self, first, second):
        pass

    def end(self):
        pass


def copies_out(level, buffer, outs, sent):
    density, momentum, magnetic = outs
    cells = density.shape[1]
    targets = [density.at[level]] + [x.at[k, level] for x in (momentum, magnetic) for k in range(2)]
    return [
        pltpu.make_async_copy(buffer.at[pl.ds(f * cells, cells), :], x, sent.at[level * FIELDS + f])
        for f, x in enumerate(targets)
    ]


def tall_of(n):
    return EXTRA + SLOTS * n + 2 * SUB


def step_scratch(n):
    return [
        pltpu.VMEM((FIELDS, tall_of(n), LANES), jnp.float32),
        pltpu.VMEM((STAGES, FIELDS, TALL * SUB, LANES), jnp.float32),
        pltpu.VMEM((2, tall_of(n), LANES), jnp.float32),
    ]


vmem = pl.BlockSpec(memory_space=pltpu.VMEM)
smem = pl.BlockSpec(memory_space=pltpu.SMEM)
f32 = lambda *s: jax.ShapeDtypeStruct(s, jnp.float32)
params = pltpu.CompilerParams(vmem_limit_bytes=VMEM_LIMIT)
cost = pl.CostEstimate(flops=9_000_000_000, bytes_accessed=29_000_000, transcendentals=0)


def first_step(plan, level, operands):
    n, radius, own_cells, total, spare, moved = plan

    def kernel(place, own, near, far, side, corner, spin, pick, near_out, far_out, *scratch):
        refs = (place, own, side.at[level], near, corner.at[level], far, spin, pick)
        step_kernel(plan, refs, ToMessage(near_out, far_out, own_cells, spare), scratch)

    return pl.pallas_call(
        kernel,
        out_shape=[f32(FIELDS * own_cells + EXTRA, radius), f32(FIELDS * (own_cells + SUB), LANES)],
        in_specs=[smem] + [vmem] * 7,
        out_specs=[vmem] * 2,
        scratch_shapes=step_scratch(n),
        compiler_params=params,
        cost_estimate=cost,
        name="first_step",
    )(*operands)


def last_step(plan, level, operands, done, levels):
    n, radius, own_cells, total, spare, moved = plan
    final = level == levels - 1
    tail = pl.ds(FIELDS * own_cells, EXTRA)
    buffer = f32(FIELDS * own_cells, radius)

    def kernel(place, own, near, far, spin, pick, *rest):
        refs = (place, own, own.at[tail, :], near, near.at[tail, :], far, spin, pick)
        if not final:
            step_kernel(plan, refs, ToBuffer(rest[0]), rest[1:])
            return
        ready, outs, scratch = rest[: levels - 1], rest[levels - 1 : levels + 2], rest[levels + 2 :]
        last, sent = scratch[-2:]
        copies = []
        for k, x in enumerate(ready):
            copies += copies_out(k, x, outs, sent)
        for copy in copies:
            copy.start()
        step_kernel(plan, refs, ToBuffer(last), scratch[:-2])
        rest_of = copies_out(level, last, outs, sent)
        for copy in rest_of:
            copy.start()
        for copy in copies + rest_of:
            copy.wait()

    if final:
        out_shape = [f32(levels, own_cells, radius), f32(2, levels, own_cells, radius), f32(2, levels, own_cells, radius)]
        more = [pltpu.VMEM((FIELDS * own_cells, radius), jnp.float32), pltpu.SemaphoreType.DMA((levels * FIELDS,))]
    else:
        out_shape = buffer
        more = []
    return pl.pallas_call(
        kernel,
        out_shape=out_shape,
        in_specs=[smem] + [vmem] * (5 + len(done)),
        out_specs=[pl.BlockSpec(memory_space=pltpu.HBM)] * 3 if final else vmem,
        scratch_shapes=step_scratch(n) + more,
        compiler_params=params,
        cost_estimate=cost,
        name="last_step",
    )(*operands, *done)


def body(density, momentum, magnetic, rotation, shifts):
    phi_count = lax.axis_size("phi")
    row_count = lax.axis_size("row")
    levels, own_cells, radius = density.shape
    total = radius * row_count
    parts = radius // LANES
    n = radius // SLOTS
    need = [max(shift_bound(part * LANES, total) + REACH - own_cells, 0) for part in range(parts)]
    spare = own_cells - need[0]
    assert row_count == 2 and radius == 2 * LANES and own_cells == HALF // 2
    assert 0 < need[0] < own_cells and need[1] <= SUB + spare and spare <= SUB

    row = lax.axis_index("row")
    place = jnp.reshape(row, (1,)).astype(jnp.int32)
    send_near = lambda x: lax.ppermute(x, "phi", [(p, (p + 1) % phi_count) for p in range(phi_count)])
    send_far = lambda x: lax.ppermute(x, "phi", [(p, (p + 2) % phi_count) for p in range(phi_count)])
    here = lambda p, r: (p % phi_count) * row_count + r
    diagonal = [(here(p, r), here(p + 1, 1 - r)) for p in range(phi_count) for r in range(row_count)]
    send_corner = lambda x: lax.ppermute(x, ("phi", "row"), diagonal)
    send_side = lambda x: lax.ppermute(x, "row", [(0, 1), (1, 0)])

    spins, turns = rotation.reshape(parts, LANES), shifts.reshape(parts, LANES)
    near_message = f32(FIELDS * own_cells, radius)
    far_message = f32(FIELDS * (own_cells + SUB), LANES)
    edge = pl.pallas_call(
        edge_kernel,
        out_shape=f32(levels, EXTRA, 2 * LANES),
        in_specs=[smem] + [pl.BlockSpec(memory_space=pltpu.HBM)] * 5,
        out_specs=vmem,
        scratch_shapes=[
            pltpu.VMEM((levels, FIELDS * own_cells, LANES), jnp.float32),
            pltpu.VMEM((parts, LANES), jnp.float32),
            pltpu.VMEM((parts, LANES), jnp.int32),
            pltpu.SemaphoreType.DMA((levels * FIELDS + 2,)),
        ],
        compiler_params=pltpu.CompilerParams(vmem_limit_bytes=EDGE_LIMIT),
        name="edges",
    )(place, density, momentum, magnetic, spins, turns)
    packed = pl.pallas_call(
        lambda *refs: pack_kernel(spare, levels, *refs),
        out_shape=[near_message] * levels + [far_message] * levels,
        in_specs=[vmem] * 3 + [pl.BlockSpec(memory_space=pl.ANY)],
        out_specs=[vmem] * (2 * levels),
        compiler_params=params,
        cost_estimate=cost,
        name="pack",
    )(density, momentum, magnetic, edge)
    owns, fars = packed[:levels], packed[levels:]
    side = send_side(edge)
    corner = send_corner(edge)
    wide = (n + 1, radius, own_cells, total, spare, EXTRA)
    plain = (n, radius, own_cells, total, spare, 0)
    i32 = jax.ShapeDtypeStruct((TALL * SUB, LANES), jnp.int32)
    tables = pl.pallas_call(
        lambda *refs: table_kernel((wide, plain), *refs),
        out_shape=[f32(TALL * SUB, LANES), i32] * 2,
        in_specs=[smem] + [vmem] * 3,
        out_specs=[vmem] * 4,
        scratch_shapes=[pltpu.VMEM((2, tall_of(n + 1), LANES), jnp.float32)],
        compiler_params=params,
        name="tables",
    )(place, side, spins, turns)
    moved = []
    for own, far in zip(owns, fars):
        if moved:
            own, far, _ = lax.optimization_barrier((own, far, tables[0]))
        moved.append((send_near(own), send_far(far)))
    states = []
    for level in range(levels):
        near, far = moved[level]
        states.append(first_step(wide, level, (place, owns[level], near, far, side, corner, *tables[:2])))
    moved = [(send_near(own), send_far(far)) for own, far in states]
    done = ()
    for level in range(levels):
        near, far = moved[level]
        operands = (place, states[level][0], near, far, *tables[2:])
        result = last_step(plain, level, operands, done if level == levels - 1 else (), levels)
        done += (result,)
    return tuple(result)


def solution(mesh):
    placed = (
        P(None, "phi", "row"),
        P(None, None, "phi", "row"),
        P(None, None, "phi", "row"),
        P("row"),
        P("row"),
    )
    return jax.shard_map(
        body,
        mesh=mesh,
        in_specs=placed,
        out_specs=(P(None, "phi", "row"), P(None, None, "phi", "row"), P(None, None, "phi", "row")),
        check_vma=False,
    )
```

```python
import jax
import jax.numpy as jnp
from jax import lax
from jax.experimental import pallas as pl
from jax.experimental.pallas import tpu as pltpu
from jax.sharding import PartitionSpec as P

STEPS = 2
SMIN = 8
SMAX = 56
STAGES = 3
REACH = 2 * STAGES
FIELDS = 5
LANES = 128
SUB = 8
HALF = LANES // 2
SLOTS = 2 * SUB
EXTRA = 2 * SUB
DEALT = 32
TALL = 40
VMEM_LIMIT = 32 * 1024 * 1024
EDGE_LIMIT = 60 * 1024 * 1024

time_step = 0.08


def shift_bound(first_row, rows):
    d = rows - 1 - first_row
    return min(SMIN + (SMAX - SMIN - 1) * d * d // ((rows - 1) * (rows - 1)) + 1, SMAX)


def minmod(lower, upper):
    return jnp.maximum(jnp.minimum(lower, 0.0), jnp.minimum(upper, jnp.maximum(lower, 0.0)))


def physical(state):
    rho, mn, mt, bn, bt = state
    inverse = pltpu.reciprocal(rho, approx=True)
    bn_sq = bn * bn
    bt_sq = bt * bt
    vn = mn * inverse
    vt = mt * inverse
    inside = (bn_sq + bt_sq) * inverse + 1.0
    root = lax.rsqrt(inside)
    ram = mn * vn + rho
    tension = bt_sq - bn_sq
    flux_t = mt * vn - bn * bt
    flux_b = bt * vn - bn * vt
    speed = jnp.abs(vn) + inside * root
    return ram, tension, flux_t, flux_b, speed


def face_twice(left, right, of_left, of_right):
    left_ram, left_tension, left_t, left_b, left_speed = of_left
    right_ram, right_tension, right_t, right_b, right_speed = of_right
    bound = jnp.maximum(left_speed, right_speed)
    jumps = [bound * (l - r) for l, r in zip(left, right)]
    return [
        (left[1] + right[1]) + jumps[0],
        ((left_ram + right_ram) + 0.5 * (left_tension + right_tension)) + jumps[1],
        (left_t + right_t) + jumps[2],
        jumps[3],
        (left_b + right_b) + jumps[4],
    ]


def swapped(five):
    return [five[0], five[2], five[1], five[4], five[3]]


def tile(i):
    return pl.ds(pl.multiple_of(i * SUB, SUB), SUB)


def rows_a_turn(n):
    return (n + 2 * REACH - 4 + 1) // 2


def run_stages(n, stages, spin, edges):
    each = rows_a_turn(n)
    half_dt = 0.5 * time_step
    low_mask, high_mask = edges
    first, last = REACH, REACH + n - 1

    right_of = lambda x: pltpu.roll(x, LANES - 1, 1)
    left_of = lambda x: pltpu.roll(x, 1, 1)

    def radial_states(halves, centres):
        jumps = [h[SUB:] - h[:-SUB] for h in halves]
        slopes = [minmod(d[:-SUB], d[SUB:]) for d in jumps]
        lower = [x - g for x, g in zip(centres, slopes)]
        upper = [x + g for x, g in zip(centres, slopes)]
        return swapped([x[:-SUB] for x in upper]), swapped([x[SUB:] for x in lower])

    def work(stage, i0, before):
        src, dst = stage, (stage & 1) + 1
        weight = jnp.where(stage == 0, 1.0, jnp.where(stage == 1, 0.25, 2.0 / 3.0))
        keep = jnp.where(stage == 0, 0.0, jnp.where(stage == 1, 0.75, 1.0 / 3.0))
        some = lambda first, count: pl.ds(pl.multiple_of((i0 + first) * SUB, SUB), count * SUB)
        here = some(0, each)
        size = each * SUB
        rows = [stages[src, f, some(-1, each + 3), :] for f in range(FIELDS)]
        halves = [0.5 * x for x in rows]
        own = [x[SUB : SUB + size] for x in rows]
        half = [x[SUB : SUB + size] for x in halves]
        after = [right_of(x) for x in half]
        left, right = radial_states(halves, [x[SUB:-SUB] for x in rows])
        jump = [x - y for x, y in zip(after, half)]
        behind = [left_of(x) for x in jump]
        of_left = physical(left)
        of_right = physical(right)
        slopes = [minmod(x, y) for x, y in zip(behind, jump)]
        lower = [right_of(x - y) for x, y in zip(own, slopes)]
        upper = [x + y for x, y in zip(own, slopes)]
        of_upper = physical(upper)
        faces = swapped(face_twice(left, right, of_left, of_right))
        of_lower = physical(lower)
        azimuth = face_twice(upper, lower, of_upper, of_lower)
        shifted = [left_of(x) for x in azimuth]
        change = [x - jnp.concatenate([y, x[:-SUB]], axis=0) for x, y in zip(faces, before)]
        turn = spin[here, :]
        source = [None, (-0.5 * turn) * own[2], (2.0 * turn) * own[1], (-1.5 * turn) * own[4], None]
        partial = [x if y is None else x + y for x, y in zip(own, source)]
        starts = [keep * stages[0, f, here, :] for f in range(FIELDS)]
        for f in range(FIELDS):
            new = partial[f] - half_dt * ((azimuth[f] - shifted[f]) + change[f])
            stages[dst, f, here, :] = weight * new + starts[f]
        return [x[-SUB:] for x in faces]

    def run(stage, _):
        for f in range(FIELDS):
            inner = stages[stage, f, tile(first), :]
            outer = stages[stage, f, tile(last), :]
            for k in (1, 2):
                stages[stage, f, tile(first - k), :] = jnp.where(low_mask, inner, stages[stage, f, tile(first - k), :])
                stages[stage, f, tile(last + k), :] = jnp.where(high_mask, outer, stages[stage, f, tile(last + k), :])
        count = n + 2 * REACH - 4 - 4 * stage
        if n % 2 == 0:
            lo = 2 * stage + 2
            rows = [stages[stage, f, pl.ds(pl.multiple_of((lo - 2) * SUB, SUB), 4 * SUB), :] for f in range(FIELDS)]
            left, right = radial_states([0.5 * x for x in rows], [x[SUB:-SUB] for x in rows])
            before = tuple(swapped(face_twice(left, right, physical(left), physical(right))))
        else:
            lo = 2 * stage + 1
            count = count + 1
            before = (jnp.zeros((SUB, LANES), jnp.float32),) * FIELDS
        turns = lax.div(count + each - 1, each)
        lax.fori_loop(0, turns, lambda c, carried: tuple(work(stage, lo + c * each, list(carried))), before)
        return 0

    lax.fori_loop(0, STAGES, run, 0)


def spread(block, first, width):
    block = pltpu.roll(block, (LANES - first) % LANES, 1)
    lane = lax.broadcasted_iota(jnp.int32, block.shape, 1)
    while width < LANES:
        block = jnp.where(lane < width, block, pltpu.roll(block, width, 1))
        width *= 2
    return block


def pack_far(far, near, own_cells, spare):
    sublane = lax.broadcasted_iota(jnp.int32, (SUB, LANES), 0)

    def one(f, _):
        start = pl.multiple_of(f * own_cells, SUB)
        base = pl.multiple_of(f * (own_cells + SUB), SUB)
        low = near[pl.ds(start, own_cells), 0:LANES]
        high = near[pl.ds(start + own_cells - 2 * SUB, 2 * SUB), LANES : 2 * LANES]
        moved = pltpu.roll(high[0:SUB], spare, 0)
        far[pl.ds(base, SUB), :] = jnp.where(sublane < spare, moved, low[0:SUB])
        far[pl.ds(base + SUB, own_cells - SUB), :] = low[SUB:]
        far[pl.ds(base + own_cells, SUB), :] = high[SUB:]
        return 0

    lax.fori_loop(0, FIELDS, one, 0)


def edge_kernel(place, density, momentum, magnetic, rotation, shifts, edge, ends, spin_in, shift_in, arrived):
    levels, own_cells, radius = density.shape
    on_low = place[0] == 0
    parts = radius // LANES
    split = 4 * own_cells
    columns = pl.ds(pl.multiple_of(jnp.where(on_low, radius - LANES, 0), LANES), LANES)
    copies = [
        pltpu.make_async_copy(rotation, spin_in, arrived.at[levels * FIELDS]),
        pltpu.make_async_copy(shifts, shift_in, arrived.at[levels * FIELDS + 1]),
    ]
    for level in range(levels):
        sources = [density.at[level, :, columns]] + [x.at[k, level, :, columns] for x in (momentum, magnetic) for k in range(2)]
        for f, x in enumerate(sources):
            at = ends.at[level, pl.ds(f * own_cells, own_cells), :]
            copies.append(pltpu.make_async_copy(x, at, arrived.at[level * FIELDS + f]))
    for copy in copies:
        copy.start()
    for copy in copies:
        copy.wait()
    wide = lambda ref: jnp.broadcast_to(
        jnp.where(on_low, ref[parts - 1 : parts, :], ref[0:1, :]).astype(jnp.float32), (own_cells, LANES)
    )
    turn = wide(spin_in) * time_step
    shift = wide(shift_in)
    zero = jnp.zeros((own_cells, LANES), jnp.float32)
    for level in range(levels):
        last = jnp.concatenate([ends[level, split:, :], turn, shift, zero], axis=0)
        for side, group in enumerate((ends[level, 0:split, :], last)):
            turned = group.T
            edge[level, :, side * LANES : (side + 1) * LANES] = jnp.where(on_low, turned[LANES - EXTRA :], turned[0:EXTRA])


def pack_kernel(spare, levels, density, momentum, magnetic, edge, *outs):
    del edge
    nears, fars = outs[:levels], outs[levels:]
    own_cells = density.shape[1]
    for level in range(levels):
        sources = [density.at[level]] + [x.at[k, level] for x in (momentum, magnetic) for k in range(2)]
        for f, x in enumerate(sources):
            nears[level][f * own_cells : (f + 1) * own_cells, :] = x[...]
        pack_far(fars[level], nears[level], own_cells, spare)


class Blocks:
    def __init__(self, row, n, radius, total, moved):
        self.on_low = row == 0
        self.n = n
        self.own_at = pl.multiple_of(jnp.where(self.on_low, EXTRA, EXTRA + moved), SUB)
        self.edge_at = pl.multiple_of(jnp.where(self.on_low, EXTRA + radius, moved), SUB)
        bounds = [[shift_bound(r * radius - (moved if r else 0) + n * k, total) for k in range(SLOTS)] for r in range(2)]
        self.bounds = [jnp.where(self.on_low, a, b) for a, b in zip(*bounds)]

    def rows_of(self, k):
        start = EXTRA - REACH + self.n * k
        return slice(start, start + DEALT)


def table_kernel(plans, place, side, rotation, shifts, *rest):
    outs, held = rest[:-1], rest[-1]
    lane = lax.broadcasted_iota(jnp.int32, (SUB, LANES), 1)
    sublane = lax.broadcasted_iota(jnp.int32, (SUB, LANES), 0)
    front = lax.broadcasted_iota(jnp.int32, (DEALT, LANES), 1) < HALF
    more = side[0, :, LANES : 2 * LANES]
    for which, (n, radius, own_cells, total, spare, moved) in enumerate(plans):
        spin, pick = outs[2 * which : 2 * which + 2]
        blocks = Blocks(place[0], n, radius, total, moved)
        for part in range(radius // LANES):
            rows = pl.ds(blocks.own_at + part * LANES, LANES)
            along = lambda ref: jnp.broadcast_to(ref[part : part + 1, :].astype(jnp.float32), (LANES, LANES)).T
            held[0, rows, :] = along(rotation) * time_step
            held[1, rows, :] = along(shifts)
        held[0, pl.ds(blocks.edge_at, EXTRA), :] = spread(more, own_cells, own_cells)
        held[1, pl.ds(blocks.edge_at, EXTRA), :] = spread(more, 2 * own_cells, own_cells)
        bound = jnp.zeros((SUB, LANES), jnp.int32)
        for j in range(SUB):
            low, high = blocks.rows_of(j), blocks.rows_of(SUB + j)
            spin[pl.ds(j, DEALT, stride=SUB), :] = jnp.where(front, held[0, low, :], held[0, high, :])
            pick[pl.ds(j, DEALT, stride=SUB), :] = jnp.where(front, held[1, low, :], held[1, high, :]).astype(jnp.int32)
            bound = jnp.where(sublane == j, jnp.where(lane < HALF, blocks.bounds[j], blocks.bounds[SUB + j]), bound)

        def one(i, _):
            pick[tile(i), :] = (lane + (REACH + bound)) - pick[tile(i), :]
            return 0

        lax.fori_loop(0, TALL, one, 0)


def step_kernel(plan, refs, write, scratch):
    n, radius, own_cells, total, spare, moved = plan
    place, own, own_edge, near, near_edge, far, spin, pick = refs
    cells, stages, packed = scratch
    row = place[0]
    lane = lax.broadcasted_iota(jnp.int32, (SUB, LANES), 1)
    sublane = lax.broadcasted_iota(jnp.int32, (SUB, LANES), 0)
    blocks = Blocks(row, n, radius, total, moved)

    edge_lane = lax.broadcasted_iota(jnp.int32, (EXTRA, LANES), 1)
    parts = radius // LANES

    def gather(f, _):
        rows = pl.ds(pl.multiple_of(f * own_cells, SUB), own_cells)
        start = pl.multiple_of(f * (own_cells + SUB), SUB)
        for part in range(parts):
            columns = slice(part * LANES, (part + 1) * LANES)
            if part == 0:
                top = far[pl.ds(start, own_cells), :]
            else:
                top = jnp.concatenate(
                    [
                        jnp.zeros((own_cells - 2 * SUB, LANES), jnp.float32),
                        pltpu.roll(far[pl.ds(start, SUB), :], SUB - spare, 0),
                        far[pl.ds(start + own_cells, SUB), :],
                    ],
                    axis=0,
                )
            fill = jnp.zeros((own_cells, LANES), jnp.float32)
            block = jnp.concatenate([top, near[rows, columns], own[rows, columns], fill], axis=0)
            cells[f, pl.ds(blocks.own_at + part * LANES, LANES), :] = block.T
        columns = pl.ds(pl.multiple_of(lax.div(f, 4) * LANES, LANES), LANES)
        lanes_at = lax.rem(f, 4) * own_cells
        cells[f, pl.ds(blocks.edge_at, EXTRA), :] = jnp.where(
            edge_lane < 2 * own_cells,
            pltpu.roll(near_edge[:, columns], lax.rem(LANES + own_cells - lanes_at, LANES), 1),
            pltpu.roll(own_edge[:, columns], lax.rem(LANES + 2 * own_cells - lanes_at, LANES), 1),
        )
        return 0

    lax.fori_loop(0, FIELDS, gather, 0)

    front = lax.broadcasted_iota(jnp.int32, (DEALT, LANES), 1) < HALF

    def deal(f, _):
        for j in range(SUB):
            low, high = j, SUB + j
            turn_low = (LANES - (2 * own_cells - REACH)) + blocks.bounds[low]
            turn_high = (HALF - (2 * own_cells - REACH)) + blocks.bounds[high]
            stages[0, f, pl.ds(j, DEALT, stride=SUB), :] = jnp.where(
                front,
                pltpu.roll(cells[f, blocks.rows_of(low), :], turn_low, 1),
                pltpu.roll(cells[f, blocks.rows_of(high), :], turn_high, 1),
            )
        return 0

    lax.fori_loop(0, FIELDS, deal, 0)

    edges = (
        (sublane == 0) & (lane < HALF) & (row == 0),
        (sublane == SUB - 1) & (lane >= HALF) & (row == total // radius - 1),
    )
    run_stages(n, stages, spin, edges)

    even = (lane & own_cells) == 0

    picked = (n + 1) // 2

    def shift(turn, _):
        for k in range(picked):
            i = turn * picked + k
            rows = tile(REACH + i)
            source = pick[rows, :]
            picks = [source & (LANES - 1), (source - own_cells) & (LANES - 1)]
            turned = [
                jnp.take_along_axis(stages[1, f, rows, :], picks[f % 2], axis=1, mode="promise_in_bounds")
                for f in range(FIELDS)
            ]
            stages[2, 0, tile(i), :] = jnp.where(even, turned[0], turned[1])
            stages[2, 1, tile(i), :] = jnp.where(even, turned[2], turned[3])
            stages[2, 2, tile(i), :] = turned[4]
        return 0

    lax.fori_loop(0, (n + picked - 1) // picked, shift, 0)
    narrow = lax.broadcasted_iota(jnp.int32, (n, LANES), 1) < HALF
    for j in range(SUB):
        one, two, three = [stages[2, g, pl.ds(j, n, stride=SUB), :] for g in range(3)]
        low = slice(EXTRA + n * j, EXTRA + n * (j + 1))
        high = slice(EXTRA + n * (SUB + j), EXTRA + n * (SUB + j + 1))
        packed[0, low, :] = jnp.where(narrow, one, pltpu.roll(two, HALF, 1))
        packed[0, high, :] = jnp.where(narrow, pltpu.roll(one, HALF, 1), two)
        packed[1, low, :] = three
        packed[1, high, :] = pltpu.roll(three, HALF, 1)
    for part in range(parts):
        rows = pl.ds(blocks.own_at + part * LANES, LANES)
        write.fields(slice(part * LANES, (part + 1) * LANES), packed[0, rows, :].T, packed[1, rows, :].T)
    write.edge(packed[0, pl.ds(blocks.edge_at, EXTRA), :], packed[1, pl.ds(blocks.edge_at, EXTRA), :])
    write.end()


class ToMessage:
    def __init__(self, near, far, own_cells, spare):
        self.near, self.far, self.own_cells, self.spare = near, far, own_cells, spare

    def fields(self, columns, four, fifth):
        split = 4 * self.own_cells
        self.near[0:split, columns] = four
        self.near[split : split + self.own_cells, columns] = fifth[0 : self.own_cells]

    def edge(self, first, second):
        tail = FIELDS * self.own_cells
        self.near[tail : tail + EXTRA, 0:LANES] = first
        self.near[tail : tail + EXTRA, LANES : 2 * LANES] = second

    def end(self):
        pack_far(self.far, self.near, self.own_cells, self.spare)


class ToBuffer:
    def __init__(self, buffer):
        self.buffer = buffer

    def fields(self, columns, four, fifth):
        split = four.shape[0]
        self.buffer[0:split, columns] = four
        self.buffer[split:, columns] = fifth[0 : self.buffer.shape[0] - split]

    def edge(self, first, second):
        pass

    def end(self):
        pass


def copies_out(level, buffer, outs, sent):
    density, momentum, magnetic = outs
    cells = density.shape[1]
    targets = [density.at[level]] + [x.at[k, level] for x in (momentum, magnetic) for k in range(2)]
    return [
        pltpu.make_async_copy(buffer.at[pl.ds(f * cells, cells), :], x, sent.at[level * FIELDS + f])
        for f, x in enumerate(targets)
    ]


def tall_of(n):
    return EXTRA + SLOTS * n + 2 * SUB


def step_scratch(n):
    return [
        pltpu.VMEM((FIELDS, tall_of(n), LANES), jnp.float32),
        pltpu.VMEM((STAGES, FIELDS, TALL * SUB, LANES), jnp.float32),
        pltpu.VMEM((2, tall_of(n), LANES), jnp.float32),
    ]


vmem = pl.BlockSpec(memory_space=pltpu.VMEM)
smem = pl.BlockSpec(memory_space=pltpu.SMEM)
f32 = lambda *s: jax.ShapeDtypeStruct(s, jnp.float32)
params = pltpu.CompilerParams(vmem_limit_bytes=VMEM_LIMIT)
cost = pl.CostEstimate(flops=9_000_000_000, bytes_accessed=29_000_000, transcendentals=0)


def first_step(plan, level, operands):
    n, radius, own_cells, total, spare, moved = plan

    def kernel(place, own, near, far, side, corner, spin, pick, near_out, far_out, *scratch):
        refs = (place, own, side.at[level], near, corner.at[level], far, spin, pick)
        step_kernel(plan, refs, ToMessage(near_out, far_out, own_cells, spare), scratch)

    return pl.pallas_call(
        kernel,
        out_shape=[f32(FIELDS * own_cells + EXTRA, radius), f32(FIELDS * (own_cells + SUB), LANES)],
        in_specs=[smem] + [vmem] * 7,
        out_specs=[vmem] * 2,
        scratch_shapes=step_scratch(n),
        compiler_params=params,
        cost_estimate=cost,
        name="first_step",
    )(*operands)


def last_step(plan, level, operands, done, levels):
    n, radius, own_cells, total, spare, moved = plan
    final = level == levels - 1
    tail = pl.ds(FIELDS * own_cells, EXTRA)
    buffer = f32(FIELDS * own_cells, radius)

    def kernel(place, own, near, far, spin, pick, *rest):
        refs = (place, own, own.at[tail, :], near, near.at[tail, :], far, spin, pick)
        if not final:
            step_kernel(plan, refs, ToBuffer(rest[0]), rest[1:])
            return
        ready, outs, scratch = rest[: levels - 1], rest[levels - 1 : levels + 2], rest[levels + 2 :]
        last, sent = scratch[-2:]
        copies = []
        for k, x in enumerate(ready):
            copies += copies_out(k, x, outs, sent)
        for copy in copies:
            copy.start()
        step_kernel(plan, refs, ToBuffer(last), scratch[:-2])
        rest_of = copies_out(level, last, outs, sent)
        for copy in rest_of:
            copy.start()
        for copy in copies + rest_of:
            copy.wait()

    if final:
        out_shape = [f32(levels, own_cells, radius), f32(2, levels, own_cells, radius), f32(2, levels, own_cells, radius)]
        more = [pltpu.VMEM((FIELDS * own_cells, radius), jnp.float32), pltpu.SemaphoreType.DMA((levels * FIELDS,))]
    else:
        out_shape = buffer
        more = []
    return pl.pallas_call(
        kernel,
        out_shape=out_shape,
        in_specs=[smem] + [vmem] * (5 + len(done)),
        out_specs=[pl.BlockSpec(memory_space=pltpu.HBM)] * 3 if final else vmem,
        scratch_shapes=step_scratch(n) + more,
        compiler_params=params,
        cost_estimate=cost,
        name="last_step",
    )(*operands, *done)


def body(density, momentum, magnetic, rotation, shifts):
    phi_count = lax.axis_size("phi")
    row_count = lax.axis_size("row")
    levels, own_cells, radius = density.shape
    total = radius * row_count
    parts = radius // LANES
    n = radius // SLOTS
    need = [max(shift_bound(part * LANES, total) + REACH - own_cells, 0) for part in range(parts)]
    spare = own_cells - need[0]
    assert row_count == 2 and radius == 2 * LANES and own_cells == HALF // 2
    assert 0 < need[0] < own_cells and need[1] <= SUB + spare and spare <= SUB

    row = lax.axis_index("row")
    place = jnp.reshape(row, (1,)).astype(jnp.int32)
    send_near = lambda x: lax.ppermute(x, "phi", [(p, (p + 1) % phi_count) for p in range(phi_count)])
    send_far = lambda x: lax.ppermute(x, "phi", [(p, (p + 2) % phi_count) for p in range(phi_count)])
    here = lambda p, r: (p % phi_count) * row_count + r
    diagonal = [(here(p, r), here(p + 1, 1 - r)) for p in range(phi_count) for r in range(row_count)]
    send_corner = lambda x: lax.ppermute(x, ("phi", "row"), diagonal)
    send_side = lambda x: lax.ppermute(x, "row", [(0, 1), (1, 0)])

    spins, turns = rotation.reshape(parts, LANES), shifts.reshape(parts, LANES)
    near_message = f32(FIELDS * own_cells, radius)
    far_message = f32(FIELDS * (own_cells + SUB), LANES)
    edge = pl.pallas_call(
        edge_kernel,
        out_shape=f32(levels, EXTRA, 2 * LANES),
        in_specs=[smem] + [pl.BlockSpec(memory_space=pltpu.HBM)] * 5,
        out_specs=vmem,
        scratch_shapes=[
            pltpu.VMEM((levels, FIELDS * own_cells, LANES), jnp.float32),
            pltpu.VMEM((parts, LANES), jnp.float32),
            pltpu.VMEM((parts, LANES), jnp.int32),
            pltpu.SemaphoreType.DMA((levels * FIELDS + 2,)),
        ],
        compiler_params=pltpu.CompilerParams(vmem_limit_bytes=EDGE_LIMIT),
        name="edges",
    )(place, density, momentum, magnetic, spins, turns)
    packed = pl.pallas_call(
        lambda *refs: pack_kernel(spare, levels, *refs),
        out_shape=[near_message] * levels + [far_message] * levels,
        in_specs=[vmem] * 3 + [pl.BlockSpec(memory_space=pl.ANY)],
        out_specs=[vmem] * (2 * levels),
        compiler_params=params,
        cost_estimate=cost,
        name="pack",
    )(density, momentum, magnetic, edge)
    owns, fars = packed[:levels], packed[levels:]
    side = send_side(edge)
    corner = send_corner(edge)
    wide = (n + 1, radius, own_cells, total, spare, EXTRA)
    plain = (n, radius, own_cells, total, spare, 0)
    i32 = jax.ShapeDtypeStruct((TALL * SUB, LANES), jnp.int32)
    tables = pl.pallas_call(
        lambda *refs: table_kernel((wide, plain), *refs),
        out_shape=[f32(TALL * SUB, LANES), i32] * 2,
        in_specs=[smem] + [vmem] * 3,
        out_specs=[vmem] * 4,
        scratch_shapes=[pltpu.VMEM((2, tall_of(n + 1), LANES), jnp.float32)],
        compiler_params=params,
        name="tables",
    )(place, side, spins, turns)
    moved = []
    for own, far in zip(owns, fars):
        if moved:
            own, far, _ = lax.optimization_barrier((own, far, tables[0]))
        moved.append((send_near(own), send_far(far)))
    states = []
    for level in range(levels):
        near, far = moved[level]
        states.append(first_step(wide, level, (place, owns[level], near, far, side, corner, *tables[:2])))
    moved = [(send_near(own), send_far(far)) for own, far in states]
    done = ()
    for level in range(levels):
        near, far = moved[level]
        operands = (place, states[level][0], near, far, *tables[2:])
        result = last_step(plain, level, operands, done if level == levels - 1 else (), levels)
        done += (result,)
    return tuple(result)


def solution(mesh):
    placed = (
        P(None, "phi", "row"),
        P(None, None, "phi", "row"),
        P(None, None, "phi", "row"),
        P("row"),
        P("row"),
    )
    return jax.shard_map(
        body,
        mesh=mesh,
        in_specs=placed,
        out_specs=(P(None, "phi", "row"), P(None, None, "phi", "row"), P(None, None, "phi", "row")),
        check_vma=False,
    )
```

```python
import jax
import jax.numpy as jnp
from jax import lax
from jax.experimental import pallas as pl
from jax.experimental.pallas import tpu as pltpu
from jax.sharding import PartitionSpec as P

STEPS = 2
SMIN = 8
SMAX = 56
STAGES = 3
REACH = 2 * STAGES
FIELDS = 5
LANES = 128
SUB = 8
HALF = LANES // 2
SLOTS = 2 * SUB
EXTRA = 2 * SUB
DEALT = 32
TALL = 40
VMEM_LIMIT = 32 * 1024 * 1024
EDGE_LIMIT = 60 * 1024 * 1024

time_step = 0.08


def shift_bound(first_row, rows):
    d = rows - 1 - first_row
    return min(SMIN + (SMAX - SMIN - 1) * d * d // ((rows - 1) * (rows - 1)) + 1, SMAX)


def minmod(lower, upper):
    return jnp.maximum(jnp.minimum(lower, 0.0), jnp.minimum(upper, jnp.maximum(lower, 0.0)))


def physical(state):
    rho, mn, mt, bn, bt = state
    inverse = pltpu.reciprocal(rho, approx=True)
    bn_sq = bn * bn
    bt_sq = bt * bt
    vn = mn * inverse
    vt = mt * inverse
    inside = (bn_sq + bt_sq) * inverse + 1.0
    root = lax.rsqrt(inside)
    ram = mn * vn + rho
    tension = bt_sq - bn_sq
    flux_t = mt * vn - bn * bt
    flux_b = bt * vn - bn * vt
    speed = jnp.abs(vn) + inside * root
    return ram, tension, flux_t, flux_b, speed


def face_twice(left, right, of_left, of_right):
    left_ram, left_tension, left_t, left_b, left_speed = of_left
    right_ram, right_tension, right_t, right_b, right_speed = of_right
    bound = jnp.maximum(left_speed, right_speed)
    jumps = [bound * (l - r) for l, r in zip(left, right)]
    return [
        (left[1] + right[1]) + jumps[0],
        ((left_ram + right_ram) + 0.5 * (left_tension + right_tension)) + jumps[1],
        (left_t + right_t) + jumps[2],
        jumps[3],
        (left_b + right_b) + jumps[4],
    ]


def swapped(five):
    return [five[0], five[2], five[1], five[4], five[3]]


def tile(i):
    return pl.ds(pl.multiple_of(i * SUB, SUB), SUB)


def rows_a_turn(n):
    return (n + 2 * REACH - 4 + 1) // 2


def run_stages(n, stages, spin, edges):
    each = rows_a_turn(n)
    half_dt = 0.5 * time_step
    low_mask, high_mask = edges
    first, last = REACH, REACH + n - 1

    right_of = lambda x: pltpu.roll(x, LANES - 1, 1)
    left_of = lambda x: pltpu.roll(x, 1, 1)

    def radial_states(halves, centres):
        jumps = [h[SUB:] - h[:-SUB] for h in halves]
        slopes = [minmod(d[:-SUB], d[SUB:]) for d in jumps]
        lower = [x - g for x, g in zip(centres, slopes)]
        upper = [x + g for x, g in zip(centres, slopes)]
        return swapped([x[:-SUB] for x in upper]), swapped([x[SUB:] for x in lower])

    def work(stage, i0, before):
        src, dst = stage, (stage & 1) + 1
        weight = jnp.where(stage == 0, 1.0, jnp.where(stage == 1, 0.25, 2.0 / 3.0))
        keep = jnp.where(stage == 0, 0.0, jnp.where(stage == 1, 0.75, 1.0 / 3.0))
        some = lambda first, count: pl.ds(pl.multiple_of((i0 + first) * SUB, SUB), count * SUB)
        here = some(0, each)
        size = each * SUB
        rows = [stages[src, f, some(-1, each + 3), :] for f in range(FIELDS)]
        halves = [0.5 * x for x in rows]
        own = [x[SUB : SUB + size] for x in rows]
        half = [x[SUB : SUB + size] for x in halves]
        after = [right_of(x) for x in half]
        left, right = radial_states(halves, [x[SUB:-SUB] for x in rows])
        jump = [x - y for x, y in zip(after, half)]
        behind = [left_of(x) for x in jump]
        of_left = physical(left)
        of_right = physical(right)
        slopes = [minmod(x, y) for x, y in zip(behind, jump)]
        lower = [right_of(x - y) for x, y in zip(own, slopes)]
        upper = [x + y for x, y in zip(own, slopes)]
        of_upper = physical(upper)
        faces = swapped(face_twice(left, right, of_left, of_right))
        of_lower = physical(lower)
        azimuth = face_twice(upper, lower, of_upper, of_lower)
        shifted = [left_of(x) for x in azimuth]
        change = [x - jnp.concatenate([y, x[:-SUB]], axis=0) for x, y in zip(faces, before)]
        turn = spin[here, :]
        source = [None, (-0.5 * turn) * own[2], (2.0 * turn) * own[1], (-1.5 * turn) * own[4], None]
        partial = [x if y is None else x + y for x, y in zip(own, source)]
        starts = [keep * stages[0, f, here, :] for f in range(FIELDS)]
        for f in range(FIELDS):
            new = partial[f] - half_dt * ((azimuth[f] - shifted[f]) + change[f])
            stages[dst, f, here, :] = weight * new + starts[f]
        return [x[-SUB:] for x in faces]

    def run(stage, _):
        for f in range(FIELDS):
            inner = stages[stage, f, tile(first), :]
            outer = stages[stage, f, tile(last), :]
            for k in (1, 2):
                stages[stage, f, tile(first - k), :] = jnp.where(low_mask, inner, stages[stage, f, tile(first - k), :])
                stages[stage, f, tile(last + k), :] = jnp.where(high_mask, outer, stages[stage, f, tile(last + k), :])
        count = n + 2 * REACH - 4 - 4 * stage
        if n % 2 == 0:
            lo = 2 * stage + 2
            rows = [stages[stage, f, pl.ds(pl.multiple_of((lo - 2) * SUB, SUB), 4 * SUB), :] for f in range(FIELDS)]
            left, right = radial_states([0.5 * x for x in rows], [x[SUB:-SUB] for x in rows])
            before = tuple(swapped(face_twice(left, right, physical(left), physical(right))))
        else:
            lo = 2 * stage + 1
            count = count + 1
            before = (jnp.zeros((SUB, LANES), jnp.float32),) * FIELDS
        turns = lax.div(count + each - 1, each)
        lax.fori_loop(0, turns, lambda c, carried: tuple(work(stage, lo + c * each, list(carried))), before)
        return 0

    lax.fori_loop(0, STAGES, run, 0)


def spread(block, first, width):
    block = pltpu.roll(block, (LANES - first) % LANES, 1)
    lane = lax.broadcasted_iota(jnp.int32, block.shape, 1)
    while width < LANES:
        block = jnp.where(lane < width, block, pltpu.roll(block, width, 1))
        width *= 2
    return block


def pack_far(far, near, own_cells, spare):
    sublane = lax.broadcasted_iota(jnp.int32, (SUB, LANES), 0)

    def one(f, _):
        start = pl.multiple_of(f * own_cells, SUB)
        base = pl.multiple_of(f * (own_cells + SUB), SUB)
        low = near[pl.ds(start, own_cells), 0:LANES]
        high = near[pl.ds(start + own_cells - 2 * SUB, 2 * SUB), LANES : 2 * LANES]
        moved = pltpu.roll(high[0:SUB], spare, 0)
        far[pl.ds(base, SUB), :] = jnp.where(sublane < spare, moved, low[0:SUB])
        far[pl.ds(base + SUB, own_cells - SUB), :] = low[SUB:]
        far[pl.ds(base + own_cells, SUB), :] = high[SUB:]
        return 0

    lax.fori_loop(0, FIELDS, one, 0)


def edge_kernel(place, density, momentum, magnetic, rotation, shifts, edge, ends, spin_in, shift_in, arrived):
    levels, own_cells, radius = density.shape
    on_low = place[0] == 0
    parts = radius // LANES
    split = 4 * own_cells
    columns = pl.ds(pl.multiple_of(jnp.where(on_low, radius - LANES, 0), LANES), LANES)
    copies = [
        pltpu.make_async_copy(rotation, spin_in, arrived.at[levels * FIELDS]),
        pltpu.make_async_copy(shifts, shift_in, arrived.at[levels * FIELDS + 1]),
    ]
    for level in range(levels):
        sources = [density.at[level, :, columns]] + [x.at[k, level, :, columns] for x in (momentum, magnetic) for k in range(2)]
        for f, x in enumerate(sources):
            at = ends.at[level, pl.ds(f * own_cells, own_cells), :]
            copies.append(pltpu.make_async_copy(x, at, arrived.at[level * FIELDS + f]))
    for copy in copies:
        copy.start()
    for copy in copies:
        copy.wait()
    wide = lambda ref: jnp.broadcast_to(
        jnp.where(on_low, ref[parts - 1 : parts, :], ref[0:1, :]).astype(jnp.float32), (own_cells, LANES)
    )
    turn = wide(spin_in) * time_step
    shift = wide(shift_in)
    zero = jnp.zeros((own_cells, LANES), jnp.float32)
    for level in range(levels):
        last = jnp.concatenate([ends[level, split:, :], turn, shift, zero], axis=0)
        for side, group in enumerate((ends[level, 0:split, :], last)):
            turned = group.T
            edge[level, :, side * LANES : (side + 1) * LANES] = jnp.where(on_low, turned[LANES - EXTRA :], turned[0:EXTRA])


def pack_kernel(spare, levels, density, momentum, magnetic, edge, *outs):
    del edge
    nears, fars = outs[:levels], outs[levels:]
    own_cells = density.shape[1]
    for level in range(levels):
        sources = [density.at[level]] + [x.at[k, level] for x in (momentum, magnetic) for k in range(2)]
        for f, x in enumerate(sources):
            nears[level][f * own_cells : (f + 1) * own_cells, :] = x[...]
        pack_far(fars[level], nears[level], own_cells, spare)


class Blocks:
    def __init__(self, row, n, radius, total, moved):
        self.on_low = row == 0
        self.n = n
        self.own_at = pl.multiple_of(jnp.where(self.on_low, EXTRA, EXTRA + moved), SUB)
        self.edge_at = pl.multiple_of(jnp.where(self.on_low, EXTRA + radius, moved), SUB)
        bounds = [[shift_bound(r * radius - (moved if r else 0) + n * k, total) for k in range(SLOTS)] for r in range(2)]
        self.bounds = [jnp.where(self.on_low, a, b) for a, b in zip(*bounds)]

    def rows_of(self, k):
        start = EXTRA - REACH + self.n * k
        return slice(start, start + DEALT)


def table_kernel(plans, place, side, rotation, shifts, *rest):
    outs, held = rest[:-1], rest[-1]
    radius = plans[0][1]
    own_cells = plans[0][2]
    wide_lane = lax.broadcasted_iota(jnp.int32, (DEALT, LANES), 1)
    front = wide_lane < HALF
    more = side[0, :, LANES : 2 * LANES]
    edges = [spread(more, own_cells, own_cells), spread(more, 2 * own_cells, own_cells)]
    own = []
    for ref, scale in ((rotation, time_step), (shifts, 1.0)):
        along = lambda part: jnp.broadcast_to(ref[part : part + 1, :].astype(jnp.float32), (LANES, LANES)).T
        own.append([along(part) * scale for part in range(radius // LANES)])
    for which, (n, radius, own_cells, total, spare, moved) in enumerate(plans):
        spin, pick = outs[2 * which : 2 * which + 2]
        blocks = Blocks(place[0], n, radius, total, moved)
        for k in range(2):
            for part, x in enumerate(own[k]):
                held[2 * which + k, pl.ds(blocks.own_at + part * LANES, LANES), :] = x
            held[2 * which + k, pl.ds(blocks.edge_at, EXTRA), :] = edges[k]
        for j in range(SUB):
            low, high = blocks.rows_of(j), blocks.rows_of(SUB + j)
            turns = [jnp.where(front, held[2 * which + k, low, :], held[2 * which + k, high, :]) for k in range(2)]
            spin[pl.ds(j, DEALT, stride=SUB), :] = turns[0]
            bound = jnp.where(front, blocks.bounds[j], blocks.bounds[SUB + j])
            pick[pl.ds(j, DEALT, stride=SUB), :] = (wide_lane + (REACH + bound)) - turns[1].astype(jnp.int32)


def step_kernel(plan, refs, write, scratch):
    n, radius, own_cells, total, spare, moved = plan
    place, own, own_edge, near, near_edge, far, spin, pick = refs
    cells, stages, packed = scratch
    row = place[0]
    lane = lax.broadcasted_iota(jnp.int32, (SUB, LANES), 1)
    sublane = lax.broadcasted_iota(jnp.int32, (SUB, LANES), 0)
    blocks = Blocks(row, n, radius, total, moved)

    edge_lane = lax.broadcasted_iota(jnp.int32, (EXTRA, LANES), 1)
    parts = radius // LANES

    front = lax.broadcasted_iota(jnp.int32, (DEALT, LANES), 1) < HALF

    def bring(f, _):
        rows = pl.ds(pl.multiple_of(f * own_cells, SUB), own_cells)
        start = pl.multiple_of(f * (own_cells + SUB), SUB)
        for part in range(parts):
            columns = slice(part * LANES, (part + 1) * LANES)
            if part == 0:
                top = far[pl.ds(start, own_cells), :]
            else:
                top = jnp.concatenate(
                    [
                        jnp.zeros((own_cells - 2 * SUB, LANES), jnp.float32),
                        pltpu.roll(far[pl.ds(start, SUB), :], SUB - spare, 0),
                        far[pl.ds(start + own_cells, SUB), :],
                    ],
                    axis=0,
                )
            fill = jnp.zeros((own_cells, LANES), jnp.float32)
            block = jnp.concatenate([top, near[rows, columns], own[rows, columns], fill], axis=0)
            cells[f, pl.ds(blocks.own_at + part * LANES, LANES), :] = block.T
        columns = pl.ds(pl.multiple_of(lax.div(f, 4) * LANES, LANES), LANES)
        lanes_at = lax.rem(f, 4) * own_cells
        cells[f, pl.ds(blocks.edge_at, EXTRA), :] = jnp.where(
            edge_lane < 2 * own_cells,
            pltpu.roll(near_edge[:, columns], lax.rem(LANES + own_cells - lanes_at, LANES), 1),
            pltpu.roll(own_edge[:, columns], lax.rem(LANES + 2 * own_cells - lanes_at, LANES), 1),
        )

        for j in range(SUB):
            low, high = j, SUB + j
            turn_low = (LANES - (2 * own_cells - REACH)) + blocks.bounds[low]
            turn_high = (HALF - (2 * own_cells - REACH)) + blocks.bounds[high]
            stages[0, f, pl.ds(j, DEALT, stride=SUB), :] = jnp.where(
                front,
                pltpu.roll(cells[f, blocks.rows_of(low), :], turn_low, 1),
                pltpu.roll(cells[f, blocks.rows_of(high), :], turn_high, 1),
            )
        return 0

    lax.fori_loop(0, FIELDS, bring, 0)

    edges = (
        (sublane == 0) & (lane < HALF) & (row == 0),
        (sublane == SUB - 1) & (lane >= HALF) & (row == total // radius - 1),
    )
    run_stages(n, stages, spin, edges)

    even = (lane & own_cells) == 0

    picked = (n + 1) // 2

    def shift(turn, _):
        for k in range(picked):
            i = turn * picked + k
            rows = tile(REACH + i)
            source = pick[rows, :]
            picks = [source & (LANES - 1), (source - own_cells) & (LANES - 1)]
            turned = [
                jnp.take_along_axis(stages[1, f, rows, :], picks[f % 2], axis=1, mode="promise_in_bounds")
                for f in range(FIELDS)
            ]
            stages[2, 0, tile(i), :] = jnp.where(even, turned[0], turned[1])
            stages[2, 1, tile(i), :] = jnp.where(even, turned[2], turned[3])
            stages[2, 2, tile(i), :] = turned[4]
        return 0

    lax.fori_loop(0, (n + picked - 1) // picked, shift, 0)
    narrow = lax.broadcasted_iota(jnp.int32, (n, LANES), 1) < HALF
    for j in range(SUB):
        one, two, three = [stages[2, g, pl.ds(j, n, stride=SUB), :] for g in range(3)]
        low = slice(EXTRA + n * j, EXTRA + n * (j + 1))
        high = slice(EXTRA + n * (SUB + j), EXTRA + n * (SUB + j + 1))
        packed[0, low, :] = jnp.where(narrow, one, pltpu.roll(two, HALF, 1))
        packed[0, high, :] = jnp.where(narrow, pltpu.roll(one, HALF, 1), two)
        packed[1, low, :] = three
        packed[1, high, :] = pltpu.roll(three, HALF, 1)
    for part in range(parts):
        rows = pl.ds(blocks.own_at + part * LANES, LANES)
        write.fields(slice(part * LANES, (part + 1) * LANES), packed[0, rows, :].T, packed[1, rows, :].T)
    write.edge(packed[0, pl.ds(blocks.edge_at, EXTRA), :], packed[1, pl.ds(blocks.edge_at, EXTRA), :])
    write.end()


class ToMessage:
    def __init__(self, near, far, own_cells, spare):
        self.near, self.far, self.own_cells, self.spare = near, far, own_cells, spare

    def fields(self, columns, four, fifth):
        split = 4 * self.own_cells
        self.near[0:split, columns] = four
        self.near[split : split + self.own_cells, columns] = fifth[0 : self.own_cells]

    def edge(self, first, second):
        tail = FIELDS * self.own_cells
        self.near[tail : tail + EXTRA, 0:LANES] = first
        self.near[tail : tail + EXTRA, LANES : 2 * LANES] = second

    def end(self):
        pack_far(self.far, self.near, self.own_cells, self.spare)


class ToBuffer:
    def __init__(self, buffer):
        self.buffer = buffer

    def fields(self, columns, four, fifth):
        split = four.shape[0]
        self.buffer[0:split, columns] = four
        self.buffer[split:, columns] = fifth[0 : self.buffer.shape[0] - split]

    def edge(self, first, second):
        pass

    def end(self):
        pass


def copies_out(level, buffer, outs, sent):
    density, momentum, magnetic = outs
    cells = density.shape[1]
    targets = [density.at[level]] + [x.at[k, level] for x in (momentum, magnetic) for k in range(2)]
    return [
        pltpu.make_async_copy(buffer.at[pl.ds(f * cells, cells), :], x, sent.at[level * FIELDS + f])
        for f, x in enumerate(targets)
    ]


def tall_of(n):
    return EXTRA + SLOTS * n + 2 * SUB


def step_scratch(n):
    return [
        pltpu.VMEM((FIELDS, tall_of(n), LANES), jnp.float32),
        pltpu.VMEM((STAGES, FIELDS, TALL * SUB, LANES), jnp.float32),
        pltpu.VMEM((2, tall_of(n), LANES), jnp.float32),
    ]


vmem = pl.BlockSpec(memory_space=pltpu.VMEM)
smem = pl.BlockSpec(memory_space=pltpu.SMEM)
f32 = lambda *s: jax.ShapeDtypeStruct(s, jnp.float32)
params = pltpu.CompilerParams(vmem_limit_bytes=VMEM_LIMIT)
cost = pl.CostEstimate(flops=9_000_000_000, bytes_accessed=29_000_000, transcendentals=0)


def first_step(plan, level, operands):
    n, radius, own_cells, total, spare, moved = plan

    def kernel(place, own, near, far, side, corner, spin, pick, near_out, far_out, *scratch):
        refs = (place, own, side.at[level], near, corner.at[level], far, spin, pick)
        step_kernel(plan, refs, ToMessage(near_out, far_out, own_cells, spare), scratch)

    return pl.pallas_call(
        kernel,
        out_shape=[f32(FIELDS * own_cells + EXTRA, radius), f32(FIELDS * (own_cells + SUB), LANES)],
        in_specs=[smem] + [vmem] * 7,
        out_specs=[vmem] * 2,
        scratch_shapes=step_scratch(n),
        compiler_params=params,
        cost_estimate=cost,
        name="first_step",
    )(*operands)


def last_step(plan, level, operands, done, levels):
    n, radius, own_cells, total, spare, moved = plan
    final = level == levels - 1
    tail = pl.ds(FIELDS * own_cells, EXTRA)
    buffer = f32(FIELDS * own_cells, radius)

    def kernel(place, own, near, far, spin, pick, *rest):
        refs = (place, own, own.at[tail, :], near, near.at[tail, :], far, spin, pick)
        if not final:
            step_kernel(plan, refs, ToBuffer(rest[0]), rest[1:])
            return
        ready, outs, scratch = rest[: levels - 1], rest[levels - 1 : levels + 2], rest[levels + 2 :]
        last, sent = scratch[-2:]
        copies = []
        for k, x in enumerate(ready):
            copies += copies_out(k, x, outs, sent)
        for copy in copies:
            copy.start()
        step_kernel(plan, refs, ToBuffer(last), scratch[:-2])
        rest_of = copies_out(level, last, outs, sent)
        for copy in rest_of:
            copy.start()
        for copy in copies + rest_of:
            copy.wait()

    if final:
        out_shape = [f32(levels, own_cells, radius), f32(2, levels, own_cells, radius), f32(2, levels, own_cells, radius)]
        more = [pltpu.VMEM((FIELDS * own_cells, radius), jnp.float32), pltpu.SemaphoreType.DMA((levels * FIELDS,))]
    else:
        out_shape = buffer
        more = []
    return pl.pallas_call(
        kernel,
        out_shape=out_shape,
        in_specs=[smem] + [vmem] * (5 + len(done)),
        out_specs=[pl.BlockSpec(memory_space=pltpu.HBM)] * 3 if final else vmem,
        scratch_shapes=step_scratch(n) + more,
        compiler_params=params,
        cost_estimate=cost,
        name="last_step",
    )(*operands, *done)


def body(density, momentum, magnetic, rotation, shifts):
    phi_count = lax.axis_size("phi")
    row_count = lax.axis_size("row")
    levels, own_cells, radius = density.shape
    total = radius * row_count
    parts = radius // LANES
    n = radius // SLOTS
    need = [max(shift_bound(part * LANES, total) + REACH - own_cells, 0) for part in range(parts)]
    spare = own_cells - need[0]
    assert row_count == 2 and radius == 2 * LANES and own_cells == HALF // 2
    assert 0 < need[0] < own_cells and need[1] <= SUB + spare and spare <= SUB

    row = lax.axis_index("row")
    place = jnp.reshape(row, (1,)).astype(jnp.int32)
    send_near = lambda x: lax.ppermute(x, "phi", [(p, (p + 1) % phi_count) for p in range(phi_count)])
    send_far = lambda x: lax.ppermute(x, "phi", [(p, (p + 2) % phi_count) for p in range(phi_count)])
    here = lambda p, r: (p % phi_count) * row_count + r
    diagonal = [(here(p, r), here(p + 1, 1 - r)) for p in range(phi_count) for r in range(row_count)]
    send_corner = lambda x: lax.ppermute(x, ("phi", "row"), diagonal)
    send_side = lambda x: lax.ppermute(x, "row", [(0, 1), (1, 0)])

    spins, turns = rotation.reshape(parts, LANES), shifts.reshape(parts, LANES)
    near_message = f32(FIELDS * own_cells, radius)
    far_message = f32(FIELDS * (own_cells + SUB), LANES)
    edge = pl.pallas_call(
        edge_kernel,
        out_shape=f32(levels, EXTRA, 2 * LANES),
        in_specs=[smem] + [pl.BlockSpec(memory_space=pltpu.HBM)] * 5,
        out_specs=vmem,
        scratch_shapes=[
            pltpu.VMEM((levels, FIELDS * own_cells, LANES), jnp.float32),
            pltpu.VMEM((parts, LANES), jnp.float32),
            pltpu.VMEM((parts, LANES), jnp.int32),
            pltpu.SemaphoreType.DMA((levels * FIELDS + 2,)),
        ],
        compiler_params=pltpu.CompilerParams(vmem_limit_bytes=EDGE_LIMIT),
        name="edges",
    )(place, density, momentum, magnetic, spins, turns)
    packed = pl.pallas_call(
        lambda *refs: pack_kernel(spare, levels, *refs),
        out_shape=[near_message] * levels + [far_message] * levels,
        in_specs=[vmem] * 3 + [pl.BlockSpec(memory_space=pl.ANY)],
        out_specs=[vmem] * (2 * levels),
        compiler_params=params,
        cost_estimate=cost,
        name="pack",
    )(density, momentum, magnetic, edge)
    owns, fars = packed[:levels], packed[levels:]
    side = send_side(edge)
    corner = send_corner(edge)
    wide = (n + 1, radius, own_cells, total, spare, EXTRA)
    plain = (n, radius, own_cells, total, spare, 0)
    i32 = jax.ShapeDtypeStruct((TALL * SUB, LANES), jnp.int32)
    tables = pl.pallas_call(
        lambda *refs: table_kernel((wide, plain), *refs),
        out_shape=[f32(TALL * SUB, LANES), i32] * 2,
        in_specs=[smem] + [vmem] * 3,
        out_specs=[vmem] * 4,
        scratch_shapes=[pltpu.VMEM((4, tall_of(n + 1), LANES), jnp.float32)],
        compiler_params=params,
        name="tables",
    )(place, side, spins, turns)
    moved = []
    for own, far in zip(owns, fars):
        if moved:
            own, far, _ = lax.optimization_barrier((own, far, tables[0]))
        moved.append((send_near(own), send_far(far)))
    states = []
    for level in range(levels):
        near, far = moved[level]
        states.append(first_step(wide, level, (place, owns[level], near, far, side, corner, *tables[:2])))
    moved = [(send_near(own), send_far(far)) for own, far in states]
    done = ()
    for level in range(levels):
        near, far = moved[level]
        operands = (place, states[level][0], near, far, *tables[2:])
        result = last_step(plain, level, operands, done if level == levels - 1 else (), levels)
        done += (result,)
    return tuple(result)


def solution(mesh):
    placed = (
        P(None, "phi", "row"),
        P(None, None, "phi", "row"),
        P(None, None, "phi", "row"),
        P("row"),
        P("row"),
    )
    return jax.shard_map(
        body,
        mesh=mesh,
        in_specs=placed,
        out_specs=(P(None, "phi", "row"), P(None, None, "phi", "row"), P(None, None, "phi", "row")),
        check_vma=False,
    )
```

```python
import jax
import jax.numpy as jnp
from jax import lax
from jax.experimental import pallas as pl
from jax.experimental.pallas import tpu as pltpu
from jax.sharding import PartitionSpec as P

STEPS = 2
SMIN = 8
SMAX = 56
STAGES = 3
REACH = 2 * STAGES
FIELDS = 5
LANES = 128
SUB = 8
HALF = LANES // 2
SLOTS = 2 * SUB
EXTRA = 2 * SUB
DEALT = 32
TALL = 40
VMEM_LIMIT = 32 * 1024 * 1024
EDGE_LIMIT = 60 * 1024 * 1024

time_step = 0.08


def shift_bound(first_row, rows):
    d = rows - 1 - first_row
    return min(SMIN + (SMAX - SMIN - 1) * d * d // ((rows - 1) * (rows - 1)) + 1, SMAX)


def minmod(lower, upper):
    return jnp.maximum(jnp.minimum(lower, 0.0), jnp.minimum(upper, jnp.maximum(lower, 0.0)))


def physical(state):
    rho, mn, mt, bn, bt = state
    inverse = pltpu.reciprocal(rho, approx=True)
    bn_sq = bn * bn
    bt_sq = bt * bt
    vn = mn * inverse
    vt = mt * inverse
    inside = (bn_sq + bt_sq) * inverse + 1.0
    root = lax.rsqrt(inside)
    ram = mn * vn + rho
    tension = bt_sq - bn_sq
    flux_t = mt * vn - bn * bt
    flux_b = bt * vn - bn * vt
    speed = jnp.abs(vn) + inside * root
    return ram, tension, flux_t, flux_b, speed


def face_twice(left, right, of_left, of_right):
    left_ram, left_tension, left_t, left_b, left_speed = of_left
    right_ram, right_tension, right_t, right_b, right_speed = of_right
    bound = jnp.maximum(left_speed, right_speed)
    jumps = [bound * (l - r) for l, r in zip(left, right)]
    return [
        (left[1] + right[1]) + jumps[0],
        ((left_ram + right_ram) + 0.5 * (left_tension + right_tension)) + jumps[1],
        (left_t + right_t) + jumps[2],
        jumps[3],
        (left_b + right_b) + jumps[4],
    ]


def swapped(five):
    return [five[0], five[2], five[1], five[4], five[3]]


def tile(i):
    return pl.ds(pl.multiple_of(i * SUB, SUB), SUB)


def rows_a_turn(n):
    return (n + 2 * REACH - 4 + 1) // 2


def run_stages(n, stages, spin, edges):
    each = rows_a_turn(n)
    half_dt = 0.5 * time_step
    low_mask, high_mask = edges
    first, last = REACH, REACH + n - 1

    right_of = lambda x: pltpu.roll(x, LANES - 1, 1)
    left_of = lambda x: pltpu.roll(x, 1, 1)

    def radial_states(halves, centres):
        jumps = [h[SUB:] - h[:-SUB] for h in halves]
        slopes = [minmod(d[:-SUB], d[SUB:]) for d in jumps]
        lower = [x - g for x, g in zip(centres, slopes)]
        upper = [x + g for x, g in zip(centres, slopes)]
        return swapped([x[:-SUB] for x in upper]), swapped([x[SUB:] for x in lower])

    def work(stage, i0, before):
        src, dst = stage, (stage & 1) + 1
        weight = jnp.where(stage == 0, 1.0, jnp.where(stage == 1, 0.25, 2.0 / 3.0))
        keep = jnp.where(stage == 0, 0.0, jnp.where(stage == 1, 0.75, 1.0 / 3.0))
        some = lambda first, count: pl.ds(pl.multiple_of((i0 + first) * SUB, SUB), count * SUB)
        here = some(0, each)
        size = each * SUB
        rows = [stages[src, f, some(-1, each + 3), :] for f in range(FIELDS)]
        halves = [0.5 * x for x in rows]
        own = [x[SUB : SUB + size] for x in rows]
        half = [x[SUB : SUB + size] for x in halves]
        after = [right_of(x) for x in half]
        left, right = radial_states(halves, [x[SUB:-SUB] for x in rows])
        jump = [x - y for x, y in zip(after, half)]
        behind = [left_of(x) for x in jump]
        of_left = physical(left)
        of_right = physical(right)
        slopes = [minmod(x, y) for x, y in zip(behind, jump)]
        lower = [right_of(x - y) for x, y in zip(own, slopes)]
        upper = [x + y for x, y in zip(own, slopes)]
        of_upper = physical(upper)
        faces = swapped(face_twice(left, right, of_left, of_right))
        of_lower = physical(lower)
        azimuth = face_twice(upper, lower, of_upper, of_lower)
        shifted = [left_of(x) for x in azimuth]
        change = [x - jnp.concatenate([y, x[:-SUB]], axis=0) for x, y in zip(faces, before)]
        turn = spin[here, :]
        source = [None, (-0.5 * turn) * own[2], (2.0 * turn) * own[1], (-1.5 * turn) * own[4], None]
        partial = [x if y is None else x + y for x, y in zip(own, source)]
        starts = [keep * stages[0, f, here, :] for f in range(FIELDS)]
        for f in range(FIELDS):
            new = partial[f] - half_dt * ((azimuth[f] - shifted[f]) + change[f])
            stages[dst, f, here, :] = weight * new + starts[f]
        return [x[-SUB:] for x in faces]

    def run(stage, _):
        for f in range(FIELDS):
            inner = stages[stage, f, tile(first), :]
            outer = stages[stage, f, tile(last), :]
            for k in (1, 2):
                stages[stage, f, tile(first - k), :] = jnp.where(low_mask, inner, stages[stage, f, tile(first - k), :])
                stages[stage, f, tile(last + k), :] = jnp.where(high_mask, outer, stages[stage, f, tile(last + k), :])
        count = n + 2 * REACH - 4 - 4 * stage
        if n % 2 == 0:
            lo = 2 * stage + 2
            rows = [stages[stage, f, pl.ds(pl.multiple_of((lo - 2) * SUB, SUB), 4 * SUB), :] for f in range(FIELDS)]
            left, right = radial_states([0.5 * x for x in rows], [x[SUB:-SUB] for x in rows])
            before = tuple(swapped(face_twice(left, right, physical(left), physical(right))))
        else:
            lo = 2 * stage + 1
            count = count + 1
            before = (jnp.zeros((SUB, LANES), jnp.float32),) * FIELDS
        turns = lax.div(count + each - 1, each)
        lax.fori_loop(0, turns, lambda c, carried: tuple(work(stage, lo + c * each, list(carried))), before)
        return 0

    lax.fori_loop(0, STAGES, run, 0)


def spread(block, first, width):
    block = pltpu.roll(block, (LANES - first) % LANES, 1)
    lane = lax.broadcasted_iota(jnp.int32, block.shape, 1)
    while width < LANES:
        block = jnp.where(lane < width, block, pltpu.roll(block, width, 1))
        width *= 2
    return block


def pack_far(far, near, own_cells):
    sublane = lax.broadcasted_iota(jnp.int32, (SUB, LANES), 0)
    left = lax.broadcasted_iota(jnp.int32, (SUB, LANES), 1) < HALF

    def one(f, _):
        start = pl.multiple_of(f * own_cells, SUB)
        low = near[pl.ds(start, own_cells), 0:LANES]
        high = near[pl.ds(start + own_cells - 2 * SUB, 2 * SUB), LANES : 2 * LANES]
        before, last = high[0:SUB], high[SUB:]
        far[pl.ds(start, SUB), :] = jnp.where(left, low[0:SUB], pltpu.roll(last, HALF, 1))
        third = pltpu.roll(pltpu.roll(before, 1, 0), HALF, 1)
        fourth = pltpu.roll(last, 2, 0)
        second = low[SUB : 2 * SUB]
        mixed = jnp.where(sublane == 0, third, jnp.where(sublane == 1, fourth, second))
        far[pl.ds(start + SUB, SUB), :] = jnp.where(left, second, mixed)
        far[pl.ds(start + 2 * SUB, own_cells - 2 * SUB), :] = low[2 * SUB :]
        return 0

    lax.fori_loop(0, FIELDS, one, 0)


def far_rows(far, start, own_cells):
    left = lax.broadcasted_iota(jnp.int32, (SUB, LANES), 1) < HALF
    first = far[pl.ds(start, SUB), :]
    mixed = far[pl.ds(start + SUB, SUB), :]
    before = pltpu.roll(pltpu.roll(mixed, SUB - 1, 0), HALF, 1)
    last = jnp.where(left, pltpu.roll(first, HALF, 1), pltpu.roll(mixed, SUB - 2, 0))
    return before, last


def edge_kernel(place, density, momentum, magnetic, rotation, shifts, edge, ends, spin_in, shift_in, arrived):
    levels, own_cells, radius = density.shape
    on_low = place[0] == 0
    parts = radius // LANES
    split = 4 * own_cells
    columns = pl.ds(pl.multiple_of(jnp.where(on_low, radius - LANES, 0), LANES), LANES)
    copies = [
        pltpu.make_async_copy(rotation, spin_in, arrived.at[levels * FIELDS]),
        pltpu.make_async_copy(shifts, shift_in, arrived.at[levels * FIELDS + 1]),
    ]
    for level in range(levels):
        sources = [density.at[level, :, columns]] + [x.at[k, level, :, columns] for x in (momentum, magnetic) for k in range(2)]
        for f, x in enumerate(sources):
            at = ends.at[level, pl.ds(f * own_cells, own_cells), :]
            copies.append(pltpu.make_async_copy(x, at, arrived.at[level * FIELDS + f]))
    for copy in copies:
        copy.start()
    for copy in copies:
        copy.wait()
    wide = lambda ref: jnp.broadcast_to(
        jnp.where(on_low, ref[parts - 1 : parts, :], ref[0:1, :]).astype(jnp.float32), (own_cells, LANES)
    )
    turn = wide(spin_in) * time_step
    shift = wide(shift_in)
    zero = jnp.zeros((own_cells, LANES), jnp.float32)
    for level in range(levels):
        last = jnp.concatenate([ends[level, split:, :], turn, shift, zero], axis=0)
        for side, group in enumerate((ends[level, 0:split, :], last)):
            turned = group.T
            edge[level, :, side * LANES : (side + 1) * LANES] = jnp.where(on_low, turned[LANES - EXTRA :], turned[0:EXTRA])


def pack_kernel(levels, density, momentum, magnetic, edge, *outs):
    del edge
    nears, fars = outs[:levels], outs[levels:]
    own_cells = density.shape[1]
    for level in range(levels):
        sources = [density.at[level]] + [x.at[k, level] for x in (momentum, magnetic) for k in range(2)]
        for f, x in enumerate(sources):
            nears[level][f * own_cells : (f + 1) * own_cells, :] = x[...]
        pack_far(fars[level], nears[level], own_cells)


class Blocks:
    def __init__(self, row, n, radius, total, moved):
        self.on_low = row == 0
        self.n = n
        self.own_at = pl.multiple_of(jnp.where(self.on_low, EXTRA, EXTRA + moved), SUB)
        self.edge_at = pl.multiple_of(jnp.where(self.on_low, EXTRA + radius, moved), SUB)
        bounds = [[shift_bound(r * radius - (moved if r else 0) + n * k, total) for k in range(SLOTS)] for r in range(2)]
        self.bounds = [jnp.where(self.on_low, a, b) for a, b in zip(*bounds)]

    def rows_of(self, k):
        start = EXTRA - REACH + self.n * k
        return slice(start, start + DEALT)


def table_kernel(plans, place, side, rotation, shifts, *rest):
    outs, held = rest[:-1], rest[-1]
    radius = plans[0][1]
    own_cells = plans[0][2]
    wide_lane = lax.broadcasted_iota(jnp.int32, (DEALT, LANES), 1)
    front = wide_lane < HALF
    more = side[0, :, LANES : 2 * LANES]
    edges = [spread(more, own_cells, own_cells), spread(more, 2 * own_cells, own_cells)]
    own = []
    for ref, scale in ((rotation, time_step), (shifts, 1.0)):
        along = lambda part: jnp.broadcast_to(ref[part : part + 1, :].astype(jnp.float32), (LANES, LANES)).T
        own.append([along(part) * scale for part in range(radius // LANES)])
    for which, (n, radius, own_cells, total, moved) in enumerate(plans):
        spin, pick = outs[2 * which : 2 * which + 2]
        blocks = Blocks(place[0], n, radius, total, moved)
        for k in range(2):
            for part, x in enumerate(own[k]):
                held[2 * which + k, pl.ds(blocks.own_at + part * LANES, LANES), :] = x
            held[2 * which + k, pl.ds(blocks.edge_at, EXTRA), :] = edges[k]
        for j in range(SUB):
            low, high = blocks.rows_of(j), blocks.rows_of(SUB + j)
            turns = [jnp.where(front, held[2 * which + k, low, :], held[2 * which + k, high, :]) for k in range(2)]
            spin[pl.ds(j, DEALT, stride=SUB), :] = turns[0]
            bound = jnp.where(front, blocks.bounds[j], blocks.bounds[SUB + j])
            pick[pl.ds(j, DEALT, stride=SUB), :] = (wide_lane + (REACH + bound)) - turns[1].astype(jnp.int32)


def step_kernel(plan, refs, write, scratch):
    n, radius, own_cells, total, moved = plan
    place, own, own_edge, near, near_edge, far, spin, pick = refs
    cells, stages, packed = scratch
    row = place[0]
    lane = lax.broadcasted_iota(jnp.int32, (SUB, LANES), 1)
    sublane = lax.broadcasted_iota(jnp.int32, (SUB, LANES), 0)
    blocks = Blocks(row, n, radius, total, moved)

    edge_lane = lax.broadcasted_iota(jnp.int32, (EXTRA, LANES), 1)
    parts = radius // LANES

    front = lax.broadcasted_iota(jnp.int32, (DEALT, LANES), 1) < HALF

    def bring(f, _):
        rows = pl.ds(pl.multiple_of(f * own_cells, SUB), own_cells)
        start = pl.multiple_of(f * own_cells, SUB)
        for part in range(parts):
            columns = slice(part * LANES, (part + 1) * LANES)
            if part == 0:
                top = far[pl.ds(start, own_cells), :]
            else:
                gap = jnp.zeros((own_cells - 2 * SUB, LANES), jnp.float32)
                top = jnp.concatenate([gap, *far_rows(far, start, own_cells)], axis=0)
            fill = jnp.zeros((own_cells, LANES), jnp.float32)
            block = jnp.concatenate([top, near[rows, columns], own[rows, columns], fill], axis=0)
            cells[f, pl.ds(blocks.own_at + part * LANES, LANES), :] = block.T
        columns = pl.ds(pl.multiple_of(lax.div(f, 4) * LANES, LANES), LANES)
        lanes_at = lax.rem(f, 4) * own_cells
        cells[f, pl.ds(blocks.edge_at, EXTRA), :] = jnp.where(
            edge_lane < 2 * own_cells,
            pltpu.roll(near_edge[:, columns], lax.rem(LANES + own_cells - lanes_at, LANES), 1),
            pltpu.roll(own_edge[:, columns], lax.rem(LANES + 2 * own_cells - lanes_at, LANES), 1),
        )

        for j in range(SUB):
            low, high = j, SUB + j
            turn_low = (LANES - (2 * own_cells - REACH)) + blocks.bounds[low]
            turn_high = (HALF - (2 * own_cells - REACH)) + blocks.bounds[high]
            stages[0, f, pl.ds(j, DEALT, stride=SUB), :] = jnp.where(
                front,
                pltpu.roll(cells[f, blocks.rows_of(low), :], turn_low, 1),
                pltpu.roll(cells[f, blocks.rows_of(high), :], turn_high, 1),
            )
        return 0

    lax.fori_loop(0, FIELDS, bring, 0)

    edges = (
        (sublane == 0) & (lane < HALF) & (row == 0),
        (sublane == SUB - 1) & (lane >= HALF) & (row == total // radius - 1),
    )
    run_stages(n, stages, spin, edges)

    even = (lane & own_cells) == 0

    picked = (n + 1) // 2

    def shift(turn, _):
        for k in range(picked):
            i = turn * picked + k
            rows = tile(REACH + i)
            source = pick[rows, :]
            picks = [source & (LANES - 1), (source - own_cells) & (LANES - 1)]
            turned = [
                jnp.take_along_axis(stages[1, f, rows, :], picks[f % 2], axis=1, mode="promise_in_bounds")
                for f in range(FIELDS)
            ]
            stages[2, 0, tile(i), :] = jnp.where(even, turned[0], turned[1])
            stages[2, 1, tile(i), :] = jnp.where(even, turned[2], turned[3])
            stages[2, 2, tile(i), :] = turned[4]
        return 0

    lax.fori_loop(0, (n + picked - 1) // picked, shift, 0)
    narrow = lax.broadcasted_iota(jnp.int32, (n, LANES), 1) < HALF
    for j in range(SUB):
        one, two, three = [stages[2, g, pl.ds(j, n, stride=SUB), :] for g in range(3)]
        low = slice(EXTRA + n * j, EXTRA + n * (j + 1))
        high = slice(EXTRA + n * (SUB + j), EXTRA + n * (SUB + j + 1))
        packed[0, low, :] = jnp.where(narrow, one, pltpu.roll(two, HALF, 1))
        packed[0, high, :] = jnp.where(narrow, pltpu.roll(one, HALF, 1), two)
        packed[1, low, :] = three
        packed[1, high, :] = pltpu.roll(three, HALF, 1)
    for part in range(parts):
        rows = pl.ds(blocks.own_at + part * LANES, LANES)
        write.fields(slice(part * LANES, (part + 1) * LANES), packed[0, rows, :].T, packed[1, rows, :].T)
    write.edge(packed[0, pl.ds(blocks.edge_at, EXTRA), :], packed[1, pl.ds(blocks.edge_at, EXTRA), :])
    write.end()


class ToMessage:
    def __init__(self, near, far, own_cells):
        self.near, self.far, self.own_cells = near, far, own_cells

    def fields(self, columns, four, fifth):
        split = 4 * self.own_cells
        self.near[0:split, columns] = four
        self.near[split : split + self.own_cells, columns] = fifth[0 : self.own_cells]

    def edge(self, first, second):
        tail = FIELDS * self.own_cells
        self.near[tail : tail + EXTRA, 0:LANES] = first
        self.near[tail : tail + EXTRA, LANES : 2 * LANES] = second

    def end(self):
        pack_far(self.far, self.near, self.own_cells)


class ToBuffer:
    def __init__(self, buffer):
        self.buffer = buffer

    def fields(self, columns, four, fifth):
        split = four.shape[0]
        self.buffer[0:split, columns] = four
        self.buffer[split:, columns] = fifth[0 : self.buffer.shape[0] - split]

    def edge(self, first, second):
        pass

    def end(self):
        pass


def copies_out(level, buffer, outs, sent):
    density, momentum, magnetic = outs
    cells = density.shape[1]
    targets = [density.at[level]] + [x.at[k, level] for x in (momentum, magnetic) for k in range(2)]
    return [
        pltpu.make_async_copy(buffer.at[pl.ds(f * cells, cells), :], x, sent.at[level * FIELDS + f])
        for f, x in enumerate(targets)
    ]


def tall_of(n):
    return EXTRA + SLOTS * n + 2 * SUB


def step_scratch(n):
    return [
        pltpu.VMEM((FIELDS, tall_of(n), LANES), jnp.float32),
        pltpu.VMEM((STAGES, FIELDS, TALL * SUB, LANES), jnp.float32),
        pltpu.VMEM((2, tall_of(n), LANES), jnp.float32),
    ]


vmem = pl.BlockSpec(memory_space=pltpu.VMEM)
smem = pl.BlockSpec(memory_space=pltpu.SMEM)
f32 = lambda *s: jax.ShapeDtypeStruct(s, jnp.float32)
params = pltpu.CompilerParams(vmem_limit_bytes=VMEM_LIMIT)
cost = pl.CostEstimate(flops=9_000_000_000, bytes_accessed=29_000_000, transcendentals=0)


def first_step(plan, level, operands):
    n, radius, own_cells, total, moved = plan

    def kernel(place, own, near, far, side, corner, spin, pick, near_out, far_out, *scratch):
        refs = (place, own, side.at[level], near, corner.at[level], far, spin, pick)
        step_kernel(plan, refs, ToMessage(near_out, far_out, own_cells), scratch)

    return pl.pallas_call(
        kernel,
        out_shape=[f32(FIELDS * own_cells + EXTRA, radius), f32(FIELDS * own_cells, LANES)],
        in_specs=[smem] + [vmem] * 7,
        out_specs=[vmem] * 2,
        scratch_shapes=step_scratch(n),
        compiler_params=params,
        cost_estimate=cost,
        name="first_step",
    )(*operands)


def last_step(plan, level, operands, done, levels):
    n, radius, own_cells, total, moved = plan
    final = level == levels - 1
    tail = pl.ds(FIELDS * own_cells, EXTRA)
    buffer = f32(FIELDS * own_cells, radius)

    def kernel(place, own, near, far, spin, pick, *rest):
        refs = (place, own, own.at[tail, :], near, near.at[tail, :], far, spin, pick)
        if not final:
            step_kernel(plan, refs, ToBuffer(rest[0]), rest[1:])
            return
        ready, outs, scratch = rest[: levels - 1], rest[levels - 1 : levels + 2], rest[levels + 2 :]
        last, sent = scratch[-2:]
        copies = []
        for k, x in enumerate(ready):
            copies += copies_out(k, x, outs, sent)
        for copy in copies:
            copy.start()
        step_kernel(plan, refs, ToBuffer(last), scratch[:-2])
        rest_of = copies_out(level, last, outs, sent)
        for copy in rest_of:
            copy.start()
        for copy in copies + rest_of:
            copy.wait()

    if final:
        out_shape = [f32(levels, own_cells, radius), f32(2, levels, own_cells, radius), f32(2, levels, own_cells, radius)]
        more = [pltpu.VMEM((FIELDS * own_cells, radius), jnp.float32), pltpu.SemaphoreType.DMA((levels * FIELDS,))]
    else:
        out_shape = buffer
        more = []
    return pl.pallas_call(
        kernel,
        out_shape=out_shape,
        in_specs=[smem] + [vmem] * (5 + len(done)),
        out_specs=[pl.BlockSpec(memory_space=pltpu.HBM)] * 3 if final else vmem,
        scratch_shapes=step_scratch(n) + more,
        compiler_params=params,
        cost_estimate=cost,
        name="last_step",
    )(*operands, *done)


def body(density, momentum, magnetic, rotation, shifts):
    phi_count = lax.axis_size("phi")
    row_count = lax.axis_size("row")
    levels, own_cells, radius = density.shape
    total = radius * row_count
    parts = radius // LANES
    n = radius // SLOTS
    need = [max(shift_bound(k * HALF, total) + REACH - own_cells, 0) for k in range(radius // HALF)]
    assert row_count == 2 and radius == 2 * LANES and own_cells == HALF // 2
    assert need[0] <= own_cells and need[1] <= own_cells - SUB - 2 and need[2] <= SUB + 1 and need[3] <= 1

    row = lax.axis_index("row")
    place = jnp.reshape(row, (1,)).astype(jnp.int32)
    send_near = lambda x: lax.ppermute(x, "phi", [(p, (p + 1) % phi_count) for p in range(phi_count)])
    send_far = lambda x: lax.ppermute(x, "phi", [(p, (p + 2) % phi_count) for p in range(phi_count)])
    here = lambda p, r: (p % phi_count) * row_count + r
    diagonal = [(here(p, r), here(p + 1, 1 - r)) for p in range(phi_count) for r in range(row_count)]
    send_corner = lambda x: lax.ppermute(x, ("phi", "row"), diagonal)
    send_side = lambda x: lax.ppermute(x, "row", [(0, 1), (1, 0)])

    spins, turns = rotation.reshape(parts, LANES), shifts.reshape(parts, LANES)
    near_message = f32(FIELDS * own_cells, radius)
    far_message = f32(FIELDS * own_cells, LANES)
    edge = pl.pallas_call(
        edge_kernel,
        out_shape=f32(levels, EXTRA, 2 * LANES),
        in_specs=[smem] + [pl.BlockSpec(memory_space=pltpu.HBM)] * 5,
        out_specs=vmem,
        scratch_shapes=[
            pltpu.VMEM((levels, FIELDS * own_cells, LANES), jnp.float32),
            pltpu.VMEM((parts, LANES), jnp.float32),
            pltpu.VMEM((parts, LANES), jnp.int32),
            pltpu.SemaphoreType.DMA((levels * FIELDS + 2,)),
        ],
        compiler_params=pltpu.CompilerParams(vmem_limit_bytes=EDGE_LIMIT),
        name="edges",
    )(place, density, momentum, magnetic, spins, turns)
    packed = pl.pallas_call(
        lambda *refs: pack_kernel(levels, *refs),
        out_shape=[near_message] * levels + [far_message] * levels,
        in_specs=[vmem] * 3 + [pl.BlockSpec(memory_space=pl.ANY)],
        out_specs=[vmem] * (2 * levels),
        compiler_params=params,
        cost_estimate=cost,
        name="pack",
    )(density, momentum, magnetic, edge)
    owns, fars = packed[:levels], packed[levels:]
    side = send_side(edge)
    corner = send_corner(edge)
    wide = (n + 1, radius, own_cells, total, EXTRA)
    plain = (n, radius, own_cells, total, 0)
    i32 = jax.ShapeDtypeStruct((TALL * SUB, LANES), jnp.int32)
    tables = pl.pallas_call(
        lambda *refs: table_kernel((wide, plain), *refs),
        out_shape=[f32(TALL * SUB, LANES), i32] * 2,
        in_specs=[smem] + [vmem] * 3,
        out_specs=[vmem] * 4,
        scratch_shapes=[pltpu.VMEM((4, tall_of(n + 1), LANES), jnp.float32)],
        compiler_params=params,
        name="tables",
    )(place, side, spins, turns)
    moved = []
    for own, far in zip(owns, fars):
        if moved:
            own, far, _ = lax.optimization_barrier((own, far, tables[0]))
        moved.append((send_near(own), send_far(far)))
    states = []
    for level in range(levels):
        near, far = moved[level]
        states.append(first_step(wide, level, (place, owns[level], near, far, side, corner, *tables[:2])))
    moved = [(send_near(own), send_far(far)) for own, far in states]
    done = ()
    for level in range(levels):
        near, far = moved[level]
        operands = (place, states[level][0], near, far, *tables[2:])
        result = last_step(plain, level, operands, done if level == levels - 1 else (), levels)
        done += (result,)
    return tuple(result)


def solution(mesh):
    placed = (
        P(None, "phi", "row"),
        P(None, None, "phi", "row"),
        P(None, None, "phi", "row"),
        P("row"),
        P("row"),
    )
    return jax.shard_map(
        body,
        mesh=mesh,
        in_specs=placed,
        out_specs=(P(None, "phi", "row"), P(None, None, "phi", "row"), P(None, None, "phi", "row")),
        check_vma=False,
    )
```

```python
import jax
import jax.numpy as jnp
from jax import lax
from jax.experimental import pallas as pl
from jax.experimental.pallas import tpu as pltpu
from jax.sharding import PartitionSpec as P

STEPS = 2
SMIN = 8
SMAX = 56
STAGES = 3
REACH = 2 * STAGES
FIELDS = 5
LANES = 128
SUB = 8
HALF = LANES // 2
SLOTS = 2 * SUB
EXTRA = 2 * SUB
DEALT = 32
TALL = 40
VMEM_LIMIT = 32 * 1024 * 1024
EDGE_LIMIT = 60 * 1024 * 1024

time_step = 0.08


def shift_bound(first_row, rows):
    d = rows - 1 - first_row
    return min(SMIN + (SMAX - SMIN - 1) * d * d // ((rows - 1) * (rows - 1)) + 1, SMAX)


def minmod(lower, upper):
    return jnp.maximum(jnp.minimum(lower, 0.0), jnp.minimum(upper, jnp.maximum(lower, 0.0)))


def physical(state):
    rho, mn, mt, bn, bt = state
    inverse = pltpu.reciprocal(rho, approx=True)
    bn_sq = bn * bn
    bt_sq = bt * bt
    vn = mn * inverse
    vt = mt * inverse
    inside = (bn_sq + bt_sq) * inverse + 1.0
    root = lax.rsqrt(inside)
    ram = mn * vn + rho
    tension = bt_sq - bn_sq
    flux_t = mt * vn - bn * bt
    flux_b = bt * vn - bn * vt
    speed = jnp.abs(vn) + inside * root
    return ram, tension, flux_t, flux_b, speed


def face_twice(left, right, of_left, of_right):
    left_ram, left_tension, left_t, left_b, left_speed = of_left
    right_ram, right_tension, right_t, right_b, right_speed = of_right
    bound = jnp.maximum(left_speed, right_speed)
    jumps = [bound * (l - r) for l, r in zip(left, right)]
    return [
        (left[1] + right[1]) + jumps[0],
        ((left_ram + right_ram) + 0.5 * (left_tension + right_tension)) + jumps[1],
        (left_t + right_t) + jumps[2],
        jumps[3],
        (left_b + right_b) + jumps[4],
    ]


def swapped(five):
    return [five[0], five[2], five[1], five[4], five[3]]


def tile(i):
    return pl.ds(pl.multiple_of(i * SUB, SUB), SUB)


def rows_a_turn(n):
    return (n + 2 * REACH - 4 + 1) // 2


def run_stages(n, stages, spin, edges):
    each = rows_a_turn(n)
    half_dt = 0.5 * time_step
    low_mask, high_mask = edges
    first, last = REACH, REACH + n - 1

    right_of = lambda x: pltpu.roll(x, LANES - 1, 1)
    left_of = lambda x: pltpu.roll(x, 1, 1)

    def radial_states(halves, centres):
        jumps = [h[SUB:] - h[:-SUB] for h in halves]
        slopes = [minmod(d[:-SUB], d[SUB:]) for d in jumps]
        lower = [x - g for x, g in zip(centres, slopes)]
        upper = [x + g for x, g in zip(centres, slopes)]
        return swapped([x[:-SUB] for x in upper]), swapped([x[SUB:] for x in lower])

    def work(stage, i0, before):
        src, dst = stage, (stage & 1) + 1
        weight = jnp.where(stage == 0, 1.0, jnp.where(stage == 1, 0.25, 2.0 / 3.0))
        keep = jnp.where(stage == 0, 0.0, jnp.where(stage == 1, 0.75, 1.0 / 3.0))
        some = lambda first, count: pl.ds(pl.multiple_of((i0 + first) * SUB, SUB), count * SUB)
        here = some(0, each)
        size = each * SUB
        rows = [stages[src, f, some(-1, each + 3), :] for f in range(FIELDS)]
        halves = [0.5 * x for x in rows]
        own = [x[SUB : SUB + size] for x in rows]
        half = [x[SUB : SUB + size] for x in halves]
        after = [right_of(x) for x in half]
        left, right = radial_states(halves, [x[SUB:-SUB] for x in rows])
        jump = [x - y for x, y in zip(after, half)]
        behind = [left_of(x) for x in jump]
        of_left = physical(left)
        of_right = physical(right)
        slopes = [minmod(x, y) for x, y in zip(behind, jump)]
        lower = [right_of(x - y) for x, y in zip(own, slopes)]
        upper = [x + y for x, y in zip(own, slopes)]
        of_upper = physical(upper)
        faces = swapped(face_twice(left, right, of_left, of_right))
        of_lower = physical(lower)
        azimuth = face_twice(upper, lower, of_upper, of_lower)
        shifted = [left_of(x) for x in azimuth]
        change = [x - jnp.concatenate([y, x[:-SUB]], axis=0) for x, y in zip(faces, before)]
        turn = spin[here, :]
        source = [None, (-0.5 * turn) * own[2], (2.0 * turn) * own[1], (-1.5 * turn) * own[4], None]
        partial = [x if y is None else x + y for x, y in zip(own, source)]
        starts = [keep * stages[0, f, here, :] for f in range(FIELDS)]
        for f in range(FIELDS):
            new = partial[f] - half_dt * ((azimuth[f] - shifted[f]) + change[f])
            stages[dst, f, here, :] = weight * new + starts[f]
        return [x[-SUB:] for x in faces]

    def run(stage, _):
        for f in range(FIELDS):
            inner = stages[stage, f, tile(first), :]
            outer = stages[stage, f, tile(last), :]
            for k in (1, 2):
                stages[stage, f, tile(first - k), :] = jnp.where(low_mask, inner, stages[stage, f, tile(first - k), :])
                stages[stage, f, tile(last + k), :] = jnp.where(high_mask, outer, stages[stage, f, tile(last + k), :])
        count = n + 2 * REACH - 4 - 4 * stage
        if n % 2 == 0:
            lo = 2 * stage + 2
            rows = [stages[stage, f, pl.ds(pl.multiple_of((lo - 2) * SUB, SUB), 4 * SUB), :] for f in range(FIELDS)]
            left, right = radial_states([0.5 * x for x in rows], [x[SUB:-SUB] for x in rows])
            before = tuple(swapped(face_twice(left, right, physical(left), physical(right))))
        else:
            lo = 2 * stage + 1
            count = count + 1
            before = (jnp.zeros((SUB, LANES), jnp.float32),) * FIELDS
        turns = lax.div(count + each - 1, each)
        lax.fori_loop(0, turns, lambda c, carried: tuple(work(stage, lo + c * each, list(carried))), before)
        return 0

    lax.fori_loop(0, STAGES, run, 0)


def spread(block, first, width):
    block = pltpu.roll(block, (LANES - first) % LANES, 1)
    lane = lax.broadcasted_iota(jnp.int32, block.shape, 1)
    while width < LANES:
        block = jnp.where(lane < width, block, pltpu.roll(block, width, 1))
        width *= 2
    return block


def pack_far(far, near, own_cells):
    sublane = lax.broadcasted_iota(jnp.int32, (SUB, LANES), 0)
    left = lax.broadcasted_iota(jnp.int32, (SUB, LANES), 1) < HALF

    for f in range(FIELDS):
        start = f * own_cells
        low = near[start : start + own_cells, 0:LANES]
        high = near[start + own_cells - 2 * SUB : start + own_cells, LANES : 2 * LANES]
        before, last = high[0:SUB], high[SUB:]
        far[start : start + SUB, :] = jnp.where(left, low[0:SUB], pltpu.roll(last, HALF, 1))
        third = pltpu.roll(pltpu.roll(before, 1, 0), HALF, 1)
        fourth = pltpu.roll(last, 2, 0)
        second = low[SUB : 2 * SUB]
        mixed = jnp.where(sublane == 0, third, jnp.where(sublane == 1, fourth, second))
        far[start + SUB : start + 2 * SUB, :] = jnp.where(left, second, mixed)
        far[start + 2 * SUB : start + own_cells, :] = low[2 * SUB :]


def far_rows(far, start):
    left = lax.broadcasted_iota(jnp.int32, (SUB, LANES), 1) < HALF
    first = far[start : start + SUB, :]
    mixed = far[start + SUB : start + 2 * SUB, :]
    before = pltpu.roll(pltpu.roll(mixed, SUB - 1, 0), HALF, 1)
    last = jnp.where(left, pltpu.roll(first, HALF, 1), pltpu.roll(mixed, SUB - 2, 0))
    return before, last


def edge_kernel(place, density, momentum, magnetic, rotation, shifts, edge, ends, spin_in, shift_in, arrived):
    levels, own_cells, radius = density.shape
    on_low = place[0] == 0
    parts = radius // LANES
    split = 4 * own_cells
    columns = pl.ds(pl.multiple_of(jnp.where(on_low, radius - LANES, 0), LANES), LANES)
    copies = [
        pltpu.make_async_copy(rotation, spin_in, arrived.at[levels * FIELDS]),
        pltpu.make_async_copy(shifts, shift_in, arrived.at[levels * FIELDS + 1]),
    ]
    for level in range(levels):
        sources = [density.at[level, :, columns]] + [x.at[k, level, :, columns] for x in (momentum, magnetic) for k in range(2)]
        for f, x in enumerate(sources):
            at = ends.at[level, pl.ds(f * own_cells, own_cells), :]
            copies.append(pltpu.make_async_copy(x, at, arrived.at[level * FIELDS + f]))
    for copy in copies:
        copy.start()
    for copy in copies:
        copy.wait()
    wide = lambda ref: jnp.broadcast_to(
        jnp.where(on_low, ref[parts - 1 : parts, :], ref[0:1, :]).astype(jnp.float32), (own_cells, LANES)
    )
    turn = wide(spin_in) * time_step
    shift = wide(shift_in)
    zero = jnp.zeros((own_cells, LANES), jnp.float32)
    for level in range(levels):
        last = jnp.concatenate([ends[level, split:, :], turn, shift, zero], axis=0)
        for side, group in enumerate((ends[level, 0:split, :], last)):
            turned = group.T
            edge[level, :, side * LANES : (side + 1) * LANES] = jnp.where(on_low, turned[LANES - EXTRA :], turned[0:EXTRA])


def pack_kernel(levels, density, momentum, magnetic, edge, *outs):
    del edge
    nears, fars = outs[:levels], outs[levels:]
    own_cells = density.shape[1]
    for level in range(levels):
        sources = [density.at[level]] + [x.at[k, level] for x in (momentum, magnetic) for k in range(2)]
        for f, x in enumerate(sources):
            nears[level][f * own_cells : (f + 1) * own_cells, :] = x[...]
        pack_far(fars[level], nears[level], own_cells)


class Blocks:
    def __init__(self, row, n, radius, total, moved):
        self.on_low = row == 0
        self.n = n
        self.own_at = pl.multiple_of(jnp.where(self.on_low, EXTRA, EXTRA + moved), SUB)
        self.edge_at = pl.multiple_of(jnp.where(self.on_low, EXTRA + radius, moved), SUB)
        bounds = [[shift_bound(r * radius - (moved if r else 0) + n * k, total) for k in range(SLOTS)] for r in range(2)]
        self.bounds = [jnp.where(self.on_low, a, b) for a, b in zip(*bounds)]

    def rows_of(self, k):
        start = EXTRA - REACH + self.n * k
        return slice(start, start + DEALT)


def table_kernel(plans, place, side, rotation, shifts, *rest):
    outs, held = rest[:-1], rest[-1]
    radius = plans[0][1]
    own_cells = plans[0][2]
    wide_lane = lax.broadcasted_iota(jnp.int32, (DEALT, LANES), 1)
    front = wide_lane < HALF
    more = side[0, :, LANES : 2 * LANES]
    edges = [spread(more, own_cells, own_cells), spread(more, 2 * own_cells, own_cells)]
    own = []
    for ref, scale in ((rotation, time_step), (shifts, 1.0)):
        along = lambda part: jnp.broadcast_to(ref[part : part + 1, :].astype(jnp.float32), (LANES, LANES)).T
        own.append([along(part) * scale for part in range(radius // LANES)])
    for which, (n, radius, own_cells, total, moved) in enumerate(plans):
        spin, pick = outs[2 * which : 2 * which + 2]
        blocks = Blocks(place[0], n, radius, total, moved)
        for k in range(2):
            for part, x in enumerate(own[k]):
                held[2 * which + k, pl.ds(blocks.own_at + part * LANES, LANES), :] = x
            held[2 * which + k, pl.ds(blocks.edge_at, EXTRA), :] = edges[k]
        for j in range(SUB):
            low, high = blocks.rows_of(j), blocks.rows_of(SUB + j)
            turns = [jnp.where(front, held[2 * which + k, low, :], held[2 * which + k, high, :]) for k in range(2)]
            spin[pl.ds(j, DEALT, stride=SUB), :] = turns[0]
            bound = jnp.where(front, blocks.bounds[j], blocks.bounds[SUB + j])
            pick[pl.ds(j, DEALT, stride=SUB), :] = (wide_lane + (REACH + bound)) - turns[1].astype(jnp.int32)


def step_kernel(plan, refs, write, scratch):
    n, radius, own_cells, total, moved = plan
    place, own, own_edge, near, near_edge, far, spin, pick = refs
    cells, stages, packed, tops = scratch
    row = place[0]
    lane = lax.broadcasted_iota(jnp.int32, (SUB, LANES), 1)
    sublane = lax.broadcasted_iota(jnp.int32, (SUB, LANES), 0)
    blocks = Blocks(row, n, radius, total, moved)

    edge_lane = lax.broadcasted_iota(jnp.int32, (EXTRA, LANES), 1)
    parts = radius // LANES

    front = lax.broadcasted_iota(jnp.int32, (DEALT, LANES), 1) < HALF

    for f in range(FIELDS):
        tops[f] = jnp.concatenate(far_rows(far, f * own_cells), axis=0)

    def bring(f, _):
        rows = pl.ds(pl.multiple_of(f * own_cells, SUB), own_cells)
        start = pl.multiple_of(f * own_cells, SUB)
        for part in range(parts):
            columns = slice(part * LANES, (part + 1) * LANES)
            if part == 0:
                top = far[pl.ds(start, own_cells), :]
            else:
                gap = jnp.zeros((own_cells - 2 * SUB, LANES), jnp.float32)
                top = jnp.concatenate([gap, tops[f]], axis=0)
            fill = jnp.zeros((own_cells, LANES), jnp.float32)
            block = jnp.concatenate([top, near[rows, columns], own[rows, columns], fill], axis=0)
            cells[f, pl.ds(blocks.own_at + part * LANES, LANES), :] = block.T
        columns = pl.ds(pl.multiple_of(lax.div(f, 4) * LANES, LANES), LANES)
        lanes_at = lax.rem(f, 4) * own_cells
        cells[f, pl.ds(blocks.edge_at, EXTRA), :] = jnp.where(
            edge_lane < 2 * own_cells,
            pltpu.roll(near_edge[:, columns], lax.rem(LANES + own_cells - lanes_at, LANES), 1),
            pltpu.roll(own_edge[:, columns], lax.rem(LANES + 2 * own_cells - lanes_at, LANES), 1),
        )

        for j in range(SUB):
            low, high = j, SUB + j
            turn_low = (LANES - (2 * own_cells - REACH)) + blocks.bounds[low]
            turn_high = (HALF - (2 * own_cells - REACH)) + blocks.bounds[high]
            stages[0, f, pl.ds(j, DEALT, stride=SUB), :] = jnp.where(
                front,
                pltpu.roll(cells[f, blocks.rows_of(low), :], turn_low, 1),
                pltpu.roll(cells[f, blocks.rows_of(high), :], turn_high, 1),
            )
        return 0

    lax.fori_loop(0, FIELDS, bring, 0)

    edges = (
        (sublane == 0) & (lane < HALF) & (row == 0),
        (sublane == SUB - 1) & (lane >= HALF) & (row == total // radius - 1),
    )
    run_stages(n, stages, spin, edges)

    even = (lane & own_cells) == 0

    picked = (n + 1) // 2

    def shift(turn, _):
        for k in range(picked):
            i = turn * picked + k
            rows = tile(REACH + i)
            source = pick[rows, :]
            picks = [source & (LANES - 1), (source - own_cells) & (LANES - 1)]
            turned = [
                jnp.take_along_axis(stages[1, f, rows, :], picks[f % 2], axis=1, mode="promise_in_bounds")
                for f in range(FIELDS)
            ]
            stages[2, 0, tile(i), :] = jnp.where(even, turned[0], turned[1])
            stages[2, 1, tile(i), :] = jnp.where(even, turned[2], turned[3])
            stages[2, 2, tile(i), :] = turned[4]
        return 0

    lax.fori_loop(0, (n + picked - 1) // picked, shift, 0)
    narrow = lax.broadcasted_iota(jnp.int32, (n, LANES), 1) < HALF
    for j in range(SUB):
        one, two, three = [stages[2, g, pl.ds(j, n, stride=SUB), :] for g in range(3)]
        low = slice(EXTRA + n * j, EXTRA + n * (j + 1))
        high = slice(EXTRA + n * (SUB + j), EXTRA + n * (SUB + j + 1))
        packed[0, low, :] = jnp.where(narrow, one, pltpu.roll(two, HALF, 1))
        packed[0, high, :] = jnp.where(narrow, pltpu.roll(one, HALF, 1), two)
        packed[1, low, :] = three
        packed[1, high, :] = pltpu.roll(three, HALF, 1)
    for part in range(parts):
        rows = pl.ds(blocks.own_at + part * LANES, LANES)
        write.fields(slice(part * LANES, (part + 1) * LANES), packed[0, rows, :].T, packed[1, rows, :].T)
    write.edge(packed[0, pl.ds(blocks.edge_at, EXTRA), :], packed[1, pl.ds(blocks.edge_at, EXTRA), :])
    write.end()


class ToMessage:
    def __init__(self, near, far, own_cells):
        self.near, self.far, self.own_cells = near, far, own_cells

    def fields(self, columns, four, fifth):
        split = 4 * self.own_cells
        self.near[0:split, columns] = four
        self.near[split : split + self.own_cells, columns] = fifth[0 : self.own_cells]

    def edge(self, first, second):
        tail = FIELDS * self.own_cells
        self.near[tail : tail + EXTRA, 0:LANES] = first
        self.near[tail : tail + EXTRA, LANES : 2 * LANES] = second

    def end(self):
        pack_far(self.far, self.near, self.own_cells)


class ToBuffer:
    def __init__(self, buffer):
        self.buffer = buffer

    def fields(self, columns, four, fifth):
        split = four.shape[0]
        self.buffer[0:split, columns] = four
        self.buffer[split:, columns] = fifth[0 : self.buffer.shape[0] - split]

    def edge(self, first, second):
        pass

    def end(self):
        pass


def copies_out(level, buffer, outs, sent):
    density, momentum, magnetic = outs
    cells = density.shape[1]
    targets = [density.at[level]] + [x.at[k, level] for x in (momentum, magnetic) for k in range(2)]
    return [
        pltpu.make_async_copy(buffer.at[pl.ds(f * cells, cells), :], x, sent.at[level * FIELDS + f])
        for f, x in enumerate(targets)
    ]


def tall_of(n):
    return EXTRA + SLOTS * n + 2 * SUB


def step_scratch(n):
    return [
        pltpu.VMEM((FIELDS, tall_of(n), LANES), jnp.float32),
        pltpu.VMEM((STAGES, FIELDS, TALL * SUB, LANES), jnp.float32),
        pltpu.VMEM((2, tall_of(n), LANES), jnp.float32),
        pltpu.VMEM((FIELDS, 2 * SUB, LANES), jnp.float32),
    ]


vmem = pl.BlockSpec(memory_space=pltpu.VMEM)
smem = pl.BlockSpec(memory_space=pltpu.SMEM)
f32 = lambda *s: jax.ShapeDtypeStruct(s, jnp.float32)
params = pltpu.CompilerParams(vmem_limit_bytes=VMEM_LIMIT)
cost = pl.CostEstimate(flops=9_000_000_000, bytes_accessed=29_000_000, transcendentals=0)


def first_step(plan, level, operands):
    n, radius, own_cells, total, moved = plan

    def kernel(place, own, near, far, side, corner, spin, pick, near_out, far_out, *scratch):
        refs = (place, own, side.at[level], near, corner.at[level], far, spin, pick)
        step_kernel(plan, refs, ToMessage(near_out, far_out, own_cells), scratch)

    return pl.pallas_call(
        kernel,
        out_shape=[f32(FIELDS * own_cells + EXTRA, radius), f32(FIELDS * own_cells, LANES)],
        in_specs=[smem] + [vmem] * 7,
        out_specs=[vmem] * 2,
        scratch_shapes=step_scratch(n),
        compiler_params=params,
        cost_estimate=cost,
        name="first_step",
    )(*operands)


def last_step(plan, level, operands, done, levels):
    n, radius, own_cells, total, moved = plan
    final = level == levels - 1
    tail = pl.ds(FIELDS * own_cells, EXTRA)
    buffer = f32(FIELDS * own_cells, radius)

    def kernel(place, own, near, far, spin, pick, *rest):
        refs = (place, own, own.at[tail, :], near, near.at[tail, :], far, spin, pick)
        if not final:
            step_kernel(plan, refs, ToBuffer(rest[0]), rest[1:])
            return
        ready, outs, scratch = rest[: levels - 1], rest[levels - 1 : levels + 2], rest[levels + 2 :]
        last, sent = scratch[-2:]
        copies = []
        for k, x in enumerate(ready):
            copies += copies_out(k, x, outs, sent)
        for copy in copies:
            copy.start()
        step_kernel(plan, refs, ToBuffer(last), scratch[:-2])
        rest_of = copies_out(level, last, outs, sent)
        for copy in rest_of:
            copy.start()
        for copy in copies + rest_of:
            copy.wait()

    if final:
        out_shape = [f32(levels, own_cells, radius), f32(2, levels, own_cells, radius), f32(2, levels, own_cells, radius)]
        more = [pltpu.VMEM((FIELDS * own_cells, radius), jnp.float32), pltpu.SemaphoreType.DMA((levels * FIELDS,))]
    else:
        out_shape = buffer
        more = []
    return pl.pallas_call(
        kernel,
        out_shape=out_shape,
        in_specs=[smem] + [vmem] * (5 + len(done)),
        out_specs=[pl.BlockSpec(memory_space=pltpu.HBM)] * 3 if final else vmem,
        scratch_shapes=step_scratch(n) + more,
        compiler_params=params,
        cost_estimate=cost,
        name="last_step",
    )(*operands, *done)


def body(density, momentum, magnetic, rotation, shifts):
    phi_count = lax.axis_size("phi")
    row_count = lax.axis_size("row")
    levels, own_cells, radius = density.shape
    total = radius * row_count
    parts = radius // LANES
    n = radius // SLOTS
    need = [max(shift_bound(k * HALF, total) + REACH - own_cells, 0) for k in range(radius // HALF)]
    assert row_count == 2 and radius == 2 * LANES and own_cells == HALF // 2
    assert need[0] <= own_cells and need[1] <= own_cells - SUB - 2 and need[2] <= SUB + 1 and need[3] <= 1

    row = lax.axis_index("row")
    place = jnp.reshape(row, (1,)).astype(jnp.int32)
    send_near = lambda x: lax.ppermute(x, "phi", [(p, (p + 1) % phi_count) for p in range(phi_count)])
    send_far = lambda x: lax.ppermute(x, "phi", [(p, (p + 2) % phi_count) for p in range(phi_count)])
    here = lambda p, r: (p % phi_count) * row_count + r
    diagonal = [(here(p, r), here(p + 1, 1 - r)) for p in range(phi_count) for r in range(row_count)]
    send_corner = lambda x: lax.ppermute(x, ("phi", "row"), diagonal)
    send_side = lambda x: lax.ppermute(x, "row", [(0, 1), (1, 0)])

    spins, turns = rotation.reshape(parts, LANES), shifts.reshape(parts, LANES)
    near_message = f32(FIELDS * own_cells, radius)
    far_message = f32(FIELDS * own_cells, LANES)
    edge = pl.pallas_call(
        edge_kernel,
        out_shape=f32(levels, EXTRA, 2 * LANES),
        in_specs=[smem] + [pl.BlockSpec(memory_space=pltpu.HBM)] * 5,
        out_specs=vmem,
        scratch_shapes=[
            pltpu.VMEM((levels, FIELDS * own_cells, LANES), jnp.float32),
            pltpu.VMEM((parts, LANES), jnp.float32),
            pltpu.VMEM((parts, LANES), jnp.int32),
            pltpu.SemaphoreType.DMA((levels * FIELDS + 2,)),
        ],
        compiler_params=pltpu.CompilerParams(vmem_limit_bytes=EDGE_LIMIT),
        name="edges",
    )(place, density, momentum, magnetic, spins, turns)
    packed = pl.pallas_call(
        lambda *refs: pack_kernel(levels, *refs),
        out_shape=[near_message] * levels + [far_message] * levels,
        in_specs=[vmem] * 3 + [pl.BlockSpec(memory_space=pl.ANY)],
        out_specs=[vmem] * (2 * levels),
        compiler_params=params,
        cost_estimate=cost,
        name="pack",
    )(density, momentum, magnetic, edge)
    owns, fars = packed[:levels], packed[levels:]
    side = send_side(edge)
    corner = send_corner(edge)
    wide = (n + 1, radius, own_cells, total, EXTRA)
    plain = (n, radius, own_cells, total, 0)
    i32 = jax.ShapeDtypeStruct((TALL * SUB, LANES), jnp.int32)
    tables = pl.pallas_call(
        lambda *refs: table_kernel((wide, plain), *refs),
        out_shape=[f32(TALL * SUB, LANES), i32] * 2,
        in_specs=[smem] + [vmem] * 3,
        out_specs=[vmem] * 4,
        scratch_shapes=[pltpu.VMEM((4, tall_of(n + 1), LANES), jnp.float32)],
        compiler_params=params,
        name="tables",
    )(place, side, spins, turns)
    moved = []
    for own, far in zip(owns, fars):
        if moved:
            own, far, _ = lax.optimization_barrier((own, far, tables[0]))
        moved.append((send_near(own), send_far(far)))
    states = []
    for level in range(levels):
        near, far = moved[level]
        states.append(first_step(wide, level, (place, owns[level], near, far, side, corner, *tables[:2])))
    moved = [(send_near(own), send_far(far)) for own, far in states]
    done = ()
    for level in range(levels):
        near, far = moved[level]
        operands = (place, states[level][0], near, far, *tables[2:])
        result = last_step(plain, level, operands, done if level == levels - 1 else (), levels)
        done += (result,)
    return tuple(result)


def solution(mesh):
    placed = (
        P(None, "phi", "row"),
        P(None, None, "phi", "row"),
        P(None, None, "phi", "row"),
        P("row"),
        P("row"),
    )
    return jax.shard_map(
        body,
        mesh=mesh,
        in_specs=placed,
        out_specs=(P(None, "phi", "row"), P(None, None, "phi", "row"), P(None, None, "phi", "row")),
        check_vma=False,
    )
```

```python
import jax
import jax.numpy as jnp
from jax import lax
from jax.experimental import pallas as pl
from jax.experimental.pallas import tpu as pltpu
from jax.sharding import PartitionSpec as P

STEPS = 2
SMIN = 8
SMAX = 56
STAGES = 3
REACH = 2 * STAGES
FIELDS = 5
LANES = 128
SUB = 8
HALF = LANES // 2
SLOTS = 2 * SUB
EXTRA = 2 * SUB
DEALT = 32
TALL = 40
VMEM_LIMIT = 32 * 1024 * 1024
EDGE_LIMIT = 60 * 1024 * 1024

time_step = 0.08


def shift_bound(first_row, rows):
    d = rows - 1 - first_row
    return min(SMIN + (SMAX - SMIN - 1) * d * d // ((rows - 1) * (rows - 1)) + 1, SMAX)


def minmod(lower, upper):
    return jnp.maximum(jnp.minimum(lower, 0.0), jnp.minimum(upper, jnp.maximum(lower, 0.0)))


def physical(state):
    rho, mn, mt, bn, bt = state
    inverse = pltpu.reciprocal(rho, approx=True)
    bn_sq = bn * bn
    bt_sq = bt * bt
    vn = mn * inverse
    vt = mt * inverse
    inside = (bn_sq + bt_sq) * inverse + 1.0
    root = lax.rsqrt(inside)
    ram = mn * vn + rho
    tension = bt_sq - bn_sq
    flux_t = mt * vn - bn * bt
    flux_b = bt * vn - bn * vt
    speed = jnp.abs(vn) + inside * root
    return ram, tension, flux_t, flux_b, speed


def face_twice(left, right, of_left, of_right):
    left_ram, left_tension, left_t, left_b, left_speed = of_left
    right_ram, right_tension, right_t, right_b, right_speed = of_right
    bound = jnp.maximum(left_speed, right_speed)
    jumps = [bound * (l - r) for l, r in zip(left, right)]
    return [
        (left[1] + right[1]) + jumps[0],
        ((left_ram + right_ram) + 0.5 * (left_tension + right_tension)) + jumps[1],
        (left_t + right_t) + jumps[2],
        jumps[3],
        (left_b + right_b) + jumps[4],
    ]


def swapped(five):
    return [five[0], five[2], five[1], five[4], five[3]]


def tile(i):
    return pl.ds(pl.multiple_of(i * SUB, SUB), SUB)


def rows_a_turn(n):
    return (n + 2 * REACH - 3 + 1) // 2


def run_stages(n, stages, spin, edges):
    each = rows_a_turn(n)
    half_dt = 0.5 * time_step
    low_mask, high_mask = edges
    first, last = REACH, REACH + n - 1

    right_of = lambda x: pltpu.roll(x, LANES - 1, 1)
    left_of = lambda x: pltpu.roll(x, 1, 1)

    def radial_states(halves, centres):
        jumps = [h[SUB:] - h[:-SUB] for h in halves]
        slopes = [minmod(d[:-SUB], d[SUB:]) for d in jumps]
        lower = [x - g for x, g in zip(centres, slopes)]
        upper = [x + g for x, g in zip(centres, slopes)]
        return swapped([x[:-SUB] for x in upper]), swapped([x[SUB:] for x in lower])

    def work(stage, i0, before):
        src, dst = stage, (stage & 1) + 1
        weight = jnp.where(stage == 0, 1.0, jnp.where(stage == 1, 0.25, 2.0 / 3.0))
        keep = jnp.where(stage == 0, 0.0, jnp.where(stage == 1, 0.75, 1.0 / 3.0))
        some = lambda first, count: pl.ds(pl.multiple_of((i0 + first) * SUB, SUB), count * SUB)
        here = some(0, each)
        size = each * SUB
        rows = [stages[src, f, some(-1, each + 3), :] for f in range(FIELDS)]
        halves = [0.5 * x for x in rows]
        own = [x[SUB : SUB + size] for x in rows]
        half = [x[SUB : SUB + size] for x in halves]
        after = [right_of(x) for x in half]
        left, right = radial_states(halves, [x[SUB:-SUB] for x in rows])
        jump = [x - y for x, y in zip(after, half)]
        behind = [left_of(x) for x in jump]
        of_left = physical(left)
        of_right = physical(right)
        slopes = [minmod(x, y) for x, y in zip(behind, jump)]
        lower = [right_of(x - y) for x, y in zip(own, slopes)]
        upper = [x + y for x, y in zip(own, slopes)]
        of_upper = physical(upper)
        faces = swapped(face_twice(left, right, of_left, of_right))
        of_lower = physical(lower)
        azimuth = face_twice(upper, lower, of_upper, of_lower)
        shifted = [left_of(x) for x in azimuth]
        change = [x - jnp.concatenate([y, x[:-SUB]], axis=0) for x, y in zip(faces, before)]
        turn = spin[here, :]
        source = [None, (-0.5 * turn) * own[2], (2.0 * turn) * own[1], (-1.5 * turn) * own[4], None]
        partial = [x if y is None else x + y for x, y in zip(own, source)]
        starts = [keep * stages[0, f, here, :] for f in range(FIELDS)]
        for f in range(FIELDS):
            new = partial[f] - half_dt * ((azimuth[f] - shifted[f]) + change[f])
            stages[dst, f, here, :] = weight * new + starts[f]
        return [x[-SUB:] for x in faces]

    def run(stage, _):
        for f in range(FIELDS):
            inner = stages[stage, f, tile(first), :]
            outer = stages[stage, f, tile(last), :]
            for k in (1, 2):
                stages[stage, f, tile(first - k), :] = jnp.where(low_mask, inner, stages[stage, f, tile(first - k), :])
                stages[stage, f, tile(last + k), :] = jnp.where(high_mask, outer, stages[stage, f, tile(last + k), :])
        lo = 2 * stage + 1
        count = n + 2 * REACH - 3 - 4 * stage
        before = (jnp.zeros((SUB, LANES), jnp.float32),) * FIELDS
        turns = lax.div(count + each - 1, each)
        lax.fori_loop(0, turns, lambda c, carried: tuple(work(stage, lo + c * each, list(carried))), before)
        return 0

    lax.fori_loop(0, STAGES, run, 0)


def spread(block, first, width):
    block = pltpu.roll(block, (LANES - first) % LANES, 1)
    lane = lax.broadcasted_iota(jnp.int32, block.shape, 1)
    while width < LANES:
        block = jnp.where(lane < width, block, pltpu.roll(block, width, 1))
        width *= 2
    return block


def pack_far(far, near, own_cells):
    sublane = lax.broadcasted_iota(jnp.int32, (SUB, LANES), 0)
    left = lax.broadcasted_iota(jnp.int32, (SUB, LANES), 1) < HALF

    for f in range(FIELDS):
        start = f * own_cells
        low = near[start : start + own_cells, 0:LANES]
        high = near[start + own_cells - 2 * SUB : start + own_cells, LANES : 2 * LANES]
        before, last = high[0:SUB], high[SUB:]
        far[start : start + SUB, :] = jnp.where(left, low[0:SUB], pltpu.roll(last, HALF, 1))
        third = pltpu.roll(pltpu.roll(before, 1, 0), HALF, 1)
        fourth = pltpu.roll(last, 2, 0)
        second = low[SUB : 2 * SUB]
        mixed = jnp.where(sublane == 0, third, jnp.where(sublane == 1, fourth, second))
        far[start + SUB : start + 2 * SUB, :] = jnp.where(left, second, mixed)
        far[start + 2 * SUB : start + own_cells, :] = low[2 * SUB :]


def far_rows(far, start):
    left = lax.broadcasted_iota(jnp.int32, (SUB, LANES), 1) < HALF
    first = far[start : start + SUB, :]
    mixed = far[start + SUB : start + 2 * SUB, :]
    before = pltpu.roll(pltpu.roll(mixed, SUB - 1, 0), HALF, 1)
    last = jnp.where(left, pltpu.roll(first, HALF, 1), pltpu.roll(mixed, SUB - 2, 0))
    return before, last


def edge_kernel(place, density, momentum, magnetic, rotation, shifts, edge, ends, spin_in, shift_in, arrived):
    levels, own_cells, radius = density.shape
    on_low = place[0] == 0
    parts = radius // LANES
    split = 4 * own_cells
    columns = pl.ds(pl.multiple_of(jnp.where(on_low, radius - LANES, 0), LANES), LANES)
    copies = [
        pltpu.make_async_copy(rotation, spin_in, arrived.at[levels * FIELDS]),
        pltpu.make_async_copy(shifts, shift_in, arrived.at[levels * FIELDS + 1]),
    ]
    for level in range(levels):
        sources = [density.at[level, :, columns]] + [x.at[k, level, :, columns] for x in (momentum, magnetic) for k in range(2)]
        for f, x in enumerate(sources):
            at = ends.at[level, pl.ds(f * own_cells, own_cells), :]
            copies.append(pltpu.make_async_copy(x, at, arrived.at[level * FIELDS + f]))
    for copy in copies:
        copy.start()
    for copy in copies:
        copy.wait()
    wide = lambda ref: jnp.broadcast_to(
        jnp.where(on_low, ref[parts - 1 : parts, :], ref[0:1, :]).astype(jnp.float32), (own_cells, LANES)
    )
    turn = wide(spin_in) * time_step
    shift = wide(shift_in)
    zero = jnp.zeros((own_cells, LANES), jnp.float32)
    for level in range(levels):
        last = jnp.concatenate([ends[level, split:, :], turn, shift, zero], axis=0)
        for side, group in enumerate((ends[level, 0:split, :], last)):
            turned = group.T
            edge[level, :, side * LANES : (side + 1) * LANES] = jnp.where(on_low, turned[LANES - EXTRA :], turned[0:EXTRA])


def pack_kernel(levels, density, momentum, magnetic, edge, *outs):
    del edge
    nears, fars = outs[:levels], outs[levels:]
    own_cells = density.shape[1]
    for level in range(levels):
        sources = [density.at[level]] + [x.at[k, level] for x in (momentum, magnetic) for k in range(2)]
        for f, x in enumerate(sources):
            nears[level][f * own_cells : (f + 1) * own_cells, :] = x[...]
        pack_far(fars[level], nears[level], own_cells)


class Blocks:
    def __init__(self, row, n, radius, total, moved):
        self.on_low = row == 0
        self.n = n
        self.own_at = pl.multiple_of(jnp.where(self.on_low, EXTRA, EXTRA + moved), SUB)
        self.edge_at = pl.multiple_of(jnp.where(self.on_low, EXTRA + radius, moved), SUB)
        bounds = [[shift_bound(r * radius - (moved if r else 0) + n * k, total) for k in range(SLOTS)] for r in range(2)]
        self.bounds = [jnp.where(self.on_low, a, b) for a, b in zip(*bounds)]

    def rows_of(self, k):
        start = EXTRA - REACH + self.n * k
        return slice(start, start + DEALT)


def table_kernel(plans, place, side, rotation, shifts, *rest):
    outs, held = rest[:-1], rest[-1]
    radius = plans[0][1]
    own_cells = plans[0][2]
    wide_lane = lax.broadcasted_iota(jnp.int32, (DEALT, LANES), 1)
    front = wide_lane < HALF
    more = side[0, :, LANES : 2 * LANES]
    edges = [spread(more, own_cells, own_cells), spread(more, 2 * own_cells, own_cells)]
    own = []
    for ref, scale in ((rotation, time_step), (shifts, 1.0)):
        along = lambda part: jnp.broadcast_to(ref[part : part + 1, :].astype(jnp.float32), (LANES, LANES)).T
        own.append([along(part) * scale for part in range(radius // LANES)])
    for which, (n, radius, own_cells, total, moved) in enumerate(plans):
        spin, pick = outs[2 * which : 2 * which + 2]
        blocks = Blocks(place[0], n, radius, total, moved)
        for k in range(2):
            for part, x in enumerate(own[k]):
                held[2 * which + k, pl.ds(blocks.own_at + part * LANES, LANES), :] = x
            held[2 * which + k, pl.ds(blocks.edge_at, EXTRA), :] = edges[k]
        for j in range(SUB):
            low, high = blocks.rows_of(j), blocks.rows_of(SUB + j)
            turns = [jnp.where(front, held[2 * which + k, low, :], held[2 * which + k, high, :]) for k in range(2)]
            spin[pl.ds(j, DEALT, stride=SUB), :] = turns[0]
            bound = jnp.where(front, blocks.bounds[j], blocks.bounds[SUB + j])
            pick[pl.ds(j, DEALT, stride=SUB), :] = (wide_lane + (REACH + bound)) - turns[1].astype(jnp.int32)


def step_kernel(plan, refs, write, scratch):
    n, radius, own_cells, total, moved = plan
    place, own, own_edge, near, near_edge, far, spin, pick = refs
    cells, stages, packed, tops = scratch
    row = place[0]
    lane = lax.broadcasted_iota(jnp.int32, (SUB, LANES), 1)
    sublane = lax.broadcasted_iota(jnp.int32, (SUB, LANES), 0)
    blocks = Blocks(row, n, radius, total, moved)

    edge_lane = lax.broadcasted_iota(jnp.int32, (EXTRA, LANES), 1)
    parts = radius // LANES

    front = lax.broadcasted_iota(jnp.int32, (DEALT, LANES), 1) < HALF

    for f in range(FIELDS):
        tops[f] = jnp.concatenate(far_rows(far, f * own_cells), axis=0)

    def bring(f, _):
        rows = pl.ds(pl.multiple_of(f * own_cells, SUB), own_cells)
        start = pl.multiple_of(f * own_cells, SUB)
        for part in range(parts):
            columns = slice(part * LANES, (part + 1) * LANES)
            if part == 0:
                top = far[pl.ds(start, own_cells), :]
            else:
                gap = jnp.zeros((own_cells - 2 * SUB, LANES), jnp.float32)
                top = jnp.concatenate([gap, tops[f]], axis=0)
            block = jnp.concatenate([top, near[rows, columns], own[rows, columns]], axis=0)
            cells[f, pl.ds(blocks.own_at + part * LANES, LANES), 0 : 3 * own_cells] = block.T
        columns = pl.ds(pl.multiple_of(lax.div(f, 4) * LANES, LANES), LANES)
        lanes_at = lax.rem(f, 4) * own_cells
        cells[f, pl.ds(blocks.edge_at, EXTRA), :] = jnp.where(
            edge_lane < 2 * own_cells,
            pltpu.roll(near_edge[:, columns], lax.rem(LANES + own_cells - lanes_at, LANES), 1),
            pltpu.roll(own_edge[:, columns], lax.rem(LANES + 2 * own_cells - lanes_at, LANES), 1),
        )

        for j in range(SUB):
            low, high = j, SUB + j
            turn_low = (LANES - (2 * own_cells - REACH)) + blocks.bounds[low]
            turn_high = (HALF - (2 * own_cells - REACH)) + blocks.bounds[high]
            stages[0, f, pl.ds(j, DEALT, stride=SUB), :] = jnp.where(
                front,
                pltpu.roll(cells[f, blocks.rows_of(low), :], turn_low, 1),
                pltpu.roll(cells[f, blocks.rows_of(high), :], turn_high, 1),
            )
        return 0

    lax.fori_loop(0, FIELDS, bring, 0)

    edges = (
        (sublane == 0) & (lane < HALF) & (row == 0),
        (sublane == SUB - 1) & (lane >= HALF) & (row == total // radius - 1),
    )
    run_stages(n, stages, spin, edges)

    even = (lane & own_cells) == 0

    picked = (n + 1) // 2

    def shift(turn, _):
        for k in range(picked):
            i = turn * picked + k
            rows = tile(REACH + i)
            source = pick[rows, :]
            picks = [source & (LANES - 1), (source - own_cells) & (LANES - 1)]
            turned = [
                jnp.take_along_axis(stages[1, f, rows, :], picks[f % 2], axis=1, mode="promise_in_bounds")
                for f in range(FIELDS)
            ]
            stages[2, 0, tile(i), :] = jnp.where(even, turned[0], turned[1])
            stages[2, 1, tile(i), :] = jnp.where(even, turned[2], turned[3])
            stages[2, 2, tile(i), :] = turned[4]
        return 0

    lax.fori_loop(0, (n + picked - 1) // picked, shift, 0)
    narrow = lax.broadcasted_iota(jnp.int32, (n, LANES), 1) < HALF
    for j in range(SUB):
        one, two, three = [stages[2, g, pl.ds(j, n, stride=SUB), :] for g in range(3)]
        low = slice(EXTRA + n * j, EXTRA + n * (j + 1))
        high = slice(EXTRA + n * (SUB + j), EXTRA + n * (SUB + j + 1))
        packed[0, low, :] = jnp.where(narrow, one, pltpu.roll(two, HALF, 1))
        packed[0, high, :] = jnp.where(narrow, pltpu.roll(one, HALF, 1), two)
        packed[1, low, :] = three
        packed[1, high, :] = pltpu.roll(three, HALF, 1)
    for part in range(parts):
        rows = pl.ds(blocks.own_at + part * LANES, LANES)
        write.fields(slice(part * LANES, (part + 1) * LANES), packed[0, rows, :].T, packed[1, rows, :].T)
    write.edge(packed[0, pl.ds(blocks.edge_at, EXTRA), :], packed[1, pl.ds(blocks.edge_at, EXTRA), :])
    write.end()


class ToMessage:
    def __init__(self, near, far, own_cells):
        self.near, self.far, self.own_cells = near, far, own_cells

    def fields(self, columns, four, fifth):
        split = 4 * self.own_cells
        self.near[0:split, columns] = four
        self.near[split : split + self.own_cells, columns] = fifth[0 : self.own_cells]

    def edge(self, first, second):
        tail = FIELDS * self.own_cells
        self.near[tail : tail + EXTRA, 0:LANES] = first
        self.near[tail : tail + EXTRA, LANES : 2 * LANES] = second

    def end(self):
        pack_far(self.far, self.near, self.own_cells)


class ToBuffer:
    def __init__(self, buffer):
        self.buffer = buffer

    def fields(self, columns, four, fifth):
        split = four.shape[0]
        self.buffer[0:split, columns] = four
        self.buffer[split:, columns] = fifth[0 : self.buffer.shape[0] - split]

    def edge(self, first, second):
        pass

    def end(self):
        pass


def copies_out(level, buffer, outs, sent):
    density, momentum, magnetic = outs
    cells = density.shape[1]
    targets = [density.at[level]] + [x.at[k, level] for x in (momentum, magnetic) for k in range(2)]
    return [
        pltpu.make_async_copy(buffer.at[pl.ds(f * cells, cells), :], x, sent.at[level * FIELDS + f])
        for f, x in enumerate(targets)
    ]


def tall_of(n):
    return EXTRA + SLOTS * n + 2 * SUB


def step_scratch(n):
    return [
        pltpu.VMEM((FIELDS, tall_of(n), LANES), jnp.float32),
        pltpu.VMEM((STAGES, FIELDS, TALL * SUB, LANES), jnp.float32),
        pltpu.VMEM((2, tall_of(n), LANES), jnp.float32),
        pltpu.VMEM((FIELDS, 2 * SUB, LANES), jnp.float32),
    ]


vmem = pl.BlockSpec(memory_space=pltpu.VMEM)
smem = pl.BlockSpec(memory_space=pltpu.SMEM)
f32 = lambda *s: jax.ShapeDtypeStruct(s, jnp.float32)
params = pltpu.CompilerParams(vmem_limit_bytes=VMEM_LIMIT)
cost = pl.CostEstimate(flops=9_000_000_000, bytes_accessed=29_000_000, transcendentals=0)


def first_step(plan, level, operands):
    n, radius, own_cells, total, moved = plan

    def kernel(place, own, near, far, side, corner, spin, pick, near_out, far_out, *scratch):
        refs = (place, own, side.at[level], near, corner.at[level], far, spin, pick)
        step_kernel(plan, refs, ToMessage(near_out, far_out, own_cells), scratch)

    return pl.pallas_call(
        kernel,
        out_shape=[f32(FIELDS * own_cells + EXTRA, radius), f32(FIELDS * own_cells, LANES)],
        in_specs=[smem] + [vmem] * 7,
        out_specs=[vmem] * 2,
        scratch_shapes=step_scratch(n),
        compiler_params=params,
        cost_estimate=cost,
        name="first_step",
    )(*operands)


def last_step(plan, level, operands, done, levels):
    n, radius, own_cells, total, moved = plan
    final = level == levels - 1
    tail = pl.ds(FIELDS * own_cells, EXTRA)
    buffer = f32(FIELDS * own_cells, radius)

    def kernel(place, own, near, far, spin, pick, *rest):
        refs = (place, own, own.at[tail, :], near, near.at[tail, :], far, spin, pick)
        if not final:
            step_kernel(plan, refs, ToBuffer(rest[0]), rest[1:])
            return
        ready, outs, scratch = rest[: levels - 1], rest[levels - 1 : levels + 2], rest[levels + 2 :]
        last, sent = scratch[-2:]
        copies = []
        for k, x in enumerate(ready):
            copies += copies_out(k, x, outs, sent)
        for copy in copies:
            copy.start()
        step_kernel(plan, refs, ToBuffer(last), scratch[:-2])
        rest_of = copies_out(level, last, outs, sent)
        for copy in rest_of:
            copy.start()
        for copy in copies + rest_of:
            copy.wait()

    if final:
        out_shape = [f32(levels, own_cells, radius), f32(2, levels, own_cells, radius), f32(2, levels, own_cells, radius)]
        more = [pltpu.VMEM((FIELDS * own_cells, radius), jnp.float32), pltpu.SemaphoreType.DMA((levels * FIELDS,))]
    else:
        out_shape = buffer
        more = []
    return pl.pallas_call(
        kernel,
        out_shape=out_shape,
        in_specs=[smem] + [vmem] * (5 + len(done)),
        out_specs=[pl.BlockSpec(memory_space=pltpu.HBM)] * 3 if final else vmem,
        scratch_shapes=step_scratch(n) + more,
        compiler_params=params,
        cost_estimate=cost,
        name="last_step",
    )(*operands, *done)


def body(density, momentum, magnetic, rotation, shifts):
    phi_count = lax.axis_size("phi")
    row_count = lax.axis_size("row")
    levels, own_cells, radius = density.shape
    total = radius * row_count
    parts = radius // LANES
    n = radius // SLOTS
    need = [max(shift_bound(k * HALF, total) + REACH - own_cells, 0) for k in range(radius // HALF)]
    assert row_count == 2 and radius == 2 * LANES and own_cells == HALF // 2
    assert need[0] <= own_cells and need[1] <= own_cells - SUB - 2 and need[2] <= SUB + 1 and need[3] <= 1

    row = lax.axis_index("row")
    place = jnp.reshape(row, (1,)).astype(jnp.int32)
    send_near = lambda x: lax.ppermute(x, "phi", [(p, (p + 1) % phi_count) for p in range(phi_count)])
    send_far = lambda x: lax.ppermute(x, "phi", [(p, (p + 2) % phi_count) for p in range(phi_count)])
    here = lambda p, r: (p % phi_count) * row_count + r
    diagonal = [(here(p, r), here(p + 1, 1 - r)) for p in range(phi_count) for r in range(row_count)]
    send_corner = lambda x: lax.ppermute(x, ("phi", "row"), diagonal)
    send_side = lambda x: lax.ppermute(x, "row", [(0, 1), (1, 0)])

    spins, turns = rotation.reshape(parts, LANES), shifts.reshape(parts, LANES)
    near_message = f32(FIELDS * own_cells, radius)
    far_message = f32(FIELDS * own_cells, LANES)
    edge = pl.pallas_call(
        edge_kernel,
        out_shape=f32(levels, EXTRA, 2 * LANES),
        in_specs=[smem] + [pl.BlockSpec(memory_space=pltpu.HBM)] * 5,
        out_specs=vmem,
        scratch_shapes=[
            pltpu.VMEM((levels, FIELDS * own_cells, LANES), jnp.float32),
            pltpu.VMEM((parts, LANES), jnp.float32),
            pltpu.VMEM((parts, LANES), jnp.int32),
            pltpu.SemaphoreType.DMA((levels * FIELDS + 2,)),
        ],
        compiler_params=pltpu.CompilerParams(vmem_limit_bytes=EDGE_LIMIT),
        name="edges",
    )(place, density, momentum, magnetic, spins, turns)
    packed = pl.pallas_call(
        lambda *refs: pack_kernel(levels, *refs),
        out_shape=[near_message] * levels + [far_message] * levels,
        in_specs=[vmem] * 3 + [pl.BlockSpec(memory_space=pl.ANY)],
        out_specs=[vmem] * (2 * levels),
        compiler_params=params,
        cost_estimate=cost,
        name="pack",
    )(density, momentum, magnetic, edge)
    owns, fars = packed[:levels], packed[levels:]
    side = send_side(edge)
    corner = send_corner(edge)
    wide = (n + 1, radius, own_cells, total, EXTRA)
    plain = (n, radius, own_cells, total, 0)
    i32 = jax.ShapeDtypeStruct((TALL * SUB, LANES), jnp.int32)
    tables = pl.pallas_call(
        lambda *refs: table_kernel((wide, plain), *refs),
        out_shape=[f32(TALL * SUB, LANES), i32] * 2,
        in_specs=[smem] + [vmem] * 3,
        out_specs=[vmem] * 4,
        scratch_shapes=[pltpu.VMEM((4, tall_of(n + 1), LANES), jnp.float32)],
        compiler_params=params,
        name="tables",
    )(place, side, spins, turns)
    moved = []
    for own, far in zip(owns, fars):
        if moved:
            own, far, _ = lax.optimization_barrier((own, far, tables[0]))
        moved.append((send_near(own), send_far(far)))
    states = []
    for level in range(levels):
        near, far = moved[level]
        states.append(first_step(wide, level, (place, owns[level], near, far, side, corner, *tables[:2])))
    moved = [(send_near(own), send_far(far)) for own, far in states]
    done = ()
    for level in range(levels):
        near, far = moved[level]
        operands = (place, states[level][0], near, far, *tables[2:])
        result = last_step(plain, level, operands, done if level == levels - 1 else (), levels)
        done += (result,)
    return tuple(result)


def solution(mesh):
    placed = (
        P(None, "phi", "row"),
        P(None, None, "phi", "row"),
        P(None, None, "phi", "row"),
        P("row"),
        P("row"),
    )
    return jax.shard_map(
        body,
        mesh=mesh,
        in_specs=placed,
        out_specs=(P(None, "phi", "row"), P(None, None, "phi", "row"), P(None, None, "phi", "row")),
        check_vma=False,
    )
```

```python
import jax
import jax.numpy as jnp
from jax import lax
from jax.experimental import pallas as pl
from jax.experimental.pallas import tpu as pltpu
from jax.sharding import PartitionSpec as P

STEPS = 2
SMIN = 8
SMAX = 56
STAGES = 3
REACH = 2 * STAGES
FIELDS = 5
LANES = 128
SUB = 8
HALF = LANES // 2
SLOTS = 2 * SUB
EXTRA = 2 * SUB
DEALT = 32
TALL = 40
VMEM_LIMIT = 32 * 1024 * 1024
EDGE_LIMIT = 60 * 1024 * 1024

time_step = 0.08


def shift_bound(first_row, rows):
    d = rows - 1 - first_row
    return min(SMIN + (SMAX - SMIN - 1) * d * d // ((rows - 1) * (rows - 1)) + 1, SMAX)


def minmod(lower, upper):
    return jnp.maximum(jnp.minimum(lower, 0.0), jnp.minimum(upper, jnp.maximum(lower, 0.0)))


def physical(state):
    rho, mn, mt, bn, bt = state
    inverse = pltpu.reciprocal(rho, approx=True)
    bn_sq = bn * bn
    bt_sq = bt * bt
    vn = mn * inverse
    vt = mt * inverse
    inside = (bn_sq + bt_sq) * inverse + 1.0
    root = lax.rsqrt(inside)
    ram = mn * vn + rho
    tension = bt_sq - bn_sq
    flux_t = mt * vn - bn * bt
    flux_b = bt * vn - bn * vt
    speed = jnp.abs(vn) + inside * root
    return ram, tension, flux_t, flux_b, speed


def face_twice(left, right, of_left, of_right):
    left_ram, left_tension, left_t, left_b, left_speed = of_left
    right_ram, right_tension, right_t, right_b, right_speed = of_right
    bound = jnp.maximum(left_speed, right_speed)
    jumps = [bound * (l - r) for l, r in zip(left, right)]
    return [
        (left[1] + right[1]) + jumps[0],
        ((left_ram + right_ram) + 0.5 * (left_tension + right_tension)) + jumps[1],
        (left_t + right_t) + jumps[2],
        jumps[3],
        (left_b + right_b) + jumps[4],
    ]


def swapped(five):
    return [five[0], five[2], five[1], five[4], five[3]]


def tile(i):
    return pl.ds(pl.multiple_of(i * SUB, SUB), SUB)


def rows_a_turn(n):
    return (n + 2 * REACH - 4 + 1) // 2


def run_stages(n, stages, spin, edges):
    each = rows_a_turn(n)
    half_dt = 0.5 * time_step
    low_mask, high_mask = edges
    first, last = REACH, REACH + n - 1

    right_of = lambda x: pltpu.roll(x, LANES - 1, 1)
    left_of = lambda x: pltpu.roll(x, 1, 1)

    def radial_states(halves, centres):
        jumps = [h[SUB:] - h[:-SUB] for h in halves]
        slopes = [minmod(d[:-SUB], d[SUB:]) for d in jumps]
        lower = [x - g for x, g in zip(centres, slopes)]
        upper = [x + g for x, g in zip(centres, slopes)]
        return swapped([x[:-SUB] for x in upper]), swapped([x[SUB:] for x in lower])

    def work(stage, i0, before):
        src, dst = stage, (stage & 1) + 1
        weight = jnp.where(stage == 0, 1.0, jnp.where(stage == 1, 0.25, 2.0 / 3.0))
        keep = jnp.where(stage == 0, 0.0, jnp.where(stage == 1, 0.75, 1.0 / 3.0))
        some = lambda first, count: pl.ds(pl.multiple_of((i0 + first) * SUB, SUB), count * SUB)
        here = some(0, each)
        size = each * SUB
        rows = [stages[src, f, some(-1, each + 3), :] for f in range(FIELDS)]
        halves = [0.5 * x for x in rows]
        own = [x[SUB : SUB + size] for x in rows]
        half = [x[SUB : SUB + size] for x in halves]
        after = [right_of(x) for x in half]
        left, right = radial_states(halves, [x[SUB:-SUB] for x in rows])
        jump = [x - y for x, y in zip(after, half)]
        behind = [left_of(x) for x in jump]
        of_left = physical(left)
        of_right = physical(right)
        slopes = [minmod(x, y) for x, y in zip(behind, jump)]
        lower = [right_of(x - y) for x, y in zip(own, slopes)]
        upper = [x + y for x, y in zip(own, slopes)]
        of_upper = physical(upper)
        faces = swapped(face_twice(left, right, of_left, of_right))
        of_lower = physical(lower)
        azimuth = face_twice(upper, lower, of_upper, of_lower)
        shifted = [left_of(x) for x in azimuth]
        change = [x - jnp.concatenate([y, x[:-SUB]], axis=0) for x, y in zip(faces, before)]
        turn = spin[here, :]
        source = [None, (-0.5 * turn) * own[2], (2.0 * turn) * own[1], (-1.5 * turn) * own[4], None]
        partial = [x if y is None else x + y for x, y in zip(own, source)]
        starts = [keep * stages[0, f, here, :] for f in range(FIELDS)]
        for f in range(FIELDS):
            new = partial[f] - half_dt * ((azimuth[f] - shifted[f]) + change[f])
            stages[dst, f, here, :] = weight * new + starts[f]
        return [x[-SUB:] for x in faces]

    def run(stage, _):
        for f in range(FIELDS):
            inner = stages[stage, f, tile(first), :]
            outer = stages[stage, f, tile(last), :]
            for k in (1, 2):
                stages[stage, f, tile(first - k), :] = jnp.where(low_mask, inner, stages[stage, f, tile(first - k), :])
                stages[stage, f, tile(last + k), :] = jnp.where(high_mask, outer, stages[stage, f, tile(last + k), :])
        count = n + 2 * REACH - 4 - 4 * stage
        if n % 2 == 0:
            lo = 2 * stage + 2
            rows = [stages[stage, f, pl.ds(pl.multiple_of((lo - 2) * SUB, SUB), 4 * SUB), :] for f in range(FIELDS)]
            left, right = radial_states([0.5 * x for x in rows], [x[SUB:-SUB] for x in rows])
            before = tuple(swapped(face_twice(left, right, physical(left), physical(right))))
        else:
            lo = 2 * stage + 1
            count = count + 1
            before = (jnp.zeros((SUB, LANES), jnp.float32),) * FIELDS
        turns = lax.div(count + each - 1, each)
        lax.fori_loop(0, turns, lambda c, carried: tuple(work(stage, lo + c * each, list(carried))), before)
        return 0

    lax.fori_loop(0, STAGES, run, 0)


def spread(block, first, width):
    block = pltpu.roll(block, (LANES - first) % LANES, 1)
    lane = lax.broadcasted_iota(jnp.int32, block.shape, 1)
    while width < LANES:
        block = jnp.where(lane < width, block, pltpu.roll(block, width, 1))
        width *= 2
    return block


def pack_far(far, near, own_cells):
    sublane = lax.broadcasted_iota(jnp.int32, (SUB, LANES), 0)
    left = lax.broadcasted_iota(jnp.int32, (SUB, LANES), 1) < HALF

    for f in range(FIELDS):
        start = f * own_cells
        low = near[start : start + own_cells, 0:LANES]
        high = near[start + own_cells - 2 * SUB : start + own_cells, LANES : 2 * LANES]
        before, last = high[0:SUB], high[SUB:]
        far[start : start + SUB, :] = jnp.where(left, low[0:SUB], pltpu.roll(last, HALF, 1))
        third = pltpu.roll(pltpu.roll(before, 1, 0), HALF, 1)
        fourth = pltpu.roll(last, 2, 0)
        second = low[SUB : 2 * SUB]
        mixed = jnp.where(sublane == 0, third, jnp.where(sublane == 1, fourth, second))
        far[start + SUB : start + 2 * SUB, :] = jnp.where(left, second, mixed)
        far[start + 2 * SUB : start + own_cells, :] = low[2 * SUB :]


def far_rows(far, start):
    left = lax.broadcasted_iota(jnp.int32, (SUB, LANES), 1) < HALF
    first = far[start : start + SUB, :]
    mixed = far[start + SUB : start + 2 * SUB, :]
    before = pltpu.roll(pltpu.roll(mixed, SUB - 1, 0), HALF, 1)
    last = jnp.where(left, pltpu.roll(first, HALF, 1), pltpu.roll(mixed, SUB - 2, 0))
    return before, last


def edge_kernel(place, density, momentum, magnetic, rotation, shifts, edge, ends, spin_in, shift_in, arrived):
    levels, own_cells, radius = density.shape
    on_low = place[0] == 0
    parts = radius // LANES
    split = 4 * own_cells
    columns = pl.ds(pl.multiple_of(jnp.where(on_low, radius - LANES, 0), LANES), LANES)
    copies = [
        pltpu.make_async_copy(rotation, spin_in, arrived.at[levels * FIELDS]),
        pltpu.make_async_copy(shifts, shift_in, arrived.at[levels * FIELDS + 1]),
    ]
    for level in range(levels):
        sources = [density.at[level, :, columns]] + [x.at[k, level, :, columns] for x in (momentum, magnetic) for k in range(2)]
        for f, x in enumerate(sources):
            at = ends.at[level, pl.ds(f * own_cells, own_cells), :]
            copies.append(pltpu.make_async_copy(x, at, arrived.at[level * FIELDS + f]))
    for copy in copies:
        copy.start()
    for copy in copies:
        copy.wait()
    wide = lambda ref: jnp.broadcast_to(
        jnp.where(on_low, ref[parts - 1 : parts, :], ref[0:1, :]).astype(jnp.float32), (own_cells, LANES)
    )
    turn = wide(spin_in) * time_step
    shift = wide(shift_in)
    zero = jnp.zeros((own_cells, LANES), jnp.float32)
    for level in range(levels):
        last = jnp.concatenate([ends[level, split:, :], turn, shift, zero], axis=0)
        for side, group in enumerate((ends[level, 0:split, :], last)):
            turned = group.T
            edge[level, :, side * LANES : (side + 1) * LANES] = jnp.where(on_low, turned[LANES - EXTRA :], turned[0:EXTRA])


def pack_kernel(levels, density, momentum, magnetic, edge, *outs):
    del edge
    nears, fars = outs[:levels], outs[levels:]
    own_cells = density.shape[1]
    for level in range(levels):
        sources = [density.at[level]] + [x.at[k, level] for x in (momentum, magnetic) for k in range(2)]
        for f, x in enumerate(sources):
            nears[level][f * own_cells : (f + 1) * own_cells, :] = x[...]
        pack_far(fars[level], nears[level], own_cells)


class Blocks:
    def __init__(self, row, n, radius, total, moved):
        self.on_low = row == 0
        self.n = n
        self.own_at = pl.multiple_of(jnp.where(self.on_low, EXTRA, EXTRA + moved), SUB)
        self.edge_at = pl.multiple_of(jnp.where(self.on_low, EXTRA + radius, moved), SUB)
        bounds = [[shift_bound(r * radius - (moved if r else 0) + n * k, total) for k in range(SLOTS)] for r in range(2)]
        self.bounds = [jnp.where(self.on_low, a, b) for a, b in zip(*bounds)]

    def rows_of(self, k):
        start = EXTRA - REACH + self.n * k
        return slice(start, start + DEALT)


def table_kernel(plans, place, side, rotation, shifts, *rest):
    outs, held = rest[:-1], rest[-1]
    radius = plans[0][1]
    own_cells = plans[0][2]
    wide_lane = lax.broadcasted_iota(jnp.int32, (DEALT, LANES), 1)
    front = wide_lane < HALF
    more = side[0, :, LANES : 2 * LANES]
    edges = [spread(more, own_cells, own_cells), spread(more, 2 * own_cells, own_cells)]
    own = []
    for ref, scale in ((rotation, time_step), (shifts, 1.0)):
        along = lambda part: jnp.broadcast_to(ref[part : part + 1, :].astype(jnp.float32), (LANES, LANES)).T
        own.append([along(part) * scale for part in range(radius // LANES)])
    for which, (n, radius, own_cells, total, moved) in enumerate(plans):
        spin, pick = outs[2 * which : 2 * which + 2]
        blocks = Blocks(place[0], n, radius, total, moved)
        for k in range(2):
            for part, x in enumerate(own[k]):
                held[2 * which + k, pl.ds(blocks.own_at + part * LANES, LANES), :] = x
            held[2 * which + k, pl.ds(blocks.edge_at, EXTRA), :] = edges[k]
        for j in range(SUB):
            low, high = blocks.rows_of(j), blocks.rows_of(SUB + j)
            turns = [jnp.where(front, held[2 * which + k, low, :], held[2 * which + k, high, :]) for k in range(2)]
            spin[pl.ds(j, DEALT, stride=SUB), :] = turns[0]
            bound = jnp.where(front, blocks.bounds[j], blocks.bounds[SUB + j])
            pick[pl.ds(j, DEALT, stride=SUB), :] = (wide_lane + (REACH + bound)) - turns[1].astype(jnp.int32)


def step_kernel(plan, refs, write, scratch):
    n, radius, own_cells, total, moved = plan
    place, own, own_edge, near, near_edge, far, spin, pick = refs
    cells, stages, packed, tops = scratch
    row = place[0]
    lane = lax.broadcasted_iota(jnp.int32, (SUB, LANES), 1)
    sublane = lax.broadcasted_iota(jnp.int32, (SUB, LANES), 0)
    blocks = Blocks(row, n, radius, total, moved)

    edge_lane = lax.broadcasted_iota(jnp.int32, (EXTRA, LANES), 1)
    parts = radius // LANES

    front = lax.broadcasted_iota(jnp.int32, (DEALT, LANES), 1) < HALF

    for f in range(FIELDS):
        tops[f] = jnp.concatenate(far_rows(far, f * own_cells), axis=0)

    def bring(turn, _):
        dealt = jnp.maximum(turn - 1, 0)
        for j in range(SUB):
            low, high = j, SUB + j
            turn_low = (LANES - (2 * own_cells - REACH)) + blocks.bounds[low]
            turn_high = (HALF - (2 * own_cells - REACH)) + blocks.bounds[high]
            stages[0, dealt, pl.ds(j, DEALT, stride=SUB), :] = jnp.where(
                front,
                pltpu.roll(cells[dealt, blocks.rows_of(low), :], turn_low, 1),
                pltpu.roll(cells[dealt, blocks.rows_of(high), :], turn_high, 1),
            )
        f = jnp.minimum(turn, FIELDS - 1)
        rows = pl.ds(pl.multiple_of(f * own_cells, SUB), own_cells)
        start = pl.multiple_of(f * own_cells, SUB)
        for part in range(parts):
            columns = slice(part * LANES, (part + 1) * LANES)
            if part == 0:
                top = far[pl.ds(start, own_cells), :]
            else:
                gap = jnp.zeros((own_cells - 2 * SUB, LANES), jnp.float32)
                top = jnp.concatenate([gap, tops[f]], axis=0)
            fill = jnp.zeros((own_cells, LANES), jnp.float32)
            block = jnp.concatenate([top, near[rows, columns], own[rows, columns], fill], axis=0)
            cells[f, pl.ds(blocks.own_at + part * LANES, LANES), :] = block.T
        columns = pl.ds(pl.multiple_of(lax.div(f, 4) * LANES, LANES), LANES)
        lanes_at = lax.rem(f, 4) * own_cells
        cells[f, pl.ds(blocks.edge_at, EXTRA), :] = jnp.where(
            edge_lane < 2 * own_cells,
            pltpu.roll(near_edge[:, columns], lax.rem(LANES + own_cells - lanes_at, LANES), 1),
            pltpu.roll(own_edge[:, columns], lax.rem(LANES + 2 * own_cells - lanes_at, LANES), 1),
        )
        return 0

    lax.fori_loop(0, FIELDS + 1, bring, 0)

    edges = (
        (sublane == 0) & (lane < HALF) & (row == 0),
        (sublane == SUB - 1) & (lane >= HALF) & (row == total // radius - 1),
    )
    run_stages(n, stages, spin, edges)

    even = (lane & own_cells) == 0

    picked = (n + 1) // 2

    def shift(turn, _):
        for k in range(picked):
            i = turn * picked + k
            rows = tile(REACH + i)
            source = pick[rows, :]
            picks = [source & (LANES - 1), (source - own_cells) & (LANES - 1)]
            turned = [
                jnp.take_along_axis(stages[1, f, rows, :], picks[f % 2], axis=1, mode="promise_in_bounds")
                for f in range(FIELDS)
            ]
            stages[2, 0, tile(i), :] = jnp.where(even, turned[0], turned[1])
            stages[2, 1, tile(i), :] = jnp.where(even, turned[2], turned[3])
            stages[2, 2, tile(i), :] = turned[4]
        return 0

    lax.fori_loop(0, (n + picked - 1) // picked, shift, 0)
    narrow = lax.broadcasted_iota(jnp.int32, (n, LANES), 1) < HALF
    for j in range(SUB):
        one, two, three = [stages[2, g, pl.ds(j, n, stride=SUB), :] for g in range(3)]
        low = slice(EXTRA + n * j, EXTRA + n * (j + 1))
        high = slice(EXTRA + n * (SUB + j), EXTRA + n * (SUB + j + 1))
        packed[0, low, :] = jnp.where(narrow, one, pltpu.roll(two, HALF, 1))
        packed[0, high, :] = jnp.where(narrow, pltpu.roll(one, HALF, 1), two)
        packed[1, low, :] = three
        packed[1, high, :] = pltpu.roll(three, HALF, 1)
    for part in range(parts):
        rows = pl.ds(blocks.own_at + part * LANES, LANES)
        write.fields(slice(part * LANES, (part + 1) * LANES), packed[0, rows, :].T, packed[1, rows, :].T)
    write.edge(packed[0, pl.ds(blocks.edge_at, EXTRA), :], packed[1, pl.ds(blocks.edge_at, EXTRA), :])
    write.end()


class ToMessage:
    def __init__(self, near, far, own_cells):
        self.near, self.far, self.own_cells = near, far, own_cells

    def fields(self, columns, four, fifth):
        split = 4 * self.own_cells
        self.near[0:split, columns] = four
        self.near[split : split + self.own_cells, columns] = fifth[0 : self.own_cells]

    def edge(self, first, second):
        tail = FIELDS * self.own_cells
        self.near[tail : tail + EXTRA, 0:LANES] = first
        self.near[tail : tail + EXTRA, LANES : 2 * LANES] = second

    def end(self):
        pack_far(self.far, self.near, self.own_cells)


class ToBuffer:
    def __init__(self, buffer):
        self.buffer = buffer

    def fields(self, columns, four, fifth):
        split = four.shape[0]
        self.buffer[0:split, columns] = four
        self.buffer[split:, columns] = fifth[0 : self.buffer.shape[0] - split]

    def edge(self, first, second):
        pass

    def end(self):
        pass


def copies_out(level, buffer, outs, sent):
    density, momentum, magnetic = outs
    cells = density.shape[1]
    targets = [density.at[level]] + [x.at[k, level] for x in (momentum, magnetic) for k in range(2)]
    return [
        pltpu.make_async_copy(buffer.at[pl.ds(f * cells, cells), :], x, sent.at[level * FIELDS + f])
        for f, x in enumerate(targets)
    ]


def tall_of(n):
    return EXTRA + SLOTS * n + 2 * SUB


def step_scratch(n):
    return [
        pltpu.VMEM((FIELDS, tall_of(n), LANES), jnp.float32),
        pltpu.VMEM((STAGES, FIELDS, TALL * SUB, LANES), jnp.float32),
        pltpu.VMEM((2, tall_of(n), LANES), jnp.float32),
        pltpu.VMEM((FIELDS, 2 * SUB, LANES), jnp.float32),
    ]


vmem = pl.BlockSpec(memory_space=pltpu.VMEM)
smem = pl.BlockSpec(memory_space=pltpu.SMEM)
f32 = lambda *s: jax.ShapeDtypeStruct(s, jnp.float32)
params = pltpu.CompilerParams(vmem_limit_bytes=VMEM_LIMIT)
cost = pl.CostEstimate(flops=9_000_000_000, bytes_accessed=29_000_000, transcendentals=0)


def first_step(plan, level, operands):
    n, radius, own_cells, total, moved = plan

    def kernel(place, own, near, far, side, corner, spin, pick, near_out, far_out, *scratch):
        refs = (place, own, side.at[level], near, corner.at[level], far, spin, pick)
        step_kernel(plan, refs, ToMessage(near_out, far_out, own_cells), scratch)

    return pl.pallas_call(
        kernel,
        out_shape=[f32(FIELDS * own_cells + EXTRA, radius), f32(FIELDS * own_cells, LANES)],
        in_specs=[smem] + [vmem] * 7,
        out_specs=[vmem] * 2,
        scratch_shapes=step_scratch(n),
        compiler_params=params,
        cost_estimate=cost,
        name="first_step",
    )(*operands)


def last_step(plan, level, operands, done, levels):
    n, radius, own_cells, total, moved = plan
    final = level == levels - 1
    tail = pl.ds(FIELDS * own_cells, EXTRA)
    buffer = f32(FIELDS * own_cells, radius)

    def kernel(place, own, near, far, spin, pick, *rest):
        refs = (place, own, own.at[tail, :], near, near.at[tail, :], far, spin, pick)
        if not final:
            step_kernel(plan, refs, ToBuffer(rest[0]), rest[1:])
            return
        ready, outs, scratch = rest[: levels - 1], rest[levels - 1 : levels + 2], rest[levels + 2 :]
        last, sent = scratch[-2:]
        copies = []
        for k, x in enumerate(ready):
            copies += copies_out(k, x, outs, sent)
        for copy in copies:
            copy.start()
        step_kernel(plan, refs, ToBuffer(last), scratch[:-2])
        rest_of = copies_out(level, last, outs, sent)
        for copy in rest_of:
            copy.start()
        for copy in copies + rest_of:
            copy.wait()

    if final:
        out_shape = [f32(levels, own_cells, radius), f32(2, levels, own_cells, radius), f32(2, levels, own_cells, radius)]
        more = [pltpu.VMEM((FIELDS * own_cells, radius), jnp.float32), pltpu.SemaphoreType.DMA((levels * FIELDS,))]
    else:
        out_shape = buffer
        more = []
    return pl.pallas_call(
        kernel,
        out_shape=out_shape,
        in_specs=[smem] + [vmem] * (5 + len(done)),
        out_specs=[pl.BlockSpec(memory_space=pltpu.HBM)] * 3 if final else vmem,
        scratch_shapes=step_scratch(n) + more,
        compiler_params=params,
        cost_estimate=cost,
        name="last_step",
    )(*operands, *done)


def body(density, momentum, magnetic, rotation, shifts):
    phi_count = lax.axis_size("phi")
    row_count = lax.axis_size("row")
    levels, own_cells, radius = density.shape
    total = radius * row_count
    parts = radius // LANES
    n = radius // SLOTS
    need = [max(shift_bound(k * HALF, total) + REACH - own_cells, 0) for k in range(radius // HALF)]
    assert row_count == 2 and radius == 2 * LANES and own_cells == HALF // 2
    assert need[0] <= own_cells and need[1] <= own_cells - SUB - 2 and need[2] <= SUB + 1 and need[3] <= 1

    row = lax.axis_index("row")
    place = jnp.reshape(row, (1,)).astype(jnp.int32)
    send_near = lambda x: lax.ppermute(x, "phi", [(p, (p + 1) % phi_count) for p in range(phi_count)])
    send_far = lambda x: lax.ppermute(x, "phi", [(p, (p + 2) % phi_count) for p in range(phi_count)])
    here = lambda p, r: (p % phi_count) * row_count + r
    diagonal = [(here(p, r), here(p + 1, 1 - r)) for p in range(phi_count) for r in range(row_count)]
    send_corner = lambda x: lax.ppermute(x, ("phi", "row"), diagonal)
    send_side = lambda x: lax.ppermute(x, "row", [(0, 1), (1, 0)])

    spins, turns = rotation.reshape(parts, LANES), shifts.reshape(parts, LANES)
    near_message = f32(FIELDS * own_cells, radius)
    far_message = f32(FIELDS * own_cells, LANES)
    edge = pl.pallas_call(
        edge_kernel,
        out_shape=f32(levels, EXTRA, 2 * LANES),
        in_specs=[smem] + [pl.BlockSpec(memory_space=pltpu.HBM)] * 5,
        out_specs=vmem,
        scratch_shapes=[
            pltpu.VMEM((levels, FIELDS * own_cells, LANES), jnp.float32),
            pltpu.VMEM((parts, LANES), jnp.float32),
            pltpu.VMEM((parts, LANES), jnp.int32),
            pltpu.SemaphoreType.DMA((levels * FIELDS + 2,)),
        ],
        compiler_params=pltpu.CompilerParams(vmem_limit_bytes=EDGE_LIMIT),
        name="edges",
    )(place, density, momentum, magnetic, spins, turns)
    packed = pl.pallas_call(
        lambda *refs: pack_kernel(levels, *refs),
        out_shape=[near_message] * levels + [far_message] * levels,
        in_specs=[vmem] * 3 + [pl.BlockSpec(memory_space=pl.ANY)],
        out_specs=[vmem] * (2 * levels),
        compiler_params=params,
        cost_estimate=cost,
        name="pack",
    )(density, momentum, magnetic, edge)
    owns, fars = packed[:levels], packed[levels:]
    side = send_side(edge)
    corner = send_corner(edge)
    wide = (n + 1, radius, own_cells, total, EXTRA)
    plain = (n, radius, own_cells, total, 0)
    i32 = jax.ShapeDtypeStruct((TALL * SUB, LANES), jnp.int32)
    tables = pl.pallas_call(
        lambda *refs: table_kernel((wide, plain), *refs),
        out_shape=[f32(TALL * SUB, LANES), i32] * 2,
        in_specs=[smem] + [vmem] * 3,
        out_specs=[vmem] * 4,
        scratch_shapes=[pltpu.VMEM((4, tall_of(n + 1), LANES), jnp.float32)],
        compiler_params=params,
        name="tables",
    )(place, side, spins, turns)
    moved = []
    for own, far in zip(owns, fars):
        if moved:
            own, far, _ = lax.optimization_barrier((own, far, tables[0]))
        moved.append((send_near(own), send_far(far)))
    states = []
    for level in range(levels):
        near, far = moved[level]
        states.append(first_step(wide, level, (place, owns[level], near, far, side, corner, *tables[:2])))
    moved = [(send_near(own), send_far(far)) for own, far in states]
    done = ()
    for level in range(levels):
        near, far = moved[level]
        operands = (place, states[level][0], near, far, *tables[2:])
        result = last_step(plain, level, operands, done if level == levels - 1 else (), levels)
        done += (result,)
    return tuple(result)


def solution(mesh):
    placed = (
        P(None, "phi", "row"),
        P(None, None, "phi", "row"),
        P(None, None, "phi", "row"),
        P("row"),
        P("row"),
    )
    return jax.shard_map(
        body,
        mesh=mesh,
        in_specs=placed,
        out_specs=(P(None, "phi", "row"), P(None, None, "phi", "row"), P(None, None, "phi", "row")),
        check_vma=False,
    )
```

```python
import jax
import jax.numpy as jnp
from jax import lax
from jax.experimental import pallas as pl
from jax.experimental.pallas import tpu as pltpu
from jax.sharding import PartitionSpec as P

STEPS = 2
SMIN = 8
SMAX = 56
STAGES = 3
REACH = 2 * STAGES
FIELDS = 5
LANES = 128
SUB = 8
HALF = LANES // 2
SLOTS = 2 * SUB
EXTRA = 2 * SUB
DEALT = 32
TALL = 40
VMEM_LIMIT = 32 * 1024 * 1024
EDGE_LIMIT = 60 * 1024 * 1024

time_step = 0.08


def shift_bound(first_row, rows):
    d = rows - 1 - first_row
    return min(SMIN + (SMAX - SMIN - 1) * d * d // ((rows - 1) * (rows - 1)) + 1, SMAX)


def minmod(lower, upper):
    return jnp.maximum(jnp.minimum(lower, 0.0), jnp.minimum(upper, jnp.maximum(lower, 0.0)))


def physical(state):
    rho, mn, mt, bn, bt = state
    inverse = pltpu.reciprocal(rho, approx=True)
    bn_sq = bn * bn
    bt_sq = bt * bt
    vn = mn * inverse
    vt = mt * inverse
    inside = (bn_sq + bt_sq) * inverse + 1.0
    root = lax.rsqrt(inside)
    ram = mn * vn + rho
    tension = bt_sq - bn_sq
    flux_t = mt * vn - bn * bt
    flux_b = bt * vn - bn * vt
    speed = jnp.abs(vn) + inside * root
    return ram, tension, flux_t, flux_b, speed


def face_twice(left, right, of_left, of_right):
    left_ram, left_tension, left_t, left_b, left_speed = of_left
    right_ram, right_tension, right_t, right_b, right_speed = of_right
    bound = jnp.maximum(left_speed, right_speed)
    jumps = [bound * (l - r) for l, r in zip(left, right)]
    return [
        (left[1] + right[1]) + jumps[0],
        ((left_ram + right_ram) + 0.5 * (left_tension + right_tension)) + jumps[1],
        (left_t + right_t) + jumps[2],
        jumps[3],
        (left_b + right_b) + jumps[4],
    ]


def swapped(five):
    return [five[0], five[2], five[1], five[4], five[3]]


def tile(i):
    return pl.ds(pl.multiple_of(i * SUB, SUB), SUB)


def rows_a_turn(n):
    return (n + 2 * REACH - 4 + 1) // 2


def run_stages(n, stages, spin, edges):
    each = rows_a_turn(n)
    half_dt = 0.5 * time_step
    low_mask, high_mask = edges
    first, last = REACH, REACH + n - 1

    right_of = lambda x: pltpu.roll(x, LANES - 1, 1)
    left_of = lambda x: pltpu.roll(x, 1, 1)

    def radial_states(halves, centres):
        jumps = [h[SUB:] - h[:-SUB] for h in halves]
        slopes = [minmod(d[:-SUB], d[SUB:]) for d in jumps]
        lower = [x - g for x, g in zip(centres, slopes)]
        upper = [x + g for x, g in zip(centres, slopes)]
        return swapped([x[:-SUB] for x in upper]), swapped([x[SUB:] for x in lower])

    def work(stage, i0, before):
        src, dst = stage, (stage & 1) + 1
        weight = jnp.where(stage == 0, 1.0, jnp.where(stage == 1, 0.25, 2.0 / 3.0))
        keep = jnp.where(stage == 0, 0.0, jnp.where(stage == 1, 0.75, 1.0 / 3.0))
        some = lambda first, count: pl.ds(pl.multiple_of((i0 + first) * SUB, SUB), count * SUB)
        here = some(0, each)
        size = each * SUB
        rows = [stages[src, f, some(-1, each + 3), :] for f in range(FIELDS)]
        halves = [0.5 * x for x in rows]
        own = [x[SUB : SUB + size] for x in rows]
        half = [x[SUB : SUB + size] for x in halves]
        after = [right_of(x) for x in half]
        left, right = radial_states(halves, [x[SUB:-SUB] for x in rows])
        jump = [x - y for x, y in zip(after, half)]
        behind = [left_of(x) for x in jump]
        of_left = physical(left)
        of_right = physical(right)
        slopes = [minmod(x, y) for x, y in zip(behind, jump)]
        lower = [right_of(x - y) for x, y in zip(own, slopes)]
        upper = [x + y for x, y in zip(own, slopes)]
        of_upper = physical(upper)
        faces = swapped(face_twice(left, right, of_left, of_right))
        of_lower = physical(lower)
        azimuth = face_twice(upper, lower, of_upper, of_lower)
        shifted = [left_of(x) for x in azimuth]
        change = [x - jnp.concatenate([y, x[:-SUB]], axis=0) for x, y in zip(faces, before)]
        turn = spin[here, :]
        source = [None, (-0.5 * turn) * own[2], (2.0 * turn) * own[1], (-1.5 * turn) * own[4], None]
        partial = [x if y is None else x + y for x, y in zip(own, source)]
        starts = [keep * stages[0, f, here, :] for f in range(FIELDS)]
        for f in range(FIELDS):
            new = partial[f] - half_dt * ((azimuth[f] - shifted[f]) + change[f])
            stages[dst, f, here, :] = weight * new + starts[f]
        return [x[-SUB:] for x in faces]

    def run(stage, _):
        for f in range(FIELDS):
            inner = stages[stage, f, tile(first), :]
            outer = stages[stage, f, tile(last), :]
            for k in (1, 2):
                stages[stage, f, tile(first - k), :] = jnp.where(low_mask, inner, stages[stage, f, tile(first - k), :])
                stages[stage, f, tile(last + k), :] = jnp.where(high_mask, outer, stages[stage, f, tile(last + k), :])
        count = n + 2 * REACH - 4 - 4 * stage
        if n % 2 == 0:
            lo = 2 * stage + 2
            rows = [stages[stage, f, pl.ds(pl.multiple_of((lo - 2) * SUB, SUB), 4 * SUB), :] for f in range(FIELDS)]
            left, right = radial_states([0.5 * x for x in rows], [x[SUB:-SUB] for x in rows])
            before = tuple(swapped(face_twice(left, right, physical(left), physical(right))))
        else:
            lo = 2 * stage + 1
            count = count + 1
            before = (jnp.zeros((SUB, LANES), jnp.float32),) * FIELDS
        turns = lax.div(count + each - 1, each)
        lax.fori_loop(0, turns, lambda c, carried: tuple(work(stage, lo + c * each, list(carried))), before)
        return 0

    lax.fori_loop(0, STAGES, run, 0)


def spread(block, first, width):
    block = pltpu.roll(block, (LANES - first) % LANES, 1)
    lane = lax.broadcasted_iota(jnp.int32, block.shape, 1)
    while width < LANES:
        block = jnp.where(lane < width, block, pltpu.roll(block, width, 1))
        width *= 2
    return block


def pack_far(far, near, own_cells):
    sublane = lax.broadcasted_iota(jnp.int32, (SUB, LANES), 0)
    left = lax.broadcasted_iota(jnp.int32, (SUB, LANES), 1) < HALF

    for f in range(FIELDS):
        start = f * own_cells
        low = near[start : start + own_cells, 0:LANES]
        high = near[start + own_cells - 2 * SUB : start + own_cells, LANES : 2 * LANES]
        before, last = high[0:SUB], high[SUB:]
        far[start : start + SUB, :] = jnp.where(left, low[0:SUB], pltpu.roll(last, HALF, 1))
        third = pltpu.roll(pltpu.roll(before, 1, 0), HALF, 1)
        fourth = pltpu.roll(last, 2, 0)
        second = low[SUB : 2 * SUB]
        mixed = jnp.where(sublane == 0, third, jnp.where(sublane == 1, fourth, second))
        far[start + SUB : start + 2 * SUB, :] = jnp.where(left, second, mixed)
        far[start + 2 * SUB : start + own_cells, :] = low[2 * SUB :]


def far_rows(far, start):
    left = lax.broadcasted_iota(jnp.int32, (SUB, LANES), 1) < HALF
    first = far[start : start + SUB, :]
    mixed = far[start + SUB : start + 2 * SUB, :]
    before = pltpu.roll(pltpu.roll(mixed, SUB - 1, 0), HALF, 1)
    last = jnp.where(left, pltpu.roll(first, HALF, 1), pltpu.roll(mixed, SUB - 2, 0))
    return before, last


def edge_kernel(place, density, momentum, magnetic, rotation, shifts, edge, ends, spin_in, shift_in, arrived):
    levels, own_cells, radius = density.shape
    on_low = place[0] == 0
    parts = radius // LANES
    split = 4 * own_cells
    columns = pl.ds(pl.multiple_of(jnp.where(on_low, radius - LANES, 0), LANES), LANES)
    copies = [
        pltpu.make_async_copy(rotation, spin_in, arrived.at[levels * FIELDS]),
        pltpu.make_async_copy(shifts, shift_in, arrived.at[levels * FIELDS + 1]),
    ]
    for level in range(levels):
        sources = [density.at[level, :, columns]] + [x.at[k, level, :, columns] for x in (momentum, magnetic) for k in range(2)]
        for f, x in enumerate(sources):
            at = ends.at[level, pl.ds(f * own_cells, own_cells), :]
            copies.append(pltpu.make_async_copy(x, at, arrived.at[level * FIELDS + f]))
    for copy in copies:
        copy.start()
    for copy in copies:
        copy.wait()
    wide = lambda ref: jnp.broadcast_to(
        jnp.where(on_low, ref[parts - 1 : parts, :], ref[0:1, :]).astype(jnp.float32), (own_cells, LANES)
    )
    turn = wide(spin_in) * time_step
    shift = wide(shift_in)
    zero = jnp.zeros((own_cells, LANES), jnp.float32)
    for level in range(levels):
        last = jnp.concatenate([ends[level, split:, :], turn, shift, zero], axis=0)
        for side, group in enumerate((ends[level, 0:split, :], last)):
            turned = group.T
            edge[level, :, side * LANES : (side + 1) * LANES] = jnp.where(on_low, turned[LANES - EXTRA :], turned[0:EXTRA])


def pack_kernel(levels, density, momentum, magnetic, edge, *outs):
    del edge
    nears, fars = outs[:levels], outs[levels:]
    own_cells = density.shape[1]
    for level in range(levels):
        sources = [density.at[level]] + [x.at[k, level] for x in (momentum, magnetic) for k in range(2)]
        for f, x in enumerate(sources):
            nears[level][f * own_cells : (f + 1) * own_cells, :] = x[...]
        pack_far(fars[level], nears[level], own_cells)


class Blocks:
    def __init__(self, row, n, radius, total, moved):
        self.on_low = row == 0
        self.n = n
        self.own_at = pl.multiple_of(jnp.where(self.on_low, EXTRA, EXTRA + moved), SUB)
        self.edge_at = pl.multiple_of(jnp.where(self.on_low, EXTRA + radius, moved), SUB)
        bounds = [[shift_bound(r * radius - (moved if r else 0) + n * k, total) for k in range(SLOTS)] for r in range(2)]
        self.bounds = [jnp.where(self.on_low, a, b) for a, b in zip(*bounds)]

    def rows_of(self, k):
        start = EXTRA - REACH + self.n * k
        return slice(start, start + DEALT)


def table_kernel(plans, place, side, rotation, shifts, *rest):
    outs, held = rest[:-1], rest[-1]
    radius = plans[0][1]
    own_cells = plans[0][2]
    wide_lane = lax.broadcasted_iota(jnp.int32, (DEALT, LANES), 1)
    front = wide_lane < HALF
    more = side[0, :, LANES : 2 * LANES]
    edges = [spread(more, own_cells, own_cells), spread(more, 2 * own_cells, own_cells)]
    own = []
    for ref, scale in ((rotation, time_step), (shifts, 1.0)):
        along = lambda part: jnp.broadcast_to(ref[part : part + 1, :].astype(jnp.float32), (LANES, LANES)).T
        own.append([along(part) * scale for part in range(radius // LANES)])
    for which, (n, radius, own_cells, total, moved) in enumerate(plans):
        spin, pick = outs[2 * which : 2 * which + 2]
        blocks = Blocks(place[0], n, radius, total, moved)
        for k in range(2):
            for part, x in enumerate(own[k]):
                held[2 * which + k, pl.ds(blocks.own_at + part * LANES, LANES), :] = x
            held[2 * which + k, pl.ds(blocks.edge_at, EXTRA), :] = edges[k]
        for j in range(SUB):
            low, high = blocks.rows_of(j), blocks.rows_of(SUB + j)
            turns = [jnp.where(front, held[2 * which + k, low, :], held[2 * which + k, high, :]) for k in range(2)]
            spin[pl.ds(j, DEALT, stride=SUB), :] = turns[0]
            bound = jnp.where(front, blocks.bounds[j], blocks.bounds[SUB + j])
            pick[pl.ds(j, DEALT, stride=SUB), :] = (wide_lane + (REACH + bound)) - turns[1].astype(jnp.int32)


def step_kernel(plan, refs, write, scratch):
    n, radius, own_cells, total, moved = plan
    place, own, own_edge, near, near_edge, far, spin, pick = refs
    cells, stages, packed, tops = scratch
    row = place[0]
    lane = lax.broadcasted_iota(jnp.int32, (SUB, LANES), 1)
    sublane = lax.broadcasted_iota(jnp.int32, (SUB, LANES), 0)
    blocks = Blocks(row, n, radius, total, moved)

    edge_lane = lax.broadcasted_iota(jnp.int32, (EXTRA, LANES), 1)
    parts = radius // LANES

    front = lax.broadcasted_iota(jnp.int32, (DEALT, LANES), 1) < HALF

    for f in range(FIELDS):
        tops[f] = jnp.concatenate(far_rows(far, f * own_cells), axis=0)

    def bring(turn, _):
        dealt = jnp.maximum(turn - 1, 0)
        for j in range(SUB):
            low, high = j, SUB + j
            turn_low = (LANES - (2 * own_cells - REACH)) + blocks.bounds[low]
            turn_high = (HALF - (2 * own_cells - REACH)) + blocks.bounds[high]
            stages[0, dealt, pl.ds(j, DEALT, stride=SUB), :] = jnp.where(
                front,
                pltpu.roll(cells[dealt, blocks.rows_of(low), :], turn_low, 1),
                pltpu.roll(cells[dealt, blocks.rows_of(high), :], turn_high, 1),
            )
        f = jnp.minimum(turn, FIELDS - 1)
        rows = pl.ds(pl.multiple_of(f * own_cells, SUB), own_cells)
        start = pl.multiple_of(f * own_cells, SUB)
        for part in range(parts):
            columns = slice(part * LANES, (part + 1) * LANES)
            if part == 0:
                top = far[pl.ds(start, own_cells), :]
            else:
                gap = jnp.zeros((own_cells - 2 * SUB, LANES), jnp.float32)
                top = jnp.concatenate([gap, tops[f]], axis=0)
            fill = jnp.zeros((own_cells, LANES), jnp.float32)
            block = jnp.concatenate([top, near[rows, columns], own[rows, columns], fill], axis=0)
            cells[f, pl.ds(blocks.own_at + part * LANES, LANES), :] = block.T
        columns = pl.ds(pl.multiple_of(lax.div(f, 4) * LANES, LANES), LANES)
        lanes_at = lax.rem(f, 4) * own_cells
        cells[f, pl.ds(blocks.edge_at, EXTRA), :] = jnp.where(
            edge_lane < 2 * own_cells,
            pltpu.roll(near_edge[:, columns], lax.rem(LANES + own_cells - lanes_at, LANES), 1),
            pltpu.roll(own_edge[:, columns], lax.rem(LANES + 2 * own_cells - lanes_at, LANES), 1),
        )
        return 0

    lax.fori_loop(0, FIELDS + 1, bring, 0)

    edges = (
        (sublane == 0) & (lane < HALF) & (row == 0),
        (sublane == SUB - 1) & (lane >= HALF) & (row == total // radius - 1),
    )
    run_stages(n, stages, spin, edges)

    even = (lane & own_cells) == 0

    picked = (n + 1) // 2

    def shift(turn, _):
        for k in range(picked):
            i = turn * picked + k
            rows = tile(REACH + i)
            source = pick[rows, :]
            picks = [source & (LANES - 1), (source - own_cells) & (LANES - 1)]
            turned = [
                jnp.take_along_axis(stages[1, f, rows, :], picks[f % 2], axis=1, mode="promise_in_bounds")
                for f in range(FIELDS)
            ]
            stages[2, 0, tile(i), :] = jnp.where(even, turned[0], turned[1])
            stages[2, 1, tile(i), :] = jnp.where(even, turned[2], turned[3])
            stages[2, 2, tile(i), :] = turned[4]
        return 0

    lax.fori_loop(0, (n + picked - 1) // picked, shift, 0)
    narrow = lax.broadcasted_iota(jnp.int32, (n, LANES), 1) < HALF
    for j in range(SUB):
        one, two, three = [stages[2, g, pl.ds(j, n, stride=SUB), :] for g in range(3)]
        low = slice(EXTRA + n * j, EXTRA + n * (j + 1))
        high = slice(EXTRA + n * (SUB + j), EXTRA + n * (SUB + j + 1))
        packed[0, low, :] = jnp.where(narrow, one, pltpu.roll(two, HALF, 1))
        packed[0, high, :] = jnp.where(narrow, pltpu.roll(one, HALF, 1), two)
        packed[1, low, :] = three
        packed[1, high, :] = pltpu.roll(three, HALF, 1)
    for part in range(parts):
        rows = pl.ds(blocks.own_at + part * LANES, LANES)
        write.fields(slice(part * LANES, (part + 1) * LANES), packed[0, rows, :].T, packed[1, rows, :].T)
    write.edge(packed[0, pl.ds(blocks.edge_at, EXTRA), :], packed[1, pl.ds(blocks.edge_at, EXTRA), :])
    write.end()


class ToMessage:
    def __init__(self, near, far, own_cells):
        self.near, self.far, self.own_cells = near, far, own_cells

    def fields(self, columns, four, fifth):
        split = 4 * self.own_cells
        self.near[0:split, columns] = four
        self.near[split : split + self.own_cells, columns] = fifth[0 : self.own_cells]

    def edge(self, first, second):
        tail = FIELDS * self.own_cells
        self.near[tail : tail + EXTRA, 0:LANES] = first
        self.near[tail : tail + EXTRA, LANES : 2 * LANES] = second

    def end(self):
        pack_far(self.far, self.near, self.own_cells)


class ToBuffer:
    def __init__(self, buffer, sent=None):
        self.buffer, self.sent = buffer, sent

    def fields(self, columns, four, fifth):
        part = columns.start // LANES
        split = four.shape[0]
        self.buffer[part, 0:split, :] = four
        self.buffer[part, split:, :] = fifth[0 : self.buffer.shape[1] - split]
        if self.sent is not None:
            self.sent(part)

    def edge(self, first, second):
        pass

    def end(self):
        pass


def copies_out(level, part, buffer, outs, sent):
    density, momentum, magnetic = outs
    cells = density.shape[1]
    columns = pl.ds(part * LANES, LANES)
    targets = [density.at[level, :, columns]] + [x.at[k, level, :, columns] for x in (momentum, magnetic) for k in range(2)]
    return [
        pltpu.make_async_copy(buffer.at[part, pl.ds(f * cells, cells), :], x, sent.at[level, part, f])
        for f, x in enumerate(targets)
    ]


def tall_of(n):
    return EXTRA + SLOTS * n + 2 * SUB


def step_scratch(n):
    return [
        pltpu.VMEM((FIELDS, tall_of(n), LANES), jnp.float32),
        pltpu.VMEM((STAGES, FIELDS, TALL * SUB, LANES), jnp.float32),
        pltpu.VMEM((2, tall_of(n), LANES), jnp.float32),
        pltpu.VMEM((FIELDS, 2 * SUB, LANES), jnp.float32),
    ]


vmem = pl.BlockSpec(memory_space=pltpu.VMEM)
smem = pl.BlockSpec(memory_space=pltpu.SMEM)
f32 = lambda *s: jax.ShapeDtypeStruct(s, jnp.float32)
params = pltpu.CompilerParams(vmem_limit_bytes=VMEM_LIMIT)
cost = pl.CostEstimate(flops=9_000_000_000, bytes_accessed=29_000_000, transcendentals=0)


def first_step(plan, level, operands):
    n, radius, own_cells, total, moved = plan

    def kernel(place, own, near, far, side, corner, spin, pick, near_out, far_out, *scratch):
        refs = (place, own, side.at[level], near, corner.at[level], far, spin, pick)
        step_kernel(plan, refs, ToMessage(near_out, far_out, own_cells), scratch)

    return pl.pallas_call(
        kernel,
        out_shape=[f32(FIELDS * own_cells + EXTRA, radius), f32(FIELDS * own_cells, LANES)],
        in_specs=[smem] + [vmem] * 7,
        out_specs=[vmem] * 2,
        scratch_shapes=step_scratch(n),
        compiler_params=params,
        cost_estimate=cost,
        name="first_step",
    )(*operands)


def last_step(plan, level, operands, done, levels):
    n, radius, own_cells, total, moved = plan
    final = level == levels - 1
    tail = pl.ds(FIELDS * own_cells, EXTRA)
    parts = radius // LANES
    buffer = f32(parts, FIELDS * own_cells, LANES)

    def kernel(place, own, near, far, spin, pick, *rest):
        refs = (place, own, own.at[tail, :], near, near.at[tail, :], far, spin, pick)
        if not final:
            step_kernel(plan, refs, ToBuffer(rest[0]), rest[1:])
            return
        ready, outs, scratch = rest[: levels - 1], rest[levels - 1 : levels + 2], rest[levels + 2 :]
        last, sent = scratch[-2:]
        copies = []

        def send(at, x, part):
            started = copies_out(at, part, x, outs, sent)
            for copy in started:
                copy.start()
            copies.extend(started)

        for k, x in enumerate(ready):
            for part in range(parts):
                send(k, x, part)
        step_kernel(plan, refs, ToBuffer(last, lambda part: send(level, last, part)), scratch[:-2])
        for copy in copies:
            copy.wait()

    if final:
        out_shape = [f32(levels, own_cells, radius), f32(2, levels, own_cells, radius), f32(2, levels, own_cells, radius)]
        more = [pltpu.VMEM(buffer.shape, jnp.float32), pltpu.SemaphoreType.DMA((levels, parts, FIELDS))]
    else:
        out_shape = buffer
        more = []
    return pl.pallas_call(
        kernel,
        out_shape=out_shape,
        in_specs=[smem] + [vmem] * (5 + len(done)),
        out_specs=[pl.BlockSpec(memory_space=pltpu.HBM)] * 3 if final else vmem,
        scratch_shapes=step_scratch(n) + more,
        compiler_params=params,
        cost_estimate=cost,
        name="last_step",
    )(*operands, *done)


def body(density, momentum, magnetic, rotation, shifts):
    phi_count = lax.axis_size("phi")
    row_count = lax.axis_size("row")
    levels, own_cells, radius = density.shape
    total = radius * row_count
    parts = radius // LANES
    n = radius // SLOTS
    need = [max(shift_bound(k * HALF, total) + REACH - own_cells, 0) for k in range(radius // HALF)]
    assert row_count == 2 and radius == 2 * LANES and own_cells == HALF // 2
    assert need[0] <= own_cells and need[1] <= own_cells - SUB - 2 and need[2] <= SUB + 1 and need[3] <= 1

    row = lax.axis_index("row")
    place = jnp.reshape(row, (1,)).astype(jnp.int32)
    send_near = lambda x: lax.ppermute(x, "phi", [(p, (p + 1) % phi_count) for p in range(phi_count)])
    send_far = lambda x: lax.ppermute(x, "phi", [(p, (p + 2) % phi_count) for p in range(phi_count)])
    here = lambda p, r: (p % phi_count) * row_count + r
    diagonal = [(here(p, r), here(p + 1, 1 - r)) for p in range(phi_count) for r in range(row_count)]
    send_corner = lambda x: lax.ppermute(x, ("phi", "row"), diagonal)
    send_side = lambda x: lax.ppermute(x, "row", [(0, 1), (1, 0)])

    spins, turns = rotation.reshape(parts, LANES), shifts.reshape(parts, LANES)
    near_message = f32(FIELDS * own_cells, radius)
    far_message = f32(FIELDS * own_cells, LANES)
    edge = pl.pallas_call(
        edge_kernel,
        out_shape=f32(levels, EXTRA, 2 * LANES),
        in_specs=[smem] + [pl.BlockSpec(memory_space=pltpu.HBM)] * 5,
        out_specs=vmem,
        scratch_shapes=[
            pltpu.VMEM((levels, FIELDS * own_cells, LANES), jnp.float32),
            pltpu.VMEM((parts, LANES), jnp.float32),
            pltpu.VMEM((parts, LANES), jnp.int32),
            pltpu.SemaphoreType.DMA((levels * FIELDS + 2,)),
        ],
        compiler_params=pltpu.CompilerParams(vmem_limit_bytes=EDGE_LIMIT),
        name="edges",
    )(place, density, momentum, magnetic, spins, turns)
    packed = pl.pallas_call(
        lambda *refs: pack_kernel(levels, *refs),
        out_shape=[near_message] * levels + [far_message] * levels,
        in_specs=[vmem] * 3 + [pl.BlockSpec(memory_space=pl.ANY)],
        out_specs=[vmem] * (2 * levels),
        compiler_params=params,
        cost_estimate=cost,
        name="pack",
    )(density, momentum, magnetic, edge)
    owns, fars = packed[:levels], packed[levels:]
    side = send_side(edge)
    corner = send_corner(edge)
    wide = (n + 1, radius, own_cells, total, EXTRA)
    plain = (n, radius, own_cells, total, 0)
    i32 = jax.ShapeDtypeStruct((TALL * SUB, LANES), jnp.int32)
    tables = pl.pallas_call(
        lambda *refs: table_kernel((wide, plain), *refs),
        out_shape=[f32(TALL * SUB, LANES), i32] * 2,
        in_specs=[smem] + [vmem] * 3,
        out_specs=[vmem] * 4,
        scratch_shapes=[pltpu.VMEM((4, tall_of(n + 1), LANES), jnp.float32)],
        compiler_params=params,
        name="tables",
    )(place, side, spins, turns)
    moved = []
    for own, far in zip(owns, fars):
        if moved:
            own, far, _ = lax.optimization_barrier((own, far, tables[0]))
        moved.append((send_near(own), send_far(far)))
    states = []
    for level in range(levels):
        near, far = moved[level]
        states.append(first_step(wide, level, (place, owns[level], near, far, side, corner, *tables[:2])))
    moved = [(send_near(own), send_far(far)) for own, far in states]
    done = ()
    for level in range(levels):
        near, far = moved[level]
        operands = (place, states[level][0], near, far, *tables[2:])
        result = last_step(plain, level, operands, done if level == levels - 1 else (), levels)
        done += (result,)
    return tuple(result)


def solution(mesh):
    placed = (
        P(None, "phi", "row"),
        P(None, None, "phi", "row"),
        P(None, None, "phi", "row"),
        P("row"),
        P("row"),
    )
    return jax.shard_map(
        body,
        mesh=mesh,
        in_specs=placed,
        out_specs=(P(None, "phi", "row"), P(None, None, "phi", "row"), P(None, None, "phi", "row")),
        check_vma=False,
    )
```

```python
import jax
import jax.numpy as jnp
from jax import lax
from jax.experimental import pallas as pl
from jax.experimental.pallas import tpu as pltpu
from jax.sharding import PartitionSpec as P

STEPS = 2
SMIN = 8
SMAX = 56
STAGES = 3
REACH = 2 * STAGES
FIELDS = 5
LANES = 128
SUB = 8
HALF = LANES // 2
SLOTS = 2 * SUB
EXTRA = 2 * SUB
DEALT = 32
TALL = 40
VMEM_LIMIT = 32 * 1024 * 1024
EDGE_LIMIT = 60 * 1024 * 1024

time_step = 0.08


def shift_bound(first_row, rows):
    d = rows - 1 - first_row
    return min(SMIN + (SMAX - SMIN - 1) * d * d // ((rows - 1) * (rows - 1)) + 1, SMAX)


def minmod(lower, upper):
    return jnp.maximum(jnp.minimum(lower, 0.0), jnp.minimum(upper, jnp.maximum(lower, 0.0)))


def physical(state):
    rho, mn, mt, bn, bt = state
    inverse = pltpu.reciprocal(rho, approx=True)
    bn_sq = bn * bn
    bt_sq = bt * bt
    vn = mn * inverse
    vt = mt * inverse
    inside = (bn_sq + bt_sq) * inverse + 1.0
    root = lax.rsqrt(inside)
    ram = mn * vn + rho
    tension = bt_sq - bn_sq
    flux_t = mt * vn - bn * bt
    flux_b = bt * vn - bn * vt
    speed = jnp.abs(vn) + inside * root
    return ram, tension, flux_t, flux_b, speed


def face_twice(left, right, of_left, of_right):
    left_ram, left_tension, left_t, left_b, left_speed = of_left
    right_ram, right_tension, right_t, right_b, right_speed = of_right
    bound = jnp.maximum(left_speed, right_speed)
    jumps = [bound * (l - r) for l, r in zip(left, right)]
    return [
        (left[1] + right[1]) + jumps[0],
        ((left_ram + right_ram) + 0.5 * (left_tension + right_tension)) + jumps[1],
        (left_t + right_t) + jumps[2],
        jumps[3],
        (left_b + right_b) + jumps[4],
    ]


def swapped(five):
    return [five[0], five[2], five[1], five[4], five[3]]


def tile(i):
    return pl.ds(pl.multiple_of(i * SUB, SUB), SUB)


def rows_a_turn(n):
    return (n + 2 * REACH - 4 + 1) // 2


def run_stages(n, stages, spin, edges):
    each = rows_a_turn(n)
    half_dt = 0.5 * time_step
    low_mask, high_mask = edges
    first, last = REACH, REACH + n - 1

    right_of = lambda x: pltpu.roll(x, LANES - 1, 1)
    left_of = lambda x: pltpu.roll(x, 1, 1)

    def radial_states(halves, centres):
        jumps = [h[SUB:] - h[:-SUB] for h in halves]
        slopes = [minmod(d[:-SUB], d[SUB:]) for d in jumps]
        lower = [x - g for x, g in zip(centres, slopes)]
        upper = [x + g for x, g in zip(centres, slopes)]
        return swapped([x[:-SUB] for x in upper]), swapped([x[SUB:] for x in lower])

    def work(stage, i0, before):
        src, dst = stage, (stage & 1) + 1
        weight = jnp.where(stage == 0, 1.0, jnp.where(stage == 1, 0.25, 2.0 / 3.0))
        keep = jnp.where(stage == 0, 0.0, jnp.where(stage == 1, 0.75, 1.0 / 3.0))
        some = lambda first, count: pl.ds(pl.multiple_of((i0 + first) * SUB, SUB), count * SUB)
        here = some(0, each)
        size = each * SUB
        rows = [stages[src, f, some(-1, each + 3), :] for f in range(FIELDS)]
        halves = [0.5 * x for x in rows]
        own = [x[SUB : SUB + size] for x in rows]
        half = [x[SUB : SUB + size] for x in halves]
        after = [right_of(x) for x in half]
        left, right = radial_states(halves, [x[SUB:-SUB] for x in rows])
        jump = [x - y for x, y in zip(after, half)]
        behind = [left_of(x) for x in jump]
        of_left = physical(left)
        of_right = physical(right)
        slopes = [minmod(x, y) for x, y in zip(behind, jump)]
        lower = [right_of(x - y) for x, y in zip(own, slopes)]
        upper = [x + y for x, y in zip(own, slopes)]
        of_upper = physical(upper)
        faces = swapped(face_twice(left, right, of_left, of_right))
        of_lower = physical(lower)
        azimuth = face_twice(upper, lower, of_upper, of_lower)
        shifted = [left_of(x) for x in azimuth]
        change = [x - jnp.concatenate([y, x[:-SUB]], axis=0) for x, y in zip(faces, before)]
        turn = spin[here, :]
        source = [None, (-0.5 * turn) * own[2], (2.0 * turn) * own[1], (-1.5 * turn) * own[4], None]
        partial = [x if y is None else x + y for x, y in zip(own, source)]
        starts = [keep * stages[0, f, here, :] for f in range(FIELDS)]
        for f in range(FIELDS):
            new = partial[f] - half_dt * ((azimuth[f] - shifted[f]) + change[f])
            stages[dst, f, here, :] = weight * new + starts[f]
        return [x[-SUB:] for x in faces]

    def run(stage, _):
        for f in range(FIELDS):
            inner = stages[stage, f, tile(first), :]
            outer = stages[stage, f, tile(last), :]
            for k in (1, 2):
                stages[stage, f, tile(first - k), :] = jnp.where(low_mask, inner, stages[stage, f, tile(first - k), :])
                stages[stage, f, tile(last + k), :] = jnp.where(high_mask, outer, stages[stage, f, tile(last + k), :])
        count = n + 2 * REACH - 4 - 4 * stage
        if n % 2 == 0:
            lo = 2 * stage + 2
            rows = [stages[stage, f, pl.ds(pl.multiple_of((lo - 2) * SUB, SUB), 4 * SUB), :] for f in range(FIELDS)]
            left, right = radial_states([0.5 * x for x in rows], [x[SUB:-SUB] for x in rows])
            before = tuple(swapped(face_twice(left, right, physical(left), physical(right))))
        else:
            lo = 2 * stage + 1
            count = count + 1
            before = (jnp.zeros((SUB, LANES), jnp.float32),) * FIELDS
        turns = lax.div(count + each - 1, each)
        lax.fori_loop(0, turns, lambda c, carried: tuple(work(stage, lo + c * each, list(carried))), before)
        return 0

    lax.fori_loop(0, STAGES, run, 0)


def spread(block, first, width):
    block = pltpu.roll(block, (LANES - first) % LANES, 1)
    lane = lax.broadcasted_iota(jnp.int32, block.shape, 1)
    while width < LANES:
        block = jnp.where(lane < width, block, pltpu.roll(block, width, 1))
        width *= 2
    return block


def pack_far(far, near, own_cells):
    sublane = lax.broadcasted_iota(jnp.int32, (SUB, LANES), 0)
    left = lax.broadcasted_iota(jnp.int32, (SUB, LANES), 1) < HALF

    for f in range(FIELDS):
        start = f * own_cells
        low = near[start : start + own_cells, 0:LANES]
        high = near[start + own_cells - 2 * SUB : start + own_cells, LANES : 2 * LANES]
        before, last = high[0:SUB], high[SUB:]
        far[start : start + SUB, :] = jnp.where(left, low[0:SUB], pltpu.roll(last, HALF, 1))
        third = pltpu.roll(pltpu.roll(before, 1, 0), HALF, 1)
        fourth = pltpu.roll(last, 2, 0)
        second = low[SUB : 2 * SUB]
        mixed = jnp.where(sublane == 0, third, jnp.where(sublane == 1, fourth, second))
        far[start + SUB : start + 2 * SUB, :] = jnp.where(left, second, mixed)
        far[start + 2 * SUB : start + own_cells, :] = low[2 * SUB :]


def far_rows(far, start):
    left = lax.broadcasted_iota(jnp.int32, (SUB, LANES), 1) < HALF
    first = far[start : start + SUB, :]
    mixed = far[start + SUB : start + 2 * SUB, :]
    before = pltpu.roll(pltpu.roll(mixed, SUB - 1, 0), HALF, 1)
    last = jnp.where(left, pltpu.roll(first, HALF, 1), pltpu.roll(mixed, SUB - 2, 0))
    return before, last


def edge_kernel(place, density, momentum, magnetic, rotation, shifts, edge, ends, spin_in, shift_in, arrived):
    levels, own_cells, radius = density.shape
    on_low = place[0] == 0
    parts = radius // LANES
    split = 4 * own_cells
    columns = pl.ds(pl.multiple_of(jnp.where(on_low, radius - LANES, 0), LANES), LANES)
    copies = [
        pltpu.make_async_copy(rotation, spin_in, arrived.at[levels * FIELDS]),
        pltpu.make_async_copy(shifts, shift_in, arrived.at[levels * FIELDS + 1]),
    ]
    for level in range(levels):
        sources = [density.at[level, :, columns]] + [x.at[k, level, :, columns] for x in (momentum, magnetic) for k in range(2)]
        for f, x in enumerate(sources):
            at = ends.at[level, pl.ds(f * own_cells, own_cells), :]
            copies.append(pltpu.make_async_copy(x, at, arrived.at[level * FIELDS + f]))
    for copy in copies:
        copy.start()
    for copy in copies:
        copy.wait()
    wide = lambda ref: jnp.broadcast_to(
        jnp.where(on_low, ref[parts - 1 : parts, :], ref[0:1, :]).astype(jnp.float32), (own_cells, LANES)
    )
    turn = wide(spin_in) * time_step
    shift = wide(shift_in)
    zero = jnp.zeros((own_cells, LANES), jnp.float32)
    for level in range(levels):
        last = jnp.concatenate([ends[level, split:, :], turn, shift, zero], axis=0)
        for side, group in enumerate((ends[level, 0:split, :], last)):
            turned = group.T
            edge[level, :, side * LANES : (side + 1) * LANES] = jnp.where(on_low, turned[LANES - EXTRA :], turned[0:EXTRA])


def pack_kernel(levels, density, momentum, magnetic, edge, *outs):
    del edge
    nears, fars = outs[:levels], outs[levels:]
    own_cells = density.shape[1]
    for level in range(levels):
        sources = [density.at[level]] + [x.at[k, level] for x in (momentum, magnetic) for k in range(2)]
        for f, x in enumerate(sources):
            nears[level][f * own_cells : (f + 1) * own_cells, :] = x[...]
        pack_far(fars[level], nears[level], own_cells)


class Blocks:
    def __init__(self, row, n, radius, total, moved):
        self.on_low = row == 0
        self.n = n
        self.own_at = pl.multiple_of(jnp.where(self.on_low, EXTRA, EXTRA + moved), SUB)
        self.edge_at = pl.multiple_of(jnp.where(self.on_low, EXTRA + radius, moved), SUB)
        bounds = [[shift_bound(r * radius - (moved if r else 0) + n * k, total) for k in range(SLOTS)] for r in range(2)]
        self.bounds = [jnp.where(self.on_low, a, b) for a, b in zip(*bounds)]

    def rows_of(self, k):
        start = EXTRA - REACH + self.n * k
        return slice(start, start + DEALT)


def table_kernel(plans, place, side, rotation, shifts, *rest):
    outs, held = rest[:-1], rest[-1]
    radius = plans[0][1]
    own_cells = plans[0][2]
    wide_lane = lax.broadcasted_iota(jnp.int32, (DEALT, LANES), 1)
    front = wide_lane < HALF
    more = side[0, :, LANES : 2 * LANES]
    edges = [spread(more, own_cells, own_cells), spread(more, 2 * own_cells, own_cells)]
    own = []
    for ref, scale in ((rotation, time_step), (shifts, 1.0)):
        along = lambda part: jnp.broadcast_to(ref[part : part + 1, :].astype(jnp.float32), (LANES, LANES)).T
        own.append([along(part) * scale for part in range(radius // LANES)])
    for which, (n, radius, own_cells, total, moved) in enumerate(plans):
        spin, pick = outs[2 * which : 2 * which + 2]
        blocks = Blocks(place[0], n, radius, total, moved)
        for k in range(2):
            for part, x in enumerate(own[k]):
                held[2 * which + k, pl.ds(blocks.own_at + part * LANES, LANES), :] = x
            held[2 * which + k, pl.ds(blocks.edge_at, EXTRA), :] = edges[k]
        for j in range(SUB):
            low, high = blocks.rows_of(j), blocks.rows_of(SUB + j)
            turns = [jnp.where(front, held[2 * which + k, low, :], held[2 * which + k, high, :]) for k in range(2)]
            spin[pl.ds(j, DEALT, stride=SUB), :] = turns[0]
            bound = jnp.where(front, blocks.bounds[j], blocks.bounds[SUB + j])
            pick[pl.ds(j, DEALT, stride=SUB), :] = (wide_lane + (REACH + bound)) - turns[1].astype(jnp.int32)


def step_kernel(plan, refs, write, scratch):
    n, radius, own_cells, total, moved = plan
    place, own, own_edge, near, near_edge, far, spin, pick = refs
    cells, stages, packed, tops = scratch
    row = place[0]
    lane = lax.broadcasted_iota(jnp.int32, (SUB, LANES), 1)
    sublane = lax.broadcasted_iota(jnp.int32, (SUB, LANES), 0)
    blocks = Blocks(row, n, radius, total, moved)

    edge_lane = lax.broadcasted_iota(jnp.int32, (EXTRA, LANES), 1)
    parts = radius // LANES

    front = lax.broadcasted_iota(jnp.int32, (DEALT, LANES), 1) < HALF

    for f in range(FIELDS):
        tops[f] = jnp.concatenate(far_rows(far, f * own_cells), axis=0)

    def bring(turn, _):
        dealt = jnp.maximum(turn - 1, 0)
        for j in range(SUB):
            low, high = j, SUB + j
            turn_low = (LANES - (2 * own_cells - REACH)) + blocks.bounds[low]
            turn_high = (HALF - (2 * own_cells - REACH)) + blocks.bounds[high]
            stages[0, dealt, pl.ds(j, DEALT, stride=SUB), :] = jnp.where(
                front,
                pltpu.roll(cells[dealt, blocks.rows_of(low), :], turn_low, 1),
                pltpu.roll(cells[dealt, blocks.rows_of(high), :], turn_high, 1),
            )
        f = jnp.minimum(turn, FIELDS - 1)
        rows = pl.ds(pl.multiple_of(f * own_cells, SUB), own_cells)
        start = pl.multiple_of(f * own_cells, SUB)
        for part in range(parts):
            columns = slice(part * LANES, (part + 1) * LANES)
            if part == 0:
                top = far[pl.ds(start, own_cells), :]
            else:
                gap = jnp.zeros((own_cells - 2 * SUB, LANES), jnp.float32)
                top = jnp.concatenate([gap, tops[f]], axis=0)
            fill = jnp.zeros((own_cells, LANES), jnp.float32)
            block = jnp.concatenate([top, near[rows, columns], own[rows, columns], fill], axis=0)
            cells[f, pl.ds(blocks.own_at + part * LANES, LANES), :] = block.T
        columns = pl.ds(pl.multiple_of(lax.div(f, 4) * LANES, LANES), LANES)
        lanes_at = lax.rem(f, 4) * own_cells
        cells[f, pl.ds(blocks.edge_at, EXTRA), :] = jnp.where(
            edge_lane < 2 * own_cells,
            pltpu.roll(near_edge[:, columns], lax.rem(LANES + own_cells - lanes_at, LANES), 1),
            pltpu.roll(own_edge[:, columns], lax.rem(LANES + 2 * own_cells - lanes_at, LANES), 1),
        )
        return 0

    lax.fori_loop(0, FIELDS + 1, bring, 0)

    edges = (
        (sublane == 0) & (lane < HALF) & (row == 0),
        (sublane == SUB - 1) & (lane >= HALF) & (row == total // radius - 1),
    )
    run_stages(n, stages, spin, edges)

    even = (lane & own_cells) == 0

    picked = (n + 1) // 2

    def shift(turn, _):
        for k in range(picked):
            i = turn * picked + k
            rows = tile(REACH + i)
            source = pick[rows, :]
            picks = [source & (LANES - 1), (source - own_cells) & (LANES - 1)]
            turned = [
                jnp.take_along_axis(stages[1, f, rows, :], picks[f % 2], axis=1, mode="promise_in_bounds")
                for f in range(FIELDS)
            ]
            stages[2, 0, tile(i), :] = jnp.where(even, turned[0], turned[1])
            stages[2, 1, tile(i), :] = jnp.where(even, turned[2], turned[3])
            stages[2, 2, tile(i), :] = turned[4]
        return 0

    lax.fori_loop(0, (n + picked - 1) // picked, shift, 0)
    narrow = lax.broadcasted_iota(jnp.int32, (n, LANES), 1) < HALF
    for j in range(SUB):
        one, two, three = [stages[2, g, pl.ds(j, n, stride=SUB), :] for g in range(3)]
        low = slice(EXTRA + n * j, EXTRA + n * (j + 1))
        high = slice(EXTRA + n * (SUB + j), EXTRA + n * (SUB + j + 1))
        packed[0, low, :] = jnp.where(narrow, one, pltpu.roll(two, HALF, 1))
        packed[0, high, :] = jnp.where(narrow, pltpu.roll(one, HALF, 1), two)
        packed[1, low, :] = three
        packed[1, high, :] = pltpu.roll(three, HALF, 1)
    for part in range(parts):
        rows = pl.ds(blocks.own_at + part * LANES, LANES)
        write.fields(slice(part * LANES, (part + 1) * LANES), packed[0, rows, :].T, packed[1, rows, :].T)
    write.edge(packed[0, pl.ds(blocks.edge_at, EXTRA), :], packed[1, pl.ds(blocks.edge_at, EXTRA), :])
    write.end()


class ToMessage:
    def __init__(self, near, far, own_cells):
        self.near, self.far, self.own_cells = near, far, own_cells

    def fields(self, columns, four, fifth):
        split = 4 * self.own_cells
        self.near[0:split, columns] = four
        self.near[split : split + self.own_cells, columns] = fifth[0 : self.own_cells]

    def edge(self, first, second):
        tail = FIELDS * self.own_cells
        self.near[tail : tail + EXTRA, 0:LANES] = first
        self.near[tail : tail + EXTRA, LANES : 2 * LANES] = second

    def end(self):
        pack_far(self.far, self.near, self.own_cells)


class ToBuffer:
    def __init__(self, buffer):
        self.buffer = buffer

    def fields(self, columns, four, fifth):
        split = four.shape[0]
        self.buffer[0:split, columns] = four
        self.buffer[split:, columns] = fifth[0 : self.buffer.shape[0] - split]

    def edge(self, first, second):
        pass

    def end(self):
        pass


def copies_out(level, buffer, outs, sent):
    density, momentum, magnetic = outs
    cells = density.shape[1]
    targets = [density.at[level]] + [x.at[k, level] for x in (momentum, magnetic) for k in range(2)]
    return [
        pltpu.make_async_copy(buffer.at[pl.ds(f * cells, cells), :], x, sent.at[level * FIELDS + f])
        for f, x in enumerate(targets)
    ]


def tall_of(n):
    return EXTRA + SLOTS * n + 2 * SUB


def step_scratch(n):
    return [
        pltpu.VMEM((FIELDS, tall_of(n), LANES), jnp.float32),
        pltpu.VMEM((STAGES, FIELDS, TALL * SUB, LANES), jnp.float32),
        pltpu.VMEM((2, tall_of(n), LANES), jnp.float32),
        pltpu.VMEM((FIELDS, 2 * SUB, LANES), jnp.float32),
    ]


vmem = pl.BlockSpec(memory_space=pltpu.VMEM)
smem = pl.BlockSpec(memory_space=pltpu.SMEM)
f32 = lambda *s: jax.ShapeDtypeStruct(s, jnp.float32)
params = pltpu.CompilerParams(vmem_limit_bytes=VMEM_LIMIT)
cost = pl.CostEstimate(flops=9_000_000_000, bytes_accessed=29_000_000, transcendentals=0)


def first_step(plan, level, operands):
    n, radius, own_cells, total, moved = plan

    def kernel(place, own, near, far, side, corner, spin, pick, near_out, far_out, *scratch):
        refs = (place, own, side.at[level], near, corner.at[level], far, spin, pick)
        step_kernel(plan, refs, ToMessage(near_out, far_out, own_cells), scratch)

    return pl.pallas_call(
        kernel,
        out_shape=[f32(FIELDS * own_cells + EXTRA, radius), f32(FIELDS * own_cells, LANES)],
        in_specs=[smem] + [vmem] * 7,
        out_specs=[vmem] * 2,
        scratch_shapes=step_scratch(n),
        compiler_params=params,
        cost_estimate=cost,
        name="first_step",
    )(*operands)


def last_step(plan, level, operands, done, levels):
    n, radius, own_cells, total, moved = plan
    final = level == levels - 1
    tail = pl.ds(FIELDS * own_cells, EXTRA)
    buffer = f32(FIELDS * own_cells, radius)

    def kernel(place, own, near, far, spin, pick, *rest):
        refs = (place, own, own.at[tail, :], near, near.at[tail, :], far, spin, pick)
        if not final:
            step_kernel(plan, refs, ToBuffer(rest[0]), rest[1:])
            return
        ready, outs, scratch = rest[: levels - 1], rest[levels - 1 : levels + 2], rest[levels + 2 :]
        last, sent = scratch[-2:]
        copies = []
        for k, x in enumerate(ready):
            copies += copies_out(k, x, outs, sent)
        for copy in copies:
            copy.start()
        step_kernel(plan, refs, ToBuffer(last), scratch[:-2])
        rest_of = copies_out(level, last, outs, sent)
        for copy in rest_of:
            copy.start()
        for copy in copies + rest_of:
            copy.wait()

    if final:
        out_shape = [f32(levels, own_cells, radius), f32(2, levels, own_cells, radius), f32(2, levels, own_cells, radius)]
        more = [pltpu.VMEM((FIELDS * own_cells, radius), jnp.float32), pltpu.SemaphoreType.DMA((levels * FIELDS,))]
    else:
        out_shape = buffer
        more = []
    return pl.pallas_call(
        kernel,
        out_shape=out_shape,
        in_specs=[smem] + [vmem] * (5 + len(done)),
        out_specs=[pl.BlockSpec(memory_space=pltpu.HBM)] * 3 if final else vmem,
        scratch_shapes=step_scratch(n) + more,
        compiler_params=params,
        cost_estimate=cost,
        name="last_step",
    )(*operands, *done)


def body(density, momentum, magnetic, rotation, shifts):
    phi_count = lax.axis_size("phi")
    row_count = lax.axis_size("row")
    levels, own_cells, radius = density.shape
    total = radius * row_count
    parts = radius // LANES
    n = radius // SLOTS
    need = [max(shift_bound(k * HALF, total) + REACH - own_cells, 0) for k in range(radius // HALF)]
    assert row_count == 2 and radius == 2 * LANES and own_cells == HALF // 2
    assert need[0] <= own_cells and need[1] <= own_cells - SUB - 2 and need[2] <= SUB + 1 and need[3] <= 1

    row = lax.axis_index("row")
    place = jnp.reshape(row, (1,)).astype(jnp.int32)
    send_near = lambda x: lax.ppermute(x, "phi", [(p, (p + 1) % phi_count) for p in range(phi_count)])
    send_far = lambda x: lax.ppermute(x, "phi", [(p, (p + 2) % phi_count) for p in range(phi_count)])
    here = lambda p, r: (p % phi_count) * row_count + r
    diagonal = [(here(p, r), here(p + 1, 1 - r)) for p in range(phi_count) for r in range(row_count)]
    send_corner = lambda x: lax.ppermute(x, ("phi", "row"), diagonal)
    send_side = lambda x: lax.ppermute(x, "row", [(0, 1), (1, 0)])

    spins, turns = rotation.reshape(parts, LANES), shifts.reshape(parts, LANES)
    near_message = f32(FIELDS * own_cells, radius)
    far_message = f32(FIELDS * own_cells, LANES)
    edge = pl.pallas_call(
        edge_kernel,
        out_shape=f32(levels, EXTRA, 2 * LANES),
        in_specs=[smem] + [pl.BlockSpec(memory_space=pltpu.HBM)] * 5,
        out_specs=vmem,
        scratch_shapes=[
            pltpu.VMEM((levels, FIELDS * own_cells, LANES), jnp.float32),
            pltpu.VMEM((parts, LANES), jnp.float32),
            pltpu.VMEM((parts, LANES), jnp.int32),
            pltpu.SemaphoreType.DMA((levels * FIELDS + 2,)),
        ],
        compiler_params=pltpu.CompilerParams(vmem_limit_bytes=EDGE_LIMIT),
        name="edges",
    )(place, density, momentum, magnetic, spins, turns)
    packed = pl.pallas_call(
        lambda *refs: pack_kernel(levels, *refs),
        out_shape=[near_message] * levels + [far_message] * levels,
        in_specs=[vmem] * 3 + [pl.BlockSpec(memory_space=pl.ANY)],
        out_specs=[vmem] * (2 * levels),
        compiler_params=params,
        cost_estimate=cost,
        name="pack",
    )(density, momentum, magnetic, edge)
    owns, fars = packed[:levels], packed[levels:]
    side = send_side(edge)
    corner = send_corner(edge)
    wide = (n + 1, radius, own_cells, total, EXTRA)
    plain = (n, radius, own_cells, total, 0)
    i32 = jax.ShapeDtypeStruct((TALL * SUB, LANES), jnp.int32)
    tables = pl.pallas_call(
        lambda *refs: table_kernel((wide, plain), *refs),
        out_shape=[f32(TALL * SUB, LANES), i32] * 2,
        in_specs=[smem] + [vmem] * 3,
        out_specs=[vmem] * 4,
        scratch_shapes=[pltpu.VMEM((4, tall_of(n + 1), LANES), jnp.float32)],
        compiler_params=params,
        name="tables",
    )(place, side, spins, turns)
    moved = []
    for own, far in zip(owns, fars):
        if moved:
            own, far, _ = lax.optimization_barrier((own, far, side))
        moved.append((send_near(own), send_far(far)))
    states = []
    for level in range(levels):
        near, far = moved[level]
        states.append(first_step(wide, level, (place, owns[level], near, far, side, corner, *tables[:2])))
    moved = [(send_near(own), send_far(far)) for own, far in states]
    done = ()
    for level in range(levels):
        near, far = moved[level]
        operands = (place, states[level][0], near, far, *tables[2:])
        result = last_step(plain, level, operands, done if level == levels - 1 else (), levels)
        done += (result,)
    return tuple(result)


def solution(mesh):
    placed = (
        P(None, "phi", "row"),
        P(None, None, "phi", "row"),
        P(None, None, "phi", "row"),
        P("row"),
        P("row"),
    )
    return jax.shard_map(
        body,
        mesh=mesh,
        in_specs=placed,
        out_specs=(P(None, "phi", "row"), P(None, None, "phi", "row"), P(None, None, "phi", "row")),
        check_vma=False,
    )
```
